32 devices in a mesh: dp: 8 (over z, x), seq: 4 (over y, core).
Axes of the slice: x: 2, y: 2, z: 4, core: 2. Of those that a mesh axis runs over, the one named last changes fastest.
Arguments:
- block_input: bfloat16 [40, 1024, 256], P('dp', 'seq'), may hold values from -6 to 6
- embedding: bfloat16 [40, 1024, 256], P('dp', 'seq'), may hold values from -6 to 6
- cotangent: bfloat16 [40, 1024, 256], P('dp', 'seq'), may hold values from -6 to 6
- qkv_weight: bfloat16 [2, 256, 768], replicated, may hold values from -0.375 to 0.375
- out_weight: bfloat16 [2, 256, 256], replicated, may hold values from -1 to 1
- out_bias: float32 [2, 256], replicated, may hold values from -1.75 to 1.75
- up_weight: bfloat16 [2, 256, 1024], replicated, may hold values from -0.375 to 0.375
- up_bias: float32 [2, 1024], replicated, may hold values from -1.75 to 1.75
- down_weight: bfloat16 [2, 1024, 256], replicated, may hold values from -0.1875 to 0.1875
- down_bias: float32 [2, 256], replicated, may hold values from -1.75 to 1.75
- norm_gain: float32 [2, 2, 256], replicated, may hold values from 0.25 to 1.75
- norm_shift: float32 [2, 2, 256], replicated, may hold values from -1.75 to 1.75
- seg_lengths: int32 [40, 16], P('dp'), may hold values from 1 to 1009, as said below
- loop_counts: int32 [40], P('dp'), may hold values from 1 to 2
- token_counts: int32 [40], P('dp'), may hold values from 128 to 1024
Outputs:
- block_output: bfloat16 [40, 1024, 256], P('dp', 'seq')
- input_grad: float32 [40, 1024, 256], P('dp', 'seq')
- embed_grad: float32 [40, 1024, 256], P('dp', 'seq')
- grad_qkv: float32 [2, 256, 768], replicated
- grad_out_weight: float32 [2, 256, 256], replicated
- grad_out_bias: float32 [2, 256], replicated
- grad_up_weight: float32 [2, 256, 1024], replicated
- grad_up_bias: float32 [2, 1024], replicated
- grad_down_weight: float32 [2, 1024, 256], replicated
- grad_down_bias: float32 [2, 256], replicated
- grad_gain: float32 [2, 2, 256], replicated
- grad_shift: float32 [2, 2, 256], replicated
The draws below stay inside these ranges and needn't reach their ends.
Inputs may be any that keep to these rules, and one draw needn't show every extreme that they name: `seg_lengths`: each row's 16 lengths sum to 1024.
All inputs are finite; a program needn't handle non-finite values.
Results may differ from the reference program's by a relative error of at most 0.014.
Values may be sent and summed in bfloat16 or wider, within the bound.
No kernel may reach another device: no remote copies, remote signals or barrier semaphores. Data moves between devices by JAX's collectives and lax.ppermute only.
A program may use at most 256 MiB of HBM per device.

```python
import jax
import jax.numpy as jnp
from jax import lax

D = 256
H = 4
HD = 64
FF = 1024
LAYERS = 2
ROW_LEN = 1024
NSEG = 16
ROWS_DEV = 5
ROWS = 40


def draw_seg_lengths(key, part):
    key = jax.random.fold_in(key, 11)
    pick_key, cut_key = jax.random.split(key)
    row_ids = jnp.arange(ROWS, dtype=jnp.int32)
    chosen = jax.random.randint(pick_key, (ROWS // ROWS_DEV,), 0, ROWS_DEV)
    spanning = row_ids % ROWS_DEV == chosen[row_ids // ROWS_DEV]

    def one_row(row_key):
        cut_points = jnp.sort(jax.random.permutation(row_key, ROW_LEN - 1)[:NSEG - 1] + 1).astype(jnp.int32)
        boundary = jnp.concatenate([jnp.zeros((1,), jnp.int32), cut_points, jnp.full((1,), ROW_LEN, jnp.int32)])
        return boundary[1:] - boundary[:-1]
    random_rows = jax.vmap(one_row)(jax.random.split(cut_key, ROWS))
    long_row = jnp.concatenate([jnp.full((1,), ROW_LEN - NSEG + 1, jnp.int32), jnp.ones((NSEG - 1,), jnp.int32)])
    return jnp.where(spanning[:, None], long_row[None, :], random_rows).astype(jnp.int32)


def draw_loop_counts(key, part):
    key = jax.random.fold_in(key, 23)
    row_ids = jnp.arange(ROWS, dtype=jnp.int32)
    group_ids = row_ids // ROWS_DEV
    ticket = jax.random.randint(key, (ROWS,), 0, ROWS // ROWS_DEV)
    counts = 1 + (ticket <= group_ids).astype(jnp.int32)
    return jnp.where(row_ids == 0, 1, counts).astype(jnp.int32)


def draw_token_counts(key, part):
    key = jax.random.fold_in(key, 37)
    row_ids = jnp.arange(ROWS, dtype=jnp.int32)
    group_ids = row_ids // ROWS_DEV
    last_group = max(ROWS // ROWS_DEV - 1, 1)
    base_len = ROW_LEN // 4 + 3 * ROW_LEN // 4 * group_ids // last_group
    jitter = jax.random.randint(key, (ROWS,), -(ROW_LEN // 8), ROW_LEN // 8 + 1)
    counts = jnp.clip(base_len + jitter, ROW_LEN // 8, ROW_LEN)
    counts = jnp.where(row_ids == 0, ROW_LEN // 8, counts)
    counts = jnp.where(row_ids == ROWS - 1, ROW_LEN, counts)
    return counts.astype(jnp.int32)


def block_scale(stream_key, extent, cuts, smallest, largest):
    def one(axis_at, blocks):
        heights = jax.random.uniform(jax.random.fold_in(jax.random.fold_in(stream_key, 6), axis_at), (blocks,), jnp.float32, smallest / len(cuts), largest / len(cuts))
        return jnp.repeat(jnp.exp(heights), extent[axis_at] // blocks).reshape((-1,) + (1,) * (len(extent) - axis_at - 1))

    level = one(*cuts[0])
    for cut in cuts[1:]:
        level = level * one(*cut)
    return level


def centred(rng, extent, width, bound, shards=(), held_as=jnp.bfloat16):
    result = width * jax.random.normal(rng, extent, jnp.float32)
    if shards:
        result = result * block_scale(rng, extent, shards, -0.22, 0.18)
    return jnp.clip(result, -bound, bound).astype(held_as)


def setup_inputs(seed: int = 0) -> dict:
    seeds = jax.random.split(jax.random.key(seed), 16)
    block_input = centred(seeds[0], (ROWS, ROW_LEN, D), 1.0, 6.0, ((0, 8), (1, 4)))
    embedding = centred(seeds[1], (ROWS, ROW_LEN, D), 1.0, 6.0, ((0, 8), (1, 4)))
    cotangent = centred(seeds[2], (ROWS, ROW_LEN, D), 1.0, 6.0, ((0, 8), (1, 4)))
    qkv_weight = centred(seeds[3], (LAYERS, D, 3 * D), D ** -0.5, 0.375)
    out_weight = centred(seeds[4], (LAYERS, D, D), (D // 8) ** -0.5, 1.0)
    out_bias = centred(seeds[5], (LAYERS, D), 0.3, 1.75, (), jnp.float32)
    up_weight = centred(seeds[6], (LAYERS, D, FF), D ** -0.5, 0.375)
    up_bias = centred(seeds[7], (LAYERS, FF), 0.3, 1.75, (), jnp.float32)
    down_weight = centred(seeds[8], (LAYERS, FF, D), FF ** -0.5, 0.1875)
    down_bias = centred(seeds[9], (LAYERS, D), 0.3, 1.75, (), jnp.float32)
    norm_gain = jnp.clip(1.0 + 0.15 * jax.random.normal(seeds[10], (LAYERS, 2, D), jnp.float32), 0.25, 1.75)
    norm_shift = centred(seeds[11], (LAYERS, 2, D), 0.3, 1.75, (), jnp.float32)
    seg_lengths = draw_seg_lengths(jax.random.fold_in(seeds[15], 71), 0)
    loop_counts = draw_loop_counts(jax.random.fold_in(seeds[15], 71), 0)
    token_counts = draw_token_counts(jax.random.fold_in(seeds[15], 71), 0)
    return {"block_input": block_input, "embedding": embedding, "cotangent": cotangent, "qkv_weight": qkv_weight, "out_weight": out_weight, "out_bias": out_bias, "up_weight": up_weight, "up_bias": up_bias, "down_weight": down_weight, "down_bias": down_bias, "norm_gain": norm_gain, "norm_shift": norm_shift, "seg_lengths": seg_lengths, "loop_counts": loop_counts, "token_counts": token_counts}


NORM_EPS = 1e-05
MASKED = -1e+30

@jax.custom_vjp
def low(v):
    return lax.optimization_barrier(v.astype(jnp.bfloat16)).astype(jnp.float32)

@jax.custom_vjp
def low_back(v):
    return v

def low_keep(v):
    return (low(v), None)

def low_pass(kept, grad):
    return (grad,)

def back_keep(v):
    return (v, None)

def back_low(kept, grad):
    return (low(grad),)
low.defvjp(low_keep, low_pass)
low_back.defvjp(back_keep, back_low)

def layer_norm(values, gain, shift):
    center = values - lax.optimization_barrier(jnp.mean(values, axis=-1, keepdims=True))
    spread = lax.optimization_barrier(jnp.mean(center * center, axis=-1, keepdims=True))
    return center * lax.rsqrt(spread + NORM_EPS) * gain + shift

def gelu_exact(values):
    return jax.nn.gelu(values, approximate=False)

def product(left_side, right_side):
    return jnp.dot(left_side, right_side, precision=lax.Precision.HIGHEST)

def block_layer(current, allowed, weights):
    qkv_weight, out_weight, out_bias, up_weight, up_bias, down_weight, down_bias, norm_gain, norm_shift = weights
    token_total = current.shape[0]
    normed = low(layer_norm(current, norm_gain[0], norm_shift[0]))
    packed = low(low_back(product(normed, qkv_weight)))
    queries = packed[:, :D].reshape(token_total, H, HD)
    key_rows = packed[:, D:2 * D].reshape(token_total, H, HD)
    value_rows = packed[:, 2 * D:].reshape(token_total, H, HD)
    scores = jnp.einsum('qhd,khd->hqk', queries, key_rows, precision=lax.Precision.HIGHEST) * HD ** (-0.5)
    scores = jnp.where(allowed[None], low_back(scores), MASKED)
    attn_probs = low(jax.nn.softmax(scores, axis=-1))
    blended = jnp.einsum('hqk,khd->qhd', attn_probs, value_rows, precision=lax.Precision.HIGHEST).reshape(token_total, D)
    blended = low(low_back(blended))
    middle = current + low_back(product(blended, out_weight)) + out_bias
    normed_two = low(layer_norm(middle, norm_gain[1], norm_shift[1]))
    up_proj = low_back(product(normed_two, up_weight) + up_bias)
    active = low(gelu_exact(up_proj))
    return middle + low_back(product(active, down_weight)) + down_bias

def run_row(params, initial, inject, seg_row, loop_row):
    positions = jnp.arange(ROW_LEN, dtype=jnp.int32)
    allowed = (seg_row[:, None] == seg_row[None, :]) & (positions[None, :] <= positions[:, None])
    current = initial
    finals = []
    for repeat in range(2):
        current = current + inject
        for layer_index in range(LAYERS):
            current = block_layer(current, allowed, tuple((member[layer_index] for member in params)))
        finals.append(current)
    return jnp.where(loop_row == 2, finals[1], finals[0])

def reference(block_input, embedding, cotangent, qkv_weight, out_weight, out_bias, up_weight, up_bias, down_weight, down_bias, norm_gain, norm_shift, seg_lengths, loop_counts, token_counts):
    params = tuple((member.astype(jnp.float32) for member in (qkv_weight, out_weight, out_bias, up_weight, up_bias, down_weight, down_bias, norm_gain, norm_shift)))
    positions = jnp.arange(ROW_LEN, dtype=jnp.int32)
    seg_ends = jnp.cumsum(seg_lengths, axis=-1).astype(jnp.int32)
    seg_ids = lax.optimization_barrier(jnp.sum((seg_ends[:, None, :] <= positions[None, :, None]).astype(jnp.int32), axis=-1))

    def forward(weights, initial, inject):

        def row_step(carry, inputs):
            return (carry, run_row(weights, inputs[0], inputs[1], inputs[2], inputs[3]))
        _, outputs = lax.scan(jax.checkpoint(row_step), jnp.zeros((), jnp.float32), (initial, inject, seg_ids, loop_counts))
        return outputs
    outputs, pullback = jax.vjp(forward, params, block_input.astype(jnp.float32), embedding.astype(jnp.float32))
    row_weight = token_counts.astype(jnp.float32) / ROW_LEN
    grad_params, grad_input, grad_embed = pullback(cotangent.astype(jnp.float32) * row_weight[:, None, None])
    total = jnp.sum(token_counts).astype(jnp.float32)
    input_scale = ROWS * ROW_LEN / total
    weight_scale = ROW_LEN / total
    scaled = tuple((member * weight_scale for member in grad_params))
    return (outputs.astype(jnp.bfloat16), grad_input * input_scale, grad_embed * input_scale, scaled[0], scaled[1], scaled[2], scaled[3], scaled[4], scaled[5], scaled[6], scaled[7], scaled[8])
```

```python
import functools

import jax
import jax.numpy as jnp
from jax import lax
from jax.experimental import pallas as pl
from jax.experimental.pallas import tpu as pltpu
from jax.sharding import PartitionSpec as P

H = 4
LAYERS = 2


NORM_EPS = 1e-05
MASKED = -1e30


def layer_norm(values, gain, shift):
    center = values - jnp.mean(values, axis=-1, keepdims=True)
    spread = jnp.mean(center * center, axis=-1, keepdims=True)
    return center * lax.rsqrt(spread + NORM_EPS) * gain + shift


def gelu_exact(values):
    return jax.nn.gelu(values, approximate=False)


def matmul(left_side, right_side):
    return jnp.dot(left_side, right_side, preferred_element_type=jnp.float32)


def left_dot(left_side, right_side):
    return lax.dot_general(
        left_side, right_side, (((0,), (0,)), ((), ())), preferred_element_type=jnp.float32
    )


def right_dot(left_side, right_side):
    return lax.dot_general(
        left_side, right_side, (((1,), (1,)), ((), ())), preferred_element_type=jnp.float32
    )


def split_heads(packed, head_count):
    return packed.reshape(packed.shape[0], head_count, packed.shape[1] // head_count)


def attend_forward(queries, key_vals, allowed, head_count, score_scale):
    model_width = queries.shape[1]
    key_rows = split_heads(key_vals[:, :model_width], head_count)
    value_rows = split_heads(key_vals[:, model_width:], head_count)
    scores = (
        jnp.einsum(
            "qhd,khd->hqk",
            split_heads(queries, head_count),
            key_rows,
            preferred_element_type=jnp.float32,
        )
        * score_scale
    )
    scores = jnp.where(allowed[None], scores, MASKED)
    row_max = jnp.max(scores, axis=-1, keepdims=True)
    shifted_exp = jnp.exp(scores - row_max)
    row_total = jnp.sum(shifted_exp, axis=-1, keepdims=True)
    attn_probs = (shifted_exp / row_total).astype(jnp.bfloat16)
    blended = jnp.einsum("hqk,khd->qhd", attn_probs, value_rows, preferred_element_type=jnp.float32)
    return (blended.reshape(queries.shape[0], model_width), (row_max + jnp.log(row_total))[..., 0])


def attention_core(
    query_part, key_part, value_part, grad_part, allowed_part, logsum_part, head_count, score_scale
):
    scores = (
        jnp.einsum(
            "qhd,khd->hqk",
            split_heads(query_part, head_count),
            split_heads(key_part, head_count),
            preferred_element_type=jnp.float32,
        )
        * score_scale
    )
    scores = jnp.where(allowed_part[None], scores, MASKED)
    attn_probs = jnp.exp(scores - logsum_part[..., None])
    grad_probs = jnp.einsum(
        "qhd,khd->hqk",
        split_heads(grad_part, head_count),
        split_heads(value_part, head_count),
        preferred_element_type=jnp.float32,
    )
    return (attn_probs, grad_probs)


def query_grads(grad_scores, key_part, head_count, score_scale):
    result = (
        jnp.einsum(
            "hqk,khd->qhd",
            grad_scores,
            split_heads(key_part, head_count),
            preferred_element_type=jnp.float32,
        )
        * score_scale
    )
    return result.reshape(result.shape[0], -1)


def keyval_grads(grad_scores, attn_probs, query_part, grad_part, head_count, score_scale):
    grad_keys = (
        jnp.einsum(
            "hqk,qhd->khd",
            grad_scores,
            split_heads(query_part, head_count),
            preferred_element_type=jnp.float32,
        )
        * score_scale
    )
    grad_values = jnp.einsum(
        "hqk,qhd->khd",
        attn_probs.astype(jnp.bfloat16),
        split_heads(grad_part, head_count),
        preferred_element_type=jnp.float32,
    )
    return jnp.concatenate(
        [grad_keys.reshape(grad_keys.shape[0], -1), grad_values.reshape(grad_values.shape[0], -1)],
        axis=-1,
    )


def on_device(
    block_input,
    embedding,
    cotangent,
    qkv_weight,
    out_weight,
    out_bias,
    up_weight,
    up_bias,
    down_weight,
    down_bias,
    norm_gain,
    norm_shift,
    seg_lengths,
    loop_counts,
    token_counts,
):
    row_count, block_len, model_width = block_input.shape
    head_count = H
    score_scale = (model_width // head_count) ** (-0.5)
    row_len = block_len * lax.axis_size("seq")
    flat_rows = row_count * block_len
    offset = lax.axis_index("seq") * block_len
    key_pos = jnp.arange(row_len, dtype=jnp.int32)
    own_pos = offset + jnp.arange(block_len, dtype=jnp.int32)
    seg_ends = jnp.cumsum(seg_lengths, axis=-1)
    seg_all = jnp.sum((seg_ends[:, None, :] <= key_pos[None, :, None]).astype(jnp.int32), axis=-1)
    seg_own = lax.dynamic_slice_in_dim(seg_all, offset, block_len, 1)
    allowed = (seg_own[:, :, None] == seg_all[:, None, :]) & (
        key_pos[None, None, :] <= own_pos[None, :, None]
    )
    current = block_input.astype(jnp.float32)
    inject = embedding.astype(jnp.float32)
    stored = []
    finals = []
    for repeat in range(2):
        current = current + inject
        for layer_index in range(LAYERS):
            forward_normed = layer_norm(
                current, norm_gain[layer_index, 0], norm_shift[layer_index, 0]
            ).astype(jnp.bfloat16)
            forward_packed = matmul(
                forward_normed.reshape(flat_rows, model_width), qkv_weight[layer_index]
            ).astype(jnp.bfloat16)
            forward_packed = forward_packed.reshape(row_count, block_len, 3 * model_width)
            forward_key_vals = lax.all_gather(
                forward_packed[:, :, model_width:], "seq", axis=1, tiled=True
            )

            def forward_row(inputs):
                return attend_forward(inputs[0], inputs[1], inputs[2], head_count, score_scale)

            forward_blended, forward_logsum = lax.map(
                forward_row, (forward_packed[:, :, :model_width], forward_key_vals, allowed)
            )
            forward_blended = forward_blended.astype(jnp.bfloat16)
            branch_out = matmul(
                forward_blended.reshape(flat_rows, model_width), out_weight[layer_index]
            ).reshape(row_count, block_len, model_width)
            forward_middle = current + branch_out + out_bias[layer_index]
            forward_normed_two = layer_norm(
                forward_middle, norm_gain[layer_index, 1], norm_shift[layer_index, 1]
            ).astype(jnp.bfloat16)
            forward_up_proj = (
                matmul(forward_normed_two.reshape(flat_rows, model_width), up_weight[layer_index])
                + up_bias[layer_index]
            )
            forward_active = gelu_exact(forward_up_proj).astype(jnp.bfloat16)
            result = (
                forward_middle
                + matmul(forward_active, down_weight[layer_index]).reshape(
                    row_count, block_len, model_width
                )
                + down_bias[layer_index]
            )
            current, stored_layer = (
                result,
                (
                    current,
                    forward_normed,
                    forward_packed,
                    forward_key_vals,
                    forward_logsum,
                    forward_blended,
                    forward_middle,
                    forward_normed_two,
                    forward_up_proj,
                    forward_active,
                ),
            )
            stored.append(stored_layer)
        finals.append(current)
    two_loops = (loop_counts == 2)[:, None, None]
    block_output = jnp.where(two_loops, finals[1], finals[0]).astype(jnp.bfloat16)
    row_weight = token_counts.astype(jnp.float32) / row_len
    grad_top = cotangent.astype(jnp.float32) * row_weight[:, None, None]
    grad_state = jnp.where(two_loops, grad_top, 0.0)
    layer_sums = [None] * LAYERS
    second_pass = grad_state
    for repeat in (1, 0):
        for layer_index in reversed(range(LAYERS)):
            backward_stored_layer = stored[repeat * LAYERS + layer_index]
            (
                backward_current,
                normed,
                packed,
                key_vals,
                logsum,
                blended,
                middle,
                normed_two,
                up_proj,
                active,
            ) = backward_stored_layer
            grad_flat = grad_state.reshape(flat_rows, model_width)
            grad_low = grad_flat.astype(jnp.bfloat16)
            grad_down = left_dot(active, grad_low)
            grad_down_bias = jnp.sum(grad_flat, axis=0)
            grad_active = right_dot(grad_low, down_weight[layer_index])
            grad_up_proj = jax.vjp(gelu_exact, up_proj)[1](grad_active)[0].astype(jnp.bfloat16)
            grad_up_bias = jnp.sum(grad_up_proj.astype(jnp.float32), axis=0)
            grad_up = left_dot(normed_two.reshape(flat_rows, model_width), grad_up_proj)
            grad_normed_two = right_dot(grad_up_proj, up_weight[layer_index]).reshape(
                row_count, block_len, model_width
            )
            pull_two = jax.vjp(
                layer_norm, middle, norm_gain[layer_index, 1], norm_shift[layer_index, 1]
            )[1]
            grad_middle, gain_two, shift_two = pull_two(grad_normed_two)
            grad_middle = grad_middle + grad_state
            middle_flat = grad_middle.reshape(flat_rows, model_width)
            middle_low = middle_flat.astype(jnp.bfloat16)
            grad_out = left_dot(blended.reshape(flat_rows, model_width), middle_low)
            grad_out_bias = jnp.sum(middle_flat, axis=0)
            grad_blend = (
                right_dot(middle_low, out_weight[layer_index])
                .astype(jnp.bfloat16)
                .reshape(row_count, block_len, model_width)
            )
            queries = packed[:, :, :model_width]

            def full_row(inputs):
                query_part, keyval_part, grad_part, allowed_part, logsum_part = inputs
                attn_probs, grad_probs = attention_core(
                    query_part,
                    keyval_part[:, :model_width],
                    keyval_part[:, model_width:],
                    grad_part,
                    allowed_part,
                    logsum_part,
                    head_count,
                    score_scale,
                )
                row_delta = jnp.sum(attn_probs * grad_probs, axis=-1, keepdims=True)
                grad_scores = (attn_probs * (grad_probs - row_delta)).astype(jnp.bfloat16)
                return (
                    query_grads(grad_scores, keyval_part[:, :model_width], head_count, score_scale),
                    keyval_grads(
                        grad_scores, attn_probs, query_part, grad_part, head_count, score_scale
                    ),
                )

            grad_query, partial_kv = lax.map(
                full_row, (queries, key_vals, grad_blend, allowed, logsum)
            )
            grad_keyval = lax.psum_scatter(
                partial_kv.astype(jnp.bfloat16), "seq", scatter_dimension=1, tiled=True
            )
            grad_packed = jnp.concatenate(
                [grad_query.astype(jnp.bfloat16), grad_keyval], axis=-1
            ).reshape(flat_rows, 3 * model_width)
            grad_qkv = left_dot(normed.reshape(flat_rows, model_width), grad_packed)
            grad_normed = right_dot(grad_packed, qkv_weight[layer_index]).reshape(
                row_count, block_len, model_width
            )
            pull_one = jax.vjp(
                layer_norm, backward_current, norm_gain[layer_index, 0], norm_shift[layer_index, 0]
            )[1]
            grad_current, gain_one, shift_one = pull_one(grad_normed)
            grad_current = grad_current + grad_middle
            grad_state = grad_current
            grad_set = (
                grad_qkv,
                grad_out,
                grad_out_bias,
                grad_up,
                grad_up_bias,
                grad_down,
                grad_down_bias,
                jnp.stack([gain_one, gain_two]),
                jnp.stack([shift_one, shift_two]),
            )
            if repeat == 1:
                layer_sums[layer_index] = grad_set
            else:
                layer_sums[layer_index] = jax.tree.map(jnp.add, layer_sums[layer_index], grad_set)
        if repeat == 1:
            second_pass = grad_state
            grad_state = jnp.where(two_loops, grad_state, grad_top)
    grad_embed = grad_state + second_pass
    stacked = jax.tree.map(lambda *members: jnp.stack(members), *layer_sums)
    (
        sum_qkv,
        sum_out,
        sum_out_bias,
        sum_up,
        sum_up_bias,
        sum_down,
        sum_down_bias,
        sum_gain,
        sum_shift,
    ) = stacked
    total = lax.psum(jnp.sum(token_counts), "dp").astype(jnp.float32)
    summed = lax.psum(
        (
            sum_qkv,
            sum_out,
            sum_out_bias,
            sum_up,
            sum_up_bias,
            sum_down,
            sum_down_bias,
            sum_gain,
            sum_shift,
        ),
        ("dp", "seq"),
    )
    input_scale = row_count * lax.axis_size("dp") * row_len / total
    weight_scale = row_len / total
    return (
        block_output,
        grad_state * input_scale,
        grad_embed * input_scale,
        summed[0] * weight_scale,
        summed[1] * weight_scale,
        summed[2] * weight_scale,
        summed[3] * weight_scale,
        summed[4] * weight_scale,
        summed[5] * weight_scale,
        summed[6] * weight_scale,
        summed[7] * weight_scale,
        summed[8] * weight_scale,
    )


BF = jnp.bfloat16
F32 = jnp.float32
ERF_TERMS = (
    7.97884941e-01,
    3.63330844e-02,
    -3.25947475e-05,
    -5.53063153e-05,
    3.96477285e-06,
    -1.32266251e-07,
    1.75627657e-09,
)
INV_SQRT_2PI = 0.3989422804014327
VMEM_LIMIT = 56 * 1024 * 1024
ONES_ROWS = 16


def dot_nn(left_side, right_side):
    return jnp.dot(left_side, right_side, preferred_element_type=F32)


def dot_nt(left_side, right_side):
    return lax.dot_general(
        left_side, right_side, (((1,), (1,)), ((), ())), preferred_element_type=F32
    )


def widen(block, width):
    return jnp.concatenate([block] * (width // block.shape[1]), axis=1)


def gelu_and_slope(z):
    square = z * z
    clipped = jnp.minimum(square, 64.0)
    series = jnp.full_like(z, ERF_TERMS[-1])
    for term in ERF_TERMS[-2::-1]:
        series = series * clipped + term
    cdf = 0.5 + 0.5 * jnp.tanh(z * series)
    density = jnp.exp(square * -0.5) * INV_SQRT_2PI
    return z * cdf, cdf + z * density


def norm_forward(values, gain, shift):
    center = values - jnp.mean(values, axis=0, keepdims=True)
    spread = jnp.mean(center * center, axis=0, keepdims=True)
    inverse = lax.rsqrt(spread + NORM_EPS)
    unit = center * inverse
    return unit, inverse, (unit * gain + shift).astype(BF)


def norm_backward(grad, unit, inverse, gain):
    scaled = grad * gain
    first = jnp.mean(scaled, axis=0, keepdims=True)
    second = jnp.mean(scaled * unit, axis=0, keepdims=True)
    return inverse * (scaled - first - unit * second)


def vec_part(vec, index, width, size):
    return widen(vec[0, index * width : index * width + size, :], width)


def project_qkv(state, qkv_t, vec, pre, kv, stat, scale):
    width = state.shape[0]
    tokens = state.shape[1]
    gain = widen(vec[0, 2 * width : 3 * width, :], tokens)
    shift = widen(vec[0, 3 * width : 4 * width, :], tokens)
    unit, inverse, normed = norm_forward(state, gain, shift)
    pre[0:width, :] = normed
    pre[2 * width : 3 * width, :] = unit.astype(BF)
    pre[width : 2 * width, :] = (dot_nn(qkv_t[0, 0:width, :], normed) * scale).astype(BF)
    kv[0:width, :] = dot_nn(qkv_t[0, width : 2 * width, :], normed).astype(BF)
    kv[width : 2 * width, :] = dot_nn(qkv_t[0, 2 * width : 3 * width, :], normed).astype(BF)
    stat[0:1, :] = inverse


def pad_head(block, odd):
    blank = jnp.zeros_like(block)
    return jnp.concatenate([blank, block] if odd else [block, blank], axis=0)


def tile_bias(first_key, start, causal, shape):
    key_at = lax.broadcasted_iota(jnp.int32, shape, 0)
    keep = key_at + first_key >= start
    if causal:
        keep = keep & (key_at <= lax.broadcasted_iota(jnp.int32, shape, 1))
    return jnp.where(keep, 0.0, MASKED)


def attend_chunk(queries, keys, values_t, chunk, low, start, bias, total, stat, blended):
    width, tokens = queries.shape
    head = width // H
    pair = 2 * head

    def scores(j, h):
        lanes = pl.ds((h // 2) * pair, pair)
        return dot_nn(keys[j, :, lanes], pad_head(queries[h * head : (h + 1) * head, :], h % 2)) + bias[...]

    bias[...] = tile_bias(chunk * tokens, start, True, (tokens, tokens))
    tops, sums = [], []
    for h in range(H):
        part = scores(chunk, h)
        top = jnp.max(part, axis=0, keepdims=True)
        weight = jnp.exp(part - top)
        tops.append(top)
        sums.append(jnp.sum(weight, axis=0, keepdims=True))
        rows = slice(h * head, (h + 1) * head)
        total[rows, :] = dot_nn(values_t[chunk, rows, :], weight.astype(BF))

    def step(j, carry):
        tops, sums = carry
        bias[...] = tile_bias(j * tokens, start, False, (tokens, tokens))
        new_tops, new_sums = [], []
        for h in range(H):
            part = scores(j, h)
            top = jnp.maximum(tops[h], jnp.max(part, axis=0, keepdims=True))
            fade = jnp.exp(tops[h] - top)
            weight = jnp.exp(part - top)
            new_tops.append(top)
            new_sums.append(sums[h] * fade + jnp.sum(weight, axis=0, keepdims=True))
            rows = slice(h * head, (h + 1) * head)
            total[rows, :] = total[rows, :] * fade + dot_nn(
                values_t[j, rows, :], weight.astype(BF)
            )
        return tuple(new_tops), tuple(new_sums)

    tops, sums = lax.fori_loop(low, chunk, step, (tuple(tops), tuple(sums)))
    for h in range(H):
        rows = slice(h * head, (h + 1) * head)
        blended[rows, :] = (total[rows, :] / sums[h]).astype(BF)
        stat[h : h + 1, :] = tops[h] + jnp.log(sums[h])


def finish_layer(state, out_t, up_t, down_t, vec, post, stat):
    width, tokens = state.shape
    hidden = up_t.shape[1]
    middle = (
        state + dot_nn(out_t[0], post[0:width, :]) + widen(vec[0, 0:width, :], tokens)
    )
    gain = widen(vec[0, 4 * width : 5 * width, :], tokens)
    shift = widen(vec[0, 5 * width : 6 * width, :], tokens)
    unit, inverse, normed = norm_forward(middle, gain, shift)
    post[width : 2 * width, :] = normed
    post[2 * width : 3 * width, :] = unit.astype(BF)
    stat[H : H + 1, :] = inverse
    block = 128
    for first in range(0, hidden, block):
        z = dot_nn(up_t[0, first : first + block, :], normed) + widen(
            vec[0, 6 * width + first : 6 * width + first + block, :], tokens
        )
        active, slope = gelu_and_slope(z)
        post[3 * width + first : 3 * width + first + block, :] = active.astype(BF)
        base = 3 * width + hidden + first
        post[base : base + block, :] = slope.astype(BF)
    return (
        middle
        + dot_nn(down_t[0], post[3 * width : 3 * width + hidden, :])
        + widen(vec[0, width : 2 * width, :], tokens)
    )


def forward_rows_kernel(
    low, state, start, vec, qkv_t, out_t, up_t, down_t,
    result, pre, kv, post, stat_pre, stat_post,
    keys, values_t, bias, total,
):
    chunk = pl.program_id(0)
    width = state.shape[1]
    scale = (width // H) ** -0.5
    project_qkv(state[0], qkv_t, vec, pre.at[0], kv.at[0], stat_pre.at[0], scale)
    keys[chunk] = kv[0, 0:width, :].T
    values_t[chunk] = kv[0, width : 2 * width, :]
    attend_chunk(
        pre.at[0, width : 2 * width, :], keys, values_t, chunk, low[chunk], start[0],
        bias, total, stat_post.at[0], post.at[0, 0:width, :],
    )
    result[0] = finish_layer(state[0], out_t, up_t, down_t, vec, post.at[0], stat_post.at[0])


def forward_rows(layer, low, start, state, vec, weights):
    chunks, width, tokens = state.shape
    qkv_t, out_t, up_t, down_t = weights
    hidden = up_t.shape[1]
    per_chunk = lambda rows: pl.BlockSpec((1, rows, tokens), lambda i, *_: (i, 0, 0))
    per_layer = lambda arr: pl.BlockSpec((1,) + arr.shape[1:], lambda i, *_: (layer, 0, 0))
    shape = lambda rows, dtype: jax.ShapeDtypeStruct((chunks, rows, tokens), dtype)
    post_rows = 3 * width + 2 * hidden
    return pl.pallas_call(
        forward_rows_kernel,
        grid_spec=pltpu.PrefetchScalarGridSpec(
            num_scalar_prefetch=1,
            grid=(chunks,),
            in_specs=[per_chunk(width), per_chunk(1)] + [per_layer(a) for a in (vec, *weights)],
            out_specs=[
                per_chunk(width), per_chunk(3 * width), per_chunk(2 * width),
                per_chunk(post_rows), per_chunk(8), per_chunk(8),
            ],
            scratch_shapes=[
                pltpu.VMEM((chunks, tokens, width), BF),
                pltpu.VMEM((chunks, width, tokens), BF),
                pltpu.VMEM((tokens, tokens), F32),
                pltpu.VMEM((width, tokens), F32),
            ],
        ),
        out_shape=[
            shape(width, F32), shape(3 * width, BF), shape(2 * width, BF),
            shape(post_rows, BF), shape(8, F32), shape(8, F32),
        ],
        compiler_params=pltpu.CompilerParams(vmem_limit_bytes=VMEM_LIMIT),
        cost_estimate=pl.CostEstimate(
            flops=chunks * tokens * 2 * 3 * (4 * width * width + 2 * width * hidden),
            bytes_accessed=chunks * tokens * 2 * 4096, transcendentals=0,
        ),
        name="forward_rows",
    )(low, state, start, vec, *weights)


def forward_split_kernel(has_last, has_next, *refs):
    refs = list(refs)
    take = lambda count: [refs.pop(0) for _ in range(count)]
    (place,) = take(1)
    (state,) = take(1)
    if has_last:
        start, pre_in, kv_in, kv_y, kv_c, vec, out_t, up_t, down_t = take(9)
    if has_next:
        vec_next, qkv_t = take(2)
    (result,) = take(1) if has_last else (None,)
    if has_last:
        post, stat_post = take(2)
    if has_next:
        pre, kv, stat_pre = take(3)
    width, tokens = state.shape
    current = state[...]
    if has_last:
        keys, values_t, bias, total = take(4)
        mine = place[0]
        for hop, arrived in ((0, kv_in), (1, kv_c.at[0]), (2, kv_y), (3, kv_c.at[1])):
            keys[mine ^ hop] = arrived[0:width, :].T
            values_t[mine ^ hop] = arrived[width : 2 * width, :]
        attend_chunk(
            pre_in.at[width : 2 * width, :], keys, values_t, mine, place[1], start[...],
            bias, total, stat_post, post.at[0:width, :],
        )
        current = finish_layer(current, out_t, up_t, down_t, vec, post, stat_post)
        result[...] = current
    if has_next:
        project_qkv(current, qkv_t, vec_next, pre, kv, stat_pre, (width // H) ** -0.5)


def forward_split(layer_last, layer_next, place, state, vec, weights, start=None, prev=None):
    width, tokens = state.shape
    qkv_t, out_t, up_t, down_t = weights
    hidden = up_t.shape[1]
    whole = lambda arr: pl.BlockSpec(arr.shape, lambda i, *_: (0,) * arr.ndim)
    of_layer = lambda layer, arr: pl.BlockSpec(
        (1,) + arr.shape[1:], lambda i, *_: (layer, 0, 0)
    )
    has_last, has_next = layer_last is not None, layer_next is not None
    args, in_specs, outs, scratch = [state], [whole(state)], [], []
    if has_last:
        extra = [start, *prev]
        args += extra + [vec, out_t, up_t, down_t]
        in_specs += [whole(a) for a in extra]
        in_specs += [of_layer(layer_last, a) for a in (vec, out_t, up_t, down_t)]
        outs += [(width, F32), (3 * width + 2 * hidden, BF), (8, F32)]
        scratch += [
            pltpu.VMEM((4, tokens, width), BF),
            pltpu.VMEM((4, width, tokens), BF),
            pltpu.VMEM((tokens, tokens), F32),
            pltpu.VMEM((width, tokens), F32),
        ]
    if has_next:
        args += [vec, qkv_t]
        in_specs += [of_layer(layer_next, a) for a in (vec, qkv_t)]
        outs += [(3 * width, BF), (2 * width, BF), (8, F32)]
    shapes = [jax.ShapeDtypeStruct((rows, tokens), dtype) for rows, dtype in outs]
    return pl.pallas_call(
        functools.partial(forward_split_kernel, has_last, has_next),
        grid_spec=pltpu.PrefetchScalarGridSpec(
            num_scalar_prefetch=1, grid=(1,), in_specs=in_specs,
            out_specs=[whole(s) for s in shapes], scratch_shapes=scratch,
        ),
        out_shape=shapes,
        compiler_params=pltpu.CompilerParams(vmem_limit_bytes=VMEM_LIMIT),
        cost_estimate=pl.CostEstimate(
            flops=tokens * 2 * 3 * (4 * width * width + 2 * width * hidden),
            bytes_accessed=tokens * 2 * 4096, transcendentals=0,
        ),
        name="forward_split",
    )(place, *args)


def backward_ffn(grad, post, stat, wout, wup, wdown, vec, hidden_grad):
    width, tokens = grad.shape
    hidden = wup.shape[2]
    low_grad = grad.astype(BF)
    block = 128
    for first in range(0, hidden, block):
        base = 3 * width + hidden + first
        hidden_grad[first : first + block, :] = (
            dot_nn(wdown[0, first : first + block, :], low_grad)
            * post[base : base + block, :].astype(F32)
        ).astype(BF)
    normed_grad = dot_nn(wup[0], hidden_grad[...])
    unit = post[2 * width : 3 * width, :].astype(F32)
    gain = widen(vec[0, 4 * width : 5 * width, :], tokens)
    middle = grad + norm_backward(normed_grad, unit, stat[H : H + 1, :], gain)
    low_middle = middle.astype(BF)
    blend_grad = dot_nn(wout[0], low_middle).astype(BF)
    return low_grad, normed_grad, unit, middle, low_middle, blend_grad


def token_sum(rows):
    return dot_nt(jnp.ones((ONES_ROWS, rows.shape[1]), BF), rows.astype(BF))


def attend_backward(
    queries, blend_grad, blended, stat, keys, values, keys_t, chunk, low, start,
    bias, query_grad, kv_grad,
):
    width, tokens = queries.shape
    head = width // H
    pair = 2 * head
    deltas = []
    for h in range(H):
        rows = slice(h * head, (h + 1) * head)
        deltas.append(
            jnp.sum(
                blend_grad[rows, :].astype(F32) * blended[rows, :].astype(F32),
                axis=0, keepdims=True,
            )
        )

    def tile(j, first):
        for h in range(H):
            rows = slice(h * head, (h + 1) * head)
            lanes = pl.ds((h // 2) * pair, pair)
            query = queries[rows, :]
            grad = blend_grad[rows, :]
            part = dot_nn(keys[j, :, lanes], pad_head(query, h % 2)) + bias[...]
            probs = jnp.exp(part - stat[h : h + 1, :])
            prob_grad = dot_nn(values[j, :, lanes], pad_head(grad, h % 2))
            score_grad = (probs * (prob_grad - deltas[h])).astype(BF)
            value_rows = slice(width + h * head, width + (h + 1) * head)
            kv_grad[j, rows, :] += dot_nt(query, score_grad)
            kv_grad[j, value_rows, :] += dot_nt(grad, probs.astype(BF))
            term = dot_nn(keys_t(j, rows), score_grad)
            if first:
                query_grad[rows, :] = term
            else:
                query_grad[rows, :] += term

    bias[...] = tile_bias(chunk * tokens, start, True, (tokens, tokens))
    tile(chunk, True)

    def step(j, carry):
        bias[...] = tile_bias(j * tokens, start, False, (tokens, tokens))
        tile(j, False)
        return carry

    lax.fori_loop(low, chunk, step, 0)


def backward_rows_kernel(
    low, grad, start, pre, post, stat_pre, stat_post, kv, vec, wqkv, wout, wup, wdown,
    post_five, low_five, hidden_five, middle_five, vec_five,
    *refs, first,
):
    refs = list(refs)
    if not first:
        base = [refs.pop(0) for _ in range(5)]
    (result, sum_qkv, sum_out, sum_up, sum_down, sum_vec,
     keys, values, bias, query_grad, kv_grad, hidden_grad, blend_scr, packed) = refs
    order = pl.program_id(0)
    chunk = pl.num_programs(0) - 1 - order
    width, tokens = grad.shape[1], grad.shape[2]
    hidden = wup.shape[2]

    def add_ffn(post, low_grad, dz, low_middle):
        sum_down[...] += dot_nt(post[3 * width : 3 * width + hidden, :], low_grad)
        sum_up[...] += dot_nt(post[width : 2 * width, :], dz)
        sum_out[...] += dot_nt(post[0:width, :], low_middle)

    @pl.when(order == 0)
    def _():
        if first:
            for ref in (sum_qkv, sum_out, sum_up, sum_down):
                ref[...] = jnp.zeros_like(ref)
            sum_vec[...] = vec_five[...]
        else:
            for ref, old in zip((sum_qkv, sum_out, sum_up, sum_down), base):
                ref[...] = old[...]
            sum_vec[...] = base[4][...] + vec_five[...]
        add_ffn(post_five, low_five[...], hidden_five[...], middle_five[...])
        kv_grad[...] = jnp.zeros_like(kv_grad)
        for j in range(kv.shape[0]):
            keys[j] = kv[j, 0:width, :].T
            values[j] = kv[j, width : 2 * width, :].T

    low_grad, normed_grad, unit, middle, low_middle, blend_grad = backward_ffn(
        grad[0], post.at[0], stat_post.at[0], wout, wup, wdown, vec, hidden_grad
    )
    add_ffn(post.at[0], low_grad, hidden_grad[...], low_middle)
    add_vec(sum_vec, width, low_grad, normed_grad, unit, low_middle, hidden_grad[...])
    blend_scr[...] = blend_grad
    attend_backward(
        pre.at[0, width : 2 * width, :], blend_scr, post.at[0, 0:width, :], stat_post.at[0],
        keys, values, lambda j, rows: kv[j, rows, :], chunk, low[chunk], start[0],
        bias, query_grad, kv_grad,
    )
    packed[0:width, :] = (query_grad[...] * (width // H) ** -0.5).astype(BF)
    packed[width : 3 * width, :] = kv_grad[chunk].astype(BF)
    result[0] = finish_backward(
        middle, pre.at[0], stat_pre.at[0], packed, wqkv, vec, sum_qkv, sum_vec
    )


def add_vec(sum_vec, width, low_grad, normed_grad, unit, low_middle, dz):
    sum_vec[:, 0:width] += token_sum(low_middle)
    sum_vec[:, width : 2 * width] += token_sum(low_grad)
    sum_vec[:, 4 * width : 5 * width] += token_sum(normed_grad * unit)
    sum_vec[:, 5 * width : 6 * width] += token_sum(normed_grad)
    sum_vec[:, 6 * width :] += token_sum(dz)


def finish_backward(middle, pre, stat, packed, wqkv, vec, sum_qkv, sum_vec):
    width, tokens = middle.shape
    sum_qkv[...] += dot_nt(pre[0:width, :], packed[...])
    normed_grad = dot_nn(wqkv[0], packed[...])
    unit = pre[2 * width : 3 * width, :].astype(F32)
    gain = widen(vec[0, 2 * width : 3 * width, :], tokens)
    sum_vec[:, 2 * width : 3 * width] += token_sum(normed_grad * unit)
    sum_vec[:, 3 * width : 4 * width] += token_sum(normed_grad)
    return middle + norm_backward(normed_grad, unit, stat[0:1, :], gain)


def backward_rows(layer, low, start, grad, saved, vec, weights, five, base):
    chunks, width, tokens = grad.shape
    pre, kv, post, stat_pre, stat_post = saved
    wqkv, wout, wup, wdown = weights
    hidden = wup.shape[2]
    flip = lambda rows: pl.BlockSpec(
        (1, rows, tokens), lambda i, *_: (chunks - 1 - i, 0, 0)
    )
    whole = lambda arr: pl.BlockSpec(arr.shape, lambda i, *_: (0,) * arr.ndim)
    per_layer = lambda arr: pl.BlockSpec((1,) + arr.shape[1:], lambda i, *_: (layer, 0, 0))
    first = base is None
    sums = [
        jax.ShapeDtypeStruct(s, F32)
        for s in (
            (width, 3 * width), (width, width), (width, hidden), (hidden, width),
            (ONES_ROWS, vec.shape[1]),
        )
    ]
    args = [grad, start, pre, post, stat_pre, stat_post, kv, vec, *weights, *five]
    in_specs = [
        flip(width), flip(1), flip(pre.shape[1]), flip(post.shape[1]), flip(8), flip(8),
        whole(kv), per_layer(vec), *[per_layer(w) for w in weights], *[whole(a) for a in five],
    ]
    if not first:
        args += list(base)
        in_specs += [whole(a) for a in base]
    return pl.pallas_call(
        functools.partial(backward_rows_kernel, first=first),
        grid_spec=pltpu.PrefetchScalarGridSpec(
            num_scalar_prefetch=1, grid=(chunks,), in_specs=in_specs,
            out_specs=[flip(width)] + [whole(s) for s in sums],
            scratch_shapes=[
                pltpu.VMEM((chunks, tokens, width), BF),
                pltpu.VMEM((chunks, tokens, width), BF),
                pltpu.VMEM((tokens, tokens), F32),
                pltpu.VMEM((width, tokens), F32),
                pltpu.VMEM((chunks, 2 * width, tokens), F32),
                pltpu.VMEM((hidden, tokens), BF),
                pltpu.VMEM((width, tokens), BF),
                pltpu.VMEM((3 * width, tokens), BF),
            ],
        ),
        out_shape=[jax.ShapeDtypeStruct(grad.shape, F32)] + sums,
        compiler_params=pltpu.CompilerParams(vmem_limit_bytes=VMEM_LIMIT),
        cost_estimate=pl.CostEstimate(
            flops=chunks * tokens * 4 * 3 * (4 * width * width + 2 * width * hidden),
            bytes_accessed=chunks * tokens * 2 * 4096, transcendentals=0,
        ),
        name="backward_rows",
    )(low, *args)


def backward_split_kernel(has_last, has_next, *refs):
    refs = list(refs)
    take = lambda count: [refs.pop(0) for _ in range(count)]
    (place,) = take(1)
    if has_last:
        middle_in, query_in, own_in, near_in, far_in, pre_last, stat_last, vec_last, wqkv = take(9)
        old_qkv, old_vec = take(2)
    top = take(1)[0] if has_next else None
    if has_next:
        start, pre, kv_in, kv_y, kv_c, post, stat_post, vec, wout, wup, wdown = take(11)
    if has_last:
        result, sum_qkv, sum_vec = take(3)
    if has_next:
        middle_out, query_out, own_out, core_out, side_out = take(5)
        low_out, hidden_out, low_middle_out, vec_out = take(4)
    if has_last:
        (packed,) = take(1)
        width, tokens = middle_in.shape
        packed[0:width, :] = query_in[...]
        packed[width : 3 * width, :] = (
            own_in[...] + near_in[0].astype(F32) + far_in[...].astype(F32)
        ).astype(BF)
        sum_qkv[...] = old_qkv[...]
        sum_vec[...] = old_vec[...]
        current = finish_backward(
            middle_in[...], pre_last, stat_last, packed, wqkv, vec_last, sum_qkv, sum_vec
        )
        result[...] = current
    if has_next:
        keys, values, keys_t, bias, query_grad, kv_grad, blend_scr = take(7)
        width, tokens = top.shape
        if has_last:
            grad = jnp.where(place[2] == 1, current, top[...])
        else:
            grad = top[...]
        mine = place[0]
        kv_grad[...] = jnp.zeros_like(kv_grad)
        for hop, arrived in ((0, kv_in), (1, kv_c.at[0]), (2, kv_y), (3, kv_c.at[1])):
            keys[mine ^ hop] = arrived[0:width, :].T
            keys_t[mine ^ hop] = arrived[0:width, :]
            values[mine ^ hop] = arrived[width : 2 * width, :].T
        low_grad, normed_grad, unit, middle, low_middle, blend_grad = backward_ffn(
            grad, post, stat_post, wout, wup, wdown, vec, hidden_out
        )
        low_out[...] = low_grad
        low_middle_out[...] = low_middle
        middle_out[...] = middle
        vec_out[...] = jnp.zeros_like(vec_out)
        add_vec(vec_out, width, low_grad, normed_grad, unit, low_middle, hidden_out[...])
        blend_scr[...] = blend_grad
        attend_backward(
            pre.at[width : 2 * width, :], blend_scr, post.at[0:width, :], stat_post,
            keys, values, lambda j, rows: keys_t[j, rows, :], mine, place[1], start[...],
            bias, query_grad, kv_grad,
        )
        query_out[...] = (query_grad[...] * (width // H) ** -0.5).astype(BF)
        own_out[...] = kv_grad[mine]
        core_out[0] = kv_grad[mine ^ 1].astype(BF)
        core_out[1] = kv_grad[mine ^ 3].astype(BF)
        side_out[...] = kv_grad[mine ^ 2]


def backward_split(layer_last, layer_next, place, vec, weights, last=None, following=None):
    wqkv, wout, wup, wdown = weights
    width, hidden = wup.shape[1:]
    whole = lambda arr: pl.BlockSpec(arr.shape, lambda i, *_: (0,) * len(arr.shape))
    of_layer = lambda layer, arr: pl.BlockSpec(
        (1,) + arr.shape[1:], lambda i, *_: (layer, 0, 0)
    )
    has_last, has_next = last is not None, following is not None
    args, in_specs, outs, scratch = [], [], [], []
    shape = jax.ShapeDtypeStruct
    if has_last:
        state_args, (old_qkv, old_vec) = last
        tokens = state_args[0].shape[1]
        args += [*state_args, vec, wqkv, old_qkv, old_vec]
        in_specs += [whole(a) for a in state_args]
        in_specs += [of_layer(layer_last, vec), of_layer(layer_last, wqkv)]
        in_specs += [whole(old_qkv), whole(old_vec)]
        outs += [
            shape((width, tokens), F32), shape(old_qkv.shape, F32), shape(old_vec.shape, F32)
        ]
        scratch += [pltpu.VMEM((3 * width, tokens), BF)]
    if has_next:
        tokens = following[0].shape[1]
        args += [*following, vec, wout, wup, wdown]
        in_specs += [whole(a) for a in following]
        in_specs += [of_layer(layer_next, a) for a in (vec, wout, wup, wdown)]
        outs += [
            shape((width, tokens), F32), shape((width, tokens), BF),
            shape((2 * width, tokens), F32), shape((2, 2 * width, tokens), BF),
            shape((2 * width, tokens), F32),
            shape((width, tokens), BF), shape((hidden, tokens), BF), shape((width, tokens), BF),
            shape((ONES_ROWS, vec.shape[1]), F32),
        ]
        scratch += [
            pltpu.VMEM((4, tokens, width), BF),
            pltpu.VMEM((4, tokens, width), BF),
            pltpu.VMEM((4, width, tokens), BF),
            pltpu.VMEM((tokens, tokens), F32),
            pltpu.VMEM((width, tokens), F32),
            pltpu.VMEM((4, 2 * width, tokens), F32),
            pltpu.VMEM((width, tokens), BF),
        ]
    return pl.pallas_call(
        functools.partial(backward_split_kernel, has_last, has_next),
        grid_spec=pltpu.PrefetchScalarGridSpec(
            num_scalar_prefetch=1, grid=(1,), in_specs=in_specs,
            out_specs=[whole(s) for s in outs], scratch_shapes=scratch,
        ),
        out_shape=outs,
        compiler_params=pltpu.CompilerParams(vmem_limit_bytes=VMEM_LIMIT),
        cost_estimate=pl.CostEstimate(
            flops=tokens * 4 * 3 * (4 * width * width + 2 * width * hidden),
            bytes_accessed=tokens * 2 * 4096, transcendentals=0,
        ),
        name="backward_split",
    )(place, *args)


def swap(values, hop):
    return lax.ppermute(
        values, "seq", [(i, i ^ hop) for i in range(lax.axis_size("seq"))]
    )


def to_rows(rows, me):
    pieces = [lax.dynamic_index_in_dim(rows, me ^ hop, 0, keepdims=False) for hop in range(4)]
    arrived = [pieces[0]] + [swap(pieces[hop], hop) for hop in range(1, 4)]
    stacked = jnp.stack(arrived)
    return jnp.stack(
        [lax.dynamic_index_in_dim(stacked, me ^ j, 0, keepdims=False) for j in range(4)]
    )


def fast_device(
    block_input, embedding, cotangent, qkv_weight, out_weight, out_bias, up_weight, up_bias,
    down_weight, down_bias, norm_gain, norm_shift, seg_lengths, loop_counts, token_counts,
):
    row_count, tokens, width = block_input.shape
    chunks = lax.axis_size("seq")
    row_len = tokens * chunks
    me = lax.axis_index("seq")
    hidden = up_weight.shape[2]

    ends = jnp.cumsum(seg_lengths, axis=-1)
    position = jnp.arange(row_len, dtype=jnp.int32)
    starts = jnp.max(
        jnp.where(ends[:, None, :] <= position[None, :, None], ends[:, None, :], 0), axis=-1
    ).astype(jnp.int32)
    own = lax.dynamic_index_in_dim(starts, me, 0, keepdims=False)
    start_rows = own.reshape(chunks, 1, tokens)
    low_rows = start_rows[:, 0, 0] // tokens
    start_split = lax.dynamic_slice(starts, (row_count - 1, me * tokens), (1, tokens))
    two_row = lax.dynamic_index_in_dim(loop_counts, me, 0, keepdims=False) == 2
    two_split = loop_counts[row_count - 1] == 2
    place = jnp.stack([me, start_split[0, 0] // tokens, two_split]).astype(jnp.int32)
    place_keep = place.at[2].set(1)
    row_weight = token_counts.astype(F32) / row_len

    flip = lambda values: jnp.swapaxes(values, -1, -2)
    vec = jnp.concatenate(
        [
            out_bias, down_bias, norm_gain[:, 0], norm_shift[:, 0], norm_gain[:, 1],
            norm_shift[:, 1], up_bias,
        ],
        axis=-1,
    )
    vec = jnp.broadcast_to(vec[:, :, None], vec.shape + (128,))
    forward_weights = tuple(flip(w) for w in (qkv_weight, out_weight, up_weight, down_weight))
    backward_weights = (qkv_weight, out_weight, up_weight, down_weight)

    input_rows = to_rows(block_input[:-1], me)
    embed_rows = flip(to_rows(embedding[:-1], me)).astype(F32)
    state = flip(input_rows).astype(F32) + embed_rows
    embed_split = flip(embedding[-1]).astype(F32)
    state_split = flip(block_input[-1]).astype(F32) + embed_split

    saved, saved_split = [], []
    finals = []
    pre, kv, stat_pre = forward_split(None, 0, place, state_split, vec, forward_weights)
    for step in range(2 * LAYERS):
        layer = step % LAYERS
        kv_y = swap(kv, 2)
        kv_c = swap(jnp.stack([kv, kv_y]), 1)
        state, *kept = forward_rows(layer, low_rows, start_rows, state, vec, forward_weights)
        saved.append(kept)
        prev = (pre, kv, kv_y, kv_c)
        last = layer == LAYERS - 1
        inner = None if last else layer + 1
        outs = forward_split(
            layer, inner, place, state_split, vec, forward_weights, start_split, prev
        )
        state_split, post, stat_post = outs[:3]
        saved_split.append((start_split, pre, kv, kv_y, kv_c, post, stat_post, stat_pre))
        if last:
            finals.append((state, state_split))
            if step < 2 * LAYERS - 1:
                state = state + embed_rows
                state_split = state_split + embed_split
                pre, kv, stat_pre = forward_split(
                    None, 0, place, state_split, vec, forward_weights
                )
        else:
            pre, kv, stat_pre = outs[3:]

    answer = flip(jnp.where(two_row, finals[1][0], finals[0][0]).astype(BF))
    answer = to_rows(answer, me)
    answer_split = flip(jnp.where(two_split, finals[1][1], finals[0][1]).astype(BF))
    block_output = jnp.concatenate([answer, answer_split[None]], axis=0)

    top = flip(to_rows(cotangent[:-1], me)).astype(F32) * lax.dynamic_index_in_dim(
        row_weight, me, 0, keepdims=False
    )
    top_split = flip(cotangent[-1]).astype(F32) * row_weight[row_count - 1]
    grad = jnp.where(two_row, top, 0.0)
    sums = [None] * LAYERS
    last = None
    layer_last = None
    second = second_split = None
    next_top = jnp.where(two_split, top_split, 0.0)
    for step in reversed(range(2 * LAYERS)):
        layer = step % LAYERS
        between = step == LAYERS - 1
        place_now = place if between else place_keep
        start_s, pre_s, kv_s, kv_y, kv_c, post_s, stat_post_s, stat_pre_s = saved_split[step]
        following = (next_top, start_s, pre_s, kv_s, kv_y, kv_c, post_s, stat_post_s)
        outs = backward_split(
            layer_last, layer, place_now, vec, backward_weights, last, following
        )
        if last is not None:
            result_split, sum_qkv, sum_vec = outs[:3]
            outs = outs[3:]
            sums[layer_last][0] = sum_qkv
            sums[layer_last][4] = sum_vec
            if between:
                second_split = result_split
        middle, query, own_kv, core, side, low_g, hidden_g, low_m, vec_five = outs
        near = swap(core, 1)
        far = swap((side + near[1].astype(F32)).astype(BF), 2)
        if between:
            second = grad
            grad = jnp.where(two_row, grad, top)
        five = (post_s, low_g, hidden_g, low_m, vec_five)
        grad, *sums[layer] = backward_rows(
            layer, low_rows, start_rows, grad, saved[step], vec, backward_weights, five,
            sums[layer],
        )
        last = ((middle, query, own_kv, near, far, pre_s, stat_pre_s), (sums[layer][0], sums[layer][4]))
        layer_last = layer
        next_top = top_split
    grad_split, sums[0][0], sums[0][4] = backward_split(
        0, None, place, vec, backward_weights, last, None
    )

    total = lax.psum(jnp.sum(token_counts), "dp").astype(F32)
    input_scale = row_count * lax.axis_size("dp") * row_len / total
    weight_scale = row_len / total
    second_home = to_rows(flip(second).astype(BF), me).astype(F32)
    first_home = to_rows(flip(grad).astype(BF), me).astype(F32)
    first_all = jnp.concatenate([first_home, flip(grad_split)[None]], axis=0)
    second_all = jnp.concatenate([second_home, flip(second_split)[None]], axis=0)
    gathered = [jnp.stack([sums[layer][k] for layer in range(LAYERS)]) for k in range(5)]
    gathered[4] = gathered[4][:, 0]
    gathered = [g.astype(F32) * weight_scale for g in lax.psum(tuple(gathered), ("dp", "seq"))]
    vec_sum = gathered[4]
    piece = lambda k: vec_sum[:, k * width : (k + 1) * width]
    return (
        block_output,
        first_all * input_scale,
        (first_all + second_all) * input_scale,
        gathered[0],
        gathered[1],
        piece(0),
        gathered[2],
        vec_sum[:, 6 * width :],
        gathered[3],
        piece(1),
        jnp.stack([piece(2), piece(4)], axis=1),
        jnp.stack([piece(3), piece(5)], axis=1),
    )


def solution(mesh):
    fast = mesh.shape["seq"] == 4

    def on_any(*args):
        if fast and args[0].shape[0] == 5:
            return fast_device(*args)
        return on_device(*args)

    return jax.shard_map(
        on_any,
        mesh=mesh,
        in_specs=(
            P("dp", "seq", None),
            P("dp", "seq", None),
            P("dp", "seq", None),
            P(),
            P(),
            P(),
            P(),
            P(),
            P(),
            P(),
            P(),
            P(),
            P("dp", None),
            P("dp"),
            P("dp"),
        ),
        out_specs=(
            P("dp", "seq", None),
            P("dp", "seq", None),
            P("dp", "seq", None),
            P(),
            P(),
            P(),
            P(),
            P(),
            P(),
            P(),
            P(),
            P(),
        ),
        check_vma=False,
    )
```

```python
import functools

import jax
import jax.numpy as jnp
from jax import lax
from jax.experimental import pallas as pl
from jax.experimental.pallas import tpu as pltpu
from jax.sharding import Mesh, PartitionSpec as P

H = 4
LAYERS = 2


NORM_EPS = 1e-05
MASKED = -1e30


def layer_norm(values, gain, shift):
    center = values - jnp.mean(values, axis=-1, keepdims=True)
    spread = jnp.mean(center * center, axis=-1, keepdims=True)
    return center * lax.rsqrt(spread + NORM_EPS) * gain + shift


def gelu_exact(values):
    return jax.nn.gelu(values, approximate=False)


def matmul(left_side, right_side):
    return jnp.dot(left_side, right_side, preferred_element_type=jnp.float32)


def left_dot(left_side, right_side):
    return lax.dot_general(
        left_side, right_side, (((0,), (0,)), ((), ())), preferred_element_type=jnp.float32
    )


def right_dot(left_side, right_side):
    return lax.dot_general(
        left_side, right_side, (((1,), (1,)), ((), ())), preferred_element_type=jnp.float32
    )


def split_heads(packed, head_count):
    return packed.reshape(packed.shape[0], head_count, packed.shape[1] // head_count)


def attend_forward(queries, key_vals, allowed, head_count, score_scale):
    model_width = queries.shape[1]
    key_rows = split_heads(key_vals[:, :model_width], head_count)
    value_rows = split_heads(key_vals[:, model_width:], head_count)
    scores = (
        jnp.einsum(
            "qhd,khd->hqk",
            split_heads(queries, head_count),
            key_rows,
            preferred_element_type=jnp.float32,
        )
        * score_scale
    )
    scores = jnp.where(allowed[None], scores, MASKED)
    row_max = jnp.max(scores, axis=-1, keepdims=True)
    shifted_exp = jnp.exp(scores - row_max)
    row_total = jnp.sum(shifted_exp, axis=-1, keepdims=True)
    attn_probs = (shifted_exp / row_total).astype(jnp.bfloat16)
    blended = jnp.einsum("hqk,khd->qhd", attn_probs, value_rows, preferred_element_type=jnp.float32)
    return (blended.reshape(queries.shape[0], model_width), (row_max + jnp.log(row_total))[..., 0])


def attention_core(
    query_part, key_part, value_part, grad_part, allowed_part, logsum_part, head_count, score_scale
):
    scores = (
        jnp.einsum(
            "qhd,khd->hqk",
            split_heads(query_part, head_count),
            split_heads(key_part, head_count),
            preferred_element_type=jnp.float32,
        )
        * score_scale
    )
    scores = jnp.where(allowed_part[None], scores, MASKED)
    attn_probs = jnp.exp(scores - logsum_part[..., None])
    grad_probs = jnp.einsum(
        "qhd,khd->hqk",
        split_heads(grad_part, head_count),
        split_heads(value_part, head_count),
        preferred_element_type=jnp.float32,
    )
    return (attn_probs, grad_probs)


def query_grads(grad_scores, key_part, head_count, score_scale):
    result = (
        jnp.einsum(
            "hqk,khd->qhd",
            grad_scores,
            split_heads(key_part, head_count),
            preferred_element_type=jnp.float32,
        )
        * score_scale
    )
    return result.reshape(result.shape[0], -1)


def keyval_grads(grad_scores, attn_probs, query_part, grad_part, head_count, score_scale):
    grad_keys = (
        jnp.einsum(
            "hqk,qhd->khd",
            grad_scores,
            split_heads(query_part, head_count),
            preferred_element_type=jnp.float32,
        )
        * score_scale
    )
    grad_values = jnp.einsum(
        "hqk,qhd->khd",
        attn_probs.astype(jnp.bfloat16),
        split_heads(grad_part, head_count),
        preferred_element_type=jnp.float32,
    )
    return jnp.concatenate(
        [grad_keys.reshape(grad_keys.shape[0], -1), grad_values.reshape(grad_values.shape[0], -1)],
        axis=-1,
    )


def on_device(
    block_input,
    embedding,
    cotangent,
    qkv_weight,
    out_weight,
    out_bias,
    up_weight,
    up_bias,
    down_weight,
    down_bias,
    norm_gain,
    norm_shift,
    seg_lengths,
    loop_counts,
    token_counts,
):
    row_count, block_len, model_width = block_input.shape
    head_count = H
    score_scale = (model_width // head_count) ** (-0.5)
    row_len = block_len * lax.axis_size("seq")
    flat_rows = row_count * block_len
    offset = lax.axis_index("seq") * block_len
    key_pos = jnp.arange(row_len, dtype=jnp.int32)
    own_pos = offset + jnp.arange(block_len, dtype=jnp.int32)
    seg_ends = jnp.cumsum(seg_lengths, axis=-1)
    seg_all = jnp.sum((seg_ends[:, None, :] <= key_pos[None, :, None]).astype(jnp.int32), axis=-1)
    seg_own = lax.dynamic_slice_in_dim(seg_all, offset, block_len, 1)
    allowed = (seg_own[:, :, None] == seg_all[:, None, :]) & (
        key_pos[None, None, :] <= own_pos[None, :, None]
    )
    current = block_input.astype(jnp.float32)
    inject = embedding.astype(jnp.float32)
    stored = []
    finals = []
    for repeat in range(2):
        current = current + inject
        for layer_index in range(LAYERS):
            forward_normed = layer_norm(
                current, norm_gain[layer_index, 0], norm_shift[layer_index, 0]
            ).astype(jnp.bfloat16)
            forward_packed = matmul(
                forward_normed.reshape(flat_rows, model_width), qkv_weight[layer_index]
            ).astype(jnp.bfloat16)
            forward_packed = forward_packed.reshape(row_count, block_len, 3 * model_width)
            forward_key_vals = lax.all_gather(
                forward_packed[:, :, model_width:], "seq", axis=1, tiled=True
            )

            def forward_row(inputs):
                return attend_forward(inputs[0], inputs[1], inputs[2], head_count, score_scale)

            forward_blended, forward_logsum = lax.map(
                forward_row, (forward_packed[:, :, :model_width], forward_key_vals, allowed)
            )
            forward_blended = forward_blended.astype(jnp.bfloat16)
            branch_out = matmul(
                forward_blended.reshape(flat_rows, model_width), out_weight[layer_index]
            ).reshape(row_count, block_len, model_width)
            forward_middle = current + branch_out + out_bias[layer_index]
            forward_normed_two = layer_norm(
                forward_middle, norm_gain[layer_index, 1], norm_shift[layer_index, 1]
            ).astype(jnp.bfloat16)
            forward_up_proj = (
                matmul(forward_normed_two.reshape(flat_rows, model_width), up_weight[layer_index])
                + up_bias[layer_index]
            )
            forward_active = gelu_exact(forward_up_proj).astype(jnp.bfloat16)
            result = (
                forward_middle
                + matmul(forward_active, down_weight[layer_index]).reshape(
                    row_count, block_len, model_width
                )
                + down_bias[layer_index]
            )
            current, stored_layer = (
                result,
                (
                    current,
                    forward_normed,
                    forward_packed,
                    forward_key_vals,
                    forward_logsum,
                    forward_blended,
                    forward_middle,
                    forward_normed_two,
                    forward_up_proj,
                    forward_active,
                ),
            )
            stored.append(stored_layer)
        finals.append(current)
    two_loops = (loop_counts == 2)[:, None, None]
    block_output = jnp.where(two_loops, finals[1], finals[0]).astype(jnp.bfloat16)
    row_weight = token_counts.astype(jnp.float32) / row_len
    grad_top = cotangent.astype(jnp.float32) * row_weight[:, None, None]
    grad_state = jnp.where(two_loops, grad_top, 0.0)
    layer_sums = [None] * LAYERS
    second_pass = grad_state
    for repeat in (1, 0):
        for layer_index in reversed(range(LAYERS)):
            backward_stored_layer = stored[repeat * LAYERS + layer_index]
            (
                backward_current,
                normed,
                packed,
                key_vals,
                logsum,
                blended,
                middle,
                normed_two,
                up_proj,
                active,
            ) = backward_stored_layer
            grad_flat = grad_state.reshape(flat_rows, model_width)
            grad_low = grad_flat.astype(jnp.bfloat16)
            grad_down = left_dot(active, grad_low)
            grad_down_bias = jnp.sum(grad_flat, axis=0)
            grad_active = right_dot(grad_low, down_weight[layer_index])
            grad_up_proj = jax.vjp(gelu_exact, up_proj)[1](grad_active)[0].astype(jnp.bfloat16)
            grad_up_bias = jnp.sum(grad_up_proj.astype(jnp.float32), axis=0)
            grad_up = left_dot(normed_two.reshape(flat_rows, model_width), grad_up_proj)
            grad_normed_two = right_dot(grad_up_proj, up_weight[layer_index]).reshape(
                row_count, block_len, model_width
            )
            pull_two = jax.vjp(
                layer_norm, middle, norm_gain[layer_index, 1], norm_shift[layer_index, 1]
            )[1]
            grad_middle, gain_two, shift_two = pull_two(grad_normed_two)
            grad_middle = grad_middle + grad_state
            middle_flat = grad_middle.reshape(flat_rows, model_width)
            middle_low = middle_flat.astype(jnp.bfloat16)
            grad_out = left_dot(blended.reshape(flat_rows, model_width), middle_low)
            grad_out_bias = jnp.sum(middle_flat, axis=0)
            grad_blend = (
                right_dot(middle_low, out_weight[layer_index])
                .astype(jnp.bfloat16)
                .reshape(row_count, block_len, model_width)
            )
            queries = packed[:, :, :model_width]

            def full_row(inputs):
                query_part, keyval_part, grad_part, allowed_part, logsum_part = inputs
                attn_probs, grad_probs = attention_core(
                    query_part,
                    keyval_part[:, :model_width],
                    keyval_part[:, model_width:],
                    grad_part,
                    allowed_part,
                    logsum_part,
                    head_count,
                    score_scale,
                )
                row_delta = jnp.sum(attn_probs * grad_probs, axis=-1, keepdims=True)
                grad_scores = (attn_probs * (grad_probs - row_delta)).astype(jnp.bfloat16)
                return (
                    query_grads(grad_scores, keyval_part[:, :model_width], head_count, score_scale),
                    keyval_grads(
                        grad_scores, attn_probs, query_part, grad_part, head_count, score_scale
                    ),
                )

            grad_query, partial_kv = lax.map(
                full_row, (queries, key_vals, grad_blend, allowed, logsum)
            )
            grad_keyval = lax.psum_scatter(
                partial_kv.astype(jnp.bfloat16), "seq", scatter_dimension=1, tiled=True
            )
            grad_packed = jnp.concatenate(
                [grad_query.astype(jnp.bfloat16), grad_keyval], axis=-1
            ).reshape(flat_rows, 3 * model_width)
            grad_qkv = left_dot(normed.reshape(flat_rows, model_width), grad_packed)
            grad_normed = right_dot(grad_packed, qkv_weight[layer_index]).reshape(
                row_count, block_len, model_width
            )
            pull_one = jax.vjp(
                layer_norm, backward_current, norm_gain[layer_index, 0], norm_shift[layer_index, 0]
            )[1]
            grad_current, gain_one, shift_one = pull_one(grad_normed)
            grad_current = grad_current + grad_middle
            grad_state = grad_current
            grad_set = (
                grad_qkv,
                grad_out,
                grad_out_bias,
                grad_up,
                grad_up_bias,
                grad_down,
                grad_down_bias,
                jnp.stack([gain_one, gain_two]),
                jnp.stack([shift_one, shift_two]),
            )
            if repeat == 1:
                layer_sums[layer_index] = grad_set
            else:
                layer_sums[layer_index] = jax.tree.map(jnp.add, layer_sums[layer_index], grad_set)
        if repeat == 1:
            second_pass = grad_state
            grad_state = jnp.where(two_loops, grad_state, grad_top)
    grad_embed = grad_state + second_pass
    stacked = jax.tree.map(lambda *members: jnp.stack(members), *layer_sums)
    (
        sum_qkv,
        sum_out,
        sum_out_bias,
        sum_up,
        sum_up_bias,
        sum_down,
        sum_down_bias,
        sum_gain,
        sum_shift,
    ) = stacked
    total = lax.psum(jnp.sum(token_counts), "dp").astype(jnp.float32)
    summed = lax.psum(
        (
            sum_qkv,
            sum_out,
            sum_out_bias,
            sum_up,
            sum_up_bias,
            sum_down,
            sum_down_bias,
            sum_gain,
            sum_shift,
        ),
        ("dp", "seq"),
    )
    input_scale = row_count * lax.axis_size("dp") * row_len / total
    weight_scale = row_len / total
    return (
        block_output,
        grad_state * input_scale,
        grad_embed * input_scale,
        summed[0] * weight_scale,
        summed[1] * weight_scale,
        summed[2] * weight_scale,
        summed[3] * weight_scale,
        summed[4] * weight_scale,
        summed[5] * weight_scale,
        summed[6] * weight_scale,
        summed[7] * weight_scale,
        summed[8] * weight_scale,
    )


BF = jnp.bfloat16
F32 = jnp.float32
ERF_TERMS = (
    7.97884941e-01,
    3.63330844e-02,
    -3.25947475e-05,
    -5.53063153e-05,
    3.96477285e-06,
    -1.32266251e-07,
    1.75627657e-09,
)
INV_SQRT_2PI = 0.3989422804014327
VMEM_LIMIT = 56 * 1024 * 1024
ONES_ROWS = 16


def dot_nn(left_side, right_side):
    return jnp.dot(left_side, right_side, preferred_element_type=F32)


def dot_nt(left_side, right_side):
    return lax.dot_general(
        left_side, right_side, (((1,), (1,)), ((), ())), preferred_element_type=F32
    )


def widen(block, width):
    return jnp.concatenate([block] * (width // block.shape[1]), axis=1)


def gelu_and_slope(z):
    square = z * z
    clipped = jnp.minimum(square, 64.0)
    series = jnp.full_like(z, ERF_TERMS[-1])
    for term in ERF_TERMS[-2::-1]:
        series = series * clipped + term
    cdf = 0.5 + 0.5 * jnp.tanh(z * series)
    density = jnp.exp(square * -0.5) * INV_SQRT_2PI
    return z * cdf, cdf + z * density


def norm_forward(values, gain, shift):
    center = values - jnp.mean(values, axis=0, keepdims=True)
    spread = jnp.mean(center * center, axis=0, keepdims=True)
    inverse = lax.rsqrt(spread + NORM_EPS)
    unit = center * inverse
    return unit, inverse, (unit * gain + shift).astype(BF)


def norm_backward(grad, unit, inverse, gain):
    scaled = grad * gain
    first = jnp.mean(scaled, axis=0, keepdims=True)
    second = jnp.mean(scaled * unit, axis=0, keepdims=True)
    return inverse * (scaled - first - unit * second)


def vec_part(vec, index, width, size):
    return widen(vec[0, index * width : index * width + size, :], width)


def project_qkv(state, qkv_t, vec, pre, kv, stat, scale):
    width = state.shape[0]
    tokens = state.shape[1]
    gain = widen(vec[0, 2 * width : 3 * width, :], tokens)
    shift = widen(vec[0, 3 * width : 4 * width, :], tokens)
    unit, inverse, normed = norm_forward(state, gain, shift)
    pre[0:width, :] = normed
    pre[2 * width : 3 * width, :] = unit.astype(BF)
    pre[width : 2 * width, :] = (dot_nn(qkv_t[0, 0:width, :], normed) * scale).astype(BF)
    kv[0:width, :] = dot_nn(qkv_t[0, width : 2 * width, :], normed).astype(BF)
    kv[width : 2 * width, :] = dot_nn(qkv_t[0, 2 * width : 3 * width, :], normed).astype(BF)
    stat[0:1, :] = inverse


def pad_head(block, odd):
    blank = jnp.zeros_like(block)
    return jnp.concatenate([blank, block] if odd else [block, blank], axis=0)


def tile_bias(first_key, start, causal, shape):
    key_at = lax.broadcasted_iota(jnp.int32, shape, 0)
    keep = key_at + first_key >= start
    if causal:
        keep = keep & (key_at <= lax.broadcasted_iota(jnp.int32, shape, 1))
    return jnp.where(keep, 0.0, MASKED)


def attend_chunk(queries, keys, values_t, chunk, low, start, bias, total, stat, blended):
    width, tokens = queries.shape
    head = width // H
    pair = 2 * head

    def scores(j, h):
        lanes = pl.ds((h // 2) * pair, pair)
        return dot_nn(keys[j, :, lanes], pad_head(queries[h * head : (h + 1) * head, :], h % 2)) + bias[...]

    head_rows = [slice(h * head, (h + 1) * head) for h in range(H)]

    def weigh(j, tops):
        parts = [scores(j, h) for h in range(H)]
        new_tops = [jnp.max(part, axis=0, keepdims=True) for part in parts]
        if tops is not None:
            new_tops = [jnp.maximum(old, new) for old, new in zip(tops, new_tops)]
        weights = [jnp.exp(part - top) for part, top in zip(parts, new_tops)]
        sums = [jnp.sum(weight, axis=0, keepdims=True) for weight in weights]
        terms = [
            dot_nn(values_t[j, rows, :], weight.astype(BF))
            for rows, weight in zip(head_rows, weights)
        ]
        return tuple(new_tops), sums, terms

    bias[...] = tile_bias(chunk * tokens, start, True, (tokens, tokens))
    tops, sums, terms = weigh(chunk, None)
    for rows, term in zip(head_rows, terms):
        total[rows, :] = term

    def step(j, carry):
        tops, sums = carry
        bias[...] = tile_bias(j * tokens, start, False, (tokens, tokens))
        new_tops, new_sums, terms = weigh(j, tops)
        fades = [jnp.exp(old - new) for old, new in zip(tops, new_tops)]
        for rows, term, fade in zip(head_rows, terms, fades):
            total[rows, :] = total[rows, :] * fade + term
        return new_tops, tuple(old * fade + new for old, fade, new in zip(sums, fades, new_sums))

    tops, sums = lax.fori_loop(low, chunk, step, (tuple(tops), tuple(sums)))
    for h in range(H):
        rows = slice(h * head, (h + 1) * head)
        blended[rows, :] = (total[rows, :] / sums[h]).astype(BF)
        stat[h : h + 1, :] = tops[h] + jnp.log(sums[h])


def finish_layer(state, out_t, up_t, down_t, vec, post, stat):
    width, tokens = state.shape
    hidden = up_t.shape[1]
    middle = (
        state + dot_nn(out_t[0], post[0:width, :]) + widen(vec[0, 0:width, :], tokens)
    )
    gain = widen(vec[0, 4 * width : 5 * width, :], tokens)
    shift = widen(vec[0, 5 * width : 6 * width, :], tokens)
    unit, inverse, normed = norm_forward(middle, gain, shift)
    post[width : 2 * width, :] = normed
    post[2 * width : 3 * width, :] = unit.astype(BF)
    stat[H : H + 1, :] = inverse
    z = dot_nn(up_t[0], normed) + widen(vec[0, 6 * width :, :], tokens)
    active, slope = gelu_and_slope(z)
    post[3 * width : 3 * width + hidden, :] = active.astype(BF)
    post[3 * width + hidden :, :] = slope.astype(BF)
    return (
        middle
        + dot_nn(down_t[0], post[3 * width : 3 * width + hidden, :])
        + widen(vec[0, width : 2 * width, :], tokens)
    )


def forward_rows_kernel(
    low, state, start, vec, qkv_t, out_t, up_t, down_t,
    result, pre, kv, post, stat_pre, stat_post,
    keys, values_t, bias, total,
):
    chunk = pl.program_id(0)
    width = state.shape[1]
    scale = (width // H) ** -0.5
    project_qkv(state[0], qkv_t, vec, pre.at[0], kv.at[0], stat_pre.at[0], scale)
    keys[chunk] = kv[0, 0:width, :].T
    values_t[chunk] = kv[0, width : 2 * width, :]
    attend_chunk(
        pre.at[0, width : 2 * width, :], keys, values_t, chunk, low[chunk], start[0],
        bias, total, stat_post.at[0], post.at[0, 0:width, :],
    )
    result[0] = finish_layer(state[0], out_t, up_t, down_t, vec, post.at[0], stat_post.at[0])


def forward_rows(layer, low, start, state, vec, weights):
    chunks, width, tokens = state.shape
    qkv_t, out_t, up_t, down_t = weights
    hidden = up_t.shape[1]
    per_chunk = lambda rows: pl.BlockSpec((1, rows, tokens), lambda i, *_: (i, 0, 0))
    per_layer = lambda arr: pl.BlockSpec((1,) + arr.shape[1:], lambda i, *_: (layer, 0, 0))
    shape = lambda rows, dtype: jax.ShapeDtypeStruct((chunks, rows, tokens), dtype)
    post_rows = 3 * width + 2 * hidden
    return pl.pallas_call(
        forward_rows_kernel,
        grid_spec=pltpu.PrefetchScalarGridSpec(
            num_scalar_prefetch=1,
            grid=(chunks,),
            in_specs=[per_chunk(width), per_chunk(1)] + [per_layer(a) for a in (vec, *weights)],
            out_specs=[
                per_chunk(width), per_chunk(3 * width), per_chunk(2 * width),
                per_chunk(post_rows), per_chunk(8), per_chunk(8),
            ],
            scratch_shapes=[
                pltpu.VMEM((chunks, tokens, width), BF),
                pltpu.VMEM((chunks, width, tokens), BF),
                pltpu.VMEM((tokens, tokens), F32),
                pltpu.VMEM((width, tokens), F32),
            ],
        ),
        out_shape=[
            shape(width, F32), shape(3 * width, BF), shape(2 * width, BF),
            shape(post_rows, BF), shape(8, F32), shape(8, F32),
        ],
        compiler_params=pltpu.CompilerParams(vmem_limit_bytes=VMEM_LIMIT),
        cost_estimate=pl.CostEstimate(
            flops=chunks * tokens * 2 * 3 * (4 * width * width + 2 * width * hidden),
            bytes_accessed=chunks * tokens * 2 * 4096, transcendentals=0,
        ),
        name="forward_rows",
    )(low, state, start, vec, *weights)


def forward_split_kernel(has_last, has_next, *refs):
    refs = list(refs)
    take = lambda count: [refs.pop(0) for _ in range(count)]
    (place,) = take(1)
    (state,) = take(1)
    if has_last:
        start, pre_in, kv_in, kv_y, kv_c, vec, out_t, up_t, down_t = take(9)
    if has_next:
        vec_next, qkv_t = take(2)
    (result,) = take(1) if has_last else (None,)
    if has_last:
        post, stat_post = take(2)
    if has_next:
        pre, kv, stat_pre = take(3)
    width, tokens = state.shape
    current = state[...]
    if has_last:
        keys, values_t, bias, total = take(4)
        mine = place[0]
        for hop, arrived in ((0, kv_in), (1, kv_c.at[0]), (2, kv_y), (3, kv_c.at[1])):
            keys[mine ^ hop] = arrived[0:width, :].T
            values_t[mine ^ hop] = arrived[width : 2 * width, :]
        attend_chunk(
            pre_in.at[width : 2 * width, :], keys, values_t, mine, place[1], start[...],
            bias, total, stat_post, post.at[0:width, :],
        )
        current = finish_layer(current, out_t, up_t, down_t, vec, post, stat_post)
        result[...] = current
    if has_next:
        project_qkv(current, qkv_t, vec_next, pre, kv, stat_pre, (width // H) ** -0.5)


def forward_split(layer_last, layer_next, place, state, vec, weights, start=None, prev=None):
    width, tokens = state.shape
    qkv_t, out_t, up_t, down_t = weights
    hidden = up_t.shape[1]
    whole = lambda arr: pl.BlockSpec(arr.shape, lambda i, *_: (0,) * arr.ndim)
    of_layer = lambda layer, arr: pl.BlockSpec(
        (1,) + arr.shape[1:], lambda i, *_: (layer, 0, 0)
    )
    has_last, has_next = layer_last is not None, layer_next is not None
    args, in_specs, outs, scratch = [state], [whole(state)], [], []
    if has_last:
        extra = [start, *prev]
        args += extra + [vec, out_t, up_t, down_t]
        in_specs += [whole(a) for a in extra]
        in_specs += [of_layer(layer_last, a) for a in (vec, out_t, up_t, down_t)]
        outs += [(width, F32), (3 * width + 2 * hidden, BF), (8, F32)]
        scratch += [
            pltpu.VMEM((4, tokens, width), BF),
            pltpu.VMEM((4, width, tokens), BF),
            pltpu.VMEM((tokens, tokens), F32),
            pltpu.VMEM((width, tokens), F32),
        ]
    if has_next:
        args += [vec, qkv_t]
        in_specs += [of_layer(layer_next, a) for a in (vec, qkv_t)]
        outs += [(3 * width, BF), (2 * width, BF), (8, F32)]
    shapes = [jax.ShapeDtypeStruct((rows, tokens), dtype) for rows, dtype in outs]
    return pl.pallas_call(
        functools.partial(forward_split_kernel, has_last, has_next),
        grid_spec=pltpu.PrefetchScalarGridSpec(
            num_scalar_prefetch=1, grid=(1,), in_specs=in_specs,
            out_specs=[whole(s) for s in shapes], scratch_shapes=scratch,
        ),
        out_shape=shapes,
        compiler_params=pltpu.CompilerParams(vmem_limit_bytes=VMEM_LIMIT),
        cost_estimate=pl.CostEstimate(
            flops=tokens * 2 * 3 * (4 * width * width + 2 * width * hidden),
            bytes_accessed=tokens * 2 * 4096, transcendentals=0,
        ),
        name="forward_split",
    )(place, *args)


def backward_ffn(grad, post, stat, wout, wup, wdown, vec, hidden_grad):
    width, tokens = grad.shape
    hidden = wup.shape[2]
    low_grad = grad.astype(BF)
    hidden_grad[...] = (
        dot_nn(wdown[0], low_grad) * post[3 * width + hidden :, :].astype(F32)
    ).astype(BF)
    normed_grad = dot_nn(wup[0], hidden_grad[...])
    unit = post[2 * width : 3 * width, :].astype(F32)
    gain = widen(vec[0, 4 * width : 5 * width, :], tokens)
    middle = grad + norm_backward(normed_grad, unit, stat[H : H + 1, :], gain)
    low_middle = middle.astype(BF)
    blend_grad = dot_nn(wout[0], low_middle).astype(BF)
    return low_grad, normed_grad, unit, middle, low_middle, blend_grad


def token_sum(rows):
    return dot_nt(jnp.ones((ONES_ROWS, rows.shape[1]), BF), rows.astype(BF))


def attend_backward(
    queries, blend_grad, blended, stat, keys, values, keys_t, chunk, low, start,
    bias, query_grad, kv_grad,
):
    width, tokens = queries.shape
    head = width // H
    pair = 2 * head
    deltas = []
    for h in range(H):
        rows = slice(h * head, (h + 1) * head)
        deltas.append(
            jnp.sum(
                blend_grad[rows, :].astype(F32) * blended[rows, :].astype(F32),
                axis=0, keepdims=True,
            )
        )

    head_rows = [slice(h * head, (h + 1) * head) for h in range(H)]

    def tile(j, first):
        parts, prob_grads = [], []
        for h, rows in enumerate(head_rows):
            lanes = pl.ds((h // 2) * pair, pair)
            parts.append(dot_nn(keys[j, :, lanes], pad_head(queries[rows, :], h % 2)))
            prob_grads.append(dot_nn(values[j, :, lanes], pad_head(blend_grad[rows, :], h % 2)))
        probs = [
            jnp.exp(part + bias[...] - stat[h : h + 1, :]) for h, part in enumerate(parts)
        ]
        score_grads = [
            (prob * (prob_grad - delta)).astype(BF)
            for prob, prob_grad, delta in zip(probs, prob_grads, deltas)
        ]
        for rows, prob, score_grad in zip(head_rows, probs, score_grads):
            value_rows = slice(width + rows.start, width + rows.stop)
            kv_grad[j, value_rows, :] += dot_nt(blend_grad[rows, :], prob.astype(BF))
            kv_grad[j, rows, :] += dot_nt(queries[rows, :], score_grad)
            term = dot_nn(keys_t(j, rows), score_grad)
            if first:
                query_grad[rows, :] = term
            else:
                query_grad[rows, :] += term

    bias[...] = tile_bias(chunk * tokens, start, True, (tokens, tokens))
    tile(chunk, True)

    def step(j, carry):
        bias[...] = tile_bias(j * tokens, start, False, (tokens, tokens))
        tile(j, False)
        return carry

    lax.fori_loop(low, chunk, step, 0)


def backward_rows_kernel(
    low, grad, start, pre, post, stat_pre, stat_post, kv, vec, wqkv, wout, wup, wdown,
    post_five, low_five, hidden_five, middle_five, vec_five,
    *refs, first,
):
    refs = list(refs)
    if first:
        (result, sum_qkv, sum_out, sum_up, sum_down, sum_vec,
         keys, values, bias, query_grad, kv_grad, hidden_grad, blend_scr, packed) = refs
    else:
        base = [refs.pop(0) for _ in range(5)]
        (result, sum_qkv, sum_vec, wire,
         keys, values, bias, query_grad, kv_grad, hidden_grad, blend_scr, packed,
         sum_out, sum_up, sum_down) = refs
    order = pl.program_id(0)
    chunk = pl.num_programs(0) - 1 - order
    width, tokens = grad.shape[1], grad.shape[2]
    hidden = wup.shape[2]

    def add_ffn(post, low_grad, dz, low_middle):
        sum_down[...] += dot_nt(post[3 * width : 3 * width + hidden, :], low_grad)
        sum_up[...] += dot_nt(post[width : 2 * width, :], dz)
        sum_out[...] += dot_nt(post[0:width, :], low_middle)

    @pl.when(order == 0)
    def _():
        if first:
            for ref in (sum_qkv, sum_out, sum_up, sum_down):
                ref[...] = jnp.zeros_like(ref)
            sum_vec[...] = vec_five[...]
        else:
            for ref, old in zip((sum_qkv, sum_out, sum_up, sum_down), base):
                ref[...] = old[...]
            sum_vec[...] = base[4][...] + vec_five[...]
        add_ffn(post_five, low_five[...], hidden_five[...], middle_five[...])
        kv_grad[...] = jnp.zeros_like(kv_grad)
        for j in range(kv.shape[0]):
            keys[j] = kv[j, 0:width, :].T
            values[j] = kv[j, width : 2 * width, :].T

    low_grad, normed_grad, unit, middle, low_middle, blend_grad = backward_ffn(
        grad[0], post.at[0], stat_post.at[0], wout, wup, wdown, vec, hidden_grad
    )
    add_ffn(post.at[0], low_grad, hidden_grad[...], low_middle)
    add_vec(sum_vec, width, low_grad, normed_grad, unit, low_middle, hidden_grad[...])
    blend_scr[...] = blend_grad
    attend_backward(
        pre.at[0, width : 2 * width, :], blend_scr, post.at[0, 0:width, :], stat_post.at[0],
        keys, values, lambda j, rows: kv[j, rows, :], chunk, low[chunk], start[0],
        bias, query_grad, kv_grad,
    )
    packed[0:width, :] = (query_grad[...] * (width // H) ** -0.5).astype(BF)
    packed[width : 3 * width, :] = kv_grad[chunk].astype(BF)
    result[0] = finish_backward(
        middle, pre.at[0], stat_pre.at[0], packed, wqkv, vec, sum_qkv, sum_vec
    )
    if not first:

        @pl.when(order == pl.num_programs(0) - 1)
        def _():
            pack_lanes(wire, (sum_out, sum_up, sum_down))


def pack_lanes(wire, blocks):
    at = 0
    for ref in blocks:
        rows = ref.shape[0]
        for first in range(0, ref.shape[1], 128):
            wire[at : at + rows, :] = ref[:, first : first + 128].astype(BF)
            at += rows


def unpack_lanes(rows, height, width):
    blocks = rows.reshape(rows.shape[:-2] + (width // 128, height, 128))
    return jnp.swapaxes(blocks, -3, -2).reshape(rows.shape[:-2] + (height, width))


def add_vec(sum_vec, width, low_grad, normed_grad, unit, low_middle, dz):
    sum_vec[:, 0:width] += token_sum(low_middle)
    sum_vec[:, width : 2 * width] += token_sum(low_grad)
    sum_vec[:, 4 * width : 5 * width] += token_sum(normed_grad * unit)
    sum_vec[:, 5 * width : 6 * width] += token_sum(normed_grad)
    sum_vec[:, 6 * width :] += token_sum(dz)


def finish_backward(middle, pre, stat, packed, wqkv, vec, sum_qkv, sum_vec):
    width, tokens = middle.shape
    sum_qkv[...] += dot_nt(pre[0:width, :], packed[...])
    normed_grad = dot_nn(wqkv[0], packed[...])
    unit = pre[2 * width : 3 * width, :].astype(F32)
    gain = widen(vec[0, 2 * width : 3 * width, :], tokens)
    sum_vec[:, 2 * width : 3 * width] += token_sum(normed_grad * unit)
    sum_vec[:, 3 * width : 4 * width] += token_sum(normed_grad)
    return middle + norm_backward(normed_grad, unit, stat[0:1, :], gain)


def backward_rows(layer, low, start, grad, saved, vec, weights, five, base):
    chunks, width, tokens = grad.shape
    pre, kv, post, stat_pre, stat_post = saved
    wqkv, wout, wup, wdown = weights
    hidden = wup.shape[2]
    flip = lambda rows: pl.BlockSpec(
        (1, rows, tokens), lambda i, *_: (chunks - 1 - i, 0, 0)
    )
    whole = lambda arr: pl.BlockSpec(arr.shape, lambda i, *_: (0,) * arr.ndim)
    per_layer = lambda arr: pl.BlockSpec((1,) + arr.shape[1:], lambda i, *_: (layer, 0, 0))
    first = base is None
    sums = [
        jax.ShapeDtypeStruct(s, F32)
        for s in (
            (width, 3 * width), (width, width), (width, hidden), (hidden, width),
            (ONES_ROWS, vec.shape[1]),
        )
    ]
    outs, extra = sums, []
    if not first:
        wire_rows = (width * width + 2 * width * hidden) // 128
        outs = [sums[0], sums[4], jax.ShapeDtypeStruct((wire_rows, 128), BF)]
        extra = [pltpu.VMEM(s.shape, F32) for s in sums[1:4]]
    args = [grad, start, pre, post, stat_pre, stat_post, kv, vec, *weights, *five]
    in_specs = [
        flip(width), flip(1), flip(pre.shape[1]), flip(post.shape[1]), flip(8), flip(8),
        whole(kv), per_layer(vec), *[per_layer(w) for w in weights], *[whole(a) for a in five],
    ]
    if not first:
        args += list(base)
        in_specs += [whole(a) for a in base]
    return pl.pallas_call(
        functools.partial(backward_rows_kernel, first=first),
        grid_spec=pltpu.PrefetchScalarGridSpec(
            num_scalar_prefetch=1, grid=(chunks,), in_specs=in_specs,
            out_specs=[flip(width)] + [whole(s) for s in outs],
            scratch_shapes=[
                pltpu.VMEM((chunks, tokens, width), BF),
                pltpu.VMEM((chunks, tokens, width), BF),
                pltpu.VMEM((tokens, tokens), F32),
                pltpu.VMEM((width, tokens), F32),
                pltpu.VMEM((chunks, 2 * width, tokens), F32),
                pltpu.VMEM((hidden, tokens), BF),
                pltpu.VMEM((width, tokens), BF),
                pltpu.VMEM((3 * width, tokens), BF),
                *extra,
            ],
        ),
        out_shape=[jax.ShapeDtypeStruct(grad.shape, F32)] + outs,
        compiler_params=pltpu.CompilerParams(vmem_limit_bytes=VMEM_LIMIT),
        cost_estimate=pl.CostEstimate(
            flops=chunks * tokens * 4 * 3 * (4 * width * width + 2 * width * hidden),
            bytes_accessed=chunks * tokens * 2 * 4096, transcendentals=0,
        ),
        name="backward_rows",
    )(low, *args)


def backward_split_kernel(has_last, has_next, final, *refs):
    refs = list(refs)
    take = lambda count: [refs.pop(0) for _ in range(count)]
    (place,) = take(1)
    if has_last:
        middle_in, query_in, own_in, near_in, far_in, pre_last, stat_last, vec_last, wqkv = take(9)
        old_qkv, old_vec = take(2)
    top = take(1)[0] if has_next else None
    if has_next:
        start, pre, kv_in, kv_y, kv_c, post, stat_post, vec, wout, wup, wdown = take(11)
    if has_last:
        result, sum_qkv, sum_vec = take(3)
    if has_next:
        middle_out, query_out, own_out, core_out, side_out = take(5)
        low_out, hidden_out, low_middle_out, vec_out = take(4)
    if has_last:
        (packed,) = take(1)
        if final:
            wire = sum_qkv
            (sum_qkv,) = take(1)
        width, tokens = middle_in.shape
        packed[0:width, :] = query_in[...]
        packed[width : 3 * width, :] = (
            own_in[...] + near_in[0].astype(F32) + far_in[...].astype(F32)
        ).astype(BF)
        sum_qkv[...] = old_qkv[...]
        sum_vec[...] = old_vec[...]
        current = finish_backward(
            middle_in[...], pre_last, stat_last, packed, wqkv, vec_last, sum_qkv, sum_vec
        )
        result[...] = current
        if final:
            pack_lanes(wire, (sum_qkv,))
    if has_next:
        keys, values, keys_t, bias, query_grad, kv_grad, blend_scr = take(7)
        width, tokens = top.shape
        if has_last:
            grad = jnp.where(place[2] == 1, current, top[...])
        else:
            grad = top[...]
        mine = place[0]
        kv_grad[...] = jnp.zeros_like(kv_grad)
        for hop, arrived in ((0, kv_in), (1, kv_c.at[0]), (2, kv_y), (3, kv_c.at[1])):
            keys[mine ^ hop] = arrived[0:width, :].T
            keys_t[mine ^ hop] = arrived[0:width, :]
            values[mine ^ hop] = arrived[width : 2 * width, :].T
        low_grad, normed_grad, unit, middle, low_middle, blend_grad = backward_ffn(
            grad, post, stat_post, wout, wup, wdown, vec, hidden_out
        )
        low_out[...] = low_grad
        low_middle_out[...] = low_middle
        middle_out[...] = middle
        vec_out[...] = jnp.zeros_like(vec_out)
        add_vec(vec_out, width, low_grad, normed_grad, unit, low_middle, hidden_out[...])
        blend_scr[...] = blend_grad
        attend_backward(
            pre.at[width : 2 * width, :], blend_scr, post.at[0:width, :], stat_post,
            keys, values, lambda j, rows: keys_t[j, rows, :], mine, place[1], start[...],
            bias, query_grad, kv_grad,
        )
        query_out[...] = (query_grad[...] * (width // H) ** -0.5).astype(BF)
        own_out[...] = kv_grad[mine]
        core_out[0] = kv_grad[mine ^ 1].astype(BF)
        core_out[1] = kv_grad[mine ^ 3].astype(BF)
        side_out[...] = kv_grad[mine ^ 2]


def backward_split(
    layer_last, layer_next, place, vec, weights, last=None, following=None, final=False
):
    wqkv, wout, wup, wdown = weights
    width, hidden = wup.shape[1:]
    whole = lambda arr: pl.BlockSpec(arr.shape, lambda i, *_: (0,) * len(arr.shape))
    of_layer = lambda layer, arr: pl.BlockSpec(
        (1,) + arr.shape[1:], lambda i, *_: (layer, 0, 0)
    )
    has_last, has_next = last is not None, following is not None
    args, in_specs, outs, scratch = [], [], [], []
    shape = jax.ShapeDtypeStruct
    if has_last:
        state_args, (old_qkv, old_vec) = last
        tokens = state_args[0].shape[1]
        args += [*state_args, vec, wqkv, old_qkv, old_vec]
        in_specs += [whole(a) for a in state_args]
        in_specs += [of_layer(layer_last, vec), of_layer(layer_last, wqkv)]
        in_specs += [whole(old_qkv), whole(old_vec)]
        kept = shape((old_qkv.size // 128, 128), BF) if final else shape(old_qkv.shape, F32)
        outs += [shape((width, tokens), F32), kept, shape(old_vec.shape, F32)]
        scratch += [pltpu.VMEM((3 * width, tokens), BF)]
        if final:
            scratch += [pltpu.VMEM(old_qkv.shape, F32)]
    if has_next:
        tokens = following[0].shape[1]
        args += [*following, vec, wout, wup, wdown]
        in_specs += [whole(a) for a in following]
        in_specs += [of_layer(layer_next, a) for a in (vec, wout, wup, wdown)]
        outs += [
            shape((width, tokens), F32), shape((width, tokens), BF),
            shape((2 * width, tokens), F32), shape((2, 2 * width, tokens), BF),
            shape((2 * width, tokens), F32),
            shape((width, tokens), BF), shape((hidden, tokens), BF), shape((width, tokens), BF),
            shape((ONES_ROWS, vec.shape[1]), F32),
        ]
        scratch += [
            pltpu.VMEM((4, tokens, width), BF),
            pltpu.VMEM((4, tokens, width), BF),
            pltpu.VMEM((4, width, tokens), BF),
            pltpu.VMEM((tokens, tokens), F32),
            pltpu.VMEM((width, tokens), F32),
            pltpu.VMEM((4, 2 * width, tokens), F32),
            pltpu.VMEM((width, tokens), BF),
        ]
    return pl.pallas_call(
        functools.partial(backward_split_kernel, has_last, has_next, final),
        grid_spec=pltpu.PrefetchScalarGridSpec(
            num_scalar_prefetch=1, grid=(1,), in_specs=in_specs,
            out_specs=[whole(s) for s in outs], scratch_shapes=scratch,
        ),
        out_shape=outs,
        compiler_params=pltpu.CompilerParams(vmem_limit_bytes=VMEM_LIMIT),
        cost_estimate=pl.CostEstimate(
            flops=tokens * 4 * 3 * (4 * width * width + 2 * width * hidden),
            bytes_accessed=tokens * 2 * 4096, transcendentals=0,
        ),
        name="backward_split",
    )(place, *args)


SEQ = ("y", "core")


def swap(values, hop):
    return lax.ppermute(values, SEQ, [(i, i ^ hop) for i in range(lax.axis_size(SEQ))])


def sum_everywhere(pieces):
    core = lax.axis_index("core")
    half = pieces.shape[0] // 2
    keep = lax.dynamic_slice_in_dim(pieces, core * half, half, 0)
    give = lax.dynamic_slice_in_dim(pieces, (1 - core) * half, half, 0)
    part = (keep.astype(F32) + swap(give, 1).astype(F32)).astype(BF)
    part = lax.all_to_all(part, ("dp", "y"), 0, 0, tiled=True)
    part = jnp.sum(part.astype(F32), axis=0).astype(BF)
    part = jnp.broadcast_to(part[None], (half,) + part.shape)
    mine = lax.all_to_all(part, ("dp", "y"), 0, 0, tiled=True)
    other = swap(mine, 1)
    low = jnp.where(core == 0, mine, other)
    high = jnp.where(core == 0, other, mine)
    return jnp.concatenate([low, high], axis=0)


def to_rows(rows, me):
    pieces = [lax.dynamic_index_in_dim(rows, me ^ hop, 0, keepdims=False) for hop in range(4)]
    arrived = [pieces[0]] + [swap(pieces[hop], hop) for hop in range(1, 4)]
    stacked = jnp.stack(arrived)
    return jnp.stack(
        [lax.dynamic_index_in_dim(stacked, me ^ j, 0, keepdims=False) for j in range(4)]
    )


def fast_device(
    block_input, embedding, cotangent, qkv_weight, out_weight, out_bias, up_weight, up_bias,
    down_weight, down_bias, norm_gain, norm_shift, seg_lengths, loop_counts, token_counts,
):
    row_count, tokens, width = block_input.shape
    chunks = lax.axis_size(SEQ)
    row_len = tokens * chunks
    me = lax.axis_index(SEQ)
    hidden = up_weight.shape[2]

    ends = jnp.cumsum(seg_lengths, axis=-1)
    position = jnp.arange(row_len, dtype=jnp.int32)
    starts = jnp.max(
        jnp.where(ends[:, None, :] <= position[None, :, None], ends[:, None, :], 0), axis=-1
    ).astype(jnp.int32)
    own = lax.dynamic_index_in_dim(starts, me, 0, keepdims=False)
    start_rows = own.reshape(chunks, 1, tokens)
    low_rows = start_rows[:, 0, 0] // tokens
    start_split = lax.dynamic_slice(starts, (row_count - 1, me * tokens), (1, tokens))
    two_row = lax.dynamic_index_in_dim(loop_counts, me, 0, keepdims=False) == 2
    two_split = loop_counts[row_count - 1] == 2
    place = jnp.stack([me, start_split[0, 0] // tokens, two_split]).astype(jnp.int32)
    place_keep = place.at[2].set(1)
    row_weight = token_counts.astype(F32) / row_len

    flip = lambda values: jnp.swapaxes(values, -1, -2)
    vec = jnp.concatenate(
        [
            out_bias, down_bias, norm_gain[:, 0], norm_shift[:, 0], norm_gain[:, 1],
            norm_shift[:, 1], up_bias,
        ],
        axis=-1,
    )
    vec = jnp.broadcast_to(vec[:, :, None], vec.shape + (128,))
    forward_weights = tuple(flip(w) for w in (qkv_weight, out_weight, up_weight, down_weight))
    backward_weights = (qkv_weight, out_weight, up_weight, down_weight)

    input_rows = to_rows(block_input[:-1], me)
    embed_rows = flip(to_rows(embedding[:-1], me)).astype(F32)
    state = flip(input_rows).astype(F32) + embed_rows
    embed_split = flip(embedding[-1]).astype(F32)
    state_split = flip(block_input[-1]).astype(F32) + embed_split

    saved, saved_split = [], []
    finals = []
    pre, kv, stat_pre = forward_split(None, 0, place, state_split, vec, forward_weights)
    for step in range(2 * LAYERS):
        layer = step % LAYERS
        kv_y = swap(kv, 2)
        kv_c = swap(jnp.stack([kv, kv_y]), 1)
        state, *kept = forward_rows(layer, low_rows, start_rows, state, vec, forward_weights)
        saved.append(kept)
        prev = (pre, kv, kv_y, kv_c)
        last = layer == LAYERS - 1
        inner = None if last else layer + 1
        outs = forward_split(
            layer, inner, place, state_split, vec, forward_weights, start_split, prev
        )
        state_split, post, stat_post = outs[:3]
        saved_split.append((start_split, pre, kv, kv_y, kv_c, post, stat_post, stat_pre))
        if last:
            finals.append((state, state_split))
            if step < 2 * LAYERS - 1:
                state = state + embed_rows
                state_split = state_split + embed_split
                pre, kv, stat_pre = forward_split(
                    None, 0, place, state_split, vec, forward_weights
                )
        else:
            pre, kv, stat_pre = outs[3:]

    answer = flip(jnp.where(two_row, finals[1][0], finals[0][0]).astype(BF))
    answer = to_rows(answer, me)
    answer_split = flip(jnp.where(two_split, finals[1][1], finals[0][1]).astype(BF))
    block_output = jnp.concatenate([answer, answer_split[None]], axis=0)

    top = flip(to_rows(cotangent[:-1], me)).astype(F32) * lax.dynamic_index_in_dim(
        row_weight, me, 0, keepdims=False
    )
    top_split = flip(cotangent[-1]).astype(F32) * row_weight[row_count - 1]
    grad = jnp.where(two_row, top, 0.0)
    sums = [None] * LAYERS
    wires = [None] * LAYERS
    last = None
    layer_last = None
    second = second_split = None
    next_top = jnp.where(two_split, top_split, 0.0)
    for step in reversed(range(2 * LAYERS)):
        layer = step % LAYERS
        between = step == LAYERS - 1
        place_now = place if between else place_keep
        start_s, pre_s, kv_s, kv_y, kv_c, post_s, stat_post_s, stat_pre_s = saved_split[step]
        following = (next_top, start_s, pre_s, kv_s, kv_y, kv_c, post_s, stat_post_s)
        outs = backward_split(
            layer_last, layer, place_now, vec, backward_weights, last, following,
            final=step == 0,
        )
        if last is not None:
            result_split, sum_qkv, sum_vec = outs[:3]
            outs = outs[3:]
            if step:
                sums[layer_last][0] = sum_qkv
                sums[layer_last][4] = sum_vec
            else:
                wires[layer_last] += [sum_qkv, sum_vec]
            if between:
                second_split = result_split
        middle, query, own_kv, core, side, low_g, hidden_g, low_m, vec_five = outs
        near = swap(core, 1)
        far = swap((side + near[1].astype(F32)).astype(BF), 2)
        if between:
            second = grad
            grad = jnp.where(two_row, grad, top)
        five = (post_s, low_g, hidden_g, low_m, vec_five)
        grad, *kept = backward_rows(
            layer, low_rows, start_rows, grad, saved[step], vec, backward_weights, five,
            sums[layer],
        )
        if sums[layer] is None:
            sums[layer] = kept
            sum_qkv, sum_vec = kept[0], kept[4]
        else:
            sum_qkv, sum_vec, wire = kept
            wires[layer] = [wire]
        last = ((middle, query, own_kv, near, far, pre_s, stat_pre_s), (sum_qkv, sum_vec))
        layer_last = layer
        next_top = top_split
    grad_split, *rest = backward_split(
        0, None, place, vec, backward_weights, last, None, final=True
    )
    wires[0] += rest

    groups = lax.axis_size("dp")
    devices = groups * chunks
    slot = lax.axis_index("dp")
    count = jnp.sum(token_counts)
    digits = jnp.stack([count // 256, count % 256]).astype(F32) * (me == 0)
    digits = jnp.where(jnp.arange(groups)[:, None] == slot, digits[None], 0.0).reshape(-1)
    small = jnp.concatenate([wires[0][2][0], wires[1][2][0], digits])
    small = jnp.pad(small, (0, -small.size % (devices * 128))).reshape(devices, -1, 128)
    split = lambda rows: rows.reshape(devices, -1, 128)
    parts = [split(wires[l][k]) for l in range(LAYERS) for k in range(2)] + [small.astype(BF)]
    summed = sum_everywhere(jnp.concatenate(parts, axis=1))
    cuts = [0]
    for part in parts:
        cuts.append(cuts[-1] + part.shape[1])
    back = [
        summed[:, low:high].reshape(-1, 128).astype(F32) for low, high in zip(cuts, cuts[1:])
    ]
    small = back[4].reshape(-1)
    vec_rows = vec.shape[1]
    digits = small[2 * vec_rows : 2 * vec_rows + 2 * groups].reshape(groups, 2)
    total = jnp.sum(digits[:, 0]) * 256.0 + jnp.sum(digits[:, 1])
    input_scale = row_count * groups * row_len / total
    weight_scale = row_len / total
    ffn = jnp.stack([back[0], back[2]]) * weight_scale
    grad_qkv = unpack_lanes(jnp.stack([back[1], back[3]]) * weight_scale, width, 3 * width)
    first_rows = width * width // 128
    second_rows = first_rows + width * hidden // 128
    grad_out = unpack_lanes(ffn[:, :first_rows], width, width)
    grad_up = unpack_lanes(ffn[:, first_rows:second_rows], width, hidden)
    grad_down = unpack_lanes(ffn[:, second_rows:], hidden, width)
    vec_sum = small[: 2 * vec_rows].reshape(LAYERS, vec_rows) * weight_scale

    second_home = to_rows(flip(second).astype(BF), me).astype(F32)
    first_home = to_rows(flip(grad).astype(BF), me).astype(F32)
    first_all = jnp.concatenate([first_home, flip(grad_split)[None]], axis=0)
    second_all = jnp.concatenate([second_home, flip(second_split)[None]], axis=0)
    piece = lambda k: vec_sum[:, k * width : (k + 1) * width]
    return (
        block_output,
        first_all * input_scale,
        (first_all + second_all) * input_scale,
        grad_qkv,
        grad_out,
        piece(0),
        grad_up,
        vec_sum[:, 6 * width :],
        grad_down,
        piece(1),
        jnp.stack([piece(2), piece(4)], axis=1),
        jnp.stack([piece(3), piece(5)], axis=1),
    )


def solution(mesh):
    if mesh.shape["seq"] == 4:
        fine = Mesh(mesh.devices.reshape(-1, 2, 2), ("dp", "y", "core"))
        return jax.shard_map(
            fast_device,
            mesh=fine,
            in_specs=(
                P("dp", SEQ, None),
                P("dp", SEQ, None),
                P("dp", SEQ, None),
                P(),
                P(),
                P(),
                P(),
                P(),
                P(),
                P(),
                P(),
                P(),
                P("dp", None),
                P("dp"),
                P("dp"),
            ),
            out_specs=(
                P("dp", SEQ, None),
                P("dp", SEQ, None),
                P("dp", SEQ, None),
                P(),
                P(),
                P(),
                P(),
                P(),
                P(),
                P(),
                P(),
                P(),
            ),
            check_vma=False,
        )
    return jax.shard_map(
        on_device,
        mesh=mesh,
        in_specs=(
            P("dp", "seq", None),
            P("dp", "seq", None),
            P("dp", "seq", None),
            P(),
            P(),
            P(),
            P(),
            P(),
            P(),
            P(),
            P(),
            P(),
            P("dp", None),
            P("dp"),
            P("dp"),
        ),
        out_specs=(
            P("dp", "seq", None),
            P("dp", "seq", None),
            P("dp", "seq", None),
            P(),
            P(),
            P(),
            P(),
            P(),
            P(),
            P(),
            P(),
            P(),
        ),
        check_vma=False,
    )
```

```python
import types

import jax
import jax.numpy as jnp
from jax import lax
from jax.experimental import pallas as pl
from jax.experimental.pallas import tpu as pltpu
from jax.sharding import Mesh, PartitionSpec as P

H = 4
LAYERS = 2


NORM_EPS = 1e-05
MASKED = -1e30


def layer_norm(values, gain, shift):
    center = values - jnp.mean(values, axis=-1, keepdims=True)
    spread = jnp.mean(center * center, axis=-1, keepdims=True)
    return center * lax.rsqrt(spread + NORM_EPS) * gain + shift


def gelu_exact(values):
    return jax.nn.gelu(values, approximate=False)


def matmul(left_side, right_side):
    return jnp.dot(left_side, right_side, preferred_element_type=jnp.float32)


def left_dot(left_side, right_side):
    return lax.dot_general(
        left_side, right_side, (((0,), (0,)), ((), ())), preferred_element_type=jnp.float32
    )


def right_dot(left_side, right_side):
    return lax.dot_general(
        left_side, right_side, (((1,), (1,)), ((), ())), preferred_element_type=jnp.float32
    )


def split_heads(packed, head_count):
    return packed.reshape(packed.shape[0], head_count, packed.shape[1] // head_count)


def attend_forward(queries, key_vals, allowed, head_count, score_scale):
    model_width = queries.shape[1]
    key_rows = split_heads(key_vals[:, :model_width], head_count)
    value_rows = split_heads(key_vals[:, model_width:], head_count)
    scores = (
        jnp.einsum(
            "qhd,khd->hqk",
            split_heads(queries, head_count),
            key_rows,
            preferred_element_type=jnp.float32,
        )
        * score_scale
    )
    scores = jnp.where(allowed[None], scores, MASKED)
    row_max = jnp.max(scores, axis=-1, keepdims=True)
    shifted_exp = jnp.exp(scores - row_max)
    row_total = jnp.sum(shifted_exp, axis=-1, keepdims=True)
    attn_probs = (shifted_exp / row_total).astype(jnp.bfloat16)
    blended = jnp.einsum("hqk,khd->qhd", attn_probs, value_rows, preferred_element_type=jnp.float32)
    return (blended.reshape(queries.shape[0], model_width), (row_max + jnp.log(row_total))[..., 0])


def attention_core(
    query_part, key_part, value_part, grad_part, allowed_part, logsum_part, head_count, score_scale
):
    scores = (
        jnp.einsum(
            "qhd,khd->hqk",
            split_heads(query_part, head_count),
            split_heads(key_part, head_count),
            preferred_element_type=jnp.float32,
        )
        * score_scale
    )
    scores = jnp.where(allowed_part[None], scores, MASKED)
    attn_probs = jnp.exp(scores - logsum_part[..., None])
    grad_probs = jnp.einsum(
        "qhd,khd->hqk",
        split_heads(grad_part, head_count),
        split_heads(value_part, head_count),
        preferred_element_type=jnp.float32,
    )
    return (attn_probs, grad_probs)


def query_grads(grad_scores, key_part, head_count, score_scale):
    result = (
        jnp.einsum(
            "hqk,khd->qhd",
            grad_scores,
            split_heads(key_part, head_count),
            preferred_element_type=jnp.float32,
        )
        * score_scale
    )
    return result.reshape(result.shape[0], -1)


def keyval_grads(grad_scores, attn_probs, query_part, grad_part, head_count, score_scale):
    grad_keys = (
        jnp.einsum(
            "hqk,qhd->khd",
            grad_scores,
            split_heads(query_part, head_count),
            preferred_element_type=jnp.float32,
        )
        * score_scale
    )
    grad_values = jnp.einsum(
        "hqk,qhd->khd",
        attn_probs.astype(jnp.bfloat16),
        split_heads(grad_part, head_count),
        preferred_element_type=jnp.float32,
    )
    return jnp.concatenate(
        [grad_keys.reshape(grad_keys.shape[0], -1), grad_values.reshape(grad_values.shape[0], -1)],
        axis=-1,
    )


def on_device(
    block_input,
    embedding,
    cotangent,
    qkv_weight,
    out_weight,
    out_bias,
    up_weight,
    up_bias,
    down_weight,
    down_bias,
    norm_gain,
    norm_shift,
    seg_lengths,
    loop_counts,
    token_counts,
):
    row_count, block_len, model_width = block_input.shape
    head_count = H
    score_scale = (model_width // head_count) ** (-0.5)
    row_len = block_len * lax.axis_size("seq")
    flat_rows = row_count * block_len
    offset = lax.axis_index("seq") * block_len
    key_pos = jnp.arange(row_len, dtype=jnp.int32)
    own_pos = offset + jnp.arange(block_len, dtype=jnp.int32)
    seg_ends = jnp.cumsum(seg_lengths, axis=-1)
    seg_all = jnp.sum((seg_ends[:, None, :] <= key_pos[None, :, None]).astype(jnp.int32), axis=-1)
    seg_own = lax.dynamic_slice_in_dim(seg_all, offset, block_len, 1)
    allowed = (seg_own[:, :, None] == seg_all[:, None, :]) & (
        key_pos[None, None, :] <= own_pos[None, :, None]
    )
    current = block_input.astype(jnp.float32)
    inject = embedding.astype(jnp.float32)
    stored = []
    finals = []
    for repeat in range(2):
        current = current + inject
        for layer_index in range(LAYERS):
            forward_normed = layer_norm(
                current, norm_gain[layer_index, 0], norm_shift[layer_index, 0]
            ).astype(jnp.bfloat16)
            forward_packed = matmul(
                forward_normed.reshape(flat_rows, model_width), qkv_weight[layer_index]
            ).astype(jnp.bfloat16)
            forward_packed = forward_packed.reshape(row_count, block_len, 3 * model_width)
            forward_key_vals = lax.all_gather(
                forward_packed[:, :, model_width:], "seq", axis=1, tiled=True
            )

            def forward_row(inputs):
                return attend_forward(inputs[0], inputs[1], inputs[2], head_count, score_scale)

            forward_blended, forward_logsum = lax.map(
                forward_row, (forward_packed[:, :, :model_width], forward_key_vals, allowed)
            )
            forward_blended = forward_blended.astype(jnp.bfloat16)
            branch_out = matmul(
                forward_blended.reshape(flat_rows, model_width), out_weight[layer_index]
            ).reshape(row_count, block_len, model_width)
            forward_middle = current + branch_out + out_bias[layer_index]
            forward_normed_two = layer_norm(
                forward_middle, norm_gain[layer_index, 1], norm_shift[layer_index, 1]
            ).astype(jnp.bfloat16)
            forward_up_proj = (
                matmul(forward_normed_two.reshape(flat_rows, model_width), up_weight[layer_index])
                + up_bias[layer_index]
            )
            forward_active = gelu_exact(forward_up_proj).astype(jnp.bfloat16)
            result = (
                forward_middle
                + matmul(forward_active, down_weight[layer_index]).reshape(
                    row_count, block_len, model_width
                )
                + down_bias[layer_index]
            )
            current, stored_layer = (
                result,
                (
                    current,
                    forward_normed,
                    forward_packed,
                    forward_key_vals,
                    forward_logsum,
                    forward_blended,
                    forward_middle,
                    forward_normed_two,
                    forward_up_proj,
                    forward_active,
                ),
            )
            stored.append(stored_layer)
        finals.append(current)
    two_loops = (loop_counts == 2)[:, None, None]
    block_output = jnp.where(two_loops, finals[1], finals[0]).astype(jnp.bfloat16)
    row_weight = token_counts.astype(jnp.float32) / row_len
    grad_top = cotangent.astype(jnp.float32) * row_weight[:, None, None]
    grad_state = jnp.where(two_loops, grad_top, 0.0)
    layer_sums = [None] * LAYERS
    second_pass = grad_state
    for repeat in (1, 0):
        for layer_index in reversed(range(LAYERS)):
            backward_stored_layer = stored[repeat * LAYERS + layer_index]
            (
                backward_current,
                normed,
                packed,
                key_vals,
                logsum,
                blended,
                middle,
                normed_two,
                up_proj,
                active,
            ) = backward_stored_layer
            grad_flat = grad_state.reshape(flat_rows, model_width)
            grad_low = grad_flat.astype(jnp.bfloat16)
            grad_down = left_dot(active, grad_low)
            grad_down_bias = jnp.sum(grad_flat, axis=0)
            grad_active = right_dot(grad_low, down_weight[layer_index])
            grad_up_proj = jax.vjp(gelu_exact, up_proj)[1](grad_active)[0].astype(jnp.bfloat16)
            grad_up_bias = jnp.sum(grad_up_proj.astype(jnp.float32), axis=0)
            grad_up = left_dot(normed_two.reshape(flat_rows, model_width), grad_up_proj)
            grad_normed_two = right_dot(grad_up_proj, up_weight[layer_index]).reshape(
                row_count, block_len, model_width
            )
            pull_two = jax.vjp(
                layer_norm, middle, norm_gain[layer_index, 1], norm_shift[layer_index, 1]
            )[1]
            grad_middle, gain_two, shift_two = pull_two(grad_normed_two)
            grad_middle = grad_middle + grad_state
            middle_flat = grad_middle.reshape(flat_rows, model_width)
            middle_low = middle_flat.astype(jnp.bfloat16)
            grad_out = left_dot(blended.reshape(flat_rows, model_width), middle_low)
            grad_out_bias = jnp.sum(middle_flat, axis=0)
            grad_blend = (
                right_dot(middle_low, out_weight[layer_index])
                .astype(jnp.bfloat16)
                .reshape(row_count, block_len, model_width)
            )
            queries = packed[:, :, :model_width]

            def full_row(inputs):
                query_part, keyval_part, grad_part, allowed_part, logsum_part = inputs
                attn_probs, grad_probs = attention_core(
                    query_part,
                    keyval_part[:, :model_width],
                    keyval_part[:, model_width:],
                    grad_part,
                    allowed_part,
                    logsum_part,
                    head_count,
                    score_scale,
                )
                row_delta = jnp.sum(attn_probs * grad_probs, axis=-1, keepdims=True)
                grad_scores = (attn_probs * (grad_probs - row_delta)).astype(jnp.bfloat16)
                return (
                    query_grads(grad_scores, keyval_part[:, :model_width], head_count, score_scale),
                    keyval_grads(
                        grad_scores, attn_probs, query_part, grad_part, head_count, score_scale
                    ),
                )

            grad_query, partial_kv = lax.map(
                full_row, (queries, key_vals, grad_blend, allowed, logsum)
            )
            grad_keyval = lax.psum_scatter(
                partial_kv.astype(jnp.bfloat16), "seq", scatter_dimension=1, tiled=True
            )
            grad_packed = jnp.concatenate(
                [grad_query.astype(jnp.bfloat16), grad_keyval], axis=-1
            ).reshape(flat_rows, 3 * model_width)
            grad_qkv = left_dot(normed.reshape(flat_rows, model_width), grad_packed)
            grad_normed = right_dot(grad_packed, qkv_weight[layer_index]).reshape(
                row_count, block_len, model_width
            )
            pull_one = jax.vjp(
                layer_norm, backward_current, norm_gain[layer_index, 0], norm_shift[layer_index, 0]
            )[1]
            grad_current, gain_one, shift_one = pull_one(grad_normed)
            grad_current = grad_current + grad_middle
            grad_state = grad_current
            grad_set = (
                grad_qkv,
                grad_out,
                grad_out_bias,
                grad_up,
                grad_up_bias,
                grad_down,
                grad_down_bias,
                jnp.stack([gain_one, gain_two]),
                jnp.stack([shift_one, shift_two]),
            )
            if repeat == 1:
                layer_sums[layer_index] = grad_set
            else:
                layer_sums[layer_index] = jax.tree.map(jnp.add, layer_sums[layer_index], grad_set)
        if repeat == 1:
            second_pass = grad_state
            grad_state = jnp.where(two_loops, grad_state, grad_top)
    grad_embed = grad_state + second_pass
    stacked = jax.tree.map(lambda *members: jnp.stack(members), *layer_sums)
    (
        sum_qkv,
        sum_out,
        sum_out_bias,
        sum_up,
        sum_up_bias,
        sum_down,
        sum_down_bias,
        sum_gain,
        sum_shift,
    ) = stacked
    total = lax.psum(jnp.sum(token_counts), "dp").astype(jnp.float32)
    summed = lax.psum(
        (
            sum_qkv,
            sum_out,
            sum_out_bias,
            sum_up,
            sum_up_bias,
            sum_down,
            sum_down_bias,
            sum_gain,
            sum_shift,
        ),
        ("dp", "seq"),
    )
    input_scale = row_count * lax.axis_size("dp") * row_len / total
    weight_scale = row_len / total
    return (
        block_output,
        grad_state * input_scale,
        grad_embed * input_scale,
        summed[0] * weight_scale,
        summed[1] * weight_scale,
        summed[2] * weight_scale,
        summed[3] * weight_scale,
        summed[4] * weight_scale,
        summed[5] * weight_scale,
        summed[6] * weight_scale,
        summed[7] * weight_scale,
        summed[8] * weight_scale,
    )


BF = jnp.bfloat16
F32 = jnp.float32
ERF_TERMS = (7.97869712e-01, 3.63922863e-02, -8.78266373e-05, -3.66934271e-05, 1.42500458e-06)
DENSITY_RATE = -0.7213475204444817
DENSITY_BASE = -1.3257480647361593
VMEM_LIMIT = 56 * 1024 * 1024
ONES_ROWS = 16


def dot_nn(left_side, right_side):
    return jnp.dot(left_side, right_side, preferred_element_type=F32)


def dot_nt(left_side, right_side):
    return lax.dot_general(
        left_side, right_side, (((1,), (1,)), ((), ())), preferred_element_type=F32
    )


def gelu_and_slope(z):
    square = z * z
    series = ERF_TERMS[-1] * square + ERF_TERMS[-2]
    for term in ERF_TERMS[-3::-1]:
        series = series * square + term
    cdf = 0.5 + 0.5 * jnp.tanh(z * series)
    density = jnp.exp2(square * DENSITY_RATE + DENSITY_BASE)
    return z * cdf, cdf + z * density


def norm_forward(values, gain, shift):
    center = values - jnp.mean(values, axis=0, keepdims=True)
    spread = jnp.mean(center * center, axis=0, keepdims=True)
    inverse = lax.rsqrt(spread + NORM_EPS)
    unit = center * inverse
    return unit, inverse, (unit * gain + shift).astype(BF)


def norm_backward(grad, unit, inverse, gain):
    scaled = grad * gain
    first = jnp.mean(scaled, axis=0, keepdims=True)
    second = jnp.mean(scaled * unit, axis=0, keepdims=True)
    return inverse * (scaled - first - unit * second)


def columns(vec):
    turned = vec[0].T

    def column(first, last):
        return jnp.concatenate(
            [turned[:, k : k + 1] for k in range(first // 128, last // 128)], axis=0
        )

    return column


def project_qkv(state, qkv_t, vec, pre, kv, stat, scale):
    width = state.shape[0]
    column = columns(vec)
    gain = column(2 * width, 3 * width)
    shift = column(3 * width, 4 * width)
    unit, inverse, normed = norm_forward(state, gain, shift)
    pre[0:width, :] = normed
    pre[2 * width : 3 * width, :] = unit.astype(BF)
    pre[width : 2 * width, :] = (dot_nn(qkv_t[0, 0:width, :], normed) * scale).astype(BF)
    kv[0:width, :] = dot_nn(qkv_t[0, width : 2 * width, :], normed).astype(BF)
    kv[width : 2 * width, :] = dot_nn(qkv_t[0, 2 * width : 3 * width, :], normed).astype(BF)
    stat[0:1, :] = inverse


def pad_head(block, odd):
    blank = jnp.zeros_like(block)
    return jnp.concatenate([blank, block] if odd else [block, blank], axis=0)


def tile_bias(first_key, start, causal, shape):
    key_at = lax.broadcasted_iota(jnp.int32, shape, 0)
    keep = key_at + first_key >= start
    if causal:
        keep = keep & (key_at <= lax.broadcasted_iota(jnp.int32, shape, 1))
    return jnp.where(keep, 0.0, MASKED)


def attend_chunk(queries, keys, values_t, chunk, low, start, bias, total, stat, blended):
    width, tokens = queries.shape
    head = width // H
    pair = 2 * head

    def scores(j, h):
        lanes = pl.ds((h // 2) * pair, pair)
        return dot_nn(keys[j, :, lanes], pad_head(queries[h * head : (h + 1) * head, :], h % 2)) + bias[...]

    head_rows = [slice(h * head, (h + 1) * head) for h in range(H)]

    def weigh(j, tops):
        parts = [scores(j, h) for h in range(H)]
        new_tops = [jnp.max(part, axis=0, keepdims=True) for part in parts]
        if tops is not None:
            new_tops = [jnp.maximum(old, new) for old, new in zip(tops, new_tops)]
        weights = [jnp.exp(part - top) for part, top in zip(parts, new_tops)]
        sums = [jnp.sum(weight, axis=0, keepdims=True) for weight in weights]
        terms = [
            dot_nn(values_t[j, rows, :], weight.astype(BF))
            for rows, weight in zip(head_rows, weights)
        ]
        return tuple(new_tops), sums, terms

    bias[...] = tile_bias(chunk * tokens, start, True, (tokens, tokens))
    tops, sums, terms = weigh(chunk, None)
    for rows, term in zip(head_rows, terms):
        total[rows, :] = term

    def step(j, carry):
        tops, sums = carry
        bias[...] = tile_bias(j * tokens, start, False, (tokens, tokens))
        new_tops, new_sums, terms = weigh(j, tops)
        fades = [jnp.exp(old - new) for old, new in zip(tops, new_tops)]
        for rows, term, fade in zip(head_rows, terms, fades):
            total[rows, :] = total[rows, :] * fade + term
        return new_tops, tuple(old * fade + new for old, fade, new in zip(sums, fades, new_sums))

    tops, sums = lax.fori_loop(low, chunk, step, (tuple(tops), tuple(sums)))
    for h in range(H):
        rows = slice(h * head, (h + 1) * head)
        blended[rows, :] = (total[rows, :] / sums[h]).astype(BF)
        stat[h : h + 1, :] = tops[h] + jnp.log(sums[h])


def finish_layer(state, out_t, up_t, down_t, vec, post, stat):
    width, tokens = state.shape
    hidden = up_t.shape[1]
    column = columns(vec)
    middle = state + dot_nn(out_t[0], post[0:width, :]) + column(0, width)
    gain = column(4 * width, 5 * width)
    shift = column(5 * width, 6 * width)
    unit, inverse, normed = norm_forward(middle, gain, shift)
    post[width : 2 * width, :] = normed
    post[2 * width : 3 * width, :] = unit.astype(BF)
    stat[H : H + 1, :] = inverse
    z = dot_nn(up_t[0], normed) + column(6 * width, 6 * width + hidden)
    active, slope = gelu_and_slope(z)
    post[3 * width : 3 * width + hidden, :] = active.astype(BF)
    post[3 * width + hidden :, :] = slope.astype(BF)
    return (
        middle
        + dot_nn(down_t[0], post[3 * width : 3 * width + hidden, :])
        + column(width, 2 * width)
    )


def launch(name, body, place, grid, ins, outs, scratch=(), flops=0):
    scratch = dict(scratch)
    names = [*ins, *outs, *scratch]

    def kernel(place_ref, *refs):
        body(place_ref, types.SimpleNamespace(**dict(zip(names, refs))))

    results = pl.pallas_call(
        kernel,
        grid_spec=pltpu.PrefetchScalarGridSpec(
            num_scalar_prefetch=1,
            grid=(grid,),
            in_specs=[spec for _, spec in ins.values()],
            out_specs=[spec for _, spec in outs.values()],
            scratch_shapes=list(scratch.values()),
        ),
        out_shape=[shape for shape, _ in outs.values()],
        compiler_params=pltpu.CompilerParams(vmem_limit_bytes=VMEM_LIMIT),
        cost_estimate=pl.CostEstimate(flops=flops, bytes_accessed=1, transcendentals=0),
        name=name,
    )(place, *[array for array, _ in ins.values()])
    return dict(zip(outs, results))


def whole(array):
    return array, pl.BlockSpec(array.shape, lambda i, *_: (0,) * len(array.shape))


def of_layer(array, layer):
    return array, pl.BlockSpec((1,) + array.shape[1:], lambda i, *_: (layer, 0, 0))


def each(array):
    return array, pl.BlockSpec((1,) + array.shape[1:], lambda i, *_: (i, 0, 0))


def each_back(array):
    count = array.shape[0]
    return array, pl.BlockSpec(
        (1,) + array.shape[1:], lambda i, *_: (count - 1 - i, 0, 0)
    )


def shaped(dims, dtype):
    return jax.ShapeDtypeStruct(dims, dtype)


def segment_starts(place, first, count):
    position = lax.broadcasted_iota(jnp.int32, (1, count), 1) + first
    starts = jnp.zeros((1, count), jnp.int32)
    end = jnp.int32(0)
    begin = jnp.int32(0)
    for k in range(3, place.shape[0]):
        end = end + place[k]
        starts = jnp.where(position >= end, end, starts)
        begin = jnp.where(first >= end, end, begin)
    return starts, begin // count


def gather_tokens(env, name, me):
    for hop in range(4):
        env.spread[me ^ hop] = getattr(env, f"{name}_{hop}")[...]


def deal_tokens(env, name, value, chunk, me):
    for hop in range(4):

        @pl.when(chunk == (me ^ hop))
        def _(hop=hop):
            getattr(env, f"{name}_{hop}")[...] = value


def token_ins(name, blocks):
    return {f"{name}_{hop}": whole(block) for hop, block in enumerate(blocks)}


def token_outs(name, tokens, width):
    return {f"{name}_{hop}": whole(shaped((tokens, width), BF)) for hop in range(4)}


def as_tokens(values):
    return values.astype(BF).T


def as_features(tokens):
    return tokens.T.astype(F32)


def forward_rows(layer, place, vec, weights, state=None, tokens=None, first_end=None):
    chunks = 4
    count = state.shape[2] if tokens is None else tokens[0].shape[0]
    qkv_t, out_t, up_t, down_t = weights
    width, hidden = out_t.shape[2], up_t.shape[1]
    post_rows = 3 * width + 2 * hidden

    def body(place, env):
        chunk = pl.program_id(0)
        me = place[0]
        current = env.state.at[0] if state is not None else None
        if tokens is not None:

            @pl.when(chunk == 0)
            def _():
                gather_tokens(env, "tokens", me)

            added = as_features(env.spread[chunk])
            env.current[...] = added if state is None else added + env.state[0]
            current = env.current
        project_qkv(
            current[...], env.qkv_t, env.vec, env.pre.at[0], env.kv.at[0], env.stat_pre.at[0],
            (width // H) ** -0.5,
        )
        env.keys[chunk] = env.kv[0, 0:width, :].T
        env.values_t[chunk] = env.kv[0, width : 2 * width, :]
        start, low = segment_starts(place, chunk * count, count)
        attend_chunk(
            env.pre.at[0, width : 2 * width, :], env.keys, env.values_t, chunk, low, start, env.bias, env.total, env.stat_post.at[0],
            env.post.at[0, 0:width, :],
        )
        result = finish_layer(
            current[...], env.out_t, env.up_t, env.down_t, env.vec, env.post.at[0],
            env.stat_post.at[0],
        )
        if first_end is None:
            env.result[0] = result
        else:
            answer = jnp.where(place[1] == 1, result, env.first_end[0])
            deal_tokens(env, "answer", as_tokens(answer), chunk, me)

    ins = {"vec": of_layer(vec, layer)}
    for name, weight in zip(("qkv_t", "out_t", "up_t", "down_t"), weights):
        ins[name] = of_layer(weight, layer)
    scratch = {
        "keys": pltpu.VMEM((chunks, count, width), BF),
        "values_t": pltpu.VMEM((chunks, width, count), BF),
        "bias": pltpu.VMEM((count, count), F32),
        "total": pltpu.VMEM((width, count), F32),
    }
    if state is not None:
        ins["state"] = each(state)
    if tokens is not None:
        ins |= token_ins("tokens", tokens)
        scratch["spread"] = pltpu.VMEM((chunks, count, width), BF)
        scratch["current"] = pltpu.VMEM((width, count), F32)
    outs = {}
    if first_end is None:
        outs["result"] = each(shaped((chunks, width, count), F32))
    else:
        ins["first_end"] = each(first_end)
        outs |= token_outs("answer", count, width)
    outs["pre"] = each(shaped((chunks, 3 * width, count), BF))
    outs["kv"] = each(shaped((chunks, 2 * width, count), BF))
    outs["post"] = each(shaped((chunks, post_rows, count), BF))
    outs["stat_pre"] = each(shaped((chunks, 8, count), F32))
    outs["stat_post"] = each(shaped((chunks, 8, count), F32))
    flops = chunks * count * 6 * (4 * width * width + 2 * width * hidden)
    return launch("forward_rows", body, place, chunks, ins, outs, scratch, flops)


def of_row(array, row):
    return array, pl.BlockSpec((1,) + array.shape[1:], lambda i, *_: (row, 0, 0))


def forward_split(
    place, vec, weights, last=None, following=None, state=None, prev=None, pre=None,
    block_input=None, embedding=None, first_end=None,
):
    qkv_t, out_t, up_t, down_t = weights
    width, hidden = out_t.shape[2], up_t.shape[1]
    row = embedding.shape[0] - 1 if embedding is not None else None
    count = embedding.shape[1] if state is None else state.shape[1]

    def body(place, env):
        me = place[0]
        if last is not None:
            for hop in range(4):
                arrived = getattr(env, f"kv_{hop}")
                env.keys[me ^ hop] = arrived[0:width, :].T
                env.values_t[me ^ hop] = arrived[width : 2 * width, :]
            start, low = segment_starts(place, me * count, count)
            attend_chunk(
                env.pre_in.at[width : 2 * width, :], env.keys, env.values_t, me, low, start,
                env.bias, env.total, env.stat_post, env.post.at[0:width, :],
            )
            current = finish_layer(
                env.state[...], env.out_t, env.up_t, env.down_t, env.vec, env.post, env.stat_post
            )
            if first_end is not None:
                answer = jnp.where(place[1] == 1, current, env.first_end[...])
                env.answer[...] = as_tokens(answer)
            else:
                env.result[...] = current
        if following is not None:
            if embedding is not None:
                added = as_features(env.embedding[0])
                if last is None:
                    current = as_features(env.block_input[0]) + added
                else:
                    current = env.result[...] + added
                env.begun[...] = current
            project_qkv(
                current, env.qkv_t, env.vec_next, env.pre, env.kv, env.stat_pre,
                (width // H) ** -0.5,
            )

    ins, outs, scratch = {}, {}, {}
    if last is not None:
        ins |= {f"kv_{hop}": whole(block) for hop, block in enumerate(prev)}
        ins |= {"state": whole(state), "pre_in": whole(pre)}
        ins["vec"] = of_layer(vec, last)
        for name, weight in zip(("out_t", "up_t", "down_t"), weights[1:]):
            ins[name] = of_layer(weight, last)
        if first_end is not None:
            ins["first_end"] = whole(first_end)
            outs["answer"] = whole(shaped((count, width), BF))
        else:
            outs["result"] = whole(shaped((width, count), F32))
        outs["post"] = whole(shaped((3 * width + 2 * hidden, count), BF))
        outs["stat_post"] = whole(shaped((8, count), F32))
        scratch = {
            "keys": pltpu.VMEM((4, count, width), BF),
            "values_t": pltpu.VMEM((4, width, count), BF),
            "bias": pltpu.VMEM((count, count), F32),
            "total": pltpu.VMEM((width, count), F32),
        }
    if following is not None:
        ins["vec_next"] = of_layer(vec, following)
        ins["qkv_t"] = of_layer(qkv_t, following)
        if embedding is not None:
            ins["embedding"] = of_row(embedding, row)
            outs["begun"] = whole(shaped((width, count), F32))
        if block_input is not None:
            ins["block_input"] = of_row(block_input, row)
        outs["pre"] = whole(shaped((3 * width, count), BF))
        outs["kv"] = whole(shaped((2 * width, count), BF))
        outs["stat_pre"] = whole(shaped((8, count), F32))
    flops = count * 6 * (4 * width * width + 2 * width * hidden)
    return launch("forward_split", body, place, 1, ins, outs, scratch, flops)


def backward_ffn(grad, post, stat, wout, wup, wdown, vec, hidden_grad):
    width, tokens = grad.shape
    hidden = wup.shape[2]
    low_grad = grad.astype(BF)
    hidden_grad[...] = (
        dot_nn(wdown[0], low_grad) * post[3 * width + hidden :, :].astype(F32)
    ).astype(BF)
    normed_grad = dot_nn(wup[0], hidden_grad[...])
    unit = post[2 * width : 3 * width, :].astype(F32)
    gain = columns(vec)(4 * width, 5 * width)
    middle = grad + norm_backward(normed_grad, unit, stat[H : H + 1, :], gain)
    low_middle = middle.astype(BF)
    blend_grad = dot_nn(wout[0], low_middle).astype(BF)
    return low_grad, normed_grad, unit, middle, low_middle, blend_grad


def token_sum(rows):
    return dot_nt(jnp.ones((ONES_ROWS, rows.shape[1]), BF), rows.astype(BF))


def attend_backward(
    queries, blend_grad, blended, stat, keys, values, keys_t, chunk, low, start,
    bias, query_grad, kv_grad,
):
    width, tokens = queries.shape
    head = width // H
    pair = 2 * head
    head_rows = [slice(h * head, (h + 1) * head) for h in range(H)]
    deltas = [
        jnp.sum(
            blend_grad[rows, :].astype(F32) * blended[rows, :].astype(F32), axis=0, keepdims=True
        )
        for rows in head_rows
    ]

    def tile(j, first):
        parts, prob_grads = [], []
        for h, rows in enumerate(head_rows):
            lanes = pl.ds((h // 2) * pair, pair)
            parts.append(dot_nn(keys[j, :, lanes], pad_head(queries[rows, :], h % 2)))
            prob_grads.append(dot_nn(values[j, :, lanes], pad_head(blend_grad[rows, :], h % 2)))
        probs = [
            jnp.exp(part + bias[...] - stat[h : h + 1, :]) for h, part in enumerate(parts)
        ]
        score_grads = [
            (prob * (prob_grad - delta)).astype(BF)
            for prob, prob_grad, delta in zip(probs, prob_grads, deltas)
        ]
        for rows, prob, score_grad in zip(head_rows, probs, score_grads):
            value_rows = slice(width + rows.start, width + rows.stop)
            kv_grad[j, value_rows, :] += dot_nt(blend_grad[rows, :], prob.astype(BF))
            kv_grad[j, rows, :] += dot_nt(queries[rows, :], score_grad)
            term = dot_nn(keys_t(j, rows), score_grad)
            if first:
                query_grad[rows, :] = term
            else:
                query_grad[rows, :] += term

    bias[...] = tile_bias(chunk * tokens, start, True, (tokens, tokens))
    tile(chunk, True)

    def step(j, carry):
        bias[...] = tile_bias(j * tokens, start, False, (tokens, tokens))
        tile(j, False)
        return carry

    lax.fori_loop(low, chunk, step, 0)


def add_vec(sum_vec, width, low_grad, normed_grad, unit, low_middle, dz):
    sum_vec[:, 0:width] += token_sum(low_middle)
    sum_vec[:, width : 2 * width] += token_sum(low_grad)
    sum_vec[:, 4 * width : 5 * width] += token_sum(normed_grad * unit)
    sum_vec[:, 5 * width : 6 * width] += token_sum(normed_grad)
    sum_vec[:, 6 * width :] += token_sum(dz)


def finish_backward(middle, pre, stat, packed, wqkv, vec, sum_qkv, sum_vec):
    width, tokens = middle.shape
    sum_qkv[...] += dot_nt(pre[0:width, :], packed[...])
    normed_grad = dot_nn(wqkv[0], packed[...])
    unit = pre[2 * width : 3 * width, :].astype(F32)
    gain = columns(vec)(2 * width, 3 * width)
    sum_vec[:, 2 * width : 3 * width] += token_sum(normed_grad * unit)
    sum_vec[:, 3 * width : 4 * width] += token_sum(normed_grad)
    return middle + norm_backward(normed_grad, unit, stat[0:1, :], gain)


def pack_lanes(wire, blocks):
    at = 0
    for ref in blocks:
        rows = ref.shape[0]
        for first in range(0, ref.shape[1], 128):
            wire[at : at + rows, :] = ref[:, first : first + 128].astype(BF)
            at += rows


def backward_rows(
    layer, place, saved, vec, weights, five, base=None, grad=None, tokens=None,
    keep=True, travel=False,
):
    chunks, _, count = saved["kv"].shape
    wqkv, wout, wup, wdown = weights
    width, hidden = wup.shape[1:]
    row_len = chunks * count
    first = base is None
    part = hidden // chunks
    vec_len = 6 * width + hidden

    def body(place, env):
        order = pl.program_id(0)
        chunk = chunks - 1 - order
        me = place[0]

        @pl.when(order == 0)
        def _():
            if tokens is not None:
                gather_tokens(env, "tokens", me)
            for ref in (env.sum_qkv, env.sum_up, env.sum_down):
                ref[...] = jnp.zeros_like(ref)
            env.sum_out[...] = dot_nt(env.blend_five[...], env.middle_five[...])
            env.sum_vec[...] = env.vec_five[...]
            if not first:
                env.sum_vec[...] += env.base_vec[...]
            env.kv_grad[...] = jnp.zeros_like(env.kv_grad)
            for j in range(chunks):
                env.keys[j] = env.kv[j, 0:width, :].T
                env.values[j] = env.kv[j, width : 2 * width, :].T

        spread = pl.ds(pl.multiple_of(order * part, part), part)
        env.sum_down[spread, :] += dot_nt(env.active_five[...], env.low_five[...])
        env.sum_up[:, spread] += dot_nt(env.normed_five[...], env.hidden_five[...])
        if not first:
            env.sum_down[spread, :] += env.base_down[...]
            env.sum_up[:, spread] += env.base_up[...]
            for ref, old in ((env.sum_qkv, env.base_qkv), (env.sum_out, env.base_out)):
                rows = old.shape[0]
                ref[pl.ds(pl.multiple_of(order * rows, rows), rows), :] += old[...]

        current = env.grad.at[0] if grad is not None else None
        if tokens is not None:
            top = as_features(env.spread[chunk]) * (place[2].astype(F32) * (1.0 / row_len))
            two = place[1] == 1
            env.current[...] = (
                jnp.where(two, top, 0.0) if grad is None else jnp.where(two, env.grad[0], top)
            )
            current = env.current
        post = env.post.at[0]
        low_grad, normed_grad, unit, middle, low_middle, blend_grad = backward_ffn(
            current[...], post, env.stat_post.at[0], env.wout, env.wup, env.wdown, env.vec,
            env.hidden_grad,
        )
        env.sum_down[...] += dot_nt(post[3 * width : 3 * width + hidden, :], low_grad)
        env.sum_up[...] += dot_nt(post[width : 2 * width, :], env.hidden_grad[...])
        env.sum_out[...] += dot_nt(post[0:width, :], low_middle)
        add_vec(
            env.sum_vec, width, low_grad, normed_grad, unit, low_middle, env.hidden_grad[...]
        )
        env.blend_grad[...] = blend_grad
        start, low = segment_starts(place, chunk * count, count)
        attend_backward(
            env.pre.at[0, width : 2 * width, :], env.blend_grad, post.at[0:width, :],
            env.stat_post.at[0], env.keys, env.values, lambda j, rows: env.kv[j, rows, :],
            chunk, low, start, env.bias, env.query_grad, env.kv_grad,
        )
        env.packed[0:width, :] = (env.query_grad[...] * (width // H) ** -0.5).astype(BF)
        env.packed[width : 3 * width, :] = env.kv_grad[chunk].astype(BF)
        result = finish_backward(
            middle, env.pre.at[0], env.stat_pre.at[0], env.packed, env.wqkv, env.vec,
            env.sum_qkv, env.sum_vec,
        )
        if keep:
            env.result[0] = result
        if travel:
            deal_tokens(env, "travel", as_tokens(result), chunk, me)
        if not first:

            @pl.when(order == chunks - 1)
            def _():
                pack_lanes(env.wire, (env.sum_out, env.sum_up, env.sum_down))

    ins = {"vec": of_layer(vec, layer), "kv": whole(saved["kv"])}
    for name in ("pre", "post", "stat_pre", "stat_post"):
        ins[name] = each_back(saved[name])
    for name, weight in zip(("wqkv", "wout", "wup", "wdown"), weights):
        ins[name] = of_layer(weight, layer)
    if grad is not None:
        ins["grad"] = each_back(grad)
    if tokens is not None:
        ins |= token_ins("tokens", tokens)
    post_five = five["post"]
    block = lambda rows, pick: (post_five, pl.BlockSpec((rows, count), lambda i, *_: (pick(i), 0)))
    ins["blend_five"] = block(width, lambda i: 0)
    ins["normed_five"] = block(width, lambda i: 1)
    ins["active_five"] = block(part, lambda i: 3 * width // part + i)
    ins["hidden_five"] = (
        five["hidden"], pl.BlockSpec((part, count), lambda i, *_: (i, 0))
    )
    for name in ("low", "middle", "vec"):
        ins[name + "_five"] = whole(five[name])
    sums = {
        "sum_qkv": (width, 3 * width), "sum_out": (width, width), "sum_up": (width, hidden),
        "sum_down": (hidden, width), "sum_vec": (ONES_ROWS, vec_len),
    }
    if not first:
        cut = lambda array, shape, at: (array, pl.BlockSpec(shape, lambda i, *_: at(i)))
        ins["base_qkv"] = cut(base["sum_qkv"], (width // chunks, 3 * width), lambda i: (i, 0))
        ins["base_out"] = cut(base["sum_out"], (width // chunks, width), lambda i: (i, 0))
        ins["base_up"] = cut(base["sum_up"], (width, part), lambda i: (0, i))
        ins["base_down"] = cut(base["sum_down"], (part, width), lambda i: (i, 0))
        ins["base_vec"] = whole(base["sum_vec"])
    outs, scratch = {}, {}
    if keep:
        outs["result"] = each_back(shaped((chunks, width, count), F32))
    if travel:
        outs |= token_outs("travel", count, width)
    for name, dims in sums.items():
        if first or name in ("sum_qkv", "sum_vec"):
            outs[name] = whole(shaped(dims, F32))
        else:
            scratch[name] = pltpu.VMEM(dims, F32)
    if not first:
        outs["wire"] = whole(shaped(((width * width + 2 * width * hidden) // 128, 128), BF))
    if tokens is not None:
        scratch["spread"] = pltpu.VMEM((chunks, count, width), BF)
        scratch["current"] = pltpu.VMEM((width, count), F32)
    scratch |= {
        "keys": pltpu.VMEM((chunks, count, width), BF),
        "values": pltpu.VMEM((chunks, count, width), BF),
        "bias": pltpu.VMEM((count, count), F32),
        "query_grad": pltpu.VMEM((width, count), F32),
        "kv_grad": pltpu.VMEM((chunks, 2 * width, count), F32),
        "hidden_grad": pltpu.VMEM((hidden, count), BF),
        "blend_grad": pltpu.VMEM((width, count), BF),
        "packed": pltpu.VMEM((3 * width, count), BF),
    }
    flops = chunks * count * 12 * (4 * width * width + 2 * width * hidden)
    return launch("backward_rows", body, place, chunks, ins, outs, scratch, flops)


def backward_split(
    place, vec, weights, last=None, following=None, ended=None, sums=None, begun=None,
    cotangent=None, final=False, keep=False, row_len=None,
):
    wqkv, wout, wup, wdown = weights
    width, hidden = wup.shape[1:]
    vec_len = 6 * width + hidden
    count = (ended or begun)["stat_pre"].shape[1]

    def body(place, env):
        me = place[0]
        if last is not None:
            sum_qkv = env.total_qkv if final else env.sum_qkv
            env.packed[0:width, :] = env.query_in[...]
            kv_total = env.own_in[...]
            for hop in range(1, 4):
                kv_total = kv_total + getattr(env, f"in_{hop}")[...].astype(F32)
            env.packed[width : 3 * width, :] = kv_total.astype(BF)
            sum_qkv[...] = env.old_qkv[...]
            env.sum_vec[...] = env.old_vec[...]
            current = finish_backward(
                env.middle_in[...], env.pre_last, env.stat_last, env.packed, env.wqkv,
                env.vec_last, sum_qkv, env.sum_vec,
            )
            if keep:
                env.result[...] = current.T
            if final:
                pack_lanes(env.wire, (sum_qkv,))
        if following is not None:
            if cotangent is not None:
                top = as_features(env.cotangent[0]) * (place[2].astype(F32) * (1.0 / row_len))
                two = place[1] == 1
                grad = jnp.where(two, top, 0.0) if last is None else jnp.where(two, current, top)
            else:
                grad = current
            env.kv_grad[...] = jnp.zeros_like(env.kv_grad)
            for hop in range(4):
                arrived = getattr(env, f"kv_{hop}")
                env.keys[me ^ hop] = arrived[0:width, :].T
                env.keys_t[me ^ hop] = arrived[0:width, :]
                env.values[me ^ hop] = arrived[width : 2 * width, :].T
            low_grad, normed_grad, unit, middle, low_middle, blend_grad = backward_ffn(
                grad, env.post, env.stat_post, env.wout, env.wup, env.wdown, env.vec, env.hidden
            )
            env.low[...] = low_grad
            env.middle[...] = low_middle
            env.middle_out[...] = middle
            env.vec_out[...] = jnp.zeros_like(env.vec_out)
            add_vec(
                env.vec_out, width, low_grad, normed_grad, unit, low_middle, env.hidden[...]
            )
            env.blend_grad[...] = blend_grad
            start, low = segment_starts(place, me * count, count)
            attend_backward(
                env.pre.at[width : 2 * width, :], env.blend_grad, env.post.at[0:width, :],
                env.stat_post, env.keys, env.values, lambda j, rows: env.keys_t[j, rows, :],
                me, low, start, env.bias, env.query_grad, env.kv_grad,
            )
            env.query_out[...] = (env.query_grad[...] * (width // H) ** -0.5).astype(BF)
            env.own_out[...] = env.kv_grad[me]
            for hop in range(1, 4):
                getattr(env, f"away_{hop}")[...] = env.kv_grad[me ^ hop].astype(BF)

    ins, outs, scratch = {}, {}, {}
    if last is not None:
        ins["middle_in"] = whole(ended["middle_out"])
        ins["query_in"] = whole(ended["query_out"])
        ins["own_in"] = whole(ended["own_out"])
        for hop in range(1, 4):
            ins[f"in_{hop}"] = whole(ended["arrived"][hop - 1])
        ins["pre_last"] = whole(ended["pre"])
        ins["stat_last"] = whole(ended["stat_pre"])
        ins["vec_last"] = of_layer(vec, last)
        ins["wqkv"] = of_layer(wqkv, last)
        ins["old_qkv"] = whole(sums["sum_qkv"])
        ins["old_vec"] = whole(sums["sum_vec"])
        if keep:
            outs["result"] = whole(shaped((count, width), F32))
        if final:
            outs["wire"] = whole(shaped((3 * width * width // 128, 128), BF))
            scratch["total_qkv"] = pltpu.VMEM((width, 3 * width), F32)
        else:
            outs["sum_qkv"] = whole(shaped((width, 3 * width), F32))
        outs["sum_vec"] = whole(shaped((ONES_ROWS, vec_len), F32))
        scratch["packed"] = pltpu.VMEM((3 * width, count), BF)
    if following is not None:
        for name in ("pre", "post", "stat_post"):
            ins[name] = whole(begun[name])
        for hop in range(4):
            ins[f"kv_{hop}"] = whole(begun["kv"][hop])
        ins["vec"] = of_layer(vec, following)
        for name, weight in zip(("wout", "wup", "wdown"), weights[1:]):
            ins[name] = of_layer(weight, following)
        if cotangent is not None:
            ins["cotangent"] = of_row(cotangent, cotangent.shape[0] - 1)
        outs["middle_out"] = whole(shaped((width, count), F32))
        outs["query_out"] = whole(shaped((width, count), BF))
        outs["own_out"] = whole(shaped((2 * width, count), F32))
        for hop in range(1, 4):
            outs[f"away_{hop}"] = whole(shaped((2 * width, count), BF))
        outs["low"] = whole(shaped((width, count), BF))
        outs["hidden"] = whole(shaped((hidden, count), BF))
        outs["middle"] = whole(shaped((width, count), BF))
        outs["vec_out"] = whole(shaped((ONES_ROWS, vec_len), F32))
        scratch |= {
            "keys": pltpu.VMEM((4, count, width), BF),
            "values": pltpu.VMEM((4, count, width), BF),
            "keys_t": pltpu.VMEM((4, width, count), BF),
            "bias": pltpu.VMEM((count, count), F32),
            "query_grad": pltpu.VMEM((width, count), F32),
            "kv_grad": pltpu.VMEM((4, 2 * width, count), F32),
            "blend_grad": pltpu.VMEM((width, count), BF),
        }
    flops = count * 12 * (4 * width * width + 2 * width * hidden)
    return launch("backward_split", body, place, 1, ins, outs, scratch, flops)


def cut_tokens(place, *pairs):
    arrays = [array for pair in pairs for array in pair]
    rows, count, width = arrays[0].shape

    def body(place, env):
        at = 0
        for index, pair in enumerate(pairs):
            value = getattr(env, f"in_{at}")[0].astype(F32)
            for extra in range(1, len(pair)):
                value = value + getattr(env, f"in_{at + extra}")[0].astype(F32)
            at += len(pair)
            for hop in range(4):

                @pl.when(pl.program_id(0) == hop)
                def _(hop=hop, index=index, value=value):
                    getattr(env, f"out{index}_{hop}")[...] = value.astype(BF)

    spec = pl.BlockSpec((1, count, width), lambda i, place: (place[0] ^ i, 0, 0))
    ins = {f"in_{k}": (array, spec) for k, array in enumerate(arrays)}
    outs = {}
    for index in range(len(pairs)):
        outs |= token_outs(f"out{index}", count, width)
    results = launch("cut_tokens", body, place, 4, ins, outs)
    return [[results[f"out{index}_{hop}"] for hop in range(4)] for index in range(len(pairs))]


def prepare(here, weights, vectors):
    out_bias, down_bias, norm_gain, norm_shift, up_bias = vectors
    layers, width = out_bias.shape
    hidden = up_bias.shape[1]
    rows = (6 * width + hidden) // 128
    rows += -rows % 8

    def body(place, env):
        layer = pl.program_id(0)
        for k in range(4):
            getattr(env, f"turned_{k}")[0] = getattr(env, f"weight_{k}")[0].T
        env.vec[...] = jnp.zeros_like(env.vec)
        pick = lambda ref: ref[pl.ds(layer, 1), :]
        parts = [pick(env.out_bias), pick(env.down_bias)]
        for k in range(2):
            parts += [env.norm_gain[0, k : k + 1, :], env.norm_shift[0, k : k + 1, :]]
        at = 0
        for part in parts + [pick(env.up_bias)]:
            for lanes in range(0, part.shape[1], 128):
                env.vec[0, at : at + 1, :] = part[:, lanes : lanes + 128]
                at += 1

    ins = {f"weight_{k}": each(weight) for k, weight in enumerate(weights)}
    ins |= {"out_bias": whole(out_bias), "down_bias": whole(down_bias), "up_bias": whole(up_bias)}
    ins |= {"norm_gain": each(norm_gain), "norm_shift": each(norm_shift)}
    outs = {
        f"turned_{k}": each(shaped((layers, weight.shape[2], weight.shape[1]), BF))
        for k, weight in enumerate(weights)
    }
    outs["vec"] = each(shaped((layers, rows, 128), F32))
    results = launch("prepare", body, here, layers, ins, outs)
    return tuple(results[f"turned_{k}"] for k in range(4)), results["vec"]


def finish_outputs(
    place, payloads, answer, answer_split, first, first_split, second, second_split,
    hidden, groups, row_len,
):
    count, width = first_split.shape
    rows = 5
    pieces = 2 * payloads[0].shape[0]
    ffn_rows = (width * width + 2 * width * hidden) // 128 // pieces
    qkv_rows = 3 * width * width // 128 // pieces
    small_at = ffn_rows + LAYERS * qkv_rows
    vec_len = 6 * width + hidden
    early_names, late_names = ("early_mine", "early_other"), ("late_mine", "late_other")

    def body(place, env):
        step = pl.program_id(0)
        me = place[0]
        at_core = me % 2

        def piece(p, first_row, height, names):
            left, right = (getattr(env, n)[p % (pieces // 2), first_row : first_row + height, :] for n in names)
            return jnp.where(at_core == p // (pieces // 2), left, right).astype(F32)

        def small_row(index):
            return piece(index // 2, small_at, 16, late_names)[index % 2 : index % 2 + 1, :]

        lane = lax.broadcasted_iota(jnp.int32, (1, 128), 1)
        total = jnp.zeros((1, 1), F32)
        for extra in range(-(-2 * groups // 128)):
            row = small_row(LAYERS * vec_len // 128 + extra)
            worth = jnp.where(lane % 2 == 0, 256.0, 1.0)
            row = jnp.where(lane + extra * 128 < 2 * groups, row * worth, 0.0)
            total = total + jnp.sum(row, axis=1, keepdims=True)
        factor = row_len / total
        token_factor = factor * float(rows * groups)

        def scatter(names, first_row, rows_each, targets):
            edges, at = [], 0
            for ref in targets:
                for lanes in range(0, ref.shape[2], 128):
                    edges.append((at, at + ref.shape[1], ref, lanes))
                    at += ref.shape[1]
            for p in range(pieces):
                values = piece(p, first_row, rows_each, names) * factor
                begin = p * rows_each
                for low, high, ref, lanes in edges:
                    left, right = max(low, begin), min(high, begin + rows_each)
                    if left < right:
                        ref[0, left - low : right - low, lanes : lanes + 128] = values[
                            left - begin : right - begin, :
                        ]

        for here in range(LAYERS):

            @pl.when(step == here)
            def _(here=here):
                names = early_names if here else late_names
                first_row = max(here - 1, 0) * ffn_rows
                scatter(names, first_row, ffn_rows, (env.out, env.up, env.down))
                scatter(late_names, ffn_rows + here * qkv_rows, qkv_rows, (env.qkv,))
                for ref, slot, at, size in (
                    (env.out_b, None, 0, width),
                    (env.down_b, None, width, width),
                    (env.gain, 0, 2 * width, width),
                    (env.shift, 0, 3 * width, width),
                    (env.gain, 1, 4 * width, width),
                    (env.shift, 1, 5 * width, width),
                    (env.up_b, None, 6 * width, hidden),
                ):
                    for lanes in range(0, size, 128):
                        row = small_row((here * vec_len + at + lanes) // 128) * factor
                        if slot is None:
                            ref[here : here + 1, lanes : lanes + 128] = row
                        else:
                            ref[here, slot : slot + 1, lanes : lanes + 128] = row

        for hop in range(4):

            @pl.when(step == (me ^ hop))
            def _(hop=hop):
                env.block_output[0] = getattr(env, f"answer_{hop}")[...]
                one = getattr(env, f"first_{hop}")[...].astype(F32)
                two = getattr(env, f"second_{hop}")[...].astype(F32)
                env.input_grad[0] = one * token_factor
                env.embed_grad[0] = (one + two) * token_factor

        @pl.when(step == 4)
        def _():
            env.block_output[0] = env.answer_split[...]
            one = env.first_split[...]
            env.input_grad[0] = one * token_factor
            env.embed_grad[0] = (one + env.second_split[...]) * token_factor

    ins = {name: whole(a) for name, a in zip((*early_names, *late_names), payloads)}
    ins |= token_ins("answer", answer) | token_ins("first", first) | token_ins("second", second)
    ins["answer_split"] = whole(answer_split)
    ins["first_split"] = whole(first_split)
    ins["second_split"] = whole(second_split)

    def per_layer(*dims):
        return shaped(dims, F32), pl.BlockSpec(
            (1,) + dims[1:], lambda i, *_: (jnp.minimum(i, LAYERS - 1), 0, 0)
        )

    outs = {
        "block_output": each(shaped((rows, count, width), BF)),
        "input_grad": each(shaped((rows, count, width), F32)),
        "embed_grad": each(shaped((rows, count, width), F32)),
        "qkv": per_layer(LAYERS, width, 3 * width),
        "out": per_layer(LAYERS, width, width),
        "out_b": whole(shaped((LAYERS, width), F32)),
        "up": per_layer(LAYERS, width, hidden),
        "up_b": whole(shaped((LAYERS, hidden), F32)),
        "down": per_layer(LAYERS, hidden, width),
        "down_b": whole(shaped((LAYERS, width), F32)),
        "gain": whole(shaped((LAYERS, 2, width), F32)),
        "shift": whole(shaped((LAYERS, 2, width), F32)),
    }
    return tuple(launch("finish_outputs", body, place, rows, ins, outs).values())


SEQ = ("y", "core")
CHIPS = ("dp", "y")


def swap(values, hop):
    return lax.ppermute(values, SEQ, [(i, i ^ hop) for i in range(lax.axis_size(SEQ))])


def swap_blocks(blocks):
    return [blocks[0]] + [swap(block, hop) for hop, block in enumerate(blocks[1:], 1)]


def sum_cores(pieces):
    core = lax.axis_index("core")
    half = pieces.shape[0] // 2
    keep = lax.dynamic_slice_in_dim(pieces, core * half, half, 0)
    give = lax.dynamic_slice_in_dim(pieces, (1 - core) * half, half, 0)
    return (keep.astype(F32) + swap(give, 1).astype(F32)).astype(BF)


def sum_chips(part):
    part = lax.all_to_all(part, CHIPS, 0, 0, tiled=True)
    return jnp.sum(part.astype(F32), axis=0).astype(BF)


def share_chips(part):
    copies = jnp.broadcast_to(part[None], (lax.axis_size(CHIPS),) + part.shape)
    return lax.all_to_all(copies, CHIPS, 0, 0, tiled=True)


def fast_device(
    block_input, embedding, cotangent, qkv_weight, out_weight, out_bias, up_weight, up_bias,
    down_weight, down_bias, norm_gain, norm_shift, seg_lengths, loop_counts, token_counts,
):
    row_count, tokens, width = block_input.shape
    chunks = lax.axis_size(SEQ)
    groups = lax.axis_size("dp")
    devices = groups * chunks
    row_len = tokens * chunks
    me = lax.axis_index(SEQ)
    hidden = up_weight.shape[2]
    tie = lax.optimization_barrier
    split = lambda rows: rows.reshape(devices, -1, 128)
    steps = LAYERS * 2

    here = jnp.reshape(me, (1,)).astype(jnp.int32)
    (sent,) = cut_tokens(here, (block_input, embedding))
    moved = swap_blocks(sent)
    backward_weights = (qkv_weight, out_weight, up_weight, down_weight)
    vectors = (out_bias, down_bias, norm_gain, norm_shift, up_bias)
    here, sent = tie((here, sent))
    forward_weights, vec = prepare(here, backward_weights, vectors)

    table = jnp.concatenate(
        [(loop_counts == 2).astype(jnp.int32)[:, None], token_counts[:, None], seg_lengths], axis=1
    )
    row = lambda at: jnp.concatenate([here, lax.dynamic_index_in_dim(table, at, 0, keepdims=False)])
    place = row(me)
    place_split = row(row_count - 1)

    saved, saved_split = [], []
    begun = forward_split(
        place_split, vec, forward_weights, following=0, block_input=block_input,
        embedding=embedding,
    )
    state_split = begun["begun"]
    state = None
    first_end = first_end_split = None
    sent_embed, sent_top = cut_tokens(here, (embedding,), (cotangent,))
    for step in range(steps):
        layer = step % LAYERS
        pre, kv, stat_pre = begun["pre"], begun["kv"], begun["stat_pre"]
        arrived = [swap(kv, hop) for hop in range(1, 4)]
        source = {}
        if step == 0:
            moved, kv = tie((moved, kv))
            source["tokens"] = moved
        elif step == LAYERS:
            state, moved_embed, kv = tie((state, moved_embed, kv))
            source["state"], source["tokens"] = state, moved_embed
        else:
            state, kv = tie((state, kv))
            source["state"] = state
        if step == 0:
            sent_embed, kv = tie((sent_embed, kv))
            moved_embed = swap_blocks(sent_embed)
        if step == LAYERS:
            sent_top, kv = tie((sent_top, kv))
            moved_top = swap_blocks(sent_top)
        if step == steps - 1:
            source["first_end"] = first_end
        kept = forward_rows(layer, place, vec, forward_weights, **source)
        saved.append(kept)
        if step == steps - 1:
            answer = [kept[f"answer_{hop}"] for hop in range(4)]
            answer, arrived = tie((answer, arrived))
        else:
            state, arrived = tie((kept["result"], arrived))
        if step == 0:
            arrived, moved_embed = tie((arrived, moved_embed))
        if step == LAYERS:
            arrived, moved_top = tie((arrived, moved_top))
        boundary = step == LAYERS - 1
        if boundary:
            first_end = state
        extra = {}
        if step < steps - 1:
            extra["following"] = (layer + 1) % LAYERS
            if boundary:
                extra["embedding"] = embedding
        else:
            extra["first_end"] = first_end_split
        blocks = (kv, *arrived)
        begun = forward_split(
            place_split, vec, forward_weights, last=layer, state=state_split,
            prev=blocks, pre=pre, **extra,
        )
        saved_split.append(
            {
                "pre": pre, "kv": blocks, "stat_pre": stat_pre,
                "post": begun["post"], "stat_post": begun["stat_post"],
            }
        )
        if step == steps - 1:
            answer_split = begun["answer"]
        else:
            state_split = begun["result"]
        if boundary:
            first_end_split = state_split
            state_split = begun["begun"]

    sums = [None] * LAYERS
    wires = [None] * LAYERS
    wires_qkv = [None] * LAYERS
    grad = None
    ended = None
    vecs = [None] * LAYERS
    for step in reversed(range(steps)):
        layer = step % LAYERS
        between = step == LAYERS - 1
        option = {}
        if step == steps - 1 or between:
            option = {"cotangent": cotangent, "row_len": row_len}
        if ended is not None:
            last = (step + 1) % LAYERS
            option |= {
                "last": last, "ended": ended, "sums": sums[last], "keep": between,
                "final": step == 0,
            }
        begun = backward_split(
            place_split, vec, backward_weights, following=layer, begun=saved_split[step], **option
        )
        if ended is not None:
            if step == 0:
                wires_qkv[last], vecs[last] = begun["wire"], begun["sum_vec"]
            else:
                sums[last] |= {"sum_qkv": begun["sum_qkv"], "sum_vec": begun["sum_vec"]}
            if between:
                second_split = begun["result"]
        arrived = [swap(begun[f"away_{hop}"], hop) for hop in range(1, 4)]
        five = {
            "post": saved_split[step]["post"], "hidden": begun["hidden"], "low": begun["low"],
            "middle": begun["middle"], "vec": begun["vec_out"],
        }
        source = {}
        if step == steps - 1:
            moved_answer = swap_blocks(answer)
            source["tokens"] = moved_top
        elif between:
            moved_second = swap_blocks(second)
            source["tokens"] = moved_top
        if grad is not None:
            source["grad"] = grad
        if step == 0:
            early = sum_cores(split(wires[1]))
            grad, early = tie((grad, early))
            source["grad"] = grad
        kept = backward_rows(
            layer, place, saved[step], vec, backward_weights, five,
            base=sums[layer], keep=step > 0, travel=step in (0, LAYERS), **source,
        )
        if step > 0:
            grad, arrived = tie((kept["result"], arrived))
        else:
            anchor, arrived = tie((kept["wire"], arrived))
            kept["wire"] = anchor
        if step == LAYERS:
            second = [kept[f"travel_{hop}"] for hop in range(4)]
        if step == steps - 1:
            arrived, moved_answer = tie((arrived, moved_answer))
        if between:
            arrived, moved_second = tie((arrived, moved_second))
        if step == 0:
            early = sum_chips(early)
            arrived, early = tie((arrived, early))
            early = share_chips(early)
            first = [kept[f"travel_{hop}"] for hop in range(4)]
        if sums[layer] is None:
            names = ("sum_qkv", "sum_out", "sum_up", "sum_down", "sum_vec")
            sums[layer] = {name: kept[name] for name in names}
        else:
            sums[layer] = {name: kept[name] for name in ("sum_qkv", "sum_vec")}
            wires[layer] = kept["wire"]
        ended = {name: begun[name] for name in ("middle_out", "query_out", "own_out")}
        ended |= {"arrived": arrived, "pre": saved_split[step]["pre"]}
        ended["stat_pre"] = saved_split[step]["stat_pre"]
    moved_first = swap_blocks(first)
    begun = backward_split(
        place_split, vec, backward_weights, last=0, ended=ended, sums=sums[0], keep=True,
        final=True,
    )
    first_split, wires_qkv[0], vecs[0] = begun["result"], begun["wire"], begun["sum_vec"]

    slot = lax.axis_index("dp")
    tally = jnp.sum(token_counts)
    digits = jnp.stack([tally // 256, tally % 256]).astype(F32) * (me == 0)
    digits = jnp.where(jnp.arange(groups)[:, None] == slot, digits[None], 0.0).reshape(-1)
    small = jnp.concatenate([values[0] for values in vecs] + [digits])
    small = jnp.pad(small, (0, 2 * devices * 128 - small.size)).reshape(devices, 2, 128)
    small = jnp.pad(small, ((0, 0), (0, 14), (0, 0)))
    parts = [split(wires[0])] + [split(wire) for wire in wires_qkv] + [small.astype(BF)]
    part = sum_cores(jnp.concatenate(parts, axis=1))
    early_other = swap(early, 1)
    part, moved_first, early, early_other = tie(
        (sum_chips(part), moved_first, early, early_other)
    )
    late = share_chips(part)
    return finish_outputs(
        place_split, (early, early_other, late, swap(late, 1)), moved_answer, answer_split,
        moved_first, first_split, moved_second, second_split, hidden, groups, float(row_len),
    )


def solution(mesh):
    if mesh.shape["seq"] == 4:
        fine = Mesh(mesh.devices.reshape(-1, 2, 2), ("dp", "y", "core"))
        return jax.shard_map(
            fast_device,
            mesh=fine,
            in_specs=(
                P("dp", SEQ, None),
                P("dp", SEQ, None),
                P("dp", SEQ, None),
                P(),
                P(),
                P(),
                P(),
                P(),
                P(),
                P(),
                P(),
                P(),
                P("dp", None),
                P("dp"),
                P("dp"),
            ),
            out_specs=(
                P("dp", SEQ, None),
                P("dp", SEQ, None),
                P("dp", SEQ, None),
                P(),
                P(),
                P(),
                P(),
                P(),
                P(),
                P(),
                P(),
                P(),
            ),
            check_vma=False,
        )
    return jax.shard_map(
        on_device,
        mesh=mesh,
        in_specs=(
            P("dp", "seq", None),
            P("dp", "seq", None),
            P("dp", "seq", None),
            P(),
            P(),
            P(),
            P(),
            P(),
            P(),
            P(),
            P(),
            P(),
            P("dp", None),
            P("dp"),
            P("dp"),
        ),
        out_specs=(
            P("dp", "seq", None),
            P("dp", "seq", None),
            P("dp", "seq", None),
            P(),
            P(),
            P(),
            P(),
            P(),
            P(),
            P(),
            P(),
            P(),
        ),
        check_vma=False,
    )
```

```python
import types

import jax
import jax.numpy as jnp
from jax import lax
from jax.experimental import pallas as pl
from jax.experimental.pallas import tpu as pltpu
from jax.sharding import Mesh, PartitionSpec as P

H = 4
LAYERS = 2


NORM_EPS = 1e-05
MASKED = -1e30


def layer_norm(values, gain, shift):
    center = values - jnp.mean(values, axis=-1, keepdims=True)
    spread = jnp.mean(center * center, axis=-1, keepdims=True)
    return center * lax.rsqrt(spread + NORM_EPS) * gain + shift


def gelu_exact(values):
    return jax.nn.gelu(values, approximate=False)


def matmul(left_side, right_side):
    return jnp.dot(left_side, right_side, preferred_element_type=jnp.float32)


def left_dot(left_side, right_side):
    return lax.dot_general(
        left_side, right_side, (((0,), (0,)), ((), ())), preferred_element_type=jnp.float32
    )


def right_dot(left_side, right_side):
    return lax.dot_general(
        left_side, right_side, (((1,), (1,)), ((), ())), preferred_element_type=jnp.float32
    )


def split_heads(packed, head_count):
    return packed.reshape(packed.shape[0], head_count, packed.shape[1] // head_count)


def attend_forward(queries, key_vals, allowed, head_count, score_scale):
    model_width = queries.shape[1]
    key_rows = split_heads(key_vals[:, :model_width], head_count)
    value_rows = split_heads(key_vals[:, model_width:], head_count)
    scores = (
        jnp.einsum(
            "qhd,khd->hqk",
            split_heads(queries, head_count),
            key_rows,
            preferred_element_type=jnp.float32,
        )
        * score_scale
    )
    scores = jnp.where(allowed[None], scores, MASKED)
    row_max = jnp.max(scores, axis=-1, keepdims=True)
    shifted_exp = jnp.exp(scores - row_max)
    row_total = jnp.sum(shifted_exp, axis=-1, keepdims=True)
    attn_probs = (shifted_exp / row_total).astype(jnp.bfloat16)
    blended = jnp.einsum("hqk,khd->qhd", attn_probs, value_rows, preferred_element_type=jnp.float32)
    return (blended.reshape(queries.shape[0], model_width), (row_max + jnp.log(row_total))[..., 0])


def attention_core(
    query_part, key_part, value_part, grad_part, allowed_part, logsum_part, head_count, score_scale
):
    scores = (
        jnp.einsum(
            "qhd,khd->hqk",
            split_heads(query_part, head_count),
            split_heads(key_part, head_count),
            preferred_element_type=jnp.float32,
        )
        * score_scale
    )
    scores = jnp.where(allowed_part[None], scores, MASKED)
    attn_probs = jnp.exp(scores - logsum_part[..., None])
    grad_probs = jnp.einsum(
        "qhd,khd->hqk",
        split_heads(grad_part, head_count),
        split_heads(value_part, head_count),
        preferred_element_type=jnp.float32,
    )
    return (attn_probs, grad_probs)


def query_grads(grad_scores, key_part, head_count, score_scale):
    result = (
        jnp.einsum(
            "hqk,khd->qhd",
            grad_scores,
            split_heads(key_part, head_count),
            preferred_element_type=jnp.float32,
        )
        * score_scale
    )
    return result.reshape(result.shape[0], -1)


def keyval_grads(grad_scores, attn_probs, query_part, grad_part, head_count, score_scale):
    grad_keys = (
        jnp.einsum(
            "hqk,qhd->khd",
            grad_scores,
            split_heads(query_part, head_count),
            preferred_element_type=jnp.float32,
        )
        * score_scale
    )
    grad_values = jnp.einsum(
        "hqk,qhd->khd",
        attn_probs.astype(jnp.bfloat16),
        split_heads(grad_part, head_count),
        preferred_element_type=jnp.float32,
    )
    return jnp.concatenate(
        [grad_keys.reshape(grad_keys.shape[0], -1), grad_values.reshape(grad_values.shape[0], -1)],
        axis=-1,
    )


def on_device(
    block_input,
    embedding,
    cotangent,
    qkv_weight,
    out_weight,
    out_bias,
    up_weight,
    up_bias,
    down_weight,
    down_bias,
    norm_gain,
    norm_shift,
    seg_lengths,
    loop_counts,
    token_counts,
):
    row_count, block_len, model_width = block_input.shape
    head_count = H
    score_scale = (model_width // head_count) ** (-0.5)
    row_len = block_len * lax.axis_size("seq")
    flat_rows = row_count * block_len
    offset = lax.axis_index("seq") * block_len
    key_pos = jnp.arange(row_len, dtype=jnp.int32)
    own_pos = offset + jnp.arange(block_len, dtype=jnp.int32)
    seg_ends = jnp.cumsum(seg_lengths, axis=-1)
    seg_all = jnp.sum((seg_ends[:, None, :] <= key_pos[None, :, None]).astype(jnp.int32), axis=-1)
    seg_own = lax.dynamic_slice_in_dim(seg_all, offset, block_len, 1)
    allowed = (seg_own[:, :, None] == seg_all[:, None, :]) & (
        key_pos[None, None, :] <= own_pos[None, :, None]
    )
    current = block_input.astype(jnp.float32)
    inject = embedding.astype(jnp.float32)
    stored = []
    finals = []
    for repeat in range(2):
        current = current + inject
        for layer_index in range(LAYERS):
            forward_normed = layer_norm(
                current, norm_gain[layer_index, 0], norm_shift[layer_index, 0]
            ).astype(jnp.bfloat16)
            forward_packed = matmul(
                forward_normed.reshape(flat_rows, model_width), qkv_weight[layer_index]
            ).astype(jnp.bfloat16)
            forward_packed = forward_packed.reshape(row_count, block_len, 3 * model_width)
            forward_key_vals = lax.all_gather(
                forward_packed[:, :, model_width:], "seq", axis=1, tiled=True
            )

            def forward_row(inputs):
                return attend_forward(inputs[0], inputs[1], inputs[2], head_count, score_scale)

            forward_blended, forward_logsum = lax.map(
                forward_row, (forward_packed[:, :, :model_width], forward_key_vals, allowed)
            )
            forward_blended = forward_blended.astype(jnp.bfloat16)
            branch_out = matmul(
                forward_blended.reshape(flat_rows, model_width), out_weight[layer_index]
            ).reshape(row_count, block_len, model_width)
            forward_middle = current + branch_out + out_bias[layer_index]
            forward_normed_two = layer_norm(
                forward_middle, norm_gain[layer_index, 1], norm_shift[layer_index, 1]
            ).astype(jnp.bfloat16)
            forward_up_proj = (
                matmul(forward_normed_two.reshape(flat_rows, model_width), up_weight[layer_index])
                + up_bias[layer_index]
            )
            forward_active = gelu_exact(forward_up_proj).astype(jnp.bfloat16)
            result = (
                forward_middle
                + matmul(forward_active, down_weight[layer_index]).reshape(
                    row_count, block_len, model_width
                )
                + down_bias[layer_index]
            )
            current, stored_layer = (
                result,
                (
                    current,
                    forward_normed,
                    forward_packed,
                    forward_key_vals,
                    forward_logsum,
                    forward_blended,
                    forward_middle,
                    forward_normed_two,
                    forward_up_proj,
                    forward_active,
                ),
            )
            stored.append(stored_layer)
        finals.append(current)
    two_loops = (loop_counts == 2)[:, None, None]
    block_output = jnp.where(two_loops, finals[1], finals[0]).astype(jnp.bfloat16)
    row_weight = token_counts.astype(jnp.float32) / row_len
    grad_top = cotangent.astype(jnp.float32) * row_weight[:, None, None]
    grad_state = jnp.where(two_loops, grad_top, 0.0)
    layer_sums = [None] * LAYERS
    second_pass = grad_state
    for repeat in (1, 0):
        for layer_index in reversed(range(LAYERS)):
            backward_stored_layer = stored[repeat * LAYERS + layer_index]
            (
                backward_current,
                normed,
                packed,
                key_vals,
                logsum,
                blended,
                middle,
                normed_two,
                up_proj,
                active,
            ) = backward_stored_layer
            grad_flat = grad_state.reshape(flat_rows, model_width)
            grad_low = grad_flat.astype(jnp.bfloat16)
            grad_down = left_dot(active, grad_low)
            grad_down_bias = jnp.sum(grad_flat, axis=0)
            grad_active = right_dot(grad_low, down_weight[layer_index])
            grad_up_proj = jax.vjp(gelu_exact, up_proj)[1](grad_active)[0].astype(jnp.bfloat16)
            grad_up_bias = jnp.sum(grad_up_proj.astype(jnp.float32), axis=0)
            grad_up = left_dot(normed_two.reshape(flat_rows, model_width), grad_up_proj)
            grad_normed_two = right_dot(grad_up_proj, up_weight[layer_index]).reshape(
                row_count, block_len, model_width
            )
            pull_two = jax.vjp(
                layer_norm, middle, norm_gain[layer_index, 1], norm_shift[layer_index, 1]
            )[1]
            grad_middle, gain_two, shift_two = pull_two(grad_normed_two)
            grad_middle = grad_middle + grad_state
            middle_flat = grad_middle.reshape(flat_rows, model_width)
            middle_low = middle_flat.astype(jnp.bfloat16)
            grad_out = left_dot(blended.reshape(flat_rows, model_width), middle_low)
            grad_out_bias = jnp.sum(middle_flat, axis=0)
            grad_blend = (
                right_dot(middle_low, out_weight[layer_index])
                .astype(jnp.bfloat16)
                .reshape(row_count, block_len, model_width)
            )
            queries = packed[:, :, :model_width]

            def full_row(inputs):
                query_part, keyval_part, grad_part, allowed_part, logsum_part = inputs
                attn_probs, grad_probs = attention_core(
                    query_part,
                    keyval_part[:, :model_width],
                    keyval_part[:, model_width:],
                    grad_part,
                    allowed_part,
                    logsum_part,
                    head_count,
                    score_scale,
                )
                row_delta = jnp.sum(attn_probs * grad_probs, axis=-1, keepdims=True)
                grad_scores = (attn_probs * (grad_probs - row_delta)).astype(jnp.bfloat16)
                return (
                    query_grads(grad_scores, keyval_part[:, :model_width], head_count, score_scale),
                    keyval_grads(
                        grad_scores, attn_probs, query_part, grad_part, head_count, score_scale
                    ),
                )

            grad_query, partial_kv = lax.map(
                full_row, (queries, key_vals, grad_blend, allowed, logsum)
            )
            grad_keyval = lax.psum_scatter(
                partial_kv.astype(jnp.bfloat16), "seq", scatter_dimension=1, tiled=True
            )
            grad_packed = jnp.concatenate(
                [grad_query.astype(jnp.bfloat16), grad_keyval], axis=-1
            ).reshape(flat_rows, 3 * model_width)
            grad_qkv = left_dot(normed.reshape(flat_rows, model_width), grad_packed)
            grad_normed = right_dot(grad_packed, qkv_weight[layer_index]).reshape(
                row_count, block_len, model_width
            )
            pull_one = jax.vjp(
                layer_norm, backward_current, norm_gain[layer_index, 0], norm_shift[layer_index, 0]
            )[1]
            grad_current, gain_one, shift_one = pull_one(grad_normed)
            grad_current = grad_current + grad_middle
            grad_state = grad_current
            grad_set = (
                grad_qkv,
                grad_out,
                grad_out_bias,
                grad_up,
                grad_up_bias,
                grad_down,
                grad_down_bias,
                jnp.stack([gain_one, gain_two]),
                jnp.stack([shift_one, shift_two]),
            )
            if repeat == 1:
                layer_sums[layer_index] = grad_set
            else:
                layer_sums[layer_index] = jax.tree.map(jnp.add, layer_sums[layer_index], grad_set)
        if repeat == 1:
            second_pass = grad_state
            grad_state = jnp.where(two_loops, grad_state, grad_top)
    grad_embed = grad_state + second_pass
    stacked = jax.tree.map(lambda *members: jnp.stack(members), *layer_sums)
    (
        sum_qkv,
        sum_out,
        sum_out_bias,
        sum_up,
        sum_up_bias,
        sum_down,
        sum_down_bias,
        sum_gain,
        sum_shift,
    ) = stacked
    total = lax.psum(jnp.sum(token_counts), "dp").astype(jnp.float32)
    summed = lax.psum(
        (
            sum_qkv,
            sum_out,
            sum_out_bias,
            sum_up,
            sum_up_bias,
            sum_down,
            sum_down_bias,
            sum_gain,
            sum_shift,
        ),
        ("dp", "seq"),
    )
    input_scale = row_count * lax.axis_size("dp") * row_len / total
    weight_scale = row_len / total
    return (
        block_output,
        grad_state * input_scale,
        grad_embed * input_scale,
        summed[0] * weight_scale,
        summed[1] * weight_scale,
        summed[2] * weight_scale,
        summed[3] * weight_scale,
        summed[4] * weight_scale,
        summed[5] * weight_scale,
        summed[6] * weight_scale,
        summed[7] * weight_scale,
        summed[8] * weight_scale,
    )


BF = jnp.bfloat16
F32 = jnp.float32
ERF_TERMS = (7.97869712e-01, 3.63922863e-02, -8.78266373e-05, -3.66934271e-05, 1.42500458e-06)
DENSITY_RATE = -0.7213475204444817
DENSITY_BASE = -1.3257480647361593
VMEM_LIMIT = 56 * 1024 * 1024
ONES_ROWS = 16


def dot_nn(left_side, right_side):
    return jnp.dot(left_side, right_side, preferred_element_type=F32)


def dot_nt(left_side, right_side):
    return lax.dot_general(
        left_side, right_side, (((1,), (1,)), ((), ())), preferred_element_type=F32
    )


def gelu_and_slope(z):
    square = z * z
    series = ERF_TERMS[-1] * square + ERF_TERMS[-2]
    for term in ERF_TERMS[-3::-1]:
        series = series * square + term
    cdf = 0.5 + 0.5 * jnp.tanh(z * series)
    density = jnp.exp2(square * DENSITY_RATE + DENSITY_BASE)
    return z * cdf, cdf + z * density


def norm_forward(values, gain, shift):
    center = values - jnp.mean(values, axis=0, keepdims=True)
    spread = jnp.mean(center * center, axis=0, keepdims=True)
    inverse = lax.rsqrt(spread + NORM_EPS)
    unit = center * inverse
    return unit, inverse, (unit * gain + shift).astype(BF)


def norm_backward(grad, unit, inverse, gain):
    scaled = grad * gain
    first = jnp.mean(scaled, axis=0, keepdims=True)
    second = jnp.mean(scaled * unit, axis=0, keepdims=True)
    return inverse * (scaled - first - unit * second)


def columns(vec):
    turned = vec[0].T

    def column(first, last):
        return jnp.concatenate(
            [turned[:, k : k + 1] for k in range(first // 128, last // 128)], axis=0
        )

    return column


def project_qkv(state, qkv_t, vec, pre, kv, stat, scale):
    width = state.shape[0]
    column = columns(vec)
    gain = column(2 * width, 3 * width)
    shift = column(3 * width, 4 * width)
    unit, inverse, normed = norm_forward(state, gain, shift)
    pre[0:width, :] = normed
    pre[2 * width : 3 * width, :] = unit.astype(BF)
    pre[width : 2 * width, :] = (dot_nn(qkv_t[0, 0:width, :], normed) * scale).astype(BF)
    kv[0:width, :] = dot_nn(qkv_t[0, width : 2 * width, :], normed).astype(BF)
    kv[width : 2 * width, :] = dot_nn(qkv_t[0, 2 * width : 3 * width, :], normed).astype(BF)
    stat[0:1, :] = inverse


def pad_head(block, odd):
    blank = jnp.zeros_like(block)
    return jnp.concatenate([blank, block] if odd else [block, blank], axis=0)


def tile_bias(first_key, start, causal, shape):
    key_at = lax.broadcasted_iota(jnp.int32, shape, 0)
    keep = key_at + first_key >= start
    if causal:
        keep = keep & (key_at <= lax.broadcasted_iota(jnp.int32, shape, 1))
    return jnp.where(keep, 0.0, MASKED)


def over_tiles(chunk, count, begin, half_tile, full_tile, carry):
    half = count // 2
    first_half = begin // half
    odd = jnp.where(first_half < 2 * chunk, first_half % 2, 0)
    carry = lax.fori_loop(0, odd, lambda _, c: half_tile(first_half // 2, c), carry)
    return lax.fori_loop((first_half + 1) // 2, chunk, full_tile, carry)


def attend_chunk(queries, keys, values_t, chunk, begin, start, bias, total, stat, blended):
    width, tokens = queries.shape
    head = width // H
    pair = 2 * head
    half = tokens // 2
    head_rows = [slice(h * head, (h + 1) * head) for h in range(H)]

    def scores(j, h, span):
        lanes = pl.ds((h // 2) * pair, pair)
        return dot_nn(keys[j, span, lanes], pad_head(queries[head_rows[h], :], h % 2))

    everything = slice(0, tokens)
    bias[...] = tile_bias(chunk * tokens, start, True, (tokens, tokens))
    parts = [scores(chunk, h, everything) for h in range(H)]
    uppers = [part[:half, :] + bias[:half, :] for part in parts]
    lowers = [part[half:, half:] + bias[half:, half:] for part in parts]
    tops, sums, weights = [], [], []
    for upper, lower in zip(uppers, lowers):
        top = jnp.max(upper, axis=0, keepdims=True)
        right = jnp.maximum(top[:, half:], jnp.max(lower, axis=0, keepdims=True))
        top = jnp.concatenate([top[:, :half], right], axis=1)
        upper = jnp.exp(upper - top)
        lower = jnp.exp(lower - right)
        added = jnp.sum(upper, axis=0, keepdims=True)
        right = added[:, half:] + jnp.sum(lower, axis=0, keepdims=True)
        tops.append(top)
        sums.append(jnp.concatenate([added[:, :half], right], axis=1))
        lower = lower.astype(BF)
        lower = jnp.concatenate([jnp.zeros_like(lower), lower], axis=1)
        weights.append(jnp.concatenate([upper.astype(BF), lower], axis=0))
    for rows, weight in zip(head_rows, weights):
        total[rows, :] = dot_nn(values_t[chunk, rows, :], weight)

    def step(j, span, size, carry):
        tops, sums = carry
        bias[:size, :] = tile_bias(j * tokens + span.start, start, False, (size, tokens))
        parts = [scores(j, h, span) + bias[:size, :] for h in range(H)]
        new_tops = [
            jnp.maximum(old, jnp.max(part, axis=0, keepdims=True))
            for old, part in zip(tops, parts)
        ]
        weights = [jnp.exp(part - top) for part, top in zip(parts, new_tops)]
        new_sums = [jnp.sum(weight, axis=0, keepdims=True) for weight in weights]
        terms = [
            dot_nn(values_t[j, rows, span], weight.astype(BF))
            for rows, weight in zip(head_rows, weights)
        ]
        fades = [jnp.exp(old - new) for old, new in zip(tops, new_tops)]
        for rows, term, fade in zip(head_rows, terms, fades):
            total[rows, :] = total[rows, :] * fade + term
        sums = [old * fade + new for old, fade, new in zip(sums, fades, new_sums)]
        return tuple(new_tops), tuple(sums)

    tops, sums = over_tiles(
        chunk, tokens, begin,
        lambda j, carry: step(j, slice(half, tokens), half, carry),
        lambda j, carry: step(j, everything, tokens, carry),
        (tuple(tops), tuple(sums)),
    )
    for h, rows in enumerate(head_rows):
        blended[rows, :] = (total[rows, :] / sums[h]).astype(BF)
        stat[h : h + 1, :] = tops[h] + jnp.log(sums[h])


def finish_layer(state, out_t, up_t, down_t, vec, post, stat):
    width, tokens = state.shape
    hidden = up_t.shape[1]
    column = columns(vec)
    middle = state + dot_nn(out_t[0], post[0:width, :]) + column(0, width)
    gain = column(4 * width, 5 * width)
    shift = column(5 * width, 6 * width)
    unit, inverse, normed = norm_forward(middle, gain, shift)
    post[width : 2 * width, :] = normed
    post[2 * width : 3 * width, :] = unit.astype(BF)
    stat[H : H + 1, :] = inverse
    z = dot_nn(up_t[0], normed) + column(6 * width, 6 * width + hidden)
    active, slope = gelu_and_slope(z)
    post[3 * width : 3 * width + hidden, :] = active.astype(BF)
    post[3 * width + hidden :, :] = slope.astype(BF)
    return (
        middle
        + dot_nn(down_t[0], post[3 * width : 3 * width + hidden, :])
        + column(width, 2 * width)
    )


def launch(name, body, place, grid, ins, outs, scratch=(), flops=0, aliases=()):
    scratch = dict(scratch)
    names = [*ins, *outs, *scratch]

    def kernel(place_ref, *refs):
        body(place_ref, types.SimpleNamespace(**dict(zip(names, refs))))

    results = pl.pallas_call(
        kernel,
        grid_spec=pltpu.PrefetchScalarGridSpec(
            num_scalar_prefetch=1,
            grid=(grid,),
            in_specs=[spec for _, spec in ins.values()],
            out_specs=[spec for _, spec in outs.values()],
            scratch_shapes=list(scratch.values()),
        ),
        out_shape=[shape for shape, _ in outs.values()],
        input_output_aliases={
            1 + list(ins).index(source): list(outs).index(target) for source, target in aliases
        },
        compiler_params=pltpu.CompilerParams(vmem_limit_bytes=VMEM_LIMIT),
        cost_estimate=pl.CostEstimate(flops=flops, bytes_accessed=1, transcendentals=0),
        name=name,
    )(place, *[array for array, _ in ins.values()])
    return dict(zip(outs, results))


def whole(array):
    return array, pl.BlockSpec(array.shape, lambda i, *_: (0,) * len(array.shape))


def of_layer(array, layer):
    return array, pl.BlockSpec((1,) + array.shape[1:], lambda i, *_: (layer, 0, 0))


def each(array):
    return array, pl.BlockSpec((1,) + array.shape[1:], lambda i, *_: (i, 0, 0))


def each_back(array):
    count = array.shape[0]
    return array, pl.BlockSpec(
        (1,) + array.shape[1:], lambda i, *_: (count - 1 - i, 0, 0)
    )


def shaped(dims, dtype):
    return jax.ShapeDtypeStruct(dims, dtype)


def segment_starts(place, first, count):
    position = lax.broadcasted_iota(jnp.int32, (1, count), 1) + first
    starts = jnp.zeros((1, count), jnp.int32)
    end = jnp.int32(0)
    begin = jnp.int32(0)
    for k in range(4, place.shape[0]):
        end = end + place[k]
        starts = jnp.where(position >= end, end, starts)
        begin = jnp.where(first >= end, end, begin)
    return starts, begin


def gather_tokens(env, name, me):
    for hop in range(4):
        env.spread[me ^ hop] = getattr(env, f"{name}_{hop}")[...]


def deal_tokens(env, name, value, chunk, me):
    for hop in range(4):

        @pl.when(chunk == (me ^ hop))
        def _(hop=hop):
            getattr(env, f"{name}_{hop}")[...] = value


def token_ins(name, blocks):
    return {f"{name}_{hop}": whole(block) for hop, block in enumerate(blocks)}


def token_outs(name, tokens, width):
    return {f"{name}_{hop}": whole(shaped((tokens, width), BF)) for hop in range(4)}


def as_tokens(values):
    return values.astype(BF).T


def as_features(tokens):
    return tokens.T.astype(F32)


def forward_rows(layer, place, vec, weights, state=None, tokens=None, first_end=None):
    chunks = 4
    count = state.shape[2] if tokens is None else tokens[0].shape[0]
    qkv_t, out_t, up_t, down_t = weights
    width, hidden = out_t.shape[2], up_t.shape[1]
    post_rows = 3 * width + 2 * hidden

    def body(place, env):
        chunk = pl.program_id(0)
        me = place[0]
        current = env.state.at[0] if state is not None else None
        if tokens is not None:

            @pl.when(chunk == 0)
            def _():
                gather_tokens(env, "tokens", me)

            added = as_features(env.spread[chunk])
            env.current[...] = added if state is None else added + env.state[0]
            current = env.current
        project_qkv(
            current[...], env.qkv_t, env.vec, env.pre.at[0], env.kv.at[0], env.stat_pre.at[0],
            (width // H) ** -0.5,
        )
        env.keys[chunk] = env.kv[0, 0:width, :].T
        env.values_t[chunk] = env.kv[0, width : 2 * width, :]
        start, begin = segment_starts(place, chunk * count, count)
        attend_chunk(
            env.pre.at[0, width : 2 * width, :], env.keys, env.values_t, chunk, begin, start, env.bias, env.total, env.stat_post.at[0],
            env.post.at[0, 0:width, :],
        )
        result = finish_layer(
            current[...], env.out_t, env.up_t, env.down_t, env.vec, env.post.at[0],
            env.stat_post.at[0],
        )
        if first_end is None:
            env.result[0] = result
        else:
            answer = jnp.where(place[2] == 1, result, env.first_end[0])
            deal_tokens(env, "answer", as_tokens(answer), chunk, me)

    ins = {"vec": of_layer(vec, layer)}
    for name, weight in zip(("qkv_t", "out_t", "up_t", "down_t"), weights):
        ins[name] = of_layer(weight, layer)
    scratch = {
        "keys": pltpu.VMEM((chunks, count, width), BF),
        "values_t": pltpu.VMEM((chunks, width, count), BF),
        "bias": pltpu.VMEM((count, count), F32),
        "total": pltpu.VMEM((width, count), F32),
    }
    if state is not None:
        ins["state"] = each(state)
    if tokens is not None:
        ins |= token_ins("tokens", tokens)
        scratch["spread"] = pltpu.VMEM((chunks, count, width), BF)
        scratch["current"] = pltpu.VMEM((width, count), F32)
    outs = {}
    if first_end is None:
        outs["result"] = each(shaped((chunks, width, count), F32))
    else:
        ins["first_end"] = each(first_end)
        outs |= token_outs("answer", count, width)
    outs["pre"] = each(shaped((chunks, 3 * width, count), BF))
    outs["kv"] = each(shaped((chunks, 2 * width, count), BF))
    outs["post"] = each(shaped((chunks, post_rows, count), BF))
    outs["stat_pre"] = each(shaped((chunks, 8, count), F32))
    outs["stat_post"] = each(shaped((chunks, 8, count), F32))
    flops = chunks * count * 6 * (4 * width * width + 2 * width * hidden)
    return launch("forward_rows", body, place, chunks, ins, outs, scratch, flops)


def split_row(array):
    return array, pl.BlockSpec((1,) + array.shape[1:], lambda i, place: (place[1], 0, 0))


def row_of_slot(slot, split, rows):
    return jnp.where(slot == split, rows - 1, slot)


def forward_split(
    place, vec, weights, last=None, following=None, state=None, prev=None, pre=None,
    block_input=None, embedding=None, first_end=None,
):
    qkv_t, out_t, up_t, down_t = weights
    width, hidden = out_t.shape[2], up_t.shape[1]
    count = embedding.shape[1] if state is None else state.shape[1]

    def body(place, env):
        me = place[0]
        if last is not None:
            for hop in range(4):
                arrived = getattr(env, f"kv_{hop}")
                env.keys[me ^ hop] = arrived[0:width, :].T
                env.values_t[me ^ hop] = arrived[width : 2 * width, :]
            start, begin = segment_starts(place, me * count, count)
            attend_chunk(
                env.pre_in.at[width : 2 * width, :], env.keys, env.values_t, me, begin, start,
                env.bias, env.total, env.stat_post, env.post.at[0:width, :],
            )
            current = finish_layer(
                env.state[...], env.out_t, env.up_t, env.down_t, env.vec, env.post, env.stat_post
            )
            if first_end is not None:
                answer = jnp.where(place[2] == 1, current, env.first_end[...])
                env.answer[...] = as_tokens(answer)
            else:
                env.result[...] = current
        if following is not None:
            if embedding is not None:
                added = as_features(env.embedding[0])
                if last is None:
                    current = as_features(env.block_input[0]) + added
                else:
                    current = env.result[...] + added
                env.begun[...] = current
            project_qkv(
                current, env.qkv_t, env.vec_next, env.pre, env.kv, env.stat_pre,
                (width // H) ** -0.5,
            )

    ins, outs, scratch = {}, {}, {}
    if last is not None:
        ins |= {f"kv_{hop}": whole(block) for hop, block in enumerate(prev)}
        ins |= {"state": whole(state), "pre_in": whole(pre)}
        ins["vec"] = of_layer(vec, last)
        for name, weight in zip(("out_t", "up_t", "down_t"), weights[1:]):
            ins[name] = of_layer(weight, last)
        if first_end is not None:
            ins["first_end"] = whole(first_end)
            outs["answer"] = whole(shaped((count, width), BF))
        else:
            outs["result"] = whole(shaped((width, count), F32))
        outs["post"] = whole(shaped((3 * width + 2 * hidden, count), BF))
        outs["stat_post"] = whole(shaped((8, count), F32))
        scratch = {
            "keys": pltpu.VMEM((4, count, width), BF),
            "values_t": pltpu.VMEM((4, width, count), BF),
            "bias": pltpu.VMEM((count, count), F32),
            "total": pltpu.VMEM((width, count), F32),
        }
    if following is not None:
        ins["vec_next"] = of_layer(vec, following)
        ins["qkv_t"] = of_layer(qkv_t, following)
        if embedding is not None:
            ins["embedding"] = split_row(embedding)
            outs["begun"] = whole(shaped((width, count), F32))
        if block_input is not None:
            ins["block_input"] = split_row(block_input)
        outs["pre"] = whole(shaped((3 * width, count), BF))
        outs["kv"] = whole(shaped((2 * width, count), BF))
        outs["stat_pre"] = whole(shaped((8, count), F32))
    flops = count * 6 * (4 * width * width + 2 * width * hidden)
    return launch("forward_split", body, place, 1, ins, outs, scratch, flops)


def backward_ffn(grad, post, stat, wout, wup, wdown, vec, hidden_grad):
    width, tokens = grad.shape
    hidden = wup.shape[2]
    low_grad = grad.astype(BF)
    hidden_grad[...] = (
        dot_nn(wdown[0], low_grad) * post[3 * width + hidden :, :].astype(F32)
    ).astype(BF)
    normed_grad = dot_nn(wup[0], hidden_grad[...])
    unit = post[2 * width : 3 * width, :].astype(F32)
    gain = columns(vec)(4 * width, 5 * width)
    middle = grad + norm_backward(normed_grad, unit, stat[H : H + 1, :], gain)
    low_middle = middle.astype(BF)
    blend_grad = dot_nn(wout[0], low_middle).astype(BF)
    return low_grad, normed_grad, unit, middle, low_middle, blend_grad


def token_sum(rows):
    return dot_nt(jnp.ones((ONES_ROWS, rows.shape[1]), BF), rows.astype(BF))


def attend_backward(
    queries, blend_grad, blended, stat, keys, values, keys_t, chunk, begin, start,
    bias, query_grad, kv_grad,
):
    width, tokens = queries.shape
    head = width // H
    pair = 2 * head
    head_rows = [slice(h * head, (h + 1) * head) for h in range(H)]
    deltas = [
        jnp.sum(
            blend_grad[rows, :].astype(F32) * blended[rows, :].astype(F32), axis=0, keepdims=True
        )
        for rows in head_rows
    ]

    half = tokens // 2
    everything = slice(0, tokens)

    def products(j, span):
        parts, prob_grads = [], []
        for h, rows in enumerate(head_rows):
            lanes = pl.ds((h // 2) * pair, pair)
            parts.append(dot_nn(keys[j, span, lanes], pad_head(queries[rows, :], h % 2)))
            prob_grads.append(
                dot_nn(values[j, span, lanes], pad_head(blend_grad[rows, :], h % 2))
            )
        return parts, prob_grads

    def collect(j, span, probs, score_grads, first):
        for rows, prob, score_grad in zip(head_rows, probs, score_grads):
            value_rows = slice(width + rows.start, width + rows.stop)
            kv_grad[j, value_rows, span] += dot_nt(blend_grad[rows, :], prob)
            kv_grad[j, rows, span] += dot_nt(queries[rows, :], score_grad)
            term = dot_nn(keys_t(j, rows, span), score_grad)
            if first:
                query_grad[rows, :] = term
            else:
                query_grad[rows, :] += term

    def weigh(part, prob_grad, mask, logsum, delta):
        prob = jnp.exp(part + mask - logsum)
        return prob.astype(BF), (prob * (prob_grad - delta)).astype(BF)

    bias[...] = tile_bias(chunk * tokens, start, True, (tokens, tokens))
    probs, score_grads = [], []
    for h, (part, prob_grad) in enumerate(zip(*products(chunk, everything))):
        logsum, delta = stat[h : h + 1, :], deltas[h]
        upper = weigh(part[:half, :], prob_grad[:half, :], bias[:half, :], logsum, delta)
        lower = weigh(
            part[half:, half:], prob_grad[half:, half:], bias[half:, half:], logsum[:, half:],
            delta[:, half:],
        )
        for kept, above, below in zip((probs, score_grads), upper, lower):
            below = jnp.concatenate([jnp.zeros_like(below), below], axis=1)
            kept.append(jnp.concatenate([above, below], axis=0))
    collect(chunk, everything, probs, score_grads, True)

    def step(j, span, size, carry):
        bias[:size, :] = tile_bias(j * tokens + span.start, start, False, (size, tokens))
        pairs = [
            weigh(part, prob_grad, bias[:size, :], stat[h : h + 1, :], deltas[h])
            for h, (part, prob_grad) in enumerate(zip(*products(j, span)))
        ]
        collect(j, span, [p for p, _ in pairs], [d for _, d in pairs], False)
        return carry

    over_tiles(
        chunk, tokens, begin,
        lambda j, carry: step(j, slice(half, tokens), half, carry),
        lambda j, carry: step(j, everything, tokens, carry),
        0,
    )


def add_vec(sum_vec, width, low_grad, normed_grad, unit, low_middle, dz):
    sum_vec[:, 0:width] += token_sum(low_middle)
    sum_vec[:, width : 2 * width] += token_sum(low_grad)
    sum_vec[:, 4 * width : 5 * width] += token_sum(normed_grad * unit)
    sum_vec[:, 5 * width : 6 * width] += token_sum(normed_grad)
    sum_vec[:, 6 * width :] += token_sum(dz)


def finish_backward(middle, pre, stat, packed, wqkv, vec, sum_qkv, sum_vec):
    width, tokens = middle.shape
    sum_qkv[...] += dot_nt(pre[0:width, :], packed[...])
    normed_grad = dot_nn(wqkv[0], packed[...])
    unit = pre[2 * width : 3 * width, :].astype(F32)
    gain = columns(vec)(2 * width, 3 * width)
    sum_vec[:, 2 * width : 3 * width] += token_sum(normed_grad * unit)
    sum_vec[:, 3 * width : 4 * width] += token_sum(normed_grad)
    return middle + norm_backward(normed_grad, unit, stat[0:1, :], gain)


def pack_lanes(wire, blocks):
    at = 0
    for ref in blocks:
        rows = ref.shape[0]
        for first in range(0, ref.shape[1], 128):
            wire[at : at + rows, :] = ref[:, first : first + 128].astype(BF)
            at += rows


def backward_rows(
    layer, place, saved, vec, weights, five, base=None, grad=None, tokens=None,
    keep=True, travel=False, part_done=None, ffn_only=False,
):
    chunks, _, count = saved["kv"].shape
    wqkv, wout, wup, wdown = weights
    width, hidden = wup.shape[1:]
    row_len = chunks * count
    first = base is None
    part = hidden // chunks
    vec_len = 6 * width + hidden
    with_ffn, with_attention = part_done is None, not ffn_only

    def body(place, env):
        order = pl.program_id(0)
        chunk = chunks - 1 - order
        me = place[0]

        @pl.when(order == 0)
        def _():
            if tokens is not None:
                gather_tokens(env, "tokens", me)
            if with_ffn:
                env.sum_up[...] = jnp.zeros_like(env.sum_up)
                env.sum_down[...] = jnp.zeros_like(env.sum_down)
                env.sum_out[...] = dot_nt(env.blend_five[...], env.middle_five[...])
                env.sum_vec[...] = env.vec_five[...]
                if not first:
                    env.sum_vec[...] += env.base_vec[...]
            else:
                env.sum_vec[...] = env.vec_done[...]
            if with_attention:
                env.sum_qkv[...] = jnp.zeros_like(env.sum_qkv)
                env.kv_grad[...] = jnp.zeros_like(env.kv_grad)
                for j in range(chunks):
                    env.keys[j] = env.kv[j, 0:width, :].T
                    env.values[j] = env.kv[j, width : 2 * width, :].T

        def add_base(ref, old):
            rows = old.shape[0]
            ref[pl.ds(pl.multiple_of(order * rows, rows), rows), :] += old[...]

        if with_ffn:
            spread = pl.ds(pl.multiple_of(order * part, part), part)
            env.sum_down[spread, :] += dot_nt(env.active_five[...], env.low_five[...])
            env.sum_up[:, spread] += dot_nt(env.normed_five[...], env.hidden_five[...])
            if not first:
                env.sum_down[spread, :] += env.base_down[...]
                env.sum_up[:, spread] += env.base_up[...]
                add_base(env.sum_out, env.base_out)
            current = env.grad.at[0] if grad is not None else None
            if tokens is not None:
                top = as_features(env.spread[chunk]) * (place[3].astype(F32) * (1.0 / row_len))
                two = place[2] == 1
                env.current[...] = (
                    jnp.where(two, top, 0.0)
                    if grad is None
                    else jnp.where(two, env.grad[0], top)
                )
                current = env.current
            post = env.post.at[0]
            low_grad, normed_grad, unit, middle, low_middle, blend_grad = backward_ffn(
                current[...], post, env.stat_post.at[0], env.wout, env.wup, env.wdown, env.vec,
                env.hidden_grad,
            )
            env.sum_down[...] += dot_nt(post[3 * width : 3 * width + hidden, :], low_grad)
            env.sum_up[...] += dot_nt(post[width : 2 * width, :], env.hidden_grad[...])
            env.sum_out[...] += dot_nt(post[0:width, :], low_middle)
            add_vec(
                env.sum_vec, width, low_grad, normed_grad, unit, low_middle, env.hidden_grad[...]
            )
            blend_ref = env.blend_grad if with_attention else env.blend_out.at[0]
            blend_ref[...] = blend_grad
            if not first:

                @pl.when(order == chunks - 1)
                def _():
                    pack_lanes(env.wire, (env.sum_out, env.sum_up, env.sum_down))

            if not with_attention:
                env.middle_out[0] = middle
                return
            blended = post.at[0:width, :]
        else:
            middle, blend_ref, blended = env.middle_in[0], env.blend_in.at[0], env.blended.at[0]
        if not first:
            add_base(env.sum_qkv, env.base_qkv)
        start, begin = segment_starts(place, chunk * count, count)
        attend_backward(
            env.pre.at[0, width : 2 * width, :], blend_ref, blended,
            env.stat_post.at[0], env.keys, env.values, lambda j, rows, span: env.kv[j, rows, span],
            chunk, begin, start, env.bias, env.query_grad, env.kv_grad,
        )
        env.packed[0:width, :] = (env.query_grad[...] * (width // H) ** -0.5).astype(BF)
        env.packed[width : 3 * width, :] = env.kv_grad[chunk].astype(BF)
        result = finish_backward(
            middle, env.pre.at[0], env.stat_pre.at[0], env.packed, env.wqkv, env.vec,
            env.sum_qkv, env.sum_vec,
        )
        if keep:
            env.result[0] = result
        if travel:
            deal_tokens(env, "travel", as_tokens(result), chunk, me)

    ins = {"vec": of_layer(vec, layer), "stat_post": each_back(saved["stat_post"])}
    outs, scratch = {}, {}
    cut = lambda array, shape, at: (array, pl.BlockSpec(shape, lambda i, *_: at(i)))
    sums = {"sum_vec": (ONES_ROWS, vec_len)}
    if with_ffn:
        ins["post"] = each_back(saved["post"])
        for name, weight in zip(("wout", "wup", "wdown"), weights[1:]):
            ins[name] = of_layer(weight, layer)
        if grad is not None:
            ins["grad"] = each_back(grad)
        if tokens is not None:
            ins |= token_ins("tokens", tokens)
            scratch["spread"] = pltpu.VMEM((chunks, count, width), BF)
            scratch["current"] = pltpu.VMEM((width, count), F32)
        post_five = five["post"]
        ins["blend_five"] = cut(post_five, (width, count), lambda i: (0, 0))
        ins["normed_five"] = cut(post_five, (width, count), lambda i: (1, 0))
        ins["active_five"] = cut(post_five, (part, count), lambda i: (3 * width // part + i, 0))
        ins["hidden_five"] = cut(five["hidden"], (part, count), lambda i: (i, 0))
        for name in ("low", "middle", "vec"):
            ins[name + "_five"] = whole(five[name])
        sums |= {"sum_out": (width, width), "sum_up": (width, hidden), "sum_down": (hidden, width)}
        scratch["hidden_grad"] = pltpu.VMEM((hidden, count), BF)
        if not first:
            ins["base_out"] = cut(base["sum_out"], (width // chunks, width), lambda i: (i, 0))
            ins["base_up"] = cut(base["sum_up"], (width, part), lambda i: (0, i))
            ins["base_down"] = cut(base["sum_down"], (part, width), lambda i: (i, 0))
            ins["base_vec"] = whole(base["sum_vec"])
            wire_rows = (width * width + 2 * width * hidden) // 128
            outs["wire"] = whole(shaped((wire_rows, 128), BF))
        if not with_attention:
            outs["blend_out"] = each_back(shaped((chunks, width, count), BF))
            outs["middle_out"] = each_back(shaped((chunks, width, count), F32))
    else:
        ins["vec_done"] = whole(part_done["sum_vec"])
        ins["middle_in"] = each_back(part_done["middle_out"])
        ins["blend_in"] = each_back(part_done["blend_out"])
        ins["blended"] = (
            saved["post"],
            pl.BlockSpec((1, width, count), lambda i, *_: (chunks - 1 - i, 0, 0)),
        )
    if with_attention:
        ins["kv"] = whole(saved["kv"])
        ins["pre"] = each_back(saved["pre"])
        ins["stat_pre"] = each_back(saved["stat_pre"])
        ins["wqkv"] = of_layer(wqkv, layer)
        sums["sum_qkv"] = (width, 3 * width)
        if not first:
            ins["base_qkv"] = cut(base["sum_qkv"], (width // chunks, 3 * width), lambda i: (i, 0))
        if keep:
            outs["result"] = each_back(shaped((chunks, width, count), F32))
        if travel:
            outs |= token_outs("travel", count, width)
        scratch |= {
            "keys": pltpu.VMEM((chunks, count, width), BF),
            "values": pltpu.VMEM((chunks, count, width), BF),
            "bias": pltpu.VMEM((count, count), F32),
            "query_grad": pltpu.VMEM((width, count), F32),
            "kv_grad": pltpu.VMEM((chunks, 2 * width, count), F32),
            "blend_grad": pltpu.VMEM((width, count), BF),
            "packed": pltpu.VMEM((3 * width, count), BF),
        }
    for name, dims in sums.items():
        if first or name in ("sum_qkv", "sum_vec"):
            outs[name] = whole(shaped(dims, F32))
        else:
            scratch[name] = pltpu.VMEM(dims, F32)
    flops = chunks * count * 12 * (4 * width * width + 2 * width * hidden)
    return launch("backward_rows", body, place, chunks, ins, outs, scratch, flops)


def backward_split(
    place, vec, weights, last=None, following=None, ended=None, sums=None, begun=None,
    cotangent=None, final=False, keep=False, row_len=None,
):
    wqkv, wout, wup, wdown = weights
    width, hidden = wup.shape[1:]
    vec_len = 6 * width + hidden
    count = (ended or begun)["stat_pre"].shape[1]

    def body(place, env):
        me = place[0]
        if last is not None:
            sum_qkv = env.total_qkv if final else env.sum_qkv
            env.packed[0:width, :] = env.query_in[...]
            kv_total = env.own_in[...]
            for hop in range(1, 4):
                kv_total = kv_total + getattr(env, f"in_{hop}")[...].astype(F32)
            env.packed[width : 3 * width, :] = kv_total.astype(BF)
            sum_qkv[...] = env.old_qkv[...]
            env.sum_vec[...] = env.old_vec[...]
            current = finish_backward(
                env.middle_in[...], env.pre_last, env.stat_last, env.packed, env.wqkv,
                env.vec_last, sum_qkv, env.sum_vec,
            )
            if keep:
                env.result[...] = current.T
            if final:
                pack_lanes(env.wire, (sum_qkv,))
        if following is not None:
            if cotangent is not None:
                top = as_features(env.cotangent[0]) * (place[3].astype(F32) * (1.0 / row_len))
                two = place[2] == 1
                grad = jnp.where(two, top, 0.0) if last is None else jnp.where(two, current, top)
            else:
                grad = current
            env.kv_grad[...] = jnp.zeros_like(env.kv_grad)
            for hop in range(4):
                arrived = getattr(env, f"kv_{hop}")
                env.keys[me ^ hop] = arrived[0:width, :].T
                env.keys_t[me ^ hop] = arrived[0:width, :]
                env.values[me ^ hop] = arrived[width : 2 * width, :].T
            low_grad, normed_grad, unit, middle, low_middle, blend_grad = backward_ffn(
                grad, env.post, env.stat_post, env.wout, env.wup, env.wdown, env.vec, env.hidden
            )
            env.low[...] = low_grad
            env.middle[...] = low_middle
            env.middle_out[...] = middle
            env.vec_out[...] = jnp.zeros_like(env.vec_out)
            add_vec(
                env.vec_out, width, low_grad, normed_grad, unit, low_middle, env.hidden[...]
            )
            env.blend_grad[...] = blend_grad
            start, begin = segment_starts(place, me * count, count)
            attend_backward(
                env.pre.at[width : 2 * width, :], env.blend_grad, env.post.at[0:width, :],
                env.stat_post, env.keys, env.values, lambda j, rows, span: env.keys_t[j, rows, span],
                me, begin, start, env.bias, env.query_grad, env.kv_grad,
            )
            env.query_out[...] = (env.query_grad[...] * (width // H) ** -0.5).astype(BF)
            env.own_out[...] = env.kv_grad[me]
            for hop in range(1, 4):
                getattr(env, f"away_{hop}")[...] = env.kv_grad[me ^ hop].astype(BF)

    ins, outs, scratch = {}, {}, {}
    if last is not None:
        ins["middle_in"] = whole(ended["middle_out"])
        ins["query_in"] = whole(ended["query_out"])
        ins["own_in"] = whole(ended["own_out"])
        for hop in range(1, 4):
            ins[f"in_{hop}"] = whole(ended["arrived"][hop - 1])
        ins["pre_last"] = whole(ended["pre"])
        ins["stat_last"] = whole(ended["stat_pre"])
        ins["vec_last"] = of_layer(vec, last)
        ins["wqkv"] = of_layer(wqkv, last)
        ins["old_qkv"] = whole(sums["sum_qkv"])
        ins["old_vec"] = whole(sums["sum_vec"])
        if keep:
            outs["result"] = whole(shaped((count, width), F32))
        if final:
            outs["wire"] = whole(shaped((3 * width * width // 128, 128), BF))
            scratch["total_qkv"] = pltpu.VMEM((width, 3 * width), F32)
        else:
            outs["sum_qkv"] = whole(shaped((width, 3 * width), F32))
        outs["sum_vec"] = whole(shaped((ONES_ROWS, vec_len), F32))
        scratch["packed"] = pltpu.VMEM((3 * width, count), BF)
    if following is not None:
        for name in ("pre", "post", "stat_post"):
            ins[name] = whole(begun[name])
        for hop in range(4):
            ins[f"kv_{hop}"] = whole(begun["kv"][hop])
        ins["vec"] = of_layer(vec, following)
        for name, weight in zip(("wout", "wup", "wdown"), weights[1:]):
            ins[name] = of_layer(weight, following)
        if cotangent is not None:
            ins["cotangent"] = split_row(cotangent)
        outs["middle_out"] = whole(shaped((width, count), F32))
        outs["query_out"] = whole(shaped((width, count), BF))
        outs["own_out"] = whole(shaped((2 * width, count), F32))
        for hop in range(1, 4):
            outs[f"away_{hop}"] = whole(shaped((2 * width, count), BF))
        outs["low"] = whole(shaped((width, count), BF))
        outs["hidden"] = whole(shaped((hidden, count), BF))
        outs["middle"] = whole(shaped((width, count), BF))
        outs["vec_out"] = whole(shaped((ONES_ROWS, vec_len), F32))
        scratch |= {
            "keys": pltpu.VMEM((4, count, width), BF),
            "values": pltpu.VMEM((4, count, width), BF),
            "keys_t": pltpu.VMEM((4, width, count), BF),
            "bias": pltpu.VMEM((count, count), F32),
            "query_grad": pltpu.VMEM((width, count), F32),
            "kv_grad": pltpu.VMEM((4, 2 * width, count), F32),
            "blend_grad": pltpu.VMEM((width, count), BF),
        }
    flops = count * 12 * (4 * width * width + 2 * width * hidden)
    return launch("backward_split", body, place, 1, ins, outs, scratch, flops)


def cut_tokens(place, *pairs):
    arrays = [array for pair in pairs for array in pair]
    rows, count, width = arrays[0].shape

    def body(place, env):
        at = 0
        for index, pair in enumerate(pairs):
            value = getattr(env, f"in_{at}")[0].astype(F32)
            for extra in range(1, len(pair)):
                value = value + getattr(env, f"in_{at + extra}")[0].astype(F32)
            at += len(pair)
            for hop in range(4):

                @pl.when(pl.program_id(0) == hop)
                def _(hop=hop, index=index, value=value):
                    getattr(env, f"out{index}_{hop}")[...] = value.astype(BF)

    spec = pl.BlockSpec(
        (1, count, width), lambda i, place: (row_of_slot(place[0] ^ i, place[1], rows), 0, 0)
    )
    ins = {f"in_{k}": (array, spec) for k, array in enumerate(arrays)}
    outs = {}
    for index in range(len(pairs)):
        outs |= token_outs(f"out{index}", count, width)
    results = launch("cut_tokens", body, place, 4, ins, outs)
    return [[results[f"out{index}_{hop}"] for hop in range(4)] for index in range(len(pairs))]


def prepare(here, weights, vectors):
    out_bias, down_bias, norm_gain, norm_shift, up_bias = vectors
    layers, width = out_bias.shape
    hidden = up_bias.shape[1]
    rows = (6 * width + hidden) // 128
    rows += -rows % 8

    def body(place, env):
        layer = pl.program_id(0)
        for k in range(4):
            getattr(env, f"turned_{k}")[0] = getattr(env, f"weight_{k}")[0].T
        env.vec[...] = jnp.zeros_like(env.vec)
        pick = lambda ref: ref[pl.ds(layer, 1), :]
        parts = [pick(env.out_bias), pick(env.down_bias)]
        for k in range(2):
            parts += [env.norm_gain[0, k : k + 1, :], env.norm_shift[0, k : k + 1, :]]
        at = 0
        for part in parts + [pick(env.up_bias)]:
            for lanes in range(0, part.shape[1], 128):
                env.vec[0, at : at + 1, :] = part[:, lanes : lanes + 128]
                at += 1

    ins = {f"weight_{k}": each(weight) for k, weight in enumerate(weights)}
    ins |= {"out_bias": whole(out_bias), "down_bias": whole(down_bias), "up_bias": whole(up_bias)}
    ins |= {"norm_gain": each(norm_gain), "norm_shift": each(norm_shift)}
    outs = {
        f"turned_{k}": each(shaped((layers, weight.shape[2], weight.shape[1]), BF))
        for k, weight in enumerate(weights)
    }
    outs["vec"] = each(shaped((layers, rows, 128), F32))
    results = launch("prepare", body, here, layers, ins, outs)
    return tuple(results[f"turned_{k}"] for k in range(4)), results["vec"]


def piece_reader(payloads, me):
    mine, other = payloads
    half = mine.shape[0]

    def piece(p, first, rows):
        left, right = (ref[p % half, first : first + rows, :] for ref in (mine, other))
        return jnp.where(me % 2 == p // half, left, right).astype(F32)

    return piece


def spread_pieces(piece, pieces, first, rows_each, targets, factor):
    edges, at = [], 0
    for ref in targets:
        for lanes in range(0, ref.shape[2], 128):
            edges.append((at, at + ref.shape[1], ref, lanes))
            at += ref.shape[1]
    for p in range(pieces):
        values = piece(p, first, rows_each) * factor
        begin = p * rows_each
        for low, high, ref, lanes in edges:
            left, right = max(low, begin), min(high, begin + rows_each)
            if left < right:
                ref[0, left - low : right - low, lanes : lanes + 128] = values[
                    left - begin : right - begin, :
                ]


def finish_tokens(
    place, payload, answer, answer_split, first, first_split, second, second_split,
    hidden, groups, row_len,
):
    count, width = first_split.shape
    rows = 5
    pieces = 2 * payload[0].shape[0]
    ffn_rows = (width * width + 2 * width * hidden) // 128 // pieces

    def body(place, env):
        step = pl.program_id(0)
        me = place[0]
        piece = piece_reader((env.mine, env.other), me)
        lane = lax.broadcasted_iota(jnp.int32, (1, 128), 1)
        total = jnp.zeros((1, 1), F32)
        for extra in range(-(-2 * groups // 128)):
            row = piece(extra, ffn_rows, 16)[0:1, :]
            worth = jnp.where(lane % 2 == 0, 256.0, 1.0)
            row = jnp.where(lane + extra * 128 < 2 * groups, row * worth, 0.0)
            total = total + jnp.sum(row, axis=1, keepdims=True)
        factor = row_len / total
        token_factor = factor * float(rows * groups)

        @pl.when(step == 0)
        def _():
            env.scale[...] = jnp.broadcast_to(factor, env.scale.shape)
            spread_pieces(piece, pieces, 0, ffn_rows, (env.out, env.up, env.down), factor)

        for hop in range(4):

            @pl.when(step == row_of_slot(me ^ hop, place[1], rows))
            def _(hop=hop):
                env.block_output[0] = getattr(env, f"answer_{hop}")[...]
                one = getattr(env, f"first_{hop}")[...].astype(F32)
                two = getattr(env, f"second_{hop}")[...].astype(F32)
                env.input_grad[0] = one * token_factor
                env.embed_grad[0] = (one + two) * token_factor

        @pl.when(step == place[1])
        def _():
            env.block_output[0] = env.answer_split[...]
            one = env.first_split[...]
            env.input_grad[0] = one * token_factor
            env.embed_grad[0] = (one + env.second_split[...]) * token_factor

    ins = {"mine": whole(payload[0]), "other": whole(payload[1])}
    ins |= token_ins("answer", answer) | token_ins("first", first) | token_ins("second", second)
    ins["answer_split"] = whole(answer_split)
    ins["first_split"] = whole(first_split)
    ins["second_split"] = whole(second_split)
    later = lambda *dims: (
        shaped(dims, F32), pl.BlockSpec((1,) + dims[1:], lambda i, *_: (LAYERS - 1, 0, 0))
    )
    outs = {
        "block_output": each(shaped((rows, count, width), BF)),
        "input_grad": each(shaped((rows, count, width), F32)),
        "embed_grad": each(shaped((rows, count, width), F32)),
        "out": later(LAYERS, width, width),
        "up": later(LAYERS, width, hidden),
        "down": later(LAYERS, hidden, width),
        "scale": whole(shaped((8, 128), F32)),
    }
    return launch("finish_tokens", body, place, rows, ins, outs)


def finish_weights(place, payload, done, width, hidden):
    pieces = 2 * payload[0].shape[0]
    ffn_rows = (width * width + 2 * width * hidden) // 128 // pieces
    qkv_rows = 3 * width * width // 128 // pieces
    small_at = ffn_rows + LAYERS * qkv_rows
    vec_len = 6 * width + hidden

    def body(place, env):
        step = pl.program_id(0)
        piece = piece_reader((env.mine, env.other), place[0])
        factor = env.scale[0:1, 0:1]

        @pl.when(step == 0)
        def _():
            spread_pieces(piece, pieces, 0, ffn_rows, (env.out, env.up, env.down), factor)
            for here in range(LAYERS):
                for ref, slot, at, size in (
                    (env.out_b, None, 0, width),
                    (env.down_b, None, width, width),
                    (env.gain, 0, 2 * width, width),
                    (env.shift, 0, 3 * width, width),
                    (env.gain, 1, 4 * width, width),
                    (env.shift, 1, 5 * width, width),
                    (env.up_b, None, 6 * width, hidden),
                ):
                    for lanes in range(0, size, 128):
                        index = (here * vec_len + at + lanes) // 128
                        row = piece(index // 2, small_at, 16)[index % 2 : index % 2 + 1, :]
                        row = row * factor
                        if slot is None:
                            ref[here : here + 1, lanes : lanes + 128] = row
                        else:
                            ref[here, slot : slot + 1, lanes : lanes + 128] = row

        for here in range(LAYERS):

            @pl.when(step == here)
            def _(here=here):
                spread_pieces(
                    piece, pieces, ffn_rows + here * qkv_rows, qkv_rows, (env.qkv,), factor
                )

    ins = {"mine": whole(payload[0]), "other": whole(payload[1]), "scale": whole(done["scale"])}
    names = ("out", "up", "down")
    for name in names:
        ins[name + "_done"] = (done[name], pl.BlockSpec(memory_space=pl.ANY))
    start = lambda array: (
        array, pl.BlockSpec((1,) + array.shape[1:], lambda i, *_: (0, 0, 0))
    )
    outs = {name: start(shaped(done[name].shape, F32)) for name in names}
    outs["qkv"] = each(shaped((LAYERS, width, 3 * width), F32))
    outs["out_b"] = whole(shaped((LAYERS, width), F32))
    outs["up_b"] = whole(shaped((LAYERS, hidden), F32))
    outs["down_b"] = whole(shaped((LAYERS, width), F32))
    outs["gain"] = whole(shaped((LAYERS, 2, width), F32))
    outs["shift"] = whole(shaped((LAYERS, 2, width), F32))
    return launch(
        "finish_weights", body, place, LAYERS, ins, outs,
        aliases=[(name + "_done", name) for name in names],
    )


SEQ = ("y", "core")
CHIPS = ("dp", "y")


def swap(values, hop):
    return lax.ppermute(values, SEQ, [(i, i ^ hop) for i in range(lax.axis_size(SEQ))])


def swap_blocks(blocks):
    return [blocks[0]] + [swap(block, hop) for hop, block in enumerate(blocks[1:], 1)]


def sum_cores(pieces):
    core = lax.axis_index("core")
    half = pieces.shape[0] // 2
    keep = lax.dynamic_slice_in_dim(pieces, core * half, half, 0)
    give = lax.dynamic_slice_in_dim(pieces, (1 - core) * half, half, 0)
    return (keep.astype(F32) + swap(give, 1).astype(F32)).astype(BF)


def sum_chips(part):
    part = lax.all_to_all(part, CHIPS, 0, 0, tiled=True)
    return jnp.sum(part.astype(F32), axis=0).astype(BF)


def share_chips(part):
    copies = jnp.broadcast_to(part[None], (lax.axis_size(CHIPS),) + part.shape)
    return lax.all_to_all(copies, CHIPS, 0, 0, tiled=True)


def count_digits(token_counts, me, devices):
    groups = lax.axis_size("dp")
    tally = jnp.sum(token_counts)
    digits = jnp.stack([tally // 256, tally % 256]).astype(F32) * (me == 0)
    slots = jnp.arange(groups)[:, None] == lax.axis_index("dp")
    digits = jnp.where(slots, digits[None], 0.0).reshape(-1)
    digits = jnp.pad(digits, (0, devices * 128 - digits.size)).reshape(devices, 1, 128)
    return jnp.pad(digits, ((0, 0), (0, 15), (0, 0))).astype(BF)


def fast_device(
    block_input, embedding, cotangent, qkv_weight, out_weight, out_bias, up_weight, up_bias,
    down_weight, down_bias, norm_gain, norm_shift, seg_lengths, loop_counts, token_counts,
):
    row_count, tokens, width = block_input.shape
    chunks = lax.axis_size(SEQ)
    groups = lax.axis_size("dp")
    devices = groups * chunks
    row_len = tokens * chunks
    me = lax.axis_index(SEQ)
    hidden = up_weight.shape[2]
    tie = lax.optimization_barrier
    split = lambda rows: rows.reshape(devices, -1, 128)
    steps = LAYERS * 2

    longest = jnp.argmax(jnp.max(seg_lengths, axis=1)).astype(jnp.int32)
    here = jnp.stack([me.astype(jnp.int32), longest])
    (sent,) = cut_tokens(here, (block_input, embedding))
    moved = swap_blocks(sent)
    backward_weights = (qkv_weight, out_weight, up_weight, down_weight)
    vectors = (out_bias, down_bias, norm_gain, norm_shift, up_bias)
    here, sent = tie((here, sent))
    forward_weights, vec = prepare(here, backward_weights, vectors)

    table = jnp.concatenate(
        [(loop_counts == 2).astype(jnp.int32)[:, None], token_counts[:, None], seg_lengths], axis=1
    )
    row = lambda at: jnp.concatenate([here, lax.dynamic_index_in_dim(table, at, 0, keepdims=False)])
    place = row(row_of_slot(me, longest, row_count))
    place_split = row(longest)

    saved, saved_split = [], []
    begun = forward_split(
        place_split, vec, forward_weights, following=0, block_input=block_input,
        embedding=embedding,
    )
    state_split = begun["begun"]
    state = None
    first_end = first_end_split = None
    sent_embed, sent_top = cut_tokens(here, (embedding,), (cotangent,))
    for step in range(steps):
        layer = step % LAYERS
        pre, kv, stat_pre = begun["pre"], begun["kv"], begun["stat_pre"]
        arrived = [swap(kv, hop) for hop in range(1, 4)]
        source = {}
        if step == 0:
            moved, kv = tie((moved, kv))
            source["tokens"] = moved
        elif step == LAYERS:
            state, moved_embed, kv = tie((state, moved_embed, kv))
            source["state"], source["tokens"] = state, moved_embed
        else:
            state, kv = tie((state, kv))
            source["state"] = state
        if step == 0:
            sent_embed, kv = tie((sent_embed, kv))
            moved_embed = swap_blocks(sent_embed)
        if step == LAYERS:
            sent_top, kv = tie((sent_top, kv))
            moved_top = swap_blocks(sent_top)
        if step == steps - 1:
            source["first_end"] = first_end
        kept = forward_rows(layer, place, vec, forward_weights, **source)
        saved.append(kept)
        if step == steps - 1:
            answer = [kept[f"answer_{hop}"] for hop in range(4)]
            answer, arrived = tie((answer, arrived))
        else:
            state, arrived = tie((kept["result"], arrived))
        if step == 0:
            arrived, moved_embed = tie((arrived, moved_embed))
        if step == LAYERS:
            arrived, moved_top = tie((arrived, moved_top))
        boundary = step == LAYERS - 1
        if boundary:
            first_end = state
        extra = {}
        if step < steps - 1:
            extra["following"] = (layer + 1) % LAYERS
            if boundary:
                extra["embedding"] = embedding
        else:
            extra["first_end"] = first_end_split
        blocks = (kv, *arrived)
        begun = forward_split(
            place_split, vec, forward_weights, last=layer, state=state_split,
            prev=blocks, pre=pre, **extra,
        )
        saved_split.append(
            {
                "pre": pre, "kv": blocks, "stat_pre": stat_pre,
                "post": begun["post"], "stat_post": begun["stat_post"],
            }
        )
        if step == steps - 1:
            answer_split = begun["answer"]
        else:
            state_split = begun["result"]
        if boundary:
            first_end_split = state_split
            state_split = begun["begun"]

    sums = [None] * LAYERS
    wires = [None] * LAYERS
    wires_qkv = [None] * LAYERS
    grad = None
    ended = None
    vecs = [None] * LAYERS
    for step in reversed(range(steps)):
        layer = step % LAYERS
        between = step == LAYERS - 1
        option = {}
        if step == steps - 1 or between:
            option = {"cotangent": cotangent, "row_len": row_len}
        if ended is not None:
            last = (step + 1) % LAYERS
            option |= {
                "last": last, "ended": ended, "sums": sums[last], "keep": between,
                "final": step == 0,
            }
        begun = backward_split(
            place_split, vec, backward_weights, following=layer, begun=saved_split[step], **option
        )
        if ended is not None:
            if step == 0:
                wires_qkv[last], vecs[last] = begun["wire"], begun["sum_vec"]
            else:
                sums[last] |= {"sum_qkv": begun["sum_qkv"], "sum_vec": begun["sum_vec"]}
            if between:
                second_split = begun["result"]
        arrived = [swap(begun[f"away_{hop}"], hop) for hop in range(1, 4)]
        five = {
            "post": saved_split[step]["post"], "hidden": begun["hidden"], "low": begun["low"],
            "middle": begun["middle"], "vec": begun["vec_out"],
        }
        source = {}
        if step == steps - 1:
            moved_answer = swap_blocks(answer)
            source["tokens"] = moved_top
        elif between:
            moved_second = swap_blocks(second)
            source["tokens"] = moved_top
        if grad is not None:
            source["grad"] = grad
        source |= {"base": sums[layer], "keep": step > 0, "travel": step in (0, LAYERS)}
        fixed = (layer, place, saved[step], vec, backward_weights, five)
        if step == 0:
            parts = [split(wires[1]), count_digits(token_counts, me, devices)]
            early = sum_cores(jnp.concatenate(parts, axis=1))
            grad, early = tie((grad, early))
            source["grad"] = grad
            half_way = backward_rows(*fixed, ffn_only=True, **source)
            early = sum_chips(early)
            half_way, early = tie((half_way, early))
            early = share_chips(early)
            kept = backward_rows(*fixed, part_done=half_way, **source)
            kept["wire"] = half_way["wire"]
        else:
            kept = backward_rows(*fixed, **source)
        if step > 0:
            grad, arrived = tie((kept["result"], arrived))
        else:
            kept["sum_qkv"], arrived = tie((kept["sum_qkv"], arrived))
        if step == LAYERS:
            second = [kept[f"travel_{hop}"] for hop in range(4)]
        if step == steps - 1:
            arrived, moved_answer = tie((arrived, moved_answer))
        if between:
            arrived, moved_second, kept["wire"] = tie((arrived, moved_second, kept["wire"]))
        if step == 0:
            arrived, early = tie((arrived, early))
            first = [kept[f"travel_{hop}"] for hop in range(4)]
        if sums[layer] is None:
            names = ("sum_qkv", "sum_out", "sum_up", "sum_down", "sum_vec")
            sums[layer] = {name: kept[name] for name in names}
        else:
            sums[layer] = {name: kept[name] for name in ("sum_qkv", "sum_vec")}
            wires[layer] = kept["wire"]
        ended = {name: begun[name] for name in ("middle_out", "query_out", "own_out")}
        ended |= {"arrived": arrived, "pre": saved_split[step]["pre"]}
        ended["stat_pre"] = saved_split[step]["stat_pre"]
    moved_first = swap_blocks(first)
    begun = backward_split(
        place_split, vec, backward_weights, last=0, ended=ended, sums=sums[0], keep=True,
        final=True,
    )
    first_split, wires_qkv[0], vecs[0] = begun["result"], begun["wire"], begun["sum_vec"]

    small = jnp.concatenate([values[0] for values in vecs])
    small = jnp.pad(small, (0, 2 * devices * 128 - small.size)).reshape(devices, 2, 128)
    small = jnp.pad(small, ((0, 0), (0, 14), (0, 0)))
    parts = [split(wires[0])] + [split(wire) for wire in wires_qkv] + [small.astype(BF)]
    part = sum_cores(jnp.concatenate(parts, axis=1))
    early_other = swap(early, 1)
    part, moved_first, early, early_other = tie(
        (sum_chips(part), moved_first, early, early_other)
    )
    late = share_chips(part)
    done = finish_tokens(
        place_split, (early, early_other), moved_answer, answer_split, moved_first, first_split,
        moved_second, second_split, hidden, groups, float(row_len),
    )
    late, done = tie((late, done))
    more = finish_weights(place_split, (late, swap(late, 1)), done, width, hidden)
    return (
        done["block_output"],
        done["input_grad"],
        done["embed_grad"],
        more["qkv"],
        more["out"],
        more["out_b"],
        more["up"],
        more["up_b"],
        more["down"],
        more["down_b"],
        more["gain"],
        more["shift"],
    )


def solution(mesh):
    if mesh.shape["seq"] == 4:
        fine = Mesh(mesh.devices.reshape(-1, 2, 2), ("dp", "y", "core"))
        return jax.shard_map(
            fast_device,
            mesh=fine,
            in_specs=(
                P("dp", SEQ, None),
                P("dp", SEQ, None),
                P("dp", SEQ, None),
                P(),
                P(),
                P(),
                P(),
                P(),
                P(),
                P(),
                P(),
                P(),
                P("dp", None),
                P("dp"),
                P("dp"),
            ),
            out_specs=(
                P("dp", SEQ, None),
                P("dp", SEQ, None),
                P("dp", SEQ, None),
                P(),
                P(),
                P(),
                P(),
                P(),
                P(),
                P(),
                P(),
                P(),
            ),
            check_vma=False,
        )
    return jax.shard_map(
        on_device,
        mesh=mesh,
        in_specs=(
            P("dp", "seq", None),
            P("dp", "seq", None),
            P("dp", "seq", None),
            P(),
            P(),
            P(),
            P(),
            P(),
            P(),
            P(),
            P(),
            P(),
            P("dp", None),
            P("dp"),
            P("dp"),
        ),
        out_specs=(
            P("dp", "seq", None),
            P("dp", "seq", None),
            P("dp", "seq", None),
            P(),
            P(),
            P(),
            P(),
            P(),
            P(),
            P(),
            P(),
            P(),
        ),
        check_vma=False,
    )
```

```python
import types

import jax
import jax.numpy as jnp
from jax import lax
from jax.experimental import pallas as pl
from jax.experimental.pallas import tpu as pltpu
from jax.sharding import Mesh, PartitionSpec as P

H = 4
LAYERS = 2


NORM_EPS = 1e-05
MASKED = -1e30


def layer_norm(values, gain, shift):
    center = values - jnp.mean(values, axis=-1, keepdims=True)
    spread = jnp.mean(center * center, axis=-1, keepdims=True)
    return center * lax.rsqrt(spread + NORM_EPS) * gain + shift


def gelu_exact(values):
    return jax.nn.gelu(values, approximate=False)


def matmul(left_side, right_side):
    return jnp.dot(left_side, right_side, preferred_element_type=jnp.float32)


def left_dot(left_side, right_side):
    return lax.dot_general(
        left_side, right_side, (((0,), (0,)), ((), ())), preferred_element_type=jnp.float32
    )


def right_dot(left_side, right_side):
    return lax.dot_general(
        left_side, right_side, (((1,), (1,)), ((), ())), preferred_element_type=jnp.float32
    )


def split_heads(packed, head_count):
    return packed.reshape(packed.shape[0], head_count, packed.shape[1] // head_count)


def attend_forward(queries, key_vals, allowed, head_count, score_scale):
    model_width = queries.shape[1]
    key_rows = split_heads(key_vals[:, :model_width], head_count)
    value_rows = split_heads(key_vals[:, model_width:], head_count)
    scores = (
        jnp.einsum(
            "qhd,khd->hqk",
            split_heads(queries, head_count),
            key_rows,
            preferred_element_type=jnp.float32,
        )
        * score_scale
    )
    scores = jnp.where(allowed[None], scores, MASKED)
    row_max = jnp.max(scores, axis=-1, keepdims=True)
    shifted_exp = jnp.exp(scores - row_max)
    row_total = jnp.sum(shifted_exp, axis=-1, keepdims=True)
    attn_probs = (shifted_exp / row_total).astype(jnp.bfloat16)
    blended = jnp.einsum("hqk,khd->qhd", attn_probs, value_rows, preferred_element_type=jnp.float32)
    return (blended.reshape(queries.shape[0], model_width), (row_max + jnp.log(row_total))[..., 0])


def attention_core(
    query_part, key_part, value_part, grad_part, allowed_part, logsum_part, head_count, score_scale
):
    scores = (
        jnp.einsum(
            "qhd,khd->hqk",
            split_heads(query_part, head_count),
            split_heads(key_part, head_count),
            preferred_element_type=jnp.float32,
        )
        * score_scale
    )
    scores = jnp.where(allowed_part[None], scores, MASKED)
    attn_probs = jnp.exp(scores - logsum_part[..., None])
    grad_probs = jnp.einsum(
        "qhd,khd->hqk",
        split_heads(grad_part, head_count),
        split_heads(value_part, head_count),
        preferred_element_type=jnp.float32,
    )
    return (attn_probs, grad_probs)


def query_grads(grad_scores, key_part, head_count, score_scale):
    result = (
        jnp.einsum(
            "hqk,khd->qhd",
            grad_scores,
            split_heads(key_part, head_count),
            preferred_element_type=jnp.float32,
        )
        * score_scale
    )
    return result.reshape(result.shape[0], -1)


def keyval_grads(grad_scores, attn_probs, query_part, grad_part, head_count, score_scale):
    grad_keys = (
        jnp.einsum(
            "hqk,qhd->khd",
            grad_scores,
            split_heads(query_part, head_count),
            preferred_element_type=jnp.float32,
        )
        * score_scale
    )
    grad_values = jnp.einsum(
        "hqk,qhd->khd",
        attn_probs.astype(jnp.bfloat16),
        split_heads(grad_part, head_count),
        preferred_element_type=jnp.float32,
    )
    return jnp.concatenate(
        [grad_keys.reshape(grad_keys.shape[0], -1), grad_values.reshape(grad_values.shape[0], -1)],
        axis=-1,
    )


def on_device(
    block_input,
    embedding,
    cotangent,
    qkv_weight,
    out_weight,
    out_bias,
    up_weight,
    up_bias,
    down_weight,
    down_bias,
    norm_gain,
    norm_shift,
    seg_lengths,
    loop_counts,
    token_counts,
):
    row_count, block_len, model_width = block_input.shape
    head_count = H
    score_scale = (model_width // head_count) ** (-0.5)
    row_len = block_len * lax.axis_size("seq")
    flat_rows = row_count * block_len
    offset = lax.axis_index("seq") * block_len
    key_pos = jnp.arange(row_len, dtype=jnp.int32)
    own_pos = offset + jnp.arange(block_len, dtype=jnp.int32)
    seg_ends = jnp.cumsum(seg_lengths, axis=-1)
    seg_all = jnp.sum((seg_ends[:, None, :] <= key_pos[None, :, None]).astype(jnp.int32), axis=-1)
    seg_own = lax.dynamic_slice_in_dim(seg_all, offset, block_len, 1)
    allowed = (seg_own[:, :, None] == seg_all[:, None, :]) & (
        key_pos[None, None, :] <= own_pos[None, :, None]
    )
    current = block_input.astype(jnp.float32)
    inject = embedding.astype(jnp.float32)
    stored = []
    finals = []
    for repeat in range(2):
        current = current + inject
        for layer_index in range(LAYERS):
            forward_normed = layer_norm(
                current, norm_gain[layer_index, 0], norm_shift[layer_index, 0]
            ).astype(jnp.bfloat16)
            forward_packed = matmul(
                forward_normed.reshape(flat_rows, model_width), qkv_weight[layer_index]
            ).astype(jnp.bfloat16)
            forward_packed = forward_packed.reshape(row_count, block_len, 3 * model_width)
            forward_key_vals = lax.all_gather(
                forward_packed[:, :, model_width:], "seq", axis=1, tiled=True
            )

            def forward_row(inputs):
                return attend_forward(inputs[0], inputs[1], inputs[2], head_count, score_scale)

            forward_blended, forward_logsum = lax.map(
                forward_row, (forward_packed[:, :, :model_width], forward_key_vals, allowed)
            )
            forward_blended = forward_blended.astype(jnp.bfloat16)
            branch_out = matmul(
                forward_blended.reshape(flat_rows, model_width), out_weight[layer_index]
            ).reshape(row_count, block_len, model_width)
            forward_middle = current + branch_out + out_bias[layer_index]
            forward_normed_two = layer_norm(
                forward_middle, norm_gain[layer_index, 1], norm_shift[layer_index, 1]
            ).astype(jnp.bfloat16)
            forward_up_proj = (
                matmul(forward_normed_two.reshape(flat_rows, model_width), up_weight[layer_index])
                + up_bias[layer_index]
            )
            forward_active = gelu_exact(forward_up_proj).astype(jnp.bfloat16)
            result = (
                forward_middle
                + matmul(forward_active, down_weight[layer_index]).reshape(
                    row_count, block_len, model_width
                )
                + down_bias[layer_index]
            )
            current, stored_layer = (
                result,
                (
                    current,
                    forward_normed,
                    forward_packed,
                    forward_key_vals,
                    forward_logsum,
                    forward_blended,
                    forward_middle,
                    forward_normed_two,
                    forward_up_proj,
                    forward_active,
                ),
            )
            stored.append(stored_layer)
        finals.append(current)
    two_loops = (loop_counts == 2)[:, None, None]
    block_output = jnp.where(two_loops, finals[1], finals[0]).astype(jnp.bfloat16)
    row_weight = token_counts.astype(jnp.float32) / row_len
    grad_top = cotangent.astype(jnp.float32) * row_weight[:, None, None]
    grad_state = jnp.where(two_loops, grad_top, 0.0)
    layer_sums = [None] * LAYERS
    second_pass = grad_state
    for repeat in (1, 0):
        for layer_index in reversed(range(LAYERS)):
            backward_stored_layer = stored[repeat * LAYERS + layer_index]
            (
                backward_current,
                normed,
                packed,
                key_vals,
                logsum,
                blended,
                middle,
                normed_two,
                up_proj,
                active,
            ) = backward_stored_layer
            grad_flat = grad_state.reshape(flat_rows, model_width)
            grad_low = grad_flat.astype(jnp.bfloat16)
            grad_down = left_dot(active, grad_low)
            grad_down_bias = jnp.sum(grad_flat, axis=0)
            grad_active = right_dot(grad_low, down_weight[layer_index])
            grad_up_proj = jax.vjp(gelu_exact, up_proj)[1](grad_active)[0].astype(jnp.bfloat16)
            grad_up_bias = jnp.sum(grad_up_proj.astype(jnp.float32), axis=0)
            grad_up = left_dot(normed_two.reshape(flat_rows, model_width), grad_up_proj)
            grad_normed_two = right_dot(grad_up_proj, up_weight[layer_index]).reshape(
                row_count, block_len, model_width
            )
            pull_two = jax.vjp(
                layer_norm, middle, norm_gain[layer_index, 1], norm_shift[layer_index, 1]
            )[1]
            grad_middle, gain_two, shift_two = pull_two(grad_normed_two)
            grad_middle = grad_middle + grad_state
            middle_flat = grad_middle.reshape(flat_rows, model_width)
            middle_low = middle_flat.astype(jnp.bfloat16)
            grad_out = left_dot(blended.reshape(flat_rows, model_width), middle_low)
            grad_out_bias = jnp.sum(middle_flat, axis=0)
            grad_blend = (
                right_dot(middle_low, out_weight[layer_index])
                .astype(jnp.bfloat16)
                .reshape(row_count, block_len, model_width)
            )
            queries = packed[:, :, :model_width]

            def full_row(inputs):
                query_part, keyval_part, grad_part, allowed_part, logsum_part = inputs
                attn_probs, grad_probs = attention_core(
                    query_part,
                    keyval_part[:, :model_width],
                    keyval_part[:, model_width:],
                    grad_part,
                    allowed_part,
                    logsum_part,
                    head_count,
                    score_scale,
                )
                row_delta = jnp.sum(attn_probs * grad_probs, axis=-1, keepdims=True)
                grad_scores = (attn_probs * (grad_probs - row_delta)).astype(jnp.bfloat16)
                return (
                    query_grads(grad_scores, keyval_part[:, :model_width], head_count, score_scale),
                    keyval_grads(
                        grad_scores, attn_probs, query_part, grad_part, head_count, score_scale
                    ),
                )

            grad_query, partial_kv = lax.map(
                full_row, (queries, key_vals, grad_blend, allowed, logsum)
            )
            grad_keyval = lax.psum_scatter(
                partial_kv.astype(jnp.bfloat16), "seq", scatter_dimension=1, tiled=True
            )
            grad_packed = jnp.concatenate(
                [grad_query.astype(jnp.bfloat16), grad_keyval], axis=-1
            ).reshape(flat_rows, 3 * model_width)
            grad_qkv = left_dot(normed.reshape(flat_rows, model_width), grad_packed)
            grad_normed = right_dot(grad_packed, qkv_weight[layer_index]).reshape(
                row_count, block_len, model_width
            )
            pull_one = jax.vjp(
                layer_norm, backward_current, norm_gain[layer_index, 0], norm_shift[layer_index, 0]
            )[1]
            grad_current, gain_one, shift_one = pull_one(grad_normed)
            grad_current = grad_current + grad_middle
            grad_state = grad_current
            grad_set = (
                grad_qkv,
                grad_out,
                grad_out_bias,
                grad_up,
                grad_up_bias,
                grad_down,
                grad_down_bias,
                jnp.stack([gain_one, gain_two]),
                jnp.stack([shift_one, shift_two]),
            )
            if repeat == 1:
                layer_sums[layer_index] = grad_set
            else:
                layer_sums[layer_index] = jax.tree.map(jnp.add, layer_sums[layer_index], grad_set)
        if repeat == 1:
            second_pass = grad_state
            grad_state = jnp.where(two_loops, grad_state, grad_top)
    grad_embed = grad_state + second_pass
    stacked = jax.tree.map(lambda *members: jnp.stack(members), *layer_sums)
    (
        sum_qkv,
        sum_out,
        sum_out_bias,
        sum_up,
        sum_up_bias,
        sum_down,
        sum_down_bias,
        sum_gain,
        sum_shift,
    ) = stacked
    total = lax.psum(jnp.sum(token_counts), "dp").astype(jnp.float32)
    summed = lax.psum(
        (
            sum_qkv,
            sum_out,
            sum_out_bias,
            sum_up,
            sum_up_bias,
            sum_down,
            sum_down_bias,
            sum_gain,
            sum_shift,
        ),
        ("dp", "seq"),
    )
    input_scale = row_count * lax.axis_size("dp") * row_len / total
    weight_scale = row_len / total
    return (
        block_output,
        grad_state * input_scale,
        grad_embed * input_scale,
        summed[0] * weight_scale,
        summed[1] * weight_scale,
        summed[2] * weight_scale,
        summed[3] * weight_scale,
        summed[4] * weight_scale,
        summed[5] * weight_scale,
        summed[6] * weight_scale,
        summed[7] * weight_scale,
        summed[8] * weight_scale,
    )


BF = jnp.bfloat16
F32 = jnp.float32
ERF_TERMS = (7.97869712e-01, 3.63922863e-02, -8.78266373e-05, -3.66934271e-05, 1.42500458e-06)
DENSITY_RATE = -0.7213475204444817
DENSITY_BASE = -1.3257480647361593
VMEM_LIMIT = 24 * 1024 * 1024
ONES_ROWS = 16


def dot_nn(left_side, right_side):
    return jnp.dot(left_side, right_side, preferred_element_type=F32)


def dot_nt(left_side, right_side):
    return lax.dot_general(
        left_side, right_side, (((1,), (1,)), ((), ())), preferred_element_type=F32
    )


def gelu_and_slope(z):
    square = z * z
    series = ERF_TERMS[-1] * square + ERF_TERMS[-2]
    for term in ERF_TERMS[-3::-1]:
        series = series * square + term
    cdf = 0.5 + 0.5 * jnp.tanh(z * series)
    density = jnp.exp2(square * DENSITY_RATE + DENSITY_BASE)
    return z * cdf, cdf + z * density


def norm_forward(values, gain, shift):
    center = values - jnp.mean(values, axis=0, keepdims=True)
    spread = jnp.mean(center * center, axis=0, keepdims=True)
    inverse = lax.rsqrt(spread + NORM_EPS)
    unit = center * inverse
    return unit, inverse, (unit * gain + shift).astype(BF)


def norm_backward(grad, unit, inverse, gain):
    scaled = grad * gain
    first = jnp.mean(scaled, axis=0, keepdims=True)
    second = jnp.mean(scaled * unit, axis=0, keepdims=True)
    return inverse * (scaled - first - unit * second)


def columns(vec):
    turned = vec[0].T

    def column(first, last):
        return jnp.concatenate(
            [turned[:, k : k + 1] for k in range(first // 128, last // 128)], axis=0
        )

    return column


def project_qkv(state, qkv_t, vec, pre, kv, stat, scale):
    width = state.shape[0]
    column = columns(vec)
    gain = column(2 * width, 3 * width)
    shift = column(3 * width, 4 * width)
    unit, inverse, normed = norm_forward(state, gain, shift)
    pre[0:width, :] = normed
    pre[2 * width : 3 * width, :] = unit.astype(BF)
    pre[width : 2 * width, :] = (dot_nn(qkv_t[0, 0:width, :], normed) * scale).astype(BF)
    kv[0:width, :] = dot_nn(qkv_t[0, width : 2 * width, :], normed).astype(BF)
    kv[width : 2 * width, :] = dot_nn(qkv_t[0, 2 * width : 3 * width, :], normed).astype(BF)
    stat[0:1, :] = inverse


def pad_head(block, odd):
    blank = jnp.zeros_like(block)
    return jnp.concatenate([blank, block] if odd else [block, blank], axis=0)


def tile_bias(first_key, start, causal, shape):
    key_at = lax.broadcasted_iota(jnp.int32, shape, 0)
    keep = key_at + first_key >= start
    if causal:
        keep = keep & (key_at <= lax.broadcasted_iota(jnp.int32, shape, 1))
    return jnp.where(keep, 0.0, MASKED)


def over_tiles(chunk, count, begin, half_tile, full_tile, carry):
    half = count // 2
    first_half = begin // half
    odd = jnp.where(first_half < 2 * chunk, first_half % 2, 0)
    carry = lax.fori_loop(0, odd, lambda _, c: half_tile(first_half // 2, c), carry)
    return lax.fori_loop((first_half + 1) // 2, chunk, full_tile, carry)


def attend_chunk(queries, keys, values_t, chunk, begin, start, bias, total, stat, blended):
    width, tokens = queries.shape
    head = width // H
    pair = 2 * head
    half = tokens // 2
    head_rows = [slice(h * head, (h + 1) * head) for h in range(H)]

    def scores(j, h, span):
        lanes = pl.ds((h // 2) * pair, pair)
        return dot_nn(keys[j, span, lanes], pad_head(queries[head_rows[h], :], h % 2))

    everything = slice(0, tokens)
    bias[...] = tile_bias(chunk * tokens, start, True, (tokens, tokens))
    parts = [scores(chunk, h, everything) for h in range(H)]
    uppers = [part[:half, :] + bias[:half, :] for part in parts]
    lowers = [part[half:, half:] + bias[half:, half:] for part in parts]
    tops, sums, weights = [], [], []
    for upper, lower in zip(uppers, lowers):
        top = jnp.max(upper, axis=0, keepdims=True)
        right = jnp.maximum(top[:, half:], jnp.max(lower, axis=0, keepdims=True))
        top = jnp.concatenate([top[:, :half], right], axis=1)
        upper = jnp.exp(upper - top)
        lower = jnp.exp(lower - right)
        added = jnp.sum(upper, axis=0, keepdims=True)
        right = added[:, half:] + jnp.sum(lower, axis=0, keepdims=True)
        tops.append(top)
        sums.append(jnp.concatenate([added[:, :half], right], axis=1))
        lower = lower.astype(BF)
        lower = jnp.concatenate([jnp.zeros_like(lower), lower], axis=1)
        weights.append(jnp.concatenate([upper.astype(BF), lower], axis=0))
    for rows, weight in zip(head_rows, weights):
        total[rows, :] = dot_nn(values_t[chunk, rows, :], weight)

    def step(j, span, size, carry):
        tops, sums = carry
        bias[:size, :] = tile_bias(j * tokens + span.start, start, False, (size, tokens))
        parts = [scores(j, h, span) + bias[:size, :] for h in range(H)]
        new_tops = [
            jnp.maximum(old, jnp.max(part, axis=0, keepdims=True))
            for old, part in zip(tops, parts)
        ]
        weights = [jnp.exp(part - top) for part, top in zip(parts, new_tops)]
        new_sums = [jnp.sum(weight, axis=0, keepdims=True) for weight in weights]
        terms = [
            dot_nn(values_t[j, rows, span], weight.astype(BF))
            for rows, weight in zip(head_rows, weights)
        ]
        fades = [jnp.exp(old - new) for old, new in zip(tops, new_tops)]
        for rows, term, fade in zip(head_rows, terms, fades):
            total[rows, :] = total[rows, :] * fade + term
        sums = [old * fade + new for old, fade, new in zip(sums, fades, new_sums)]
        return tuple(new_tops), tuple(sums)

    tops, sums = over_tiles(
        chunk, tokens, begin,
        lambda j, carry: step(j, slice(half, tokens), half, carry),
        lambda j, carry: step(j, everything, tokens, carry),
        (tuple(tops), tuple(sums)),
    )
    for h, rows in enumerate(head_rows):
        blended[rows, :] = (total[rows, :] / sums[h]).astype(BF)
        stat[h : h + 1, :] = tops[h] + jnp.log(sums[h])


def finish_layer(state, out_t, up_t, down_t, vec, post, stat):
    width, tokens = state.shape
    hidden = up_t.shape[1]
    column = columns(vec)
    middle = state + dot_nn(out_t[0], post[0:width, :]) + column(0, width)
    gain = column(4 * width, 5 * width)
    shift = column(5 * width, 6 * width)
    unit, inverse, normed = norm_forward(middle, gain, shift)
    post[width : 2 * width, :] = normed
    post[2 * width : 3 * width, :] = unit.astype(BF)
    stat[H : H + 1, :] = inverse
    z = dot_nn(up_t[0], normed) + column(6 * width, 6 * width + hidden)
    active, slope = gelu_and_slope(z)
    post[3 * width : 3 * width + hidden, :] = active.astype(BF)
    post[3 * width + hidden :, :] = slope.astype(BF)
    return (
        middle
        + dot_nn(down_t[0], post[3 * width : 3 * width + hidden, :])
        + column(width, 2 * width)
    )


def launch(
    name, body, place, grid, ins, outs, scratch=(), flops=0, aliases=(), near=(), free=()
):
    scratch = dict(scratch)
    names = [*ins, *outs, *scratch]

    def kernel(place_ref, *refs):
        body(place_ref, types.SimpleNamespace(**dict(zip(names, refs))))

    space = lambda key: pltpu.VMEM if key in near else pltpu.HBM
    results = pl.pallas_call(
        kernel,
        grid_spec=pltpu.PrefetchScalarGridSpec(
            num_scalar_prefetch=1,
            grid=(grid,),
            in_specs=[spec for _, spec in ins.values()],
            out_specs=[spec for _, spec in outs.values()],
            scratch_shapes=list(scratch.values()),
        ),
        out_shape=[
            shape if key in free else space(key)(shape.shape, shape.dtype)
            for key, (shape, _) in outs.items()
        ],
        input_output_aliases={
            1 + list(ins).index(source): list(outs).index(target) for source, target in aliases
        },
        compiler_params=pltpu.CompilerParams(vmem_limit_bytes=VMEM_LIMIT),
        cost_estimate=pl.CostEstimate(flops=flops, bytes_accessed=1, transcendentals=0),
        name=name,
    )(
        place,
        *[
            array if key in free else pltpu.with_memory_space_constraint(array, space(key))
            for key, (array, _) in ins.items()
        ],
    )
    return dict(zip(outs, results))


def whole(array):
    return array, pl.BlockSpec(array.shape, lambda i, *_: (0,) * len(array.shape))


def of_layer(array, layer):
    return array, pl.BlockSpec((1,) + array.shape[1:], lambda i, *_: (layer, 0, 0))


def each(array):
    return array, pl.BlockSpec((1,) + array.shape[1:], lambda i, *_: (i, 0, 0))


def each_back(array):
    count = array.shape[0]
    return array, pl.BlockSpec(
        (1,) + array.shape[1:], lambda i, *_: (count - 1 - i, 0, 0)
    )


def shaped(dims, dtype):
    return jax.ShapeDtypeStruct(dims, dtype)


def segment_starts(place, first, count):
    position = lax.broadcasted_iota(jnp.int32, (1, count), 1) + first
    starts = jnp.zeros((1, count), jnp.int32)
    end = jnp.int32(0)
    begin = jnp.int32(0)
    for k in range(4, place.shape[0]):
        end = end + place[k]
        starts = jnp.where(position >= end, end, starts)
        begin = jnp.where(first >= end, end, begin)
    return starts, begin


def gather_tokens(env, name, me):
    for hop in range(4):
        env.spread[me ^ hop] = getattr(env, f"{name}_{hop}")[...]


def deal_tokens(env, name, value, chunk, me):
    for hop in range(4):

        @pl.when(chunk == (me ^ hop))
        def _(hop=hop):
            getattr(env, f"{name}_{hop}")[...] = value


def token_ins(name, blocks):
    return {f"{name}_{hop}": whole(block) for hop, block in enumerate(blocks)}


def token_outs(name, tokens, width):
    return {f"{name}_{hop}": whole(shaped((tokens, width), BF)) for hop in range(4)}


def as_tokens(values):
    return values.astype(BF).T


def as_features(tokens):
    return tokens.T.astype(F32)


def forward_rows(layer, place, vec, weights, state=None, tokens=None, first_end=None):
    chunks = 4
    count = state.shape[2] if tokens is None else tokens[0].shape[0]
    qkv_t, out_t, up_t, down_t = weights
    width, hidden = out_t.shape[2], up_t.shape[1]
    post_rows = 3 * width + 2 * hidden

    def body(place, env):
        chunk = pl.program_id(0)
        me = place[0]
        current = env.state.at[0] if state is not None else None
        if tokens is not None:

            @pl.when(chunk == 0)
            def _():
                gather_tokens(env, "tokens", me)

            added = as_features(env.spread[chunk])
            env.current[...] = added if state is None else added + env.state[0]
            current = env.current
        project_qkv(
            current[...], env.qkv_t, env.vec, env.pre.at[0], env.kv.at[0], env.stat_pre.at[0],
            (width // H) ** -0.5,
        )
        env.keys[chunk] = env.kv[0, 0:width, :].T
        env.values_t[chunk] = env.kv[0, width : 2 * width, :]
        start, begin = segment_starts(place, chunk * count, count)
        attend_chunk(
            env.pre.at[0, width : 2 * width, :], env.keys, env.values_t, chunk, begin, start, env.bias, env.total, env.stat_post.at[0],
            env.post.at[0, 0:width, :],
        )
        result = finish_layer(
            current[...], env.out_t, env.up_t, env.down_t, env.vec, env.post.at[0],
            env.stat_post.at[0],
        )
        if first_end is None:
            env.result[0] = result
        else:
            answer = jnp.where(place[2] == 1, result, env.first_end[0])
            deal_tokens(env, "answer", as_tokens(answer), chunk, me)

    ins = {"vec": of_layer(vec, layer)}
    for name, weight in zip(("qkv_t", "out_t", "up_t", "down_t"), weights):
        ins[name] = of_layer(weight, layer)
    scratch = {
        "keys": pltpu.VMEM((chunks, count, width), BF),
        "values_t": pltpu.VMEM((chunks, width, count), BF),
        "bias": pltpu.VMEM((count, count), F32),
        "total": pltpu.VMEM((width, count), F32),
    }
    if state is not None:
        ins["state"] = each(state)
    if tokens is not None:
        ins |= token_ins("tokens", tokens)
        scratch["spread"] = pltpu.VMEM((chunks, count, width), BF)
        scratch["current"] = pltpu.VMEM((width, count), F32)
    outs = {}
    if first_end is None:
        outs["result"] = each(shaped((chunks, width, count), F32))
    else:
        ins["first_end"] = each(first_end)
        outs |= token_outs("answer", count, width)
    outs["pre"] = each(shaped((chunks, 3 * width, count), BF))
    outs["kv"] = each(shaped((chunks, 2 * width, count), BF))
    outs["post"] = each(shaped((chunks, post_rows, count), BF))
    outs["stat_pre"] = each(shaped((chunks, 8, count), F32))
    outs["stat_post"] = each(shaped((chunks, 8, count), F32))
    flops = chunks * count * 6 * (4 * width * width + 2 * width * hidden)
    return launch(
        "forward_rows", body, place, chunks, ins, outs, scratch, flops,
        near=["state", "result", "vec", "qkv_t", "out_t", "up_t", "down_t"]
        + [f"tokens_{hop}" for hop in range(4) if state is None],
    )


def split_row(array):
    return array, pl.BlockSpec((1,) + array.shape[1:], lambda i, place: (place[1], 0, 0))


def row_of_slot(slot, split, rows):
    return jnp.where(slot == split, rows - 1, slot)


def forward_split(
    place, vec, weights, last=None, following=None, state=None, prev=None, pre=None,
    block_input=None, embedding=None, first_end=None,
):
    qkv_t, out_t, up_t, down_t = weights
    width, hidden = out_t.shape[2], up_t.shape[1]
    count = embedding.shape[1] if state is None else state.shape[1]

    def body(place, env):
        me = place[0]
        if last is not None:
            for hop in range(4):
                arrived = getattr(env, f"kv_{hop}")
                env.keys[me ^ hop] = arrived[0:width, :].T
                env.values_t[me ^ hop] = arrived[width : 2 * width, :]
            start, begin = segment_starts(place, me * count, count)
            attend_chunk(
                env.pre_in.at[width : 2 * width, :], env.keys, env.values_t, me, begin, start,
                env.bias, env.total, env.stat_post, env.post.at[0:width, :],
            )
            current = finish_layer(
                env.state[...], env.out_t, env.up_t, env.down_t, env.vec, env.post, env.stat_post
            )
            if first_end is not None:
                answer = jnp.where(place[2] == 1, current, env.first_end[...])
                env.answer[...] = as_tokens(answer)
            else:
                env.result[...] = current
        if following is not None:
            if embedding is not None:
                added = as_features(env.embedding[0])
                if last is None:
                    current = as_features(env.block_input[0]) + added
                else:
                    current = env.result[...] + added
                env.begun[...] = current
            project_qkv(
                current, env.qkv_t, env.vec_next, env.pre, env.kv, env.stat_pre,
                (width // H) ** -0.5,
            )

    ins, outs, scratch = {}, {}, {}
    if last is not None:
        ins |= {f"kv_{hop}": whole(block) for hop, block in enumerate(prev)}
        ins |= {"state": whole(state), "pre_in": whole(pre)}
        ins["vec"] = of_layer(vec, last)
        for name, weight in zip(("out_t", "up_t", "down_t"), weights[1:]):
            ins[name] = of_layer(weight, last)
        if first_end is not None:
            ins["first_end"] = whole(first_end)
            outs["answer"] = whole(shaped((count, width), BF))
        else:
            outs["result"] = whole(shaped((width, count), F32))
        outs["post"] = whole(shaped((3 * width + 2 * hidden, count), BF))
        outs["stat_post"] = whole(shaped((8, count), F32))
        scratch = {
            "keys": pltpu.VMEM((4, count, width), BF),
            "values_t": pltpu.VMEM((4, width, count), BF),
            "bias": pltpu.VMEM((count, count), F32),
            "total": pltpu.VMEM((width, count), F32),
        }
    if following is not None:
        ins["vec_next"] = of_layer(vec, following)
        ins["qkv_t"] = of_layer(qkv_t, following)
        if embedding is not None:
            ins["embedding"] = split_row(embedding)
            outs["begun"] = whole(shaped((width, count), F32))
        if block_input is not None:
            ins["block_input"] = split_row(block_input)
        outs["pre"] = whole(shaped((3 * width, count), BF))
        outs["kv"] = whole(shaped((2 * width, count), BF))
        outs["stat_pre"] = whole(shaped((8, count), F32))
    flops = count * 6 * (4 * width * width + 2 * width * hidden)
    return launch(
        "forward_split", body, place, 1, ins, outs, scratch, flops,
        near=["state", "result", "begun", "pre", "pre_in", "kv", "vec", "vec_next", "qkv_t", "out_t", "up_t", "down_t"]
        + [f"kv_{hop}" for hop in range(4)],
    )


def backward_ffn(grad, post, stat, wout, wup, wdown, vec, hidden_grad):
    width, tokens = grad.shape
    hidden = wup.shape[2]
    low_grad = grad.astype(BF)
    hidden_grad[...] = (
        dot_nn(wdown[0], low_grad) * post[3 * width + hidden :, :].astype(F32)
    ).astype(BF)
    normed_grad = dot_nn(wup[0], hidden_grad[...])
    unit = post[2 * width : 3 * width, :].astype(F32)
    gain = columns(vec)(4 * width, 5 * width)
    middle = grad + norm_backward(normed_grad, unit, stat[H : H + 1, :], gain)
    low_middle = middle.astype(BF)
    blend_grad = dot_nn(wout[0], low_middle).astype(BF)
    return low_grad, normed_grad, unit, middle, low_middle, blend_grad


def token_sum(rows):
    return dot_nt(jnp.ones((ONES_ROWS, rows.shape[1]), BF), rows.astype(BF))


def attend_backward(
    queries, blend_grad, blended, stat, keys, values, keys_t, chunk, begin, start,
    bias, query_grad, kv_grad,
):
    width, tokens = queries.shape
    head = width // H
    pair = 2 * head
    head_rows = [slice(h * head, (h + 1) * head) for h in range(H)]
    deltas = [
        jnp.sum(
            blend_grad[rows, :].astype(F32) * blended[rows, :].astype(F32), axis=0, keepdims=True
        )
        for rows in head_rows
    ]

    half = tokens // 2
    everything = slice(0, tokens)

    def products(j, span):
        parts, prob_grads = [], []
        for h, rows in enumerate(head_rows):
            lanes = pl.ds((h // 2) * pair, pair)
            parts.append(dot_nn(keys[j, span, lanes], pad_head(queries[rows, :], h % 2)))
            prob_grads.append(
                dot_nn(values[j, span, lanes], pad_head(blend_grad[rows, :], h % 2))
            )
        return parts, prob_grads

    def collect(j, span, probs, score_grads, first):
        for rows, prob, score_grad in zip(head_rows, probs, score_grads):
            value_rows = slice(width + rows.start, width + rows.stop)
            kv_grad[j, value_rows, span] += dot_nt(blend_grad[rows, :], prob)
            kv_grad[j, rows, span] += dot_nt(queries[rows, :], score_grad)
            term = dot_nn(keys_t(j, rows, span), score_grad)
            if first:
                query_grad[rows, :] = term
            else:
                query_grad[rows, :] += term

    def weigh(part, prob_grad, mask, logsum, delta):
        prob = jnp.exp(part + mask - logsum)
        return prob.astype(BF), (prob * (prob_grad - delta)).astype(BF)

    bias[...] = tile_bias(chunk * tokens, start, True, (tokens, tokens))
    probs, score_grads = [], []
    for h, (part, prob_grad) in enumerate(zip(*products(chunk, everything))):
        logsum, delta = stat[h : h + 1, :], deltas[h]
        upper = weigh(part[:half, :], prob_grad[:half, :], bias[:half, :], logsum, delta)
        lower = weigh(
            part[half:, half:], prob_grad[half:, half:], bias[half:, half:], logsum[:, half:],
            delta[:, half:],
        )
        for kept, above, below in zip((probs, score_grads), upper, lower):
            below = jnp.concatenate([jnp.zeros_like(below), below], axis=1)
            kept.append(jnp.concatenate([above, below], axis=0))
    collect(chunk, everything, probs, score_grads, True)

    def step(j, span, size, carry):
        bias[:size, :] = tile_bias(j * tokens + span.start, start, False, (size, tokens))
        pairs = [
            weigh(part, prob_grad, bias[:size, :], stat[h : h + 1, :], deltas[h])
            for h, (part, prob_grad) in enumerate(zip(*products(j, span)))
        ]
        collect(j, span, [p for p, _ in pairs], [d for _, d in pairs], False)
        return carry

    over_tiles(
        chunk, tokens, begin,
        lambda j, carry: step(j, slice(half, tokens), half, carry),
        lambda j, carry: step(j, everything, tokens, carry),
        0,
    )


def add_vec(sum_vec, width, low_grad, normed_grad, unit, low_middle, dz):
    sum_vec[:, 0:width] += token_sum(low_middle)
    sum_vec[:, width : 2 * width] += token_sum(low_grad)
    sum_vec[:, 4 * width : 5 * width] += token_sum(normed_grad * unit)
    sum_vec[:, 5 * width : 6 * width] += token_sum(normed_grad)
    sum_vec[:, 6 * width :] += token_sum(dz)


def finish_backward(middle, pre, stat, packed, wqkv, vec, sum_qkv, sum_vec):
    width, tokens = middle.shape
    sum_qkv[...] += dot_nt(pre[0:width, :], packed[...])
    normed_grad = dot_nn(wqkv[0], packed[...])
    unit = pre[2 * width : 3 * width, :].astype(F32)
    gain = columns(vec)(2 * width, 3 * width)
    sum_vec[:, 2 * width : 3 * width] += token_sum(normed_grad * unit)
    sum_vec[:, 3 * width : 4 * width] += token_sum(normed_grad)
    return middle + norm_backward(normed_grad, unit, stat[0:1, :], gain)


def pack_lanes(wire, blocks):
    at = 0
    for ref in blocks:
        rows = ref.shape[0]
        for first in range(0, ref.shape[1], 128):
            wire[at : at + rows, :] = ref[:, first : first + 128].astype(BF)
            at += rows


def backward_rows(
    layer, place, saved, vec, weights, five, base=None, grad=None, tokens=None,
    keep=True, travel=False, part_done=None, ffn_only=False,
):
    chunks, _, count = saved["kv"].shape
    wqkv, wout, wup, wdown = weights
    width, hidden = wup.shape[1:]
    row_len = chunks * count
    first = base is None
    part = hidden // chunks
    vec_len = 6 * width + hidden
    with_ffn, with_attention = part_done is None, not ffn_only

    def body(place, env):
        order = pl.program_id(0)
        chunk = chunks - 1 - order
        me = place[0]

        @pl.when(order == 0)
        def _():
            if tokens is not None:
                gather_tokens(env, "tokens", me)
            if with_ffn:
                env.sum_up[...] = jnp.zeros_like(env.sum_up)
                env.sum_down[...] = jnp.zeros_like(env.sum_down)
                env.sum_out[...] = dot_nt(env.blend_five[...], env.middle_five[...])
                env.sum_vec[...] = env.vec_five[...]
                if not first:
                    env.sum_vec[...] += env.base_vec[...]
            else:
                env.sum_vec[...] = env.vec_done[...]
            if with_attention:
                env.sum_qkv[...] = jnp.zeros_like(env.sum_qkv)
                env.kv_grad[...] = jnp.zeros_like(env.kv_grad)
                for j in range(chunks):
                    env.keys[j] = env.kv[j, 0:width, :].T
                    env.values[j] = env.kv[j, width : 2 * width, :].T

        def add_base(ref, old):
            rows = old.shape[0]
            ref[pl.ds(pl.multiple_of(order * rows, rows), rows), :] += old[...]

        if with_ffn:
            spread = pl.ds(pl.multiple_of(order * part, part), part)
            env.sum_down[spread, :] += dot_nt(env.active_five[...], env.low_five[...])
            env.sum_up[:, spread] += dot_nt(env.normed_five[...], env.hidden_five[...])
            if not first:
                env.sum_down[spread, :] += env.base_down[...]
                env.sum_up[:, spread] += env.base_up[...]
                add_base(env.sum_out, env.base_out)
            current = env.grad.at[0] if grad is not None else None
            if tokens is not None:
                top = as_features(env.spread[chunk]) * (place[3].astype(F32) * (1.0 / row_len))
                two = place[2] == 1
                env.current[...] = (
                    jnp.where(two, top, 0.0)
                    if grad is None
                    else jnp.where(two, env.grad[0], top)
                )
                current = env.current
            post = env.post.at[0]
            low_grad, normed_grad, unit, middle, low_middle, blend_grad = backward_ffn(
                current[...], post, env.stat_post.at[0], env.wout, env.wup, env.wdown, env.vec,
                env.hidden_grad,
            )
            env.sum_down[...] += dot_nt(post[3 * width : 3 * width + hidden, :], low_grad)
            env.sum_up[...] += dot_nt(post[width : 2 * width, :], env.hidden_grad[...])
            env.sum_out[...] += dot_nt(post[0:width, :], low_middle)
            add_vec(
                env.sum_vec, width, low_grad, normed_grad, unit, low_middle, env.hidden_grad[...]
            )
            blend_ref = env.blend_grad if with_attention else env.blend_out.at[0]
            blend_ref[...] = blend_grad
            if not first:

                @pl.when(order == chunks - 1)
                def _():
                    pack_lanes(env.wire, (env.sum_out, env.sum_up, env.sum_down))

            if not with_attention:
                env.middle_out[0] = middle
                return
            blended = post.at[0:width, :]
        else:
            middle, blend_ref, blended = env.middle_in[0], env.blend_in.at[0], env.blended.at[0]
        if not first:
            add_base(env.sum_qkv, env.base_qkv)
        start, begin = segment_starts(place, chunk * count, count)
        attend_backward(
            env.pre.at[0, width : 2 * width, :], blend_ref, blended,
            env.stat_post.at[0], env.keys, env.values, lambda j, rows, span: env.kv[j, rows, span],
            chunk, begin, start, env.bias, env.query_grad, env.kv_grad,
        )
        env.packed[0:width, :] = (env.query_grad[...] * (width // H) ** -0.5).astype(BF)
        env.packed[width : 3 * width, :] = env.kv_grad[chunk].astype(BF)
        result = finish_backward(
            middle, env.pre.at[0], env.stat_pre.at[0], env.packed, env.wqkv, env.vec,
            env.sum_qkv, env.sum_vec,
        )
        if keep:
            env.result[0] = result
        if travel:
            deal_tokens(env, "travel", as_tokens(result), chunk, me)

    ins = {"vec": of_layer(vec, layer), "stat_post": each_back(saved["stat_post"])}
    outs, scratch = {}, {}
    cut = lambda array, shape, at: (array, pl.BlockSpec(shape, lambda i, *_: at(i)))
    sums = {"sum_vec": (ONES_ROWS, vec_len)}
    if with_ffn:
        ins["post"] = each_back(saved["post"])
        for name, weight in zip(("wout", "wup", "wdown"), weights[1:]):
            ins[name] = of_layer(weight, layer)
        if grad is not None:
            ins["grad"] = each_back(grad)
        if tokens is not None:
            ins |= token_ins("tokens", tokens)
            scratch["spread"] = pltpu.VMEM((chunks, count, width), BF)
            scratch["current"] = pltpu.VMEM((width, count), F32)
        post_five = five["post"]
        ins["blend_five"] = cut(post_five, (width, count), lambda i: (0, 0))
        ins["normed_five"] = cut(post_five, (width, count), lambda i: (1, 0))
        ins["active_five"] = cut(post_five, (part, count), lambda i: (3 * width // part + i, 0))
        ins["hidden_five"] = cut(five["hidden"], (part, count), lambda i: (i, 0))
        for name in ("low", "middle", "vec"):
            ins[name + "_five"] = whole(five[name])
        sums |= {"sum_out": (width, width), "sum_up": (width, hidden), "sum_down": (hidden, width)}
        scratch["hidden_grad"] = pltpu.VMEM((hidden, count), BF)
        if not first:
            ins["base_out"] = cut(base["sum_out"], (width // chunks, width), lambda i: (i, 0))
            ins["base_up"] = cut(base["sum_up"], (width, part), lambda i: (0, i))
            ins["base_down"] = cut(base["sum_down"], (part, width), lambda i: (i, 0))
            ins["base_vec"] = whole(base["sum_vec"])
            wire_rows = (width * width + 2 * width * hidden) // 128
            outs["wire"] = whole(shaped((wire_rows, 128), BF))
        if not with_attention:
            outs["blend_out"] = each_back(shaped((chunks, width, count), BF))
            outs["middle_out"] = each_back(shaped((chunks, width, count), F32))
    else:
        ins["vec_done"] = whole(part_done["sum_vec"])
        ins["middle_in"] = each_back(part_done["middle_out"])
        ins["blend_in"] = each_back(part_done["blend_out"])
        ins["blended"] = (
            saved["post"],
            pl.BlockSpec((1, width, count), lambda i, *_: (chunks - 1 - i, 0, 0)),
        )
    if with_attention:
        ins["kv"] = whole(saved["kv"])
        ins["pre"] = each_back(saved["pre"])
        ins["stat_pre"] = each_back(saved["stat_pre"])
        ins["wqkv"] = of_layer(wqkv, layer)
        sums["sum_qkv"] = (width, 3 * width)
        if not first:
            ins["base_qkv"] = cut(base["sum_qkv"], (width // chunks, 3 * width), lambda i: (i, 0))
        if keep:
            outs["result"] = each_back(shaped((chunks, width, count), F32))
        if travel:
            outs |= token_outs("travel", count, width)
        scratch |= {
            "keys": pltpu.VMEM((chunks, count, width), BF),
            "values": pltpu.VMEM((chunks, count, width), BF),
            "bias": pltpu.VMEM((count, count), F32),
            "query_grad": pltpu.VMEM((width, count), F32),
            "kv_grad": pltpu.VMEM((chunks, 2 * width, count), F32),
            "blend_grad": pltpu.VMEM((width, count), BF),
            "packed": pltpu.VMEM((3 * width, count), BF),
        }
    for name, dims in sums.items():
        if first or name in ("sum_qkv", "sum_vec"):
            outs[name] = whole(shaped(dims, F32))
        else:
            scratch[name] = pltpu.VMEM(dims, F32)
    flops = chunks * count * 12 * (4 * width * width + 2 * width * hidden)
    return launch(
        "backward_rows", body, place, chunks, ins, outs, scratch, flops,
        near=[
            "grad", "result", "hidden_five", "low_five", "middle_five", "vec_five", "middle_in",
            "middle_out", "blend_in", "blend_out",
        ],
    )


def backward_split(
    place, vec, weights, last=None, following=None, ended=None, sums=None, begun=None,
    cotangent=None, final=False, keep=False, row_len=None,
):
    wqkv, wout, wup, wdown = weights
    width, hidden = wup.shape[1:]
    vec_len = 6 * width + hidden
    count = (ended or begun)["stat_pre"].shape[1]

    def body(place, env):
        me = place[0]
        if last is not None:
            sum_qkv = env.total_qkv if final else env.sum_qkv
            env.packed[0:width, :] = env.query_in[...]
            kv_total = env.own_in[...]
            for hop in range(1, 4):
                kv_total = kv_total + getattr(env, f"in_{hop}")[...].astype(F32)
            env.packed[width : 3 * width, :] = kv_total.astype(BF)
            sum_qkv[...] = env.old_qkv[...]
            env.sum_vec[...] = env.old_vec[...]
            current = finish_backward(
                env.middle_in[...], env.pre_last, env.stat_last, env.packed, env.wqkv,
                env.vec_last, sum_qkv, env.sum_vec,
            )
            if keep:
                env.result[...] = current.T
            if final:
                pack_lanes(env.wire, (sum_qkv,))
        if following is not None:
            if cotangent is not None:
                top = as_features(env.cotangent[0]) * (place[3].astype(F32) * (1.0 / row_len))
                two = place[2] == 1
                grad = jnp.where(two, top, 0.0) if last is None else jnp.where(two, current, top)
            else:
                grad = current
            env.kv_grad[...] = jnp.zeros_like(env.kv_grad)
            for hop in range(4):
                arrived = getattr(env, f"kv_{hop}")
                env.keys[me ^ hop] = arrived[0:width, :].T
                env.keys_t[me ^ hop] = arrived[0:width, :]
                env.values[me ^ hop] = arrived[width : 2 * width, :].T
            low_grad, normed_grad, unit, middle, low_middle, blend_grad = backward_ffn(
                grad, env.post, env.stat_post, env.wout, env.wup, env.wdown, env.vec, env.hidden
            )
            env.low[...] = low_grad
            env.middle[...] = low_middle
            env.middle_out[...] = middle
            env.vec_out[...] = jnp.zeros_like(env.vec_out)
            add_vec(
                env.vec_out, width, low_grad, normed_grad, unit, low_middle, env.hidden[...]
            )
            env.blend_grad[...] = blend_grad
            start, begin = segment_starts(place, me * count, count)
            attend_backward(
                env.pre.at[width : 2 * width, :], env.blend_grad, env.post.at[0:width, :],
                env.stat_post, env.keys, env.values, lambda j, rows, span: env.keys_t[j, rows, span],
                me, begin, start, env.bias, env.query_grad, env.kv_grad,
            )
            env.query_out[...] = (env.query_grad[...] * (width // H) ** -0.5).astype(BF)
            env.own_out[...] = env.kv_grad[me]
            for hop in range(1, 4):
                getattr(env, f"away_{hop}")[...] = env.kv_grad[me ^ hop].astype(BF)

    ins, outs, scratch = {}, {}, {}
    if last is not None:
        ins["middle_in"] = whole(ended["middle_out"])
        ins["query_in"] = whole(ended["query_out"])
        ins["own_in"] = whole(ended["own_out"])
        for hop in range(1, 4):
            ins[f"in_{hop}"] = whole(ended["arrived"][hop - 1])
        ins["pre_last"] = whole(ended["pre"])
        ins["stat_last"] = whole(ended["stat_pre"])
        ins["vec_last"] = of_layer(vec, last)
        ins["wqkv"] = of_layer(wqkv, last)
        ins["old_qkv"] = whole(sums["sum_qkv"])
        ins["old_vec"] = whole(sums["sum_vec"])
        if keep:
            outs["result"] = whole(shaped((count, width), F32))
        if final:
            outs["wire"] = whole(shaped((3 * width * width // 128, 128), BF))
            scratch["total_qkv"] = pltpu.VMEM((width, 3 * width), F32)
        else:
            outs["sum_qkv"] = whole(shaped((width, 3 * width), F32))
        outs["sum_vec"] = whole(shaped((ONES_ROWS, vec_len), F32))
        scratch["packed"] = pltpu.VMEM((3 * width, count), BF)
    if following is not None:
        for name in ("pre", "post", "stat_post"):
            ins[name] = whole(begun[name])
        for hop in range(4):
            ins[f"kv_{hop}"] = whole(begun["kv"][hop])
        ins["vec"] = of_layer(vec, following)
        for name, weight in zip(("wout", "wup", "wdown"), weights[1:]):
            ins[name] = of_layer(weight, following)
        if cotangent is not None:
            ins["cotangent"] = split_row(cotangent)
        outs["middle_out"] = whole(shaped((width, count), F32))
        outs["query_out"] = whole(shaped((width, count), BF))
        outs["own_out"] = whole(shaped((2 * width, count), F32))
        for hop in range(1, 4):
            outs[f"away_{hop}"] = whole(shaped((2 * width, count), BF))
        outs["low"] = whole(shaped((width, count), BF))
        outs["hidden"] = whole(shaped((hidden, count), BF))
        outs["middle"] = whole(shaped((width, count), BF))
        outs["vec_out"] = whole(shaped((ONES_ROWS, vec_len), F32))
        scratch |= {
            "keys": pltpu.VMEM((4, count, width), BF),
            "values": pltpu.VMEM((4, count, width), BF),
            "keys_t": pltpu.VMEM((4, width, count), BF),
            "bias": pltpu.VMEM((count, count), F32),
            "query_grad": pltpu.VMEM((width, count), F32),
            "kv_grad": pltpu.VMEM((4, 2 * width, count), F32),
            "blend_grad": pltpu.VMEM((width, count), BF),
        }
    flops = count * 12 * (4 * width * width + 2 * width * hidden)
    return launch(
        "backward_split", body, place, 1, ins, outs, scratch, flops,
        near=[
            "middle_in", "query_in", "own_in", "in_1", "in_2", "in_3", "middle_out", "query_out",
            "own_out", "away_1", "away_2", "away_3", "low", "hidden", "middle", "vec_out",
        ],
    )


def cut_tokens(place, *pairs, near=False):
    arrays = [array for pair in pairs for array in pair]
    rows, count, width = arrays[0].shape

    def body(place, env):
        at = 0
        for index, pair in enumerate(pairs):
            value = getattr(env, f"in_{at}")[0].astype(F32)
            for extra in range(1, len(pair)):
                value = value + getattr(env, f"in_{at + extra}")[0].astype(F32)
            at += len(pair)
            for hop in range(4):

                @pl.when(pl.program_id(0) == hop)
                def _(hop=hop, index=index, value=value):
                    getattr(env, f"out{index}_{hop}")[...] = value.astype(BF)

    spec = pl.BlockSpec(
        (1, count, width), lambda i, place: (row_of_slot(place[0] ^ i, place[1], rows), 0, 0)
    )
    ins = {f"in_{k}": (array, spec) for k, array in enumerate(arrays)}
    outs = {}
    for index in range(len(pairs)):
        outs |= token_outs(f"out{index}", count, width)
    results = launch(
        "cut_tokens", body, place, 4, ins, outs, near=list(outs) if near else ()
    )
    return [[results[f"out{index}_{hop}"] for hop in range(4)] for index in range(len(pairs))]


def prepare(here, weights, vectors):
    out_bias, down_bias, norm_gain, norm_shift, up_bias = vectors
    layers, width = out_bias.shape
    hidden = up_bias.shape[1]
    rows = (6 * width + hidden) // 128
    rows += -rows % 8

    def body(place, env):
        layer = pl.program_id(0)
        for k in range(4):
            getattr(env, f"turned_{k}")[0] = getattr(env, f"weight_{k}")[0].T
        env.vec[...] = jnp.zeros_like(env.vec)
        pick = lambda ref: ref[pl.ds(layer, 1), :]
        parts = [pick(env.out_bias), pick(env.down_bias)]
        for k in range(2):
            parts += [env.norm_gain[0, k : k + 1, :], env.norm_shift[0, k : k + 1, :]]
        at = 0
        for part in parts + [pick(env.up_bias)]:
            for lanes in range(0, part.shape[1], 128):
                env.vec[0, at : at + 1, :] = part[:, lanes : lanes + 128]
                at += 1

    ins = {f"weight_{k}": each(weight) for k, weight in enumerate(weights)}
    ins |= {"out_bias": whole(out_bias), "down_bias": whole(down_bias), "up_bias": whole(up_bias)}
    ins |= {"norm_gain": each(norm_gain), "norm_shift": each(norm_shift)}
    outs = {
        f"turned_{k}": each(shaped((layers, weight.shape[2], weight.shape[1]), BF))
        for k, weight in enumerate(weights)
    }
    outs["vec"] = each(shaped((layers, rows, 128), F32))
    results = launch("prepare", body, here, layers, ins, outs, near=list(outs))
    return tuple(results[f"turned_{k}"] for k in range(4)), results["vec"]


def piece_reader(payloads, me):
    mine, other = payloads
    half = mine.shape[0]

    def piece(p, first, rows):
        left, right = (ref[p % half, first : first + rows, :] for ref in (mine, other))
        return jnp.where(me % 2 == p // half, left, right).astype(F32)

    return piece


def spread_pieces(piece, pieces, first, rows_each, targets, factor):
    edges, at = [], 0
    for ref in targets:
        for lanes in range(0, ref.shape[2], 128):
            edges.append((at, at + ref.shape[1], ref, lanes))
            at += ref.shape[1]
    for p in range(pieces):
        values = piece(p, first, rows_each) * factor
        begin = p * rows_each
        for low, high, ref, lanes in edges:
            left, right = max(low, begin), min(high, begin + rows_each)
            if left < right:
                ref[0, left - low : right - low, lanes : lanes + 128] = values[
                    left - begin : right - begin, :
                ]


def finish_tokens(
    place, payload, answer, answer_split, first, first_split, second, second_split,
    hidden, groups, row_len,
):
    count, width = first_split.shape
    rows = 5
    pieces = 2 * payload[0].shape[0]
    ffn_rows = (width * width + 2 * width * hidden) // 128 // pieces

    def body(place, env):
        step = pl.program_id(0)
        me = place[0]
        piece = piece_reader((env.mine, env.other), me)
        lane = lax.broadcasted_iota(jnp.int32, (1, 128), 1)
        total = jnp.zeros((1, 1), F32)
        for extra in range(-(-2 * groups // 128)):
            row = piece(extra, ffn_rows, 16)[0:1, :]
            worth = jnp.where(lane % 2 == 0, 256.0, 1.0)
            row = jnp.where(lane + extra * 128 < 2 * groups, row * worth, 0.0)
            total = total + jnp.sum(row, axis=1, keepdims=True)
        factor = row_len / total
        token_factor = factor * float(rows * groups)

        @pl.when(step == 0)
        def _():
            env.scale[...] = jnp.broadcast_to(factor, env.scale.shape)
            spread_pieces(piece, pieces, 0, ffn_rows, (env.out, env.up, env.down), factor)

        for hop in range(4):

            @pl.when(step == row_of_slot(me ^ hop, place[1], rows))
            def _(hop=hop):
                env.block_output[0] = getattr(env, f"answer_{hop}")[...]
                one = getattr(env, f"first_{hop}")[...].astype(F32)
                two = getattr(env, f"second_{hop}")[...].astype(F32)
                env.input_grad[0] = one * token_factor
                env.embed_grad[0] = (one + two) * token_factor

        @pl.when(step == place[1])
        def _():
            env.block_output[0] = env.answer_split[...]
            one = env.first_split[...]
            env.input_grad[0] = one * token_factor
            env.embed_grad[0] = (one + env.second_split[...]) * token_factor

    ins = {"mine": whole(payload[0]), "other": whole(payload[1])}
    ins |= token_ins("answer", answer) | token_ins("first", first) | token_ins("second", second)
    ins["answer_split"] = whole(answer_split)
    ins["first_split"] = whole(first_split)
    ins["second_split"] = whole(second_split)
    later = lambda *dims: (
        shaped(dims, F32), pl.BlockSpec((1,) + dims[1:], lambda i, *_: (LAYERS - 1, 0, 0))
    )
    outs = {
        "block_output": each(shaped((rows, count, width), BF)),
        "input_grad": each(shaped((rows, count, width), F32)),
        "embed_grad": each(shaped((rows, count, width), F32)),
        "out": later(LAYERS, width, width),
        "up": later(LAYERS, width, hidden),
        "down": later(LAYERS, hidden, width),
        "scale": whole(shaped((8, 128), F32)),
    }
    return launch(
        "finish_tokens", body, place, rows, ins, outs, free=("mine", "other")
    )


def finish_weights(place, payload, done, width, hidden):
    pieces = 2 * payload[0].shape[0]
    ffn_rows = (width * width + 2 * width * hidden) // 128 // pieces
    qkv_rows = 3 * width * width // 128 // pieces
    small_at = ffn_rows + LAYERS * qkv_rows
    vec_len = 6 * width + hidden

    def body(place, env):
        step = pl.program_id(0)
        piece = piece_reader((env.mine, env.other), place[0])
        factor = env.scale[0:1, 0:1]

        @pl.when(step == 0)
        def _():
            spread_pieces(piece, pieces, 0, ffn_rows, (env.out, env.up, env.down), factor)
            for here in range(LAYERS):
                for ref, slot, at, size in (
                    (env.out_b, None, 0, width),
                    (env.down_b, None, width, width),
                    (env.gain, 0, 2 * width, width),
                    (env.shift, 0, 3 * width, width),
                    (env.gain, 1, 4 * width, width),
                    (env.shift, 1, 5 * width, width),
                    (env.up_b, None, 6 * width, hidden),
                ):
                    for lanes in range(0, size, 128):
                        index = (here * vec_len + at + lanes) // 128
                        row = piece(index // 2, small_at, 16)[index % 2 : index % 2 + 1, :]
                        row = row * factor
                        if slot is None:
                            ref[here : here + 1, lanes : lanes + 128] = row
                        else:
                            ref[here, slot : slot + 1, lanes : lanes + 128] = row

        for here in range(LAYERS):

            @pl.when(step == here)
            def _(here=here):
                spread_pieces(
                    piece, pieces, ffn_rows + here * qkv_rows, qkv_rows, (env.qkv,), factor
                )

    ins = {"mine": whole(payload[0]), "other": whole(payload[1]), "scale": whole(done["scale"])}
    names = ("out", "up", "down")
    for name in names:
        ins[name + "_done"] = (done[name], pl.BlockSpec(memory_space=pl.ANY))
    start = lambda array: (
        array, pl.BlockSpec((1,) + array.shape[1:], lambda i, *_: (0, 0, 0))
    )
    outs = {name: start(shaped(done[name].shape, F32)) for name in names}
    outs["qkv"] = each(shaped((LAYERS, width, 3 * width), F32))
    outs["out_b"] = whole(shaped((LAYERS, width), F32))
    outs["up_b"] = whole(shaped((LAYERS, hidden), F32))
    outs["down_b"] = whole(shaped((LAYERS, width), F32))
    outs["gain"] = whole(shaped((LAYERS, 2, width), F32))
    outs["shift"] = whole(shaped((LAYERS, 2, width), F32))
    return launch(
        "finish_weights", body, place, LAYERS, ins, outs,
        aliases=[(name + "_done", name) for name in names],
        free=("mine", "other"),
    )


SEQ = ("y", "core")
CHIPS = ("dp", "y")


def swap(values, hop):
    return lax.ppermute(values, SEQ, [(i, i ^ hop) for i in range(lax.axis_size(SEQ))])


def swap_blocks(blocks):
    return [blocks[0]] + [swap(block, hop) for hop, block in enumerate(blocks[1:], 1)]


def sum_cores(pieces):
    core = lax.axis_index("core")
    half = pieces.shape[0] // 2
    keep = lax.dynamic_slice_in_dim(pieces, core * half, half, 0)
    give = lax.dynamic_slice_in_dim(pieces, (1 - core) * half, half, 0)
    return (keep.astype(F32) + swap(give, 1).astype(F32)).astype(BF)


def sum_chips(part):
    part = lax.all_to_all(part, CHIPS, 0, 0, tiled=True)
    return jnp.sum(part.astype(F32), axis=0).astype(BF)


def share_chips(part):
    copies = jnp.broadcast_to(part[None], (lax.axis_size(CHIPS),) + part.shape)
    return lax.all_to_all(copies, CHIPS, 0, 0, tiled=True)


def count_digits(token_counts, me, devices):
    groups = lax.axis_size("dp")
    tally = jnp.sum(token_counts)
    digits = jnp.stack([tally // 256, tally % 256]).astype(F32) * (me == 0)
    slots = jnp.arange(groups)[:, None] == lax.axis_index("dp")
    digits = jnp.where(slots, digits[None], 0.0).reshape(-1)
    digits = jnp.pad(digits, (0, devices * 128 - digits.size)).reshape(devices, 1, 128)
    return jnp.pad(digits, ((0, 0), (0, 15), (0, 0))).astype(BF)


def fast_device(
    block_input, embedding, cotangent, qkv_weight, out_weight, out_bias, up_weight, up_bias,
    down_weight, down_bias, norm_gain, norm_shift, seg_lengths, loop_counts, token_counts,
):
    row_count, tokens, width = block_input.shape
    chunks = lax.axis_size(SEQ)
    groups = lax.axis_size("dp")
    devices = groups * chunks
    row_len = tokens * chunks
    me = lax.axis_index(SEQ)
    hidden = up_weight.shape[2]
    tie = lax.optimization_barrier
    split = lambda rows: rows.reshape(devices, -1, 128)
    steps = LAYERS * 2

    longest = jnp.argmax(jnp.max(seg_lengths, axis=1)).astype(jnp.int32)
    here = jnp.stack([me.astype(jnp.int32), longest])
    (sent,) = cut_tokens(here, (block_input, embedding), near=True)
    moved = swap_blocks(sent)
    backward_weights = (qkv_weight, out_weight, up_weight, down_weight)
    vectors = (out_bias, down_bias, norm_gain, norm_shift, up_bias)
    here, sent = tie((here, sent))
    forward_weights, vec = prepare(here, backward_weights, vectors)

    table = jnp.concatenate(
        [(loop_counts == 2).astype(jnp.int32)[:, None], token_counts[:, None], seg_lengths], axis=1
    )
    row = lambda at: jnp.concatenate([here, lax.dynamic_index_in_dim(table, at, 0, keepdims=False)])
    place = row(row_of_slot(me, longest, row_count))
    place_split = row(longest)

    saved, saved_split = [], []
    begun = forward_split(
        place_split, vec, forward_weights, following=0, block_input=block_input,
        embedding=embedding,
    )
    state_split = begun["begun"]
    state = None
    first_end = first_end_split = None
    sent_embed, sent_top = cut_tokens(here, (embedding,), (cotangent,))
    for step in range(steps):
        layer = step % LAYERS
        pre, kv, stat_pre = begun["pre"], begun["kv"], begun["stat_pre"]
        arrived = [swap(kv, hop) for hop in range(1, 4)]
        source = {}
        if step == 0:
            moved, kv = tie((moved, kv))
            source["tokens"] = moved
        elif step == LAYERS:
            state, moved_embed, kv = tie((state, moved_embed, kv))
            source["state"], source["tokens"] = state, moved_embed
        else:
            state, kv = tie((state, kv))
            source["state"] = state
        if step == 0:
            sent_embed, kv = tie((sent_embed, kv))
            moved_embed = swap_blocks(sent_embed)
        if step == LAYERS:
            sent_top, kv = tie((sent_top, kv))
            moved_top = swap_blocks(sent_top)
        if step == steps - 1:
            source["first_end"] = first_end
        kept = forward_rows(layer, place, vec, forward_weights, **source)
        saved.append(kept)
        if step == steps - 1:
            answer = [kept[f"answer_{hop}"] for hop in range(4)]
            answer, arrived = tie((answer, arrived))
        else:
            state, arrived = tie((kept["result"], arrived))
        if step == 0:
            arrived, moved_embed = tie((arrived, moved_embed))
        if step == LAYERS:
            arrived, moved_top = tie((arrived, moved_top))
        boundary = step == LAYERS - 1
        if boundary:
            first_end = state
        extra = {}
        if step < steps - 1:
            extra["following"] = (layer + 1) % LAYERS
            if boundary:
                extra["embedding"] = embedding
        else:
            extra["first_end"] = first_end_split
        blocks = (kv, *arrived)
        begun = forward_split(
            place_split, vec, forward_weights, last=layer, state=state_split,
            prev=blocks, pre=pre, **extra,
        )
        saved_split.append(
            {
                "pre": pre, "kv": blocks, "stat_pre": stat_pre,
                "post": begun["post"], "stat_post": begun["stat_post"],
            }
        )
        if step == steps - 1:
            answer_split = begun["answer"]
        else:
            state_split = begun["result"]
        if boundary:
            first_end_split = state_split
            state_split = begun["begun"]

    sums = [None] * LAYERS
    wires = [None] * LAYERS
    wires_qkv = [None] * LAYERS
    grad = None
    ended = None
    vecs = [None] * LAYERS
    for step in reversed(range(steps)):
        layer = step % LAYERS
        between = step == LAYERS - 1
        option = {}
        if step == steps - 1 or between:
            option = {"cotangent": cotangent, "row_len": row_len}
        if ended is not None:
            last = (step + 1) % LAYERS
            option |= {
                "last": last, "ended": ended, "sums": sums[last], "keep": between,
                "final": step == 0,
            }
        begun = backward_split(
            place_split, vec, backward_weights, following=layer, begun=saved_split[step], **option
        )
        if ended is not None:
            if step == 0:
                wires_qkv[last], vecs[last] = begun["wire"], begun["sum_vec"]
            else:
                sums[last] |= {"sum_qkv": begun["sum_qkv"], "sum_vec": begun["sum_vec"]}
            if between:
                second_split = begun["result"]
        arrived = [swap(begun[f"away_{hop}"], hop) for hop in range(1, 4)]
        five = {
            "post": saved_split[step]["post"], "hidden": begun["hidden"], "low": begun["low"],
            "middle": begun["middle"], "vec": begun["vec_out"],
        }
        source = {}
        if step == steps - 1:
            moved_answer = swap_blocks(answer)
            source["tokens"] = moved_top
        elif between:
            moved_second = swap_blocks(second)
            source["tokens"] = moved_top
        if grad is not None:
            source["grad"] = grad
        source |= {"base": sums[layer], "keep": step > 0, "travel": step in (0, LAYERS)}
        fixed = (layer, place, saved[step], vec, backward_weights, five)
        if step == 0:
            parts = [split(wires[1]), count_digits(token_counts, me, devices)]
            early = sum_cores(jnp.concatenate(parts, axis=1))
            grad, early = tie((grad, early))
            source["grad"] = grad
            half_way = backward_rows(*fixed, ffn_only=True, **source)
            early = sum_chips(early)
            half_way, early = tie((half_way, early))
            early = share_chips(early)
            kept = backward_rows(*fixed, part_done=half_way, **source)
            kept["wire"] = half_way["wire"]
        else:
            kept = backward_rows(*fixed, **source)
        if step > 0:
            grad, arrived = tie((kept["result"], arrived))
        else:
            kept["sum_qkv"], arrived = tie((kept["sum_qkv"], arrived))
        if step == LAYERS:
            second = [kept[f"travel_{hop}"] for hop in range(4)]
        if step == steps - 1:
            arrived, moved_answer = tie((arrived, moved_answer))
        if between:
            arrived, moved_second, kept["wire"] = tie((arrived, moved_second, kept["wire"]))
        if step == 0:
            arrived, early = tie((arrived, early))
            first = [kept[f"travel_{hop}"] for hop in range(4)]
        if sums[layer] is None:
            names = ("sum_qkv", "sum_out", "sum_up", "sum_down", "sum_vec")
            sums[layer] = {name: kept[name] for name in names}
        else:
            sums[layer] = {name: kept[name] for name in ("sum_qkv", "sum_vec")}
            wires[layer] = kept["wire"]
        ended = {name: begun[name] for name in ("middle_out", "query_out", "own_out")}
        ended |= {"arrived": arrived, "pre": saved_split[step]["pre"]}
        ended["stat_pre"] = saved_split[step]["stat_pre"]
    moved_first = swap_blocks(first)
    begun = backward_split(
        place_split, vec, backward_weights, last=0, ended=ended, sums=sums[0], keep=True,
        final=True,
    )
    first_split, wires_qkv[0], vecs[0] = begun["result"], begun["wire"], begun["sum_vec"]

    small = jnp.concatenate([values[0] for values in vecs])
    small = jnp.pad(small, (0, 2 * devices * 128 - small.size)).reshape(devices, 2, 128)
    small = jnp.pad(small, ((0, 0), (0, 14), (0, 0)))
    parts = [split(wires[0])] + [split(wire) for wire in wires_qkv] + [small.astype(BF)]
    part = sum_cores(jnp.concatenate(parts, axis=1))
    early_other = swap(early, 1)
    part, moved_first, early, early_other = tie(
        (sum_chips(part), moved_first, early, early_other)
    )
    late = share_chips(part)
    done = finish_tokens(
        place_split, (early, early_other), moved_answer, answer_split, moved_first, first_split,
        moved_second, second_split, hidden, groups, float(row_len),
    )
    late, done = tie((late, done))
    more = finish_weights(place_split, (late, swap(late, 1)), done, width, hidden)
    return (
        done["block_output"],
        done["input_grad"],
        done["embed_grad"],
        more["qkv"],
        more["out"],
        more["out_b"],
        more["up"],
        more["up_b"],
        more["down"],
        more["down_b"],
        more["gain"],
        more["shift"],
    )


def solution(mesh):
    if mesh.shape["seq"] == 4:
        fine = Mesh(mesh.devices.reshape(-1, 2, 2), ("dp", "y", "core"))
        return jax.shard_map(
            fast_device,
            mesh=fine,
            in_specs=(
                P("dp", SEQ, None),
                P("dp", SEQ, None),
                P("dp", SEQ, None),
                P(),
                P(),
                P(),
                P(),
                P(),
                P(),
                P(),
                P(),
                P(),
                P("dp", None),
                P("dp"),
                P("dp"),
            ),
            out_specs=(
                P("dp", SEQ, None),
                P("dp", SEQ, None),
                P("dp", SEQ, None),
                P(),
                P(),
                P(),
                P(),
                P(),
                P(),
                P(),
                P(),
                P(),
            ),
            check_vma=False,
        )
    return jax.shard_map(
        on_device,
        mesh=mesh,
        in_specs=(
            P("dp", "seq", None),
            P("dp", "seq", None),
            P("dp", "seq", None),
            P(),
            P(),
            P(),
            P(),
            P(),
            P(),
            P(),
            P(),
            P(),
            P("dp", None),
            P("dp"),
            P("dp"),
        ),
        out_specs=(
            P("dp", "seq", None),
            P("dp", "seq", None),
            P("dp", "seq", None),
            P(),
            P(),
            P(),
            P(),
            P(),
            P(),
            P(),
            P(),
            P(),
        ),
        check_vma=False,
    )
```

```python
import types

import jax
import jax.numpy as jnp
from jax import lax
from jax.experimental import pallas as pl
from jax.experimental.pallas import tpu as pltpu
from jax.sharding import Mesh, PartitionSpec as P

H = 4
LAYERS = 2


NORM_EPS = 1e-05
MASKED = -1e30


def layer_norm(values, gain, shift):
    center = values - jnp.mean(values, axis=-1, keepdims=True)
    spread = jnp.mean(center * center, axis=-1, keepdims=True)
    return center * lax.rsqrt(spread + NORM_EPS) * gain + shift


def gelu_exact(values):
    return jax.nn.gelu(values, approximate=False)


def matmul(left_side, right_side):
    return jnp.dot(left_side, right_side, preferred_element_type=jnp.float32)


def left_dot(left_side, right_side):
    return lax.dot_general(
        left_side, right_side, (((0,), (0,)), ((), ())), preferred_element_type=jnp.float32
    )


def right_dot(left_side, right_side):
    return lax.dot_general(
        left_side, right_side, (((1,), (1,)), ((), ())), preferred_element_type=jnp.float32
    )


def split_heads(packed, head_count):
    return packed.reshape(packed.shape[0], head_count, packed.shape[1] // head_count)


def attend_forward(queries, key_vals, allowed, head_count, score_scale):
    model_width = queries.shape[1]
    key_rows = split_heads(key_vals[:, :model_width], head_count)
    value_rows = split_heads(key_vals[:, model_width:], head_count)
    scores = (
        jnp.einsum(
            "qhd,khd->hqk",
            split_heads(queries, head_count),
            key_rows,
            preferred_element_type=jnp.float32,
        )
        * score_scale
    )
    scores = jnp.where(allowed[None], scores, MASKED)
    row_max = jnp.max(scores, axis=-1, keepdims=True)
    shifted_exp = jnp.exp(scores - row_max)
    row_total = jnp.sum(shifted_exp, axis=-1, keepdims=True)
    attn_probs = (shifted_exp / row_total).astype(jnp.bfloat16)
    blended = jnp.einsum("hqk,khd->qhd", attn_probs, value_rows, preferred_element_type=jnp.float32)
    return (blended.reshape(queries.shape[0], model_width), (row_max + jnp.log(row_total))[..., 0])


def attention_core(
    query_part, key_part, value_part, grad_part, allowed_part, logsum_part, head_count, score_scale
):
    scores = (
        jnp.einsum(
            "qhd,khd->hqk",
            split_heads(query_part, head_count),
            split_heads(key_part, head_count),
            preferred_element_type=jnp.float32,
        )
        * score_scale
    )
    scores = jnp.where(allowed_part[None], scores, MASKED)
    attn_probs = jnp.exp(scores - logsum_part[..., None])
    grad_probs = jnp.einsum(
        "qhd,khd->hqk",
        split_heads(grad_part, head_count),
        split_heads(value_part, head_count),
        preferred_element_type=jnp.float32,
    )
    return (attn_probs, grad_probs)


def query_grads(grad_scores, key_part, head_count, score_scale):
    result = (
        jnp.einsum(
            "hqk,khd->qhd",
            grad_scores,
            split_heads(key_part, head_count),
            preferred_element_type=jnp.float32,
        )
        * score_scale
    )
    return result.reshape(result.shape[0], -1)


def keyval_grads(grad_scores, attn_probs, query_part, grad_part, head_count, score_scale):
    grad_keys = (
        jnp.einsum(
            "hqk,qhd->khd",
            grad_scores,
            split_heads(query_part, head_count),
            preferred_element_type=jnp.float32,
        )
        * score_scale
    )
    grad_values = jnp.einsum(
        "hqk,qhd->khd",
        attn_probs.astype(jnp.bfloat16),
        split_heads(grad_part, head_count),
        preferred_element_type=jnp.float32,
    )
    return jnp.concatenate(
        [grad_keys.reshape(grad_keys.shape[0], -1), grad_values.reshape(grad_values.shape[0], -1)],
        axis=-1,
    )


def on_device(
    block_input,
    embedding,
    cotangent,
    qkv_weight,
    out_weight,
    out_bias,
    up_weight,
    up_bias,
    down_weight,
    down_bias,
    norm_gain,
    norm_shift,
    seg_lengths,
    loop_counts,
    token_counts,
):
    row_count, block_len, model_width = block_input.shape
    head_count = H
    score_scale = (model_width // head_count) ** (-0.5)
    row_len = block_len * lax.axis_size("seq")
    flat_rows = row_count * block_len
    offset = lax.axis_index("seq") * block_len
    key_pos = jnp.arange(row_len, dtype=jnp.int32)
    own_pos = offset + jnp.arange(block_len, dtype=jnp.int32)
    seg_ends = jnp.cumsum(seg_lengths, axis=-1)
    seg_all = jnp.sum((seg_ends[:, None, :] <= key_pos[None, :, None]).astype(jnp.int32), axis=-1)
    seg_own = lax.dynamic_slice_in_dim(seg_all, offset, block_len, 1)
    allowed = (seg_own[:, :, None] == seg_all[:, None, :]) & (
        key_pos[None, None, :] <= own_pos[None, :, None]
    )
    current = block_input.astype(jnp.float32)
    inject = embedding.astype(jnp.float32)
    stored = []
    finals = []
    for repeat in range(2):
        current = current + inject
        for layer_index in range(LAYERS):
            forward_normed = layer_norm(
                current, norm_gain[layer_index, 0], norm_shift[layer_index, 0]
            ).astype(jnp.bfloat16)
            forward_packed = matmul(
                forward_normed.reshape(flat_rows, model_width), qkv_weight[layer_index]
            ).astype(jnp.bfloat16)
            forward_packed = forward_packed.reshape(row_count, block_len, 3 * model_width)
            forward_key_vals = lax.all_gather(
                forward_packed[:, :, model_width:], "seq", axis=1, tiled=True
            )

            def forward_row(inputs):
                return attend_forward(inputs[0], inputs[1], inputs[2], head_count, score_scale)

            forward_blended, forward_logsum = lax.map(
                forward_row, (forward_packed[:, :, :model_width], forward_key_vals, allowed)
            )
            forward_blended = forward_blended.astype(jnp.bfloat16)
            branch_out = matmul(
                forward_blended.reshape(flat_rows, model_width), out_weight[layer_index]
            ).reshape(row_count, block_len, model_width)
            forward_middle = current + branch_out + out_bias[layer_index]
            forward_normed_two = layer_norm(
                forward_middle, norm_gain[layer_index, 1], norm_shift[layer_index, 1]
            ).astype(jnp.bfloat16)
            forward_up_proj = (
                matmul(forward_normed_two.reshape(flat_rows, model_width), up_weight[layer_index])
                + up_bias[layer_index]
            )
            forward_active = gelu_exact(forward_up_proj).astype(jnp.bfloat16)
            result = (
                forward_middle
                + matmul(forward_active, down_weight[layer_index]).reshape(
                    row_count, block_len, model_width
                )
                + down_bias[layer_index]
            )
            current, stored_layer = (
                result,
                (
                    current,
                    forward_normed,
                    forward_packed,
                    forward_key_vals,
                    forward_logsum,
                    forward_blended,
                    forward_middle,
                    forward_normed_two,
                    forward_up_proj,
                    forward_active,
                ),
            )
            stored.append(stored_layer)
        finals.append(current)
    two_loops = (loop_counts == 2)[:, None, None]
    block_output = jnp.where(two_loops, finals[1], finals[0]).astype(jnp.bfloat16)
    row_weight = token_counts.astype(jnp.float32) / row_len
    grad_top = cotangent.astype(jnp.float32) * row_weight[:, None, None]
    grad_state = jnp.where(two_loops, grad_top, 0.0)
    layer_sums = [None] * LAYERS
    second_pass = grad_state
    for repeat in (1, 0):
        for layer_index in reversed(range(LAYERS)):
            backward_stored_layer = stored[repeat * LAYERS + layer_index]
            (
                backward_current,
                normed,
                packed,
                key_vals,
                logsum,
                blended,
                middle,
                normed_two,
                up_proj,
                active,
            ) = backward_stored_layer
            grad_flat = grad_state.reshape(flat_rows, model_width)
            grad_low = grad_flat.astype(jnp.bfloat16)
            grad_down = left_dot(active, grad_low)
            grad_down_bias = jnp.sum(grad_flat, axis=0)
            grad_active = right_dot(grad_low, down_weight[layer_index])
            grad_up_proj = jax.vjp(gelu_exact, up_proj)[1](grad_active)[0].astype(jnp.bfloat16)
            grad_up_bias = jnp.sum(grad_up_proj.astype(jnp.float32), axis=0)
            grad_up = left_dot(normed_two.reshape(flat_rows, model_width), grad_up_proj)
            grad_normed_two = right_dot(grad_up_proj, up_weight[layer_index]).reshape(
                row_count, block_len, model_width
            )
            pull_two = jax.vjp(
                layer_norm, middle, norm_gain[layer_index, 1], norm_shift[layer_index, 1]
            )[1]
            grad_middle, gain_two, shift_two = pull_two(grad_normed_two)
            grad_middle = grad_middle + grad_state
            middle_flat = grad_middle.reshape(flat_rows, model_width)
            middle_low = middle_flat.astype(jnp.bfloat16)
            grad_out = left_dot(blended.reshape(flat_rows, model_width), middle_low)
            grad_out_bias = jnp.sum(middle_flat, axis=0)
            grad_blend = (
                right_dot(middle_low, out_weight[layer_index])
                .astype(jnp.bfloat16)
                .reshape(row_count, block_len, model_width)
            )
            queries = packed[:, :, :model_width]

            def full_row(inputs):
                query_part, keyval_part, grad_part, allowed_part, logsum_part = inputs
                attn_probs, grad_probs = attention_core(
                    query_part,
                    keyval_part[:, :model_width],
                    keyval_part[:, model_width:],
                    grad_part,
                    allowed_part,
                    logsum_part,
                    head_count,
                    score_scale,
                )
                row_delta = jnp.sum(attn_probs * grad_probs, axis=-1, keepdims=True)
                grad_scores = (attn_probs * (grad_probs - row_delta)).astype(jnp.bfloat16)
                return (
                    query_grads(grad_scores, keyval_part[:, :model_width], head_count, score_scale),
                    keyval_grads(
                        grad_scores, attn_probs, query_part, grad_part, head_count, score_scale
                    ),
                )

            grad_query, partial_kv = lax.map(
                full_row, (queries, key_vals, grad_blend, allowed, logsum)
            )
            grad_keyval = lax.psum_scatter(
                partial_kv.astype(jnp.bfloat16), "seq", scatter_dimension=1, tiled=True
            )
            grad_packed = jnp.concatenate(
                [grad_query.astype(jnp.bfloat16), grad_keyval], axis=-1
            ).reshape(flat_rows, 3 * model_width)
            grad_qkv = left_dot(normed.reshape(flat_rows, model_width), grad_packed)
            grad_normed = right_dot(grad_packed, qkv_weight[layer_index]).reshape(
                row_count, block_len, model_width
            )
            pull_one = jax.vjp(
                layer_norm, backward_current, norm_gain[layer_index, 0], norm_shift[layer_index, 0]
            )[1]
            grad_current, gain_one, shift_one = pull_one(grad_normed)
            grad_current = grad_current + grad_middle
            grad_state = grad_current
            grad_set = (
                grad_qkv,
                grad_out,
                grad_out_bias,
                grad_up,
                grad_up_bias,
                grad_down,
                grad_down_bias,
                jnp.stack([gain_one, gain_two]),
                jnp.stack([shift_one, shift_two]),
            )
            if repeat == 1:
                layer_sums[layer_index] = grad_set
            else:
                layer_sums[layer_index] = jax.tree.map(jnp.add, layer_sums[layer_index], grad_set)
        if repeat == 1:
            second_pass = grad_state
            grad_state = jnp.where(two_loops, grad_state, grad_top)
    grad_embed = grad_state + second_pass
    stacked = jax.tree.map(lambda *members: jnp.stack(members), *layer_sums)
    (
        sum_qkv,
        sum_out,
        sum_out_bias,
        sum_up,
        sum_up_bias,
        sum_down,
        sum_down_bias,
        sum_gain,
        sum_shift,
    ) = stacked
    total = lax.psum(jnp.sum(token_counts), "dp").astype(jnp.float32)
    summed = lax.psum(
        (
            sum_qkv,
            sum_out,
            sum_out_bias,
            sum_up,
            sum_up_bias,
            sum_down,
            sum_down_bias,
            sum_gain,
            sum_shift,
        ),
        ("dp", "seq"),
    )
    input_scale = row_count * lax.axis_size("dp") * row_len / total
    weight_scale = row_len / total
    return (
        block_output,
        grad_state * input_scale,
        grad_embed * input_scale,
        summed[0] * weight_scale,
        summed[1] * weight_scale,
        summed[2] * weight_scale,
        summed[3] * weight_scale,
        summed[4] * weight_scale,
        summed[5] * weight_scale,
        summed[6] * weight_scale,
        summed[7] * weight_scale,
        summed[8] * weight_scale,
    )


BF = jnp.bfloat16
F32 = jnp.float32
ERF_TERMS = (7.97869712e-01, 3.63922863e-02, -8.78266373e-05, -3.66934271e-05, 1.42500458e-06)
DENSITY_RATE = -0.7213475204444817
DENSITY_BASE = -1.3257480647361593
VMEM_LIMIT = 24 * 1024 * 1024
ONES_ROWS = 16


def dot_nn(left_side, right_side):
    return jnp.dot(left_side, right_side, preferred_element_type=F32)


def dot_nt(left_side, right_side):
    return lax.dot_general(
        left_side, right_side, (((1,), (1,)), ((), ())), preferred_element_type=F32
    )


def gelu_and_slope(z):
    square = z * z
    series = ERF_TERMS[-1] * square + ERF_TERMS[-2]
    for term in ERF_TERMS[-3::-1]:
        series = series * square + term
    cdf = 0.5 + 0.5 * jnp.tanh(z * series)
    density = jnp.exp2(square * DENSITY_RATE + DENSITY_BASE)
    return z * cdf, cdf + z * density


def norm_forward(values, gain, shift):
    center = values - jnp.mean(values, axis=0, keepdims=True)
    spread = jnp.mean(center * center, axis=0, keepdims=True)
    inverse = lax.rsqrt(spread + NORM_EPS)
    unit = center * inverse
    return unit, inverse, (unit * gain + shift).astype(BF)


def norm_backward(grad, unit, inverse, gain):
    scaled = grad * gain
    first = jnp.mean(scaled, axis=0, keepdims=True)
    second = jnp.mean(scaled * unit, axis=0, keepdims=True)
    return inverse * (scaled - first - unit * second)


def columns(vec):
    turned = vec[0].T

    def column(first, last):
        return jnp.concatenate(
            [turned[:, k : k + 1] for k in range(first // 128, last // 128)], axis=0
        )

    return column


def project_qkv(state, qkv_t, vec, pre, kv, stat, scale):
    width = state.shape[0]
    column = columns(vec)
    gain = column(2 * width, 3 * width)
    shift = column(3 * width, 4 * width)
    unit, inverse, normed = norm_forward(state, gain, shift)
    pre[0:width, :] = normed
    pre[2 * width : 3 * width, :] = unit.astype(BF)
    pre[width : 2 * width, :] = (dot_nn(qkv_t[0, 0:width, :], normed) * scale).astype(BF)
    kv[0:width, :] = dot_nn(qkv_t[0, width : 2 * width, :], normed).astype(BF)
    kv[width : 2 * width, :] = dot_nn(qkv_t[0, 2 * width : 3 * width, :], normed).astype(BF)
    stat[0:1, :] = inverse


def pad_head(block, odd):
    blank = jnp.zeros_like(block)
    return jnp.concatenate([blank, block] if odd else [block, blank], axis=0)


def tile_bias(first_key, start, causal, shape):
    key_at = lax.broadcasted_iota(jnp.int32, shape, 0)
    keep = key_at + first_key >= start
    if causal:
        keep = keep & (key_at <= lax.broadcasted_iota(jnp.int32, shape, 1))
    return jnp.where(keep, 0.0, MASKED)


def over_tiles(chunk, count, begin, half_tile, full_tile, carry):
    half = count // 2
    first_half = begin // half
    odd = jnp.where(first_half < 2 * chunk, first_half % 2, 0)
    carry = lax.fori_loop(0, odd, lambda _, c: half_tile(first_half // 2, c), carry)
    return lax.fori_loop((first_half + 1) // 2, chunk, full_tile, carry)


def attend_chunk(queries, keys, values_t, chunk, begin, start, bias, total, stat, blended):
    width, tokens = queries.shape
    head = width // H
    pair = 2 * head
    half = tokens // 2
    head_rows = [slice(h * head, (h + 1) * head) for h in range(H)]

    def scores(j, h, span):
        lanes = pl.ds((h // 2) * pair, pair)
        return dot_nn(keys[j, span, lanes], pad_head(queries[head_rows[h], :], h % 2))

    everything = slice(0, tokens)
    bias[...] = tile_bias(chunk * tokens, start, True, (tokens, tokens))
    parts = [scores(chunk, h, everything) for h in range(H)]
    uppers = [part[:half, :] + bias[:half, :] for part in parts]
    lowers = [part[half:, half:] + bias[half:, half:] for part in parts]
    tops, sums, weights = [], [], []
    for upper, lower in zip(uppers, lowers):
        top = jnp.max(upper, axis=0, keepdims=True)
        right = jnp.maximum(top[:, half:], jnp.max(lower, axis=0, keepdims=True))
        top = jnp.concatenate([top[:, :half], right], axis=1)
        upper = jnp.exp(upper - top)
        lower = jnp.exp(lower - right)
        added = jnp.sum(upper, axis=0, keepdims=True)
        right = added[:, half:] + jnp.sum(lower, axis=0, keepdims=True)
        tops.append(top)
        sums.append(jnp.concatenate([added[:, :half], right], axis=1))
        lower = lower.astype(BF)
        lower = jnp.concatenate([jnp.zeros_like(lower), lower], axis=1)
        weights.append(jnp.concatenate([upper.astype(BF), lower], axis=0))
    for rows, weight in zip(head_rows, weights):
        total[rows, :] = dot_nn(values_t[chunk, rows, :], weight)

    def step(j, span, size, carry):
        tops, sums = carry
        bias[:size, :] = tile_bias(j * tokens + span.start, start, False, (size, tokens))
        parts = [scores(j, h, span) + bias[:size, :] for h in range(H)]
        new_tops = [
            jnp.maximum(old, jnp.max(part, axis=0, keepdims=True))
            for old, part in zip(tops, parts)
        ]
        weights = [jnp.exp(part - top) for part, top in zip(parts, new_tops)]
        new_sums = [jnp.sum(weight, axis=0, keepdims=True) for weight in weights]
        terms = [
            dot_nn(values_t[j, rows, span], weight.astype(BF))
            for rows, weight in zip(head_rows, weights)
        ]
        fades = [jnp.exp(old - new) for old, new in zip(tops, new_tops)]
        for rows, term, fade in zip(head_rows, terms, fades):
            total[rows, :] = total[rows, :] * fade + term
        sums = [old * fade + new for old, fade, new in zip(sums, fades, new_sums)]
        return tuple(new_tops), tuple(sums)

    tops, sums = over_tiles(
        chunk, tokens, begin,
        lambda j, carry: step(j, slice(half, tokens), half, carry),
        lambda j, carry: step(j, everything, tokens, carry),
        (tuple(tops), tuple(sums)),
    )
    for h, rows in enumerate(head_rows):
        blended[rows, :] = (total[rows, :] / sums[h]).astype(BF)
        stat[h : h + 1, :] = tops[h] + jnp.log(sums[h])


def finish_layer(state, out_t, up_t, down_t, vec, post, stat):
    width, tokens = state.shape
    hidden = up_t.shape[1]
    column = columns(vec)
    middle = state + dot_nn(out_t[0], post[0:width, :]) + column(0, width)
    gain = column(4 * width, 5 * width)
    shift = column(5 * width, 6 * width)
    unit, inverse, normed = norm_forward(middle, gain, shift)
    post[width : 2 * width, :] = normed
    post[2 * width : 3 * width, :] = unit.astype(BF)
    stat[H : H + 1, :] = inverse
    z = dot_nn(up_t[0], normed) + column(6 * width, 6 * width + hidden)
    active, slope = gelu_and_slope(z)
    post[3 * width : 3 * width + hidden, :] = active.astype(BF)
    post[3 * width + hidden :, :] = slope.astype(BF)
    return (
        middle
        + dot_nn(down_t[0], post[3 * width : 3 * width + hidden, :])
        + column(width, 2 * width)
    )


def launch(
    name, body, place, grid, ins, outs, scratch=(), flops=0, aliases=(), near=(), free=(),
    on_split=True,
):
    scratch = dict(scratch)
    names = [*ins, *outs, *scratch]

    def kernel(here, loops, counts, lengths, *refs):
        me, split = here[0], here[1]
        row = split if on_split else row_of_slot(me, split, loops.shape[0])
        facts = types.SimpleNamespace(
            me=me, split=split, slot=here[2], two=loops[row] == 2, count=counts[row], counts=counts,
            lengths=[lengths[row, k] for k in range(lengths.shape[1])],
        )
        body(facts, types.SimpleNamespace(**dict(zip(names, refs))))

    space = lambda key: pltpu.VMEM if key in near else pltpu.HBM
    results = pl.pallas_call(
        kernel,
        grid_spec=pltpu.PrefetchScalarGridSpec(
            num_scalar_prefetch=len(place),
            grid=(grid,),
            in_specs=[spec for _, spec in ins.values()],
            out_specs=[spec for _, spec in outs.values()],
            scratch_shapes=list(scratch.values()),
        ),
        out_shape=[
            shape if key in free else space(key)(shape.shape, shape.dtype)
            for key, (shape, _) in outs.items()
        ],
        input_output_aliases={
            len(place) + list(ins).index(source): list(outs).index(target) for source, target in aliases
        },
        compiler_params=pltpu.CompilerParams(vmem_limit_bytes=VMEM_LIMIT),
        cost_estimate=pl.CostEstimate(flops=flops, bytes_accessed=1, transcendentals=0),
        name=name,
    )(
        *place,
        *[
            array if key in free else pltpu.with_memory_space_constraint(array, space(key))
            for key, (array, _) in ins.items()
        ],
    )
    return dict(zip(outs, results))


def whole(array):
    return array, pl.BlockSpec(array.shape, lambda i, *_: (0,) * len(array.shape))


def of_layer(array, layer):
    return array, pl.BlockSpec((1,) + array.shape[1:], lambda i, *_: (layer, 0, 0))


def each(array):
    return array, pl.BlockSpec((1,) + array.shape[1:], lambda i, *_: (i, 0, 0))


def each_back(array):
    count = array.shape[0]
    return array, pl.BlockSpec(
        (1,) + array.shape[1:], lambda i, *_: (count - 1 - i, 0, 0)
    )


def shaped(dims, dtype):
    return jax.ShapeDtypeStruct(dims, dtype)


def segment_starts(place, first, count):
    position = lax.broadcasted_iota(jnp.int32, (1, count), 1) + first
    starts = jnp.zeros((1, count), jnp.int32)
    end = jnp.int32(0)
    begin = jnp.int32(0)
    for length in place.lengths:
        end = end + length
        starts = jnp.where(position >= end, end, starts)
        begin = jnp.where(first >= end, end, begin)
    return starts, begin


def gather_tokens(env, name, me):
    for hop in range(4):
        env.spread[me ^ hop] = getattr(env, f"{name}_{hop}")[...]


def deal_tokens(env, name, value, chunk, me):
    for hop in range(4):

        @pl.when(chunk == (me ^ hop))
        def _(hop=hop):
            getattr(env, f"{name}_{hop}")[...] = value


def token_ins(name, blocks):
    return {f"{name}_{hop}": whole(block) for hop, block in enumerate(blocks)}


def token_outs(name, tokens, width):
    return {f"{name}_{hop}": whole(shaped((tokens, width), BF)) for hop in range(4)}


def as_tokens(values):
    return values.astype(BF).T


def as_features(tokens):
    return tokens.T.astype(F32)


def forward_rows(layer, place, vec, weights, state=None, tokens=None, first_end=None):
    chunks = 4
    count = state.shape[2] if tokens is None else tokens[0].shape[0]
    qkv_t, out_t, up_t, down_t = weights
    width, hidden = out_t.shape[2], up_t.shape[1]
    post_rows = 3 * width + 2 * hidden

    def body(place, env):
        chunk = pl.program_id(0)
        me = place.me
        current = env.state.at[0] if state is not None else None
        if tokens is not None:

            @pl.when(chunk == 0)
            def _():
                gather_tokens(env, "tokens", me)

            added = as_features(env.spread[chunk])
            env.current[...] = added if state is None else added + env.state[0]
            current = env.current
        project_qkv(
            current[...], env.qkv_t, env.vec, env.pre.at[0], env.kv.at[0], env.stat_pre.at[0],
            (width // H) ** -0.5,
        )
        env.keys[chunk] = env.kv[0, 0:width, :].T
        env.values_t[chunk] = env.kv[0, width : 2 * width, :]
        start, begin = segment_starts(place, chunk * count, count)
        attend_chunk(
            env.pre.at[0, width : 2 * width, :], env.keys, env.values_t, chunk, begin, start, env.bias, env.total, env.stat_post.at[0],
            env.post.at[0, 0:width, :],
        )
        result = finish_layer(
            current[...], env.out_t, env.up_t, env.down_t, env.vec, env.post.at[0],
            env.stat_post.at[0],
        )
        if first_end is None:
            env.result[0] = result
        else:
            answer = jnp.where(place.two, result, env.first_end[0])
            deal_tokens(env, "answer", as_tokens(answer), chunk, me)

    ins = {"vec": of_layer(vec, layer)}
    for name, weight in zip(("qkv_t", "out_t", "up_t", "down_t"), weights):
        ins[name] = of_layer(weight, layer)
    scratch = {
        "keys": pltpu.VMEM((chunks, count, width), BF),
        "values_t": pltpu.VMEM((chunks, width, count), BF),
        "bias": pltpu.VMEM((count, count), F32),
        "total": pltpu.VMEM((width, count), F32),
    }
    if state is not None:
        ins["state"] = each(state)
    if tokens is not None:
        ins |= token_ins("tokens", tokens)
        scratch["spread"] = pltpu.VMEM((chunks, count, width), BF)
        scratch["current"] = pltpu.VMEM((width, count), F32)
    outs = {}
    if first_end is None:
        outs["result"] = each(shaped((chunks, width, count), F32))
    else:
        ins["first_end"] = each(first_end)
        outs |= token_outs("answer", count, width)
    outs["pre"] = each(shaped((chunks, 3 * width, count), BF))
    outs["kv"] = each(shaped((chunks, 2 * width, count), BF))
    outs["post"] = each(shaped((chunks, post_rows, count), BF))
    outs["stat_pre"] = each(shaped((chunks, 8, count), F32))
    outs["stat_post"] = each(shaped((chunks, 8, count), F32))
    flops = chunks * count * 6 * (4 * width * width + 2 * width * hidden)
    return launch(
        "forward_rows", body, place, chunks, ins, outs, scratch, flops,
        on_split=False,
        near=["state", "result", "vec", "qkv_t", "out_t", "up_t", "down_t"]
        + [f"tokens_{hop}" for hop in range(4) if state is None],
    )


def split_row(array):
    return array, pl.BlockSpec((1,) + array.shape[1:], lambda i, here, *_: (here[1], 0, 0))


def row_of_slot(slot, split, rows):
    return jnp.where(slot == split, rows - 1, slot)


def forward_split(
    place, vec, weights, last=None, following=None, state=None, prev=None, pre=None,
    block_input=None, embedding=None, first_end=None,
):
    qkv_t, out_t, up_t, down_t = weights
    width, hidden = out_t.shape[2], up_t.shape[1]
    count = embedding.shape[1] if state is None else state.shape[1]

    def body(place, env):
        me = place.me
        if last is not None:
            for hop in range(4):
                arrived = getattr(env, f"kv_{hop}")
                env.keys[me ^ hop] = arrived[0:width, :].T
                env.values_t[me ^ hop] = arrived[width : 2 * width, :]
            start, begin = segment_starts(place, me * count, count)
            attend_chunk(
                env.pre_in.at[width : 2 * width, :], env.keys, env.values_t, me, begin, start,
                env.bias, env.total, env.stat_post, env.post.at[0:width, :],
            )
            current = finish_layer(
                env.state[...], env.out_t, env.up_t, env.down_t, env.vec, env.post, env.stat_post
            )
            if first_end is not None:
                answer = jnp.where(place.two, current, env.first_end[...])
                env.answer[...] = as_tokens(answer)
            else:
                env.result[...] = current
        if following is not None:
            if embedding is not None:
                added = as_features(env.embedding[0])
                if last is None:
                    current = as_features(env.block_input[0]) + added
                else:
                    current = env.result[...] + added
                env.begun[...] = current
            project_qkv(
                current, env.qkv_t, env.vec_next, env.pre, env.kv, env.stat_pre,
                (width // H) ** -0.5,
            )

    ins, outs, scratch = {}, {}, {}
    if last is not None:
        ins |= {f"kv_{hop}": whole(block) for hop, block in enumerate(prev)}
        ins |= {"state": whole(state), "pre_in": whole(pre)}
        ins["vec"] = of_layer(vec, last)
        for name, weight in zip(("out_t", "up_t", "down_t"), weights[1:]):
            ins[name] = of_layer(weight, last)
        if first_end is not None:
            ins["first_end"] = whole(first_end)
            outs["answer"] = whole(shaped((count, width), BF))
        else:
            outs["result"] = whole(shaped((width, count), F32))
        outs["post"] = whole(shaped((3 * width + 2 * hidden, count), BF))
        outs["stat_post"] = whole(shaped((8, count), F32))
        scratch = {
            "keys": pltpu.VMEM((4, count, width), BF),
            "values_t": pltpu.VMEM((4, width, count), BF),
            "bias": pltpu.VMEM((count, count), F32),
            "total": pltpu.VMEM((width, count), F32),
        }
    if following is not None:
        ins["vec_next"] = of_layer(vec, following)
        ins["qkv_t"] = of_layer(qkv_t, following)
        if embedding is not None:
            ins["embedding"] = split_row(embedding)
            outs["begun"] = whole(shaped((width, count), F32))
        if block_input is not None:
            ins["block_input"] = split_row(block_input)
        outs["pre"] = whole(shaped((3 * width, count), BF))
        outs["kv"] = whole(shaped((2 * width, count), BF))
        outs["stat_pre"] = whole(shaped((8, count), F32))
    flops = 0 if last is None else count * 6 * (4 * width * width + 2 * width * hidden)
    return launch(
        "forward_split", body, place, 1, ins, outs, scratch, flops,
        near=["state", "result", "begun", "pre", "pre_in", "kv", "vec", "vec_next", "qkv_t", "out_t", "up_t", "down_t"]
        + [f"kv_{hop}" for hop in range(4)],
    )


def backward_ffn(grad, post, stat, wout, wup, wdown, vec, hidden_grad):
    width, tokens = grad.shape
    hidden = wup.shape[2]
    low_grad = grad.astype(BF)
    hidden_grad[...] = (
        dot_nn(wdown[0], low_grad) * post[3 * width + hidden :, :].astype(F32)
    ).astype(BF)
    normed_grad = dot_nn(wup[0], hidden_grad[...])
    unit = post[2 * width : 3 * width, :].astype(F32)
    gain = columns(vec)(4 * width, 5 * width)
    middle = grad + norm_backward(normed_grad, unit, stat[H : H + 1, :], gain)
    low_middle = middle.astype(BF)
    blend_grad = dot_nn(wout[0], low_middle).astype(BF)
    return low_grad, normed_grad, unit, middle, low_middle, blend_grad


def token_sum(rows):
    return dot_nt(jnp.ones((ONES_ROWS, rows.shape[1]), BF), rows.astype(BF))


def attend_backward(
    queries, blend_grad, blended, stat, keys, values, keys_t, chunk, begin, start,
    bias, query_grad, kv_grad,
):
    width, tokens = queries.shape
    head = width // H
    pair = 2 * head
    head_rows = [slice(h * head, (h + 1) * head) for h in range(H)]
    deltas = [
        jnp.sum(
            blend_grad[rows, :].astype(F32) * blended[rows, :].astype(F32), axis=0, keepdims=True
        )
        for rows in head_rows
    ]

    half = tokens // 2
    everything = slice(0, tokens)

    def products(j, span):
        parts, prob_grads = [], []
        for h, rows in enumerate(head_rows):
            lanes = pl.ds((h // 2) * pair, pair)
            parts.append(dot_nn(keys[j, span, lanes], pad_head(queries[rows, :], h % 2)))
            prob_grads.append(
                dot_nn(values[j, span, lanes], pad_head(blend_grad[rows, :], h % 2))
            )
        return parts, prob_grads

    def collect(j, span, probs, score_grads, first):
        for rows, prob, score_grad in zip(head_rows, probs, score_grads):
            value_rows = slice(width + rows.start, width + rows.stop)
            kv_grad[j, value_rows, span] += dot_nt(blend_grad[rows, :], prob)
            kv_grad[j, rows, span] += dot_nt(queries[rows, :], score_grad)
            term = dot_nn(keys_t(j, rows, span), score_grad)
            if first:
                query_grad[rows, :] = term
            else:
                query_grad[rows, :] += term

    def weigh(part, prob_grad, mask, logsum, delta):
        prob = jnp.exp(part + mask - logsum)
        return prob.astype(BF), (prob * (prob_grad - delta)).astype(BF)

    bias[...] = tile_bias(chunk * tokens, start, True, (tokens, tokens))
    probs, score_grads = [], []
    for h, (part, prob_grad) in enumerate(zip(*products(chunk, everything))):
        logsum, delta = stat[h : h + 1, :], deltas[h]
        upper = weigh(part[:half, :], prob_grad[:half, :], bias[:half, :], logsum, delta)
        lower = weigh(
            part[half:, half:], prob_grad[half:, half:], bias[half:, half:], logsum[:, half:],
            delta[:, half:],
        )
        for kept, above, below in zip((probs, score_grads), upper, lower):
            below = jnp.concatenate([jnp.zeros_like(below), below], axis=1)
            kept.append(jnp.concatenate([above, below], axis=0))
    collect(chunk, everything, probs, score_grads, True)

    def step(j, span, size, carry):
        bias[:size, :] = tile_bias(j * tokens + span.start, start, False, (size, tokens))
        pairs = [
            weigh(part, prob_grad, bias[:size, :], stat[h : h + 1, :], deltas[h])
            for h, (part, prob_grad) in enumerate(zip(*products(j, span)))
        ]
        collect(j, span, [p for p, _ in pairs], [d for _, d in pairs], False)
        return carry

    over_tiles(
        chunk, tokens, begin,
        lambda j, carry: step(j, slice(half, tokens), half, carry),
        lambda j, carry: step(j, everything, tokens, carry),
        0,
    )


def add_vec(sum_vec, width, low_grad, normed_grad, unit, low_middle, dz):
    sum_vec[:, 0:width] += token_sum(low_middle)
    sum_vec[:, width : 2 * width] += token_sum(low_grad)
    sum_vec[:, 4 * width : 5 * width] += token_sum(normed_grad * unit)
    sum_vec[:, 5 * width : 6 * width] += token_sum(normed_grad)
    sum_vec[:, 6 * width :] += token_sum(dz)


def finish_backward(middle, pre, stat, packed, wqkv, vec, sum_qkv, sum_vec):
    width, tokens = middle.shape
    sum_qkv[...] += dot_nt(pre[0:width, :], packed[...])
    normed_grad = dot_nn(wqkv[0], packed[...])
    unit = pre[2 * width : 3 * width, :].astype(F32)
    gain = columns(vec)(2 * width, 3 * width)
    sum_vec[:, 2 * width : 3 * width] += token_sum(normed_grad * unit)
    sum_vec[:, 3 * width : 4 * width] += token_sum(normed_grad)
    return middle + norm_backward(normed_grad, unit, stat[0:1, :], gain)


def pack_lanes(wire, blocks):
    at = 0
    for ref in blocks:
        rows = ref.shape[0]
        for first in range(0, ref.shape[1], 128):
            wire[at : at + rows, :] = ref[:, first : first + 128].astype(BF)
            at += rows


def put_pieces(keep, give, source, first, height, core):
    half = keep.shape[0]
    for ref, side in ((keep, core), (give, 1 - core)):
        for p in range(half):
            at = pl.multiple_of((side * half + p) * height, 16)
            ref[p, first : first + height, :] = source[pl.ds(at, height), :]


def count_digits(place, groups):
    tally = place.counts[0]
    for k in range(1, place.counts.shape[0]):
        tally = tally + place.counts[k]
    lane = lax.broadcasted_iota(jnp.int32, (16, 128), 1)
    row = lax.broadcasted_iota(jnp.int32, (16, 128), 0)
    digit = jnp.where(lane % 2 == 0, tally // 256, tally % 256)
    keep = (lane // 2 == place.slot) & (row == 0) & (place.me == 0)
    return jnp.where(keep, digit, 0).astype(F32).astype(BF)


def backward_rows(
    layer, place, saved, vec, weights, five, base=None, grad=None, tokens=None,
    keep=True, travel=False, part_done=None, ffn_only=False, half=0, digits=False,
):
    chunks, _, count = saved["kv"].shape
    wqkv, wout, wup, wdown = weights
    width, hidden = wup.shape[1:]
    row_len = chunks * count
    first = base is None
    part = hidden // chunks
    vec_len = 6 * width + hidden
    with_ffn, with_attention = part_done is None, not ffn_only

    def body(place, env):
        order = pl.program_id(0)
        chunk = chunks - 1 - order
        me = place.me

        @pl.when(order == 0)
        def _():
            if tokens is not None:
                gather_tokens(env, "tokens", me)
            if with_ffn:
                env.sum_up[...] = jnp.zeros_like(env.sum_up)
                env.sum_down[...] = jnp.zeros_like(env.sum_down)
                env.sum_out[...] = dot_nt(env.blend_five[...], env.middle_five[...])
                env.sum_vec[...] = env.vec_five[...]
                if not first:
                    env.sum_vec[...] += env.base_vec[...]
            else:
                env.sum_vec[...] = env.vec_done[...]
            if with_attention:
                env.sum_qkv[...] = jnp.zeros_like(env.sum_qkv)
                env.kv_grad[...] = jnp.zeros_like(env.kv_grad)
                for j in range(chunks):
                    env.keys[j] = env.kv[j, 0:width, :].T
                    env.values[j] = env.kv[j, width : 2 * width, :].T

        def add_base(ref, old):
            rows = old.shape[0]
            ref[pl.ds(pl.multiple_of(order * rows, rows), rows), :] += old[...]

        if with_ffn:
            spread = pl.ds(pl.multiple_of(order * part, part), part)
            env.sum_down[spread, :] += dot_nt(env.active_five[...], env.low_five[...])
            env.sum_up[:, spread] += dot_nt(env.normed_five[...], env.hidden_five[...])
            if not first:
                env.sum_down[spread, :] += env.base_down[...]
                env.sum_up[:, spread] += env.base_up[...]
                add_base(env.sum_out, env.base_out)
            current = env.grad.at[0] if grad is not None else None
            if tokens is not None:
                top = as_features(env.spread[chunk]) * (place.count.astype(F32) * (1.0 / row_len))
                two = place.two
                env.current[...] = (
                    jnp.where(two, top, 0.0)
                    if grad is None
                    else jnp.where(two, env.grad[0], top)
                )
                current = env.current
            post = env.post.at[0]
            low_grad, normed_grad, unit, middle, low_middle, blend_grad = backward_ffn(
                current[...], post, env.stat_post.at[0], env.wout, env.wup, env.wdown, env.vec,
                env.hidden_grad,
            )
            env.sum_down[...] += dot_nt(post[3 * width : 3 * width + hidden, :], low_grad)
            env.sum_up[...] += dot_nt(post[width : 2 * width, :], env.hidden_grad[...])
            env.sum_out[...] += dot_nt(post[0:width, :], low_middle)
            add_vec(
                env.sum_vec, width, low_grad, normed_grad, unit, low_middle, env.hidden_grad[...]
            )
            blend_ref = env.blend_grad if with_attention else env.blend_out.at[0]
            blend_ref[...] = blend_grad
            if not first:

                @pl.when(order == chunks - 1)
                def _():
                    pack_lanes(env.wire, (env.sum_out, env.sum_up, env.sum_down))
                    height = env.wire.shape[0] // (2 * half)
                    put_pieces(env.keep, env.give, env.wire, 0, height, me % 2)
                    if digits:
                        blank = jnp.zeros((16, 128), BF)
                        for p in range(half):
                            env.keep[p, height:, :] = count_digits(place, half) if p == 0 else blank
                            env.give[p, height:, :] = blank

            if not with_attention:
                env.middle_out[0] = middle
                return
            blended = post.at[0:width, :]
        else:
            middle, blend_ref, blended = env.middle_in[0], env.blend_in.at[0], env.blended.at[0]
        if not first:
            add_base(env.sum_qkv, env.base_qkv)
        start, begin = segment_starts(place, chunk * count, count)
        attend_backward(
            env.pre.at[0, width : 2 * width, :], blend_ref, blended,
            env.stat_post.at[0], env.keys, env.values, lambda j, rows, span: env.kv[j, rows, span],
            chunk, begin, start, env.bias, env.query_grad, env.kv_grad,
        )
        env.packed[0:width, :] = (env.query_grad[...] * (width // H) ** -0.5).astype(BF)
        env.packed[width : 3 * width, :] = env.kv_grad[chunk].astype(BF)
        result = finish_backward(
            middle, env.pre.at[0], env.stat_pre.at[0], env.packed, env.wqkv, env.vec,
            env.sum_qkv, env.sum_vec,
        )
        if keep:
            env.result[0] = result
        if travel:
            deal_tokens(env, "travel", as_tokens(result), chunk, me)

    ins = {"vec": of_layer(vec, layer), "stat_post": each_back(saved["stat_post"])}
    outs, scratch = {}, {}
    cut = lambda array, shape, at: (array, pl.BlockSpec(shape, lambda i, *_: at(i)))
    sums = {"sum_vec": (ONES_ROWS, vec_len)}
    if with_ffn:
        ins["post"] = each_back(saved["post"])
        for name, weight in zip(("wout", "wup", "wdown"), weights[1:]):
            ins[name] = of_layer(weight, layer)
        if grad is not None:
            ins["grad"] = each_back(grad)
        if tokens is not None:
            ins |= token_ins("tokens", tokens)
            scratch["spread"] = pltpu.VMEM((chunks, count, width), BF)
            scratch["current"] = pltpu.VMEM((width, count), F32)
        post_five = five["post"]
        ins["blend_five"] = cut(post_five, (width, count), lambda i: (0, 0))
        ins["normed_five"] = cut(post_five, (width, count), lambda i: (1, 0))
        ins["active_five"] = cut(post_five, (part, count), lambda i: (3 * width // part + i, 0))
        ins["hidden_five"] = cut(five["hidden"], (part, count), lambda i: (i, 0))
        for name in ("low", "middle", "vec"):
            ins[name + "_five"] = whole(five[name])
        sums |= {"sum_out": (width, width), "sum_up": (width, hidden), "sum_down": (hidden, width)}
        scratch["hidden_grad"] = pltpu.VMEM((hidden, count), BF)
        if not first:
            ins["base_out"] = cut(base["sum_out"], (width // chunks, width), lambda i: (i, 0))
            ins["base_up"] = cut(base["sum_up"], (width, part), lambda i: (0, i))
            ins["base_down"] = cut(base["sum_down"], (part, width), lambda i: (i, 0))
            ins["base_vec"] = whole(base["sum_vec"])
            wire_rows = (width * width + 2 * width * hidden) // 128
            scratch["wire"] = pltpu.VMEM((wire_rows, 128), BF)
            height = wire_rows // (2 * half) + (16 if digits else 0)
            outs["keep"] = whole(shaped((half, height, 128), BF))
            outs["give"] = whole(shaped((half, height, 128), BF))
        if not with_attention:
            outs["blend_out"] = each_back(shaped((chunks, width, count), BF))
            outs["middle_out"] = each_back(shaped((chunks, width, count), F32))
    else:
        ins["vec_done"] = whole(part_done["sum_vec"])
        ins["middle_in"] = each_back(part_done["middle_out"])
        ins["blend_in"] = each_back(part_done["blend_out"])
        ins["blended"] = (
            saved["post"],
            pl.BlockSpec((1, width, count), lambda i, *_: (chunks - 1 - i, 0, 0)),
        )
    if with_attention:
        ins["kv"] = whole(saved["kv"])
        ins["pre"] = each_back(saved["pre"])
        ins["stat_pre"] = each_back(saved["stat_pre"])
        ins["wqkv"] = of_layer(wqkv, layer)
        sums["sum_qkv"] = (width, 3 * width)
        if not first:
            ins["base_qkv"] = cut(base["sum_qkv"], (width // chunks, 3 * width), lambda i: (i, 0))
        if keep:
            outs["result"] = each_back(shaped((chunks, width, count), F32))
        if travel:
            outs |= token_outs("travel", count, width)
        scratch |= {
            "keys": pltpu.VMEM((chunks, count, width), BF),
            "values": pltpu.VMEM((chunks, count, width), BF),
            "bias": pltpu.VMEM((count, count), F32),
            "query_grad": pltpu.VMEM((width, count), F32),
            "kv_grad": pltpu.VMEM((chunks, 2 * width, count), F32),
            "blend_grad": pltpu.VMEM((width, count), BF),
            "packed": pltpu.VMEM((3 * width, count), BF),
        }
    for name, dims in sums.items():
        if first or name in ("sum_qkv", "sum_vec"):
            outs[name] = whole(shaped(dims, F32))
        else:
            scratch[name] = pltpu.VMEM(dims, F32)
    flops = chunks * count * 12 * (4 * width * width + 2 * width * hidden)
    return launch(
        "backward_rows", body, place, chunks, ins, outs, scratch, flops, on_split=False,
        near=["grad", "result", "hidden_five", "low_five", "middle_five", "vec_five"],
    )


def backward_split(
    place, vec, weights, last=None, following=None, ended=None, sums=None, begun=None,
    cotangent=None, final=False, keep=False, row_len=None, others=None, half=0,
):
    wqkv, wout, wup, wdown = weights
    width, hidden = wup.shape[1:]
    vec_len = 6 * width + hidden
    count = (ended or begun)["stat_pre"].shape[1]

    def body(place, env):
        me = place.me
        if last is not None:
            sum_qkv = env.total_qkv if final else env.sum_qkv
            env.packed[0:width, :] = env.query_in[...]
            kv_total = env.own_in[...]
            for hop in range(1, 4):
                kv_total = kv_total + getattr(env, f"in_{hop}")[...].astype(F32)
            env.packed[width : 3 * width, :] = kv_total.astype(BF)
            sum_qkv[...] = env.old_qkv[...]
            env.sum_vec[...] = env.old_vec[...]
            current = finish_backward(
                env.middle_in[...], env.pre_last, env.stat_last, env.packed, env.wqkv,
                env.vec_last, sum_qkv, env.sum_vec,
            )
            if keep:
                env.result[...] = current.T
            if final:
                pack_lanes(env.wire, (sum_qkv,))
            if others is not None:
                core = me % 2
                height = env.wire.shape[0] // (2 * half)
                put_pieces(env.keep, env.give, env.wire, 0, height, core)
                put_pieces(env.keep, env.give, env.wire_other, height, height, core)
                env.small[...] = jnp.zeros_like(env.small)
                for at, ref in ((0, env.sum_vec), (vec_len // 128, env.vec_other)):
                    for k in range(vec_len // 128):
                        env.small[at + k : at + k + 1, :] = ref[0:1, 128 * k : 128 * k + 128]
                for p in range(half):
                    left = env.small[2 * p : 2 * p + 2, :]
                    right = env.small[2 * (p + half) : 2 * (p + half) + 2, :]
                    for ref, first in ((env.keep, core == 0), (env.give, core == 1)):
                        rows = jnp.where(first, left, right)
                        blank = jnp.zeros((14, 128), F32)
                        ref[p, 2 * height :, :] = jnp.concatenate([rows, blank]).astype(BF)
        if following is not None:
            if cotangent is not None:
                top = as_features(env.cotangent[0]) * (place.count.astype(F32) * (1.0 / row_len))
                two = place.two
                grad = jnp.where(two, top, 0.0) if last is None else jnp.where(two, current, top)
            else:
                grad = current
            env.kv_grad[...] = jnp.zeros_like(env.kv_grad)
            for hop in range(4):
                arrived = getattr(env, f"kv_{hop}")
                env.keys[me ^ hop] = arrived[0:width, :].T
                env.keys_t[me ^ hop] = arrived[0:width, :]
                env.values[me ^ hop] = arrived[width : 2 * width, :].T
            low_grad, normed_grad, unit, middle, low_middle, blend_grad = backward_ffn(
                grad, env.post, env.stat_post, env.wout, env.wup, env.wdown, env.vec, env.hidden
            )
            env.low[...] = low_grad
            env.middle[...] = low_middle
            env.middle_out[...] = middle
            env.vec_out[...] = jnp.zeros_like(env.vec_out)
            add_vec(
                env.vec_out, width, low_grad, normed_grad, unit, low_middle, env.hidden[...]
            )
            env.blend_grad[...] = blend_grad
            start, begin = segment_starts(place, me * count, count)
            attend_backward(
                env.pre.at[width : 2 * width, :], env.blend_grad, env.post.at[0:width, :],
                env.stat_post, env.keys, env.values, lambda j, rows, span: env.keys_t[j, rows, span],
                me, begin, start, env.bias, env.query_grad, env.kv_grad,
            )
            env.query_out[...] = (env.query_grad[...] * (width // H) ** -0.5).astype(BF)
            env.own_out[...] = env.kv_grad[me]
            for hop in range(1, 4):
                getattr(env, f"away_{hop}")[...] = env.kv_grad[me ^ hop].astype(BF)

    ins, outs, scratch = {}, {}, {}
    if last is not None:
        ins["middle_in"] = whole(ended["middle_out"])
        ins["query_in"] = whole(ended["query_out"])
        ins["own_in"] = whole(ended["own_out"])
        for hop in range(1, 4):
            ins[f"in_{hop}"] = whole(ended["arrived"][hop - 1])
        ins["pre_last"] = whole(ended["pre"])
        ins["stat_last"] = whole(ended["stat_pre"])
        ins["vec_last"] = of_layer(vec, last)
        ins["wqkv"] = of_layer(wqkv, last)
        ins["old_qkv"] = whole(sums["sum_qkv"])
        ins["old_vec"] = whole(sums["sum_vec"])
        if keep:
            outs["result"] = whole(shaped((count, width), F32))
        if others is not None:
            ins["wire_other"] = whole(others["wire"])
            ins["vec_other"] = whole(others["vec"])
            wire_rows = 3 * width * width // 128
            height = 2 * (wire_rows // (2 * half)) + 16
            outs["keep"] = whole(shaped((half, height, 128), BF))
            outs["give"] = whole(shaped((half, height, 128), BF))
            scratch["wire"] = pltpu.VMEM((wire_rows, 128), BF)
            scratch["small"] = pltpu.VMEM((4 * half, 128), F32)
        elif final:
            outs["wire"] = whole(shaped((3 * width * width // 128, 128), BF))
        if final:
            scratch["total_qkv"] = pltpu.VMEM((width, 3 * width), F32)
        else:
            outs["sum_qkv"] = whole(shaped((width, 3 * width), F32))
        outs["sum_vec"] = whole(shaped((ONES_ROWS, vec_len), F32))
        scratch["packed"] = pltpu.VMEM((3 * width, count), BF)
    if following is not None:
        for name in ("pre", "post", "stat_post"):
            ins[name] = whole(begun[name])
        for hop in range(4):
            ins[f"kv_{hop}"] = whole(begun["kv"][hop])
        ins["vec"] = of_layer(vec, following)
        for name, weight in zip(("wout", "wup", "wdown"), weights[1:]):
            ins[name] = of_layer(weight, following)
        if cotangent is not None:
            ins["cotangent"] = split_row(cotangent)
        outs["middle_out"] = whole(shaped((width, count), F32))
        outs["query_out"] = whole(shaped((width, count), BF))
        outs["own_out"] = whole(shaped((2 * width, count), F32))
        for hop in range(1, 4):
            outs[f"away_{hop}"] = whole(shaped((2 * width, count), BF))
        outs["low"] = whole(shaped((width, count), BF))
        outs["hidden"] = whole(shaped((hidden, count), BF))
        outs["middle"] = whole(shaped((width, count), BF))
        outs["vec_out"] = whole(shaped((ONES_ROWS, vec_len), F32))
        scratch |= {
            "keys": pltpu.VMEM((4, count, width), BF),
            "values": pltpu.VMEM((4, count, width), BF),
            "keys_t": pltpu.VMEM((4, width, count), BF),
            "bias": pltpu.VMEM((count, count), F32),
            "query_grad": pltpu.VMEM((width, count), F32),
            "kv_grad": pltpu.VMEM((4, 2 * width, count), F32),
            "blend_grad": pltpu.VMEM((width, count), BF),
        }
    flops = count * 12 * (4 * width * width + 2 * width * hidden)
    return launch(
        "backward_split", body, place, 1, ins, outs, scratch, flops,
        near=[
            "middle_in", "query_in", "own_in", "in_1", "in_2", "in_3", "middle_out", "query_out",
            "own_out", "away_1", "away_2", "away_3", "low", "hidden", "middle", "vec_out",
        ],
    )


def cut_tokens(place, *pairs, near=False):
    arrays = [array for pair in pairs for array in pair]
    rows, count, width = arrays[0].shape

    def body(place, env):
        at = 0
        for index, pair in enumerate(pairs):
            value = getattr(env, f"in_{at}")[0].astype(F32)
            for extra in range(1, len(pair)):
                value = value + getattr(env, f"in_{at + extra}")[0].astype(F32)
            at += len(pair)
            for hop in range(4):

                @pl.when(pl.program_id(0) == hop)
                def _(hop=hop, index=index, value=value):
                    getattr(env, f"out{index}_{hop}")[...] = value.astype(BF)

    spec = pl.BlockSpec(
        (1, count, width),
        lambda i, here, *_: (row_of_slot(here[0] ^ i, here[1], rows), 0, 0),
    )
    ins = {f"in_{k}": (array, spec) for k, array in enumerate(arrays)}
    outs = {}
    for index in range(len(pairs)):
        outs |= token_outs(f"out{index}", count, width)
    results = launch(
        "cut_tokens", body, place, 4, ins, outs, near=list(outs) if near else ()
    )
    return [[results[f"out{index}_{hop}"] for hop in range(4)] for index in range(len(pairs))]


def prepare(place, weights, vectors):
    out_bias, down_bias, norm_gain, norm_shift, up_bias = vectors
    layers, width = out_bias.shape
    hidden = up_bias.shape[1]
    rows = (6 * width + hidden) // 128
    rows += -rows % 8

    def body(place, env):
        layer = pl.program_id(0)
        for k in range(4):
            getattr(env, f"turned_{k}")[0] = getattr(env, f"weight_{k}")[0].T
        env.vec[...] = jnp.zeros_like(env.vec)
        pick = lambda ref: ref[pl.ds(layer, 1), :]
        parts = [pick(env.out_bias), pick(env.down_bias)]
        for k in range(2):
            parts += [env.norm_gain[0, k : k + 1, :], env.norm_shift[0, k : k + 1, :]]
        at = 0
        for part in parts + [pick(env.up_bias)]:
            for lanes in range(0, part.shape[1], 128):
                env.vec[0, at : at + 1, :] = part[:, lanes : lanes + 128]
                at += 1

    ins = {f"weight_{k}": each(weight) for k, weight in enumerate(weights)}
    ins |= {"out_bias": whole(out_bias), "down_bias": whole(down_bias), "up_bias": whole(up_bias)}
    ins |= {"norm_gain": each(norm_gain), "norm_shift": each(norm_shift)}
    outs = {
        f"turned_{k}": each(shaped((layers, weight.shape[2], weight.shape[1]), BF))
        for k, weight in enumerate(weights)
    }
    outs["vec"] = each(shaped((layers, rows, 128), F32))
    results = launch("prepare", body, place, layers, ins, outs, near=list(outs))
    return tuple(results[f"turned_{k}"] for k in range(4)), results["vec"]


def piece_reader(payloads, me):
    mine, other = payloads
    half = mine.shape[0]

    def piece(p, first, rows):
        left, right = (ref[p % half, first : first + rows, :] for ref in (mine, other))
        return jnp.where(me % 2 == p // half, left, right).astype(F32)

    return piece


def spread_pieces(piece, pieces, first, rows_each, targets, factor):
    edges, at = [], 0
    for ref in targets:
        for lanes in range(0, ref.shape[2], 128):
            edges.append((at, at + ref.shape[1], ref, lanes))
            at += ref.shape[1]
    for p in range(pieces):
        values = piece(p, first, rows_each) * factor
        begin = p * rows_each
        for low, high, ref, lanes in edges:
            left, right = max(low, begin), min(high, begin + rows_each)
            if left < right:
                ref[0, left - low : right - low, lanes : lanes + 128] = values[
                    left - begin : right - begin, :
                ]


def finish_tokens(
    place, payload, answer, answer_split, first, first_split, second, second_split,
    hidden, groups, row_len,
):
    count, width = first_split.shape
    rows = 5
    pieces = 2 * payload[0].shape[0]
    ffn_rows = (width * width + 2 * width * hidden) // 128 // pieces

    def body(place, env):
        step = pl.program_id(0)
        me = place.me
        piece = piece_reader((env.mine, env.other), me)
        lane = lax.broadcasted_iota(jnp.int32, (1, 128), 1)
        total = jnp.zeros((1, 1), F32)
        for extra in range(-(-2 * groups // 128)):
            row = piece(extra, ffn_rows, 16)[0:1, :]
            worth = jnp.where(lane % 2 == 0, 256.0, 1.0)
            row = jnp.where(lane + extra * 128 < 2 * groups, row * worth, 0.0)
            total = total + jnp.sum(row, axis=1, keepdims=True)
        factor = row_len / total
        token_factor = factor * float(rows * groups)

        @pl.when(step == 0)
        def _():
            env.scale[...] = jnp.broadcast_to(factor, env.scale.shape)
            spread_pieces(piece, pieces, 0, ffn_rows, (env.out, env.up, env.down), factor)

        for hop in range(4):

            @pl.when(step == row_of_slot(me ^ hop, place.split, rows))
            def _(hop=hop):
                env.block_output[0] = getattr(env, f"answer_{hop}")[...]
                one = getattr(env, f"first_{hop}")[...].astype(F32)
                two = getattr(env, f"second_{hop}")[...].astype(F32)
                env.input_grad[0] = one * token_factor
                env.embed_grad[0] = (one + two) * token_factor

        @pl.when(step == place.split)
        def _():
            env.block_output[0] = env.answer_split[...]
            one = env.first_split[...]
            env.input_grad[0] = one * token_factor
            env.embed_grad[0] = (one + env.second_split[...]) * token_factor

    ins = {"mine": whole(payload[0]), "other": whole(payload[1])}
    ins |= token_ins("answer", answer) | token_ins("first", first) | token_ins("second", second)
    ins["answer_split"] = whole(answer_split)
    ins["first_split"] = whole(first_split)
    ins["second_split"] = whole(second_split)
    later = lambda *dims: (
        shaped(dims, F32), pl.BlockSpec((1,) + dims[1:], lambda i, *_: (LAYERS - 1, 0, 0))
    )
    outs = {
        "block_output": each(shaped((rows, count, width), BF)),
        "input_grad": each(shaped((rows, count, width), F32)),
        "embed_grad": each(shaped((rows, count, width), F32)),
        "out": later(LAYERS, width, width),
        "up": later(LAYERS, width, hidden),
        "down": later(LAYERS, hidden, width),
        "scale": whole(shaped((8, 128), F32)),
    }
    return launch(
        "finish_tokens", body, place, rows, ins, outs, free=("mine", "other")
    )


def finish_weights(place, payload, done, width, hidden):
    pieces = 2 * payload[0].shape[0]
    ffn_rows = (width * width + 2 * width * hidden) // 128 // pieces
    qkv_rows = 3 * width * width // 128 // pieces
    small_at = ffn_rows + LAYERS * qkv_rows
    vec_len = 6 * width + hidden

    def body(place, env):
        step = pl.program_id(0)
        piece = piece_reader((env.mine, env.other), place.me)
        factor = env.scale[0:1, 0:1]

        @pl.when(step == 0)
        def _():
            spread_pieces(piece, pieces, 0, ffn_rows, (env.out, env.up, env.down), factor)
            for here in range(LAYERS):
                for ref, slot, at, size in (
                    (env.out_b, None, 0, width),
                    (env.down_b, None, width, width),
                    (env.gain, 0, 2 * width, width),
                    (env.shift, 0, 3 * width, width),
                    (env.gain, 1, 4 * width, width),
                    (env.shift, 1, 5 * width, width),
                    (env.up_b, None, 6 * width, hidden),
                ):
                    for lanes in range(0, size, 128):
                        index = (here * vec_len + at + lanes) // 128
                        row = piece(index // 2, small_at, 16)[index % 2 : index % 2 + 1, :]
                        row = row * factor
                        if slot is None:
                            ref[here : here + 1, lanes : lanes + 128] = row
                        else:
                            ref[here, slot : slot + 1, lanes : lanes + 128] = row

        for here in range(LAYERS):

            @pl.when(step == here)
            def _(here=here):
                spread_pieces(
                    piece, pieces, ffn_rows + here * qkv_rows, qkv_rows, (env.qkv,), factor
                )

    ins = {"mine": whole(payload[0]), "other": whole(payload[1]), "scale": whole(done["scale"])}
    names = ("out", "up", "down")
    for name in names:
        ins[name + "_done"] = (done[name], pl.BlockSpec(memory_space=pl.ANY))
    start = lambda array: (
        array, pl.BlockSpec((1,) + array.shape[1:], lambda i, *_: (0, 0, 0))
    )
    outs = {name: start(shaped(done[name].shape, F32)) for name in names}
    outs["qkv"] = each(shaped((LAYERS, width, 3 * width), F32))
    outs["out_b"] = whole(shaped((LAYERS, width), F32))
    outs["up_b"] = whole(shaped((LAYERS, hidden), F32))
    outs["down_b"] = whole(shaped((LAYERS, width), F32))
    outs["gain"] = whole(shaped((LAYERS, 2, width), F32))
    outs["shift"] = whole(shaped((LAYERS, 2, width), F32))
    return launch(
        "finish_weights", body, place, LAYERS, ins, outs,
        aliases=[(name + "_done", name) for name in names],
        free=("mine", "other"),
    )


SEQ = ("y", "core")
CHIPS = ("dp", "y")


def swap(values, hop):
    return lax.ppermute(values, SEQ, [(i, i ^ hop) for i in range(lax.axis_size(SEQ))])


def swap_blocks(blocks):
    return [blocks[0]] + [swap(block, hop) for hop, block in enumerate(blocks[1:], 1)]


def sum_cores(keep, got):
    return (keep.astype(F32) + got.astype(F32)).astype(BF)


def sum_chips(part):
    part = lax.all_to_all(part, CHIPS, 0, 0, tiled=True)
    return jnp.sum(part.astype(F32), axis=0).astype(BF)


def share_chips(part):
    copies = jnp.broadcast_to(part[None], (lax.axis_size(CHIPS),) + part.shape)
    return lax.all_to_all(copies, CHIPS, 0, 0, tiled=True)


def fast_device(
    block_input, embedding, cotangent, qkv_weight, out_weight, out_bias, up_weight, up_bias,
    down_weight, down_bias, norm_gain, norm_shift, seg_lengths, loop_counts, token_counts,
):
    row_count, tokens, width = block_input.shape
    chunks = lax.axis_size(SEQ)
    groups = lax.axis_size("dp")
    devices = groups * chunks
    row_len = tokens * chunks
    me = lax.axis_index(SEQ)
    hidden = up_weight.shape[2]
    tie = lax.optimization_barrier
    half = devices // 2
    steps = LAYERS * 2

    longest = jnp.argmax(seg_lengths.reshape(-1)) // seg_lengths.shape[1]
    here = jnp.stack([me, longest, lax.axis_index("dp")]).astype(jnp.int32)
    place = (here, loop_counts, token_counts, seg_lengths)
    sent, sent_embed, sent_top = cut_tokens(
        place, (block_input, embedding), (embedding,), (cotangent,)
    )
    moved = swap_blocks(sent)
    here, sent = tie((here, sent))
    place = (here, loop_counts, token_counts, seg_lengths)
    backward_weights = (qkv_weight, out_weight, up_weight, down_weight)
    vectors = (out_bias, down_bias, norm_gain, norm_shift, up_bias)
    forward_weights, vec = prepare(place, backward_weights, vectors)

    moved_embed, moved_top = ([blocks[0]] + [None] * 3 for blocks in (sent_embed, sent_top))
    waiting = [(sent_embed, moved_embed, hop) for hop in range(1, 4)]
    waiting += [(sent_top, moved_top, hop) for hop in range(1, 4)]
    saved, saved_split = [], []
    begun = forward_split(
        place, vec, forward_weights, following=0, block_input=block_input,
        embedding=embedding,
    )
    state_split = begun["begun"]
    state = None
    first_end = first_end_split = None
    for step in range(steps):
        layer = step % LAYERS
        pre, kv, stat_pre = begun["pre"], begun["kv"], begun["stat_pre"]
        arrived = [swap(kv, hop) for hop in range(1, 4)]
        source = {}
        if step == 0:
            moved, kv = tie((moved, kv))
            source["tokens"] = moved
        elif step == LAYERS:
            state, moved_embed, kv = tie((state, moved_embed, kv))
            source["state"], source["tokens"] = state, moved_embed
        else:
            state, kv = tie((state, kv))
            source["state"] = state
        riders = waiting[2 * step : 2 * step + 2]
        blocks_out, kv = tie(([blocks[hop] for blocks, _, hop in riders], kv))
        riding = [swap(block, hop) for block, (_, _, hop) in zip(blocks_out, riders)]
        if step == steps - 1:
            source["first_end"] = first_end
        kept = forward_rows(layer, place, vec, forward_weights, **source)
        saved.append(kept)
        if step == steps - 1:
            answer = [kept[f"answer_{hop}"] for hop in range(4)]
            answer, arrived = tie((answer, arrived))
        else:
            state, arrived = tie((kept["result"], arrived))
        arrived, riding = tie((arrived, riding))
        for block, (_, target, hop) in zip(riding, riders):
            target[hop] = block
        boundary = step == LAYERS - 1
        if boundary:
            first_end = state
        extra = {}
        if step < steps - 1:
            extra["following"] = (layer + 1) % LAYERS
            if boundary:
                extra["embedding"] = embedding
        else:
            extra["first_end"] = first_end_split
        blocks = (kv, *arrived)
        begun = forward_split(
            place, vec, forward_weights, last=layer, state=state_split,
            prev=blocks, pre=pre, **extra,
        )
        saved_split.append(
            {
                "pre": pre, "kv": blocks, "stat_pre": stat_pre,
                "post": begun["post"], "stat_post": begun["stat_post"],
            }
        )
        if step == steps - 1:
            answer_split = begun["answer"]
        else:
            state_split = begun["result"]
        if boundary:
            first_end_split = state_split
            state_split = begun["begun"]

    sums = [None] * LAYERS
    early = None
    grad = None
    ended = None
    for step in reversed(range(steps)):
        layer = step % LAYERS
        between = step == LAYERS - 1
        option = {}
        if step == steps - 1 or between:
            option = {"cotangent": cotangent, "row_len": row_len}
        if ended is not None:
            last = (step + 1) % LAYERS
            option |= {
                "last": last, "ended": ended, "sums": sums[last], "keep": between,
                "final": step == 0,
            }
        begun = backward_split(
            place, vec, backward_weights, following=layer, begun=saved_split[step], **option
        )
        if ended is not None:
            if step == 0:
                others = {"wire": begun["wire"], "vec": begun["sum_vec"]}
            else:
                sums[last] |= {"sum_qkv": begun["sum_qkv"], "sum_vec": begun["sum_vec"]}
            if between:
                second_split = begun["result"]
        arrived = [swap(begun[f"away_{hop}"], hop) for hop in range(1, 4)]
        five = {
            "post": saved_split[step]["post"], "hidden": begun["hidden"], "low": begun["low"],
            "middle": begun["middle"], "vec": begun["vec_out"],
        }
        source = {}
        if step == steps - 1:
            moved_answer = [answer[0]] + [None] * 3
            waiting = [(answer, moved_answer, hop) for hop in range(1, 4)]
            source["tokens"] = moved_top
        elif between:
            moved_second = [second[0]] + [None] * 3
            waiting += [(second, moved_second, hop) for hop in range(1, 4)]
            source["tokens"] = moved_top
        riders, waiting = waiting[:2], waiting[2:]
        riding = [swap(blocks[hop], hop) for blocks, _, hop in riders]
        if grad is not None:
            source["grad"] = grad
        if step < LAYERS:
            source |= {"half": half, "digits": step == 1}
        source |= {"base": sums[layer], "keep": step > 0, "travel": step in (0, LAYERS)}
        fixed = (layer, place, saved[step], vec, backward_weights, five)
        if step == 0:
            early = sum_cores(*early)
            grad, early = tie((grad, early))
            source["grad"] = grad
            half_way = backward_rows(*fixed, ffn_only=True, **source)
            early = sum_chips(early)
            half_way, early, arrived = tie((half_way, early, arrived))
            early = share_chips(early)
            got = swap(half_way["give"], 1)
            kept = backward_rows(*fixed, part_done=half_way, **source)
            arrived, got = tie((arrived, got))
        else:
            kept = backward_rows(*fixed, **source)
        if step > 0:
            grad, arrived = tie((kept["result"], arrived))
        else:
            kept["sum_qkv"], arrived = tie((kept["sum_qkv"], arrived))
        if step == LAYERS:
            second = [kept[f"travel_{hop}"] for hop in range(4)]
        if between:
            arrived, riding, kept["give"] = tie((arrived, riding, kept["give"]))
            early = (kept["keep"], swap(kept["give"], 1))
        else:
            arrived, riding = tie((arrived, riding))
        for block, (_, target, hop) in zip(riding, riders):
            target[hop] = block
        if step == 0:
            arrived, early = tie((arrived, early))
            first = [kept[f"travel_{hop}"] for hop in range(4)]
        if sums[layer] is None:
            names = ("sum_qkv", "sum_out", "sum_up", "sum_down", "sum_vec")
            sums[layer] = {name: kept[name] for name in names}
        else:
            sums[layer] = {name: kept[name] for name in ("sum_qkv", "sum_vec")}
        ended = {name: begun[name] for name in ("middle_out", "query_out", "own_out")}
        ended |= {"arrived": arrived, "pre": saved_split[step]["pre"]}
        ended["stat_pre"] = saved_split[step]["stat_pre"]
    moved_first = swap_blocks(first)
    begun = backward_split(
        place, vec, backward_weights, last=0, ended=ended, sums=sums[0], keep=True,
        final=True, others=others, half=half,
    )
    first_split = begun["result"]

    part = jnp.concatenate(
        [
            sum_cores(half_way["keep"], got),
            sum_cores(begun["keep"], swap(begun["give"], 1)),
        ],
        axis=1,
    )
    early_other = swap(early, 1)
    part, moved_first, early, early_other = tie(
        (sum_chips(part), moved_first, early, early_other)
    )
    late = share_chips(part)
    done = finish_tokens(
        place, (early, early_other), moved_answer, answer_split, moved_first, first_split,
        moved_second, second_split, hidden, groups, float(row_len),
    )
    late, done = tie((late, done))
    more = finish_weights(place, (late, swap(late, 1)), done, width, hidden)
    return (
        done["block_output"],
        done["input_grad"],
        done["embed_grad"],
        more["qkv"],
        more["out"],
        more["out_b"],
        more["up"],
        more["up_b"],
        more["down"],
        more["down_b"],
        more["gain"],
        more["shift"],
    )


def solution(mesh):
    if mesh.shape["seq"] == 4:
        fine = Mesh(mesh.devices.reshape(-1, 2, 2), ("dp", "y", "core"))
        return jax.shard_map(
            fast_device,
            mesh=fine,
            in_specs=(
                P("dp", SEQ, None),
                P("dp", SEQ, None),
                P("dp", SEQ, None),
                P(),
                P(),
                P(),
                P(),
                P(),
                P(),
                P(),
                P(),
                P(),
                P("dp", None),
                P("dp"),
                P("dp"),
            ),
            out_specs=(
                P("dp", SEQ, None),
                P("dp", SEQ, None),
                P("dp", SEQ, None),
                P(),
                P(),
                P(),
                P(),
                P(),
                P(),
                P(),
                P(),
                P(),
            ),
            check_vma=False,
        )
    return jax.shard_map(
        on_device,
        mesh=mesh,
        in_specs=(
            P("dp", "seq", None),
            P("dp", "seq", None),
            P("dp", "seq", None),
            P(),
            P(),
            P(),
            P(),
            P(),
            P(),
            P(),
            P(),
            P(),
            P("dp", None),
            P("dp"),
            P("dp"),
        ),
        out_specs=(
            P("dp", "seq", None),
            P("dp", "seq", None),
            P("dp", "seq", None),
            P(),
            P(),
            P(),
            P(),
            P(),
            P(),
            P(),
            P(),
            P(),
        ),
        check_vma=False,
    )
```

```python
import types

import jax
import jax.numpy as jnp
from jax import lax
from jax.experimental import pallas as pl
from jax.experimental.pallas import tpu as pltpu
from jax.sharding import Mesh, PartitionSpec as P

H = 4
LAYERS = 2


NORM_EPS = 1e-05
MASKED = -1e30


def layer_norm(values, gain, shift):
    center = values - jnp.mean(values, axis=-1, keepdims=True)
    spread = jnp.mean(center * center, axis=-1, keepdims=True)
    return center * lax.rsqrt(spread + NORM_EPS) * gain + shift


def gelu_exact(values):
    return jax.nn.gelu(values, approximate=False)


def matmul(left_side, right_side):
    return jnp.dot(left_side, right_side, preferred_element_type=jnp.float32)


def left_dot(left_side, right_side):
    return lax.dot_general(
        left_side, right_side, (((0,), (0,)), ((), ())), preferred_element_type=jnp.float32
    )


def right_dot(left_side, right_side):
    return lax.dot_general(
        left_side, right_side, (((1,), (1,)), ((), ())), preferred_element_type=jnp.float32
    )


def split_heads(packed, head_count):
    return packed.reshape(packed.shape[0], head_count, packed.shape[1] // head_count)


def attend_forward(queries, key_vals, allowed, head_count, score_scale):
    model_width = queries.shape[1]
    key_rows = split_heads(key_vals[:, :model_width], head_count)
    value_rows = split_heads(key_vals[:, model_width:], head_count)
    scores = (
        jnp.einsum(
            "qhd,khd->hqk",
            split_heads(queries, head_count),
            key_rows,
            preferred_element_type=jnp.float32,
        )
        * score_scale
    )
    scores = jnp.where(allowed[None], scores, MASKED)
    row_max = jnp.max(scores, axis=-1, keepdims=True)
    shifted_exp = jnp.exp(scores - row_max)
    row_total = jnp.sum(shifted_exp, axis=-1, keepdims=True)
    attn_probs = (shifted_exp / row_total).astype(jnp.bfloat16)
    blended = jnp.einsum("hqk,khd->qhd", attn_probs, value_rows, preferred_element_type=jnp.float32)
    return (blended.reshape(queries.shape[0], model_width), (row_max + jnp.log(row_total))[..., 0])


def attention_core(
    query_part, key_part, value_part, grad_part, allowed_part, logsum_part, head_count, score_scale
):
    scores = (
        jnp.einsum(
            "qhd,khd->hqk",
            split_heads(query_part, head_count),
            split_heads(key_part, head_count),
            preferred_element_type=jnp.float32,
        )
        * score_scale
    )
    scores = jnp.where(allowed_part[None], scores, MASKED)
    attn_probs = jnp.exp(scores - logsum_part[..., None])
    grad_probs = jnp.einsum(
        "qhd,khd->hqk",
        split_heads(grad_part, head_count),
        split_heads(value_part, head_count),
        preferred_element_type=jnp.float32,
    )
    return (attn_probs, grad_probs)


def query_grads(grad_scores, key_part, head_count, score_scale):
    result = (
        jnp.einsum(
            "hqk,khd->qhd",
            grad_scores,
            split_heads(key_part, head_count),
            preferred_element_type=jnp.float32,
        )
        * score_scale
    )
    return result.reshape(result.shape[0], -1)


def keyval_grads(grad_scores, attn_probs, query_part, grad_part, head_count, score_scale):
    grad_keys = (
        jnp.einsum(
            "hqk,qhd->khd",
            grad_scores,
            split_heads(query_part, head_count),
            preferred_element_type=jnp.float32,
        )
        * score_scale
    )
    grad_values = jnp.einsum(
        "hqk,qhd->khd",
        attn_probs.astype(jnp.bfloat16),
        split_heads(grad_part, head_count),
        preferred_element_type=jnp.float32,
    )
    return jnp.concatenate(
        [grad_keys.reshape(grad_keys.shape[0], -1), grad_values.reshape(grad_values.shape[0], -1)],
        axis=-1,
    )


def on_device(
    block_input,
    embedding,
    cotangent,
    qkv_weight,
    out_weight,
    out_bias,
    up_weight,
    up_bias,
    down_weight,
    down_bias,
    norm_gain,
    norm_shift,
    seg_lengths,
    loop_counts,
    token_counts,
):
    row_count, block_len, model_width = block_input.shape
    head_count = H
    score_scale = (model_width // head_count) ** (-0.5)
    row_len = block_len * lax.axis_size("seq")
    flat_rows = row_count * block_len
    offset = lax.axis_index("seq") * block_len
    key_pos = jnp.arange(row_len, dtype=jnp.int32)
    own_pos = offset + jnp.arange(block_len, dtype=jnp.int32)
    seg_ends = jnp.cumsum(seg_lengths, axis=-1)
    seg_all = jnp.sum((seg_ends[:, None, :] <= key_pos[None, :, None]).astype(jnp.int32), axis=-1)
    seg_own = lax.dynamic_slice_in_dim(seg_all, offset, block_len, 1)
    allowed = (seg_own[:, :, None] == seg_all[:, None, :]) & (
        key_pos[None, None, :] <= own_pos[None, :, None]
    )
    current = block_input.astype(jnp.float32)
    inject = embedding.astype(jnp.float32)
    stored = []
    finals = []
    for repeat in range(2):
        current = current + inject
        for layer_index in range(LAYERS):
            forward_normed = layer_norm(
                current, norm_gain[layer_index, 0], norm_shift[layer_index, 0]
            ).astype(jnp.bfloat16)
            forward_packed = matmul(
                forward_normed.reshape(flat_rows, model_width), qkv_weight[layer_index]
            ).astype(jnp.bfloat16)
            forward_packed = forward_packed.reshape(row_count, block_len, 3 * model_width)
            forward_key_vals = lax.all_gather(
                forward_packed[:, :, model_width:], "seq", axis=1, tiled=True
            )

            def forward_row(inputs):
                return attend_forward(inputs[0], inputs[1], inputs[2], head_count, score_scale)

            forward_blended, forward_logsum = lax.map(
                forward_row, (forward_packed[:, :, :model_width], forward_key_vals, allowed)
            )
            forward_blended = forward_blended.astype(jnp.bfloat16)
            branch_out = matmul(
                forward_blended.reshape(flat_rows, model_width), out_weight[layer_index]
            ).reshape(row_count, block_len, model_width)
            forward_middle = current + branch_out + out_bias[layer_index]
            forward_normed_two = layer_norm(
                forward_middle, norm_gain[layer_index, 1], norm_shift[layer_index, 1]
            ).astype(jnp.bfloat16)
            forward_up_proj = (
                matmul(forward_normed_two.reshape(flat_rows, model_width), up_weight[layer_index])
                + up_bias[layer_index]
            )
            forward_active = gelu_exact(forward_up_proj).astype(jnp.bfloat16)
            result = (
                forward_middle
                + matmul(forward_active, down_weight[layer_index]).reshape(
                    row_count, block_len, model_width
                )
                + down_bias[layer_index]
            )
            current, stored_layer = (
                result,
                (
                    current,
                    forward_normed,
                    forward_packed,
                    forward_key_vals,
                    forward_logsum,
                    forward_blended,
                    forward_middle,
                    forward_normed_two,
                    forward_up_proj,
                    forward_active,
                ),
            )
            stored.append(stored_layer)
        finals.append(current)
    two_loops = (loop_counts == 2)[:, None, None]
    block_output = jnp.where(two_loops, finals[1], finals[0]).astype(jnp.bfloat16)
    row_weight = token_counts.astype(jnp.float32) / row_len
    grad_top = cotangent.astype(jnp.float32) * row_weight[:, None, None]
    grad_state = jnp.where(two_loops, grad_top, 0.0)
    layer_sums = [None] * LAYERS
    second_pass = grad_state
    for repeat in (1, 0):
        for layer_index in reversed(range(LAYERS)):
            backward_stored_layer = stored[repeat * LAYERS + layer_index]
            (
                backward_current,
                normed,
                packed,
                key_vals,
                logsum,
                blended,
                middle,
                normed_two,
                up_proj,
                active,
            ) = backward_stored_layer
            grad_flat = grad_state.reshape(flat_rows, model_width)
            grad_low = grad_flat.astype(jnp.bfloat16)
            grad_down = left_dot(active, grad_low)
            grad_down_bias = jnp.sum(grad_flat, axis=0)
            grad_active = right_dot(grad_low, down_weight[layer_index])
            grad_up_proj = jax.vjp(gelu_exact, up_proj)[1](grad_active)[0].astype(jnp.bfloat16)
            grad_up_bias = jnp.sum(grad_up_proj.astype(jnp.float32), axis=0)
            grad_up = left_dot(normed_two.reshape(flat_rows, model_width), grad_up_proj)
            grad_normed_two = right_dot(grad_up_proj, up_weight[layer_index]).reshape(
                row_count, block_len, model_width
            )
            pull_two = jax.vjp(
                layer_norm, middle, norm_gain[layer_index, 1], norm_shift[layer_index, 1]
            )[1]
            grad_middle, gain_two, shift_two = pull_two(grad_normed_two)
            grad_middle = grad_middle + grad_state
            middle_flat = grad_middle.reshape(flat_rows, model_width)
            middle_low = middle_flat.astype(jnp.bfloat16)
            grad_out = left_dot(blended.reshape(flat_rows, model_width), middle_low)
            grad_out_bias = jnp.sum(middle_flat, axis=0)
            grad_blend = (
                right_dot(middle_low, out_weight[layer_index])
                .astype(jnp.bfloat16)
                .reshape(row_count, block_len, model_width)
            )
            queries = packed[:, :, :model_width]

            def full_row(inputs):
                query_part, keyval_part, grad_part, allowed_part, logsum_part = inputs
                attn_probs, grad_probs = attention_core(
                    query_part,
                    keyval_part[:, :model_width],
                    keyval_part[:, model_width:],
                    grad_part,
                    allowed_part,
                    logsum_part,
                    head_count,
                    score_scale,
                )
                row_delta = jnp.sum(attn_probs * grad_probs, axis=-1, keepdims=True)
                grad_scores = (attn_probs * (grad_probs - row_delta)).astype(jnp.bfloat16)
                return (
                    query_grads(grad_scores, keyval_part[:, :model_width], head_count, score_scale),
                    keyval_grads(
                        grad_scores, attn_probs, query_part, grad_part, head_count, score_scale
                    ),
                )

            grad_query, partial_kv = lax.map(
                full_row, (queries, key_vals, grad_blend, allowed, logsum)
            )
            grad_keyval = lax.psum_scatter(
                partial_kv.astype(jnp.bfloat16), "seq", scatter_dimension=1, tiled=True
            )
            grad_packed = jnp.concatenate(
                [grad_query.astype(jnp.bfloat16), grad_keyval], axis=-1
            ).reshape(flat_rows, 3 * model_width)
            grad_qkv = left_dot(normed.reshape(flat_rows, model_width), grad_packed)
            grad_normed = right_dot(grad_packed, qkv_weight[layer_index]).reshape(
                row_count, block_len, model_width
            )
            pull_one = jax.vjp(
                layer_norm, backward_current, norm_gain[layer_index, 0], norm_shift[layer_index, 0]
            )[1]
            grad_current, gain_one, shift_one = pull_one(grad_normed)
            grad_current = grad_current + grad_middle
            grad_state = grad_current
            grad_set = (
                grad_qkv,
                grad_out,
                grad_out_bias,
                grad_up,
                grad_up_bias,
                grad_down,
                grad_down_bias,
                jnp.stack([gain_one, gain_two]),
                jnp.stack([shift_one, shift_two]),
            )
            if repeat == 1:
                layer_sums[layer_index] = grad_set
            else:
                layer_sums[layer_index] = jax.tree.map(jnp.add, layer_sums[layer_index], grad_set)
        if repeat == 1:
            second_pass = grad_state
            grad_state = jnp.where(two_loops, grad_state, grad_top)
    grad_embed = grad_state + second_pass
    stacked = jax.tree.map(lambda *members: jnp.stack(members), *layer_sums)
    (
        sum_qkv,
        sum_out,
        sum_out_bias,
        sum_up,
        sum_up_bias,
        sum_down,
        sum_down_bias,
        sum_gain,
        sum_shift,
    ) = stacked
    total = lax.psum(jnp.sum(token_counts), "dp").astype(jnp.float32)
    summed = lax.psum(
        (
            sum_qkv,
            sum_out,
            sum_out_bias,
            sum_up,
            sum_up_bias,
            sum_down,
            sum_down_bias,
            sum_gain,
            sum_shift,
        ),
        ("dp", "seq"),
    )
    input_scale = row_count * lax.axis_size("dp") * row_len / total
    weight_scale = row_len / total
    return (
        block_output,
        grad_state * input_scale,
        grad_embed * input_scale,
        summed[0] * weight_scale,
        summed[1] * weight_scale,
        summed[2] * weight_scale,
        summed[3] * weight_scale,
        summed[4] * weight_scale,
        summed[5] * weight_scale,
        summed[6] * weight_scale,
        summed[7] * weight_scale,
        summed[8] * weight_scale,
    )


BF = jnp.bfloat16
F32 = jnp.float32
ERF_TERMS = (7.97869712e-01, 3.63922863e-02, -8.78266373e-05, -3.66934271e-05, 1.42500458e-06)
DENSITY_RATE = -0.7213475204444817
DENSITY_BASE = -1.3257480647361593
VMEM_LIMIT = 24 * 1024 * 1024
ONES_ROWS = 16


def dot_nn(left_side, right_side):
    return jnp.dot(left_side, right_side, preferred_element_type=F32)


def dot_nt(left_side, right_side):
    return lax.dot_general(
        left_side, right_side, (((1,), (1,)), ((), ())), preferred_element_type=F32
    )


def gelu_and_slope(z):
    square = z * z
    series = ERF_TERMS[-1] * square + ERF_TERMS[-2]
    for term in ERF_TERMS[-3::-1]:
        series = series * square + term
    cdf = 0.5 + 0.5 * jnp.tanh(z * series)
    density = jnp.exp2(square * DENSITY_RATE + DENSITY_BASE)
    return z * cdf, cdf + z * density


def norm_forward(values, gain, shift):
    center = values - jnp.mean(values, axis=0, keepdims=True)
    spread = jnp.mean(center * center, axis=0, keepdims=True)
    inverse = lax.rsqrt(spread + NORM_EPS)
    unit = center * inverse
    return unit, inverse, (unit * gain + shift).astype(BF)


def norm_backward(grad, unit, inverse, gain):
    scaled = grad * gain
    first = jnp.mean(scaled, axis=0, keepdims=True)
    second = jnp.mean(scaled * unit, axis=0, keepdims=True)
    return inverse * (scaled - first - unit * second)


def columns(vec, tokens, spread=False):
    turned = vec[0].T

    def column(first, last):
        parts = [turned[:, k : k + 1] for k in range(first // 128, last // 128)]
        if spread:
            parts = [jnp.broadcast_to(part, (128, 128)) for part in parts]
            parts = [jnp.concatenate([part] * (tokens // 128), axis=1) for part in parts]
        return jnp.concatenate(parts, axis=0)

    return column


def project_qkv(state, qkv_t, vec, pre, kv, stat, scale, spread=False):
    width = state.shape[0]
    column = columns(vec, state.shape[1], spread)
    gain = column(2 * width, 3 * width)
    shift = column(3 * width, 4 * width)
    unit, inverse, normed = norm_forward(state, gain, shift)
    pre[0:width, :] = normed
    pre[2 * width : 3 * width, :] = unit.astype(BF)
    pre[width : 2 * width, :] = (dot_nn(qkv_t[0, 0:width, :], normed) * scale).astype(BF)
    kv[0:width, :] = dot_nn(qkv_t[0, width : 2 * width, :], normed).astype(BF)
    kv[width : 2 * width, :] = dot_nn(qkv_t[0, 2 * width : 3 * width, :], normed).astype(BF)
    stat[0:1, :] = inverse


def pad_head(block, odd):
    blank = jnp.zeros_like(block)
    return jnp.concatenate([blank, block] if odd else [block, blank], axis=0)


def tile_bias(first_key, start, causal, shape):
    key_at = lax.broadcasted_iota(jnp.int32, shape, 0)
    keep = key_at + first_key >= start
    if causal:
        keep = keep & (key_at <= lax.broadcasted_iota(jnp.int32, shape, 1))
    return jnp.where(keep, 0.0, MASKED)


def over_tiles(chunk, count, begin, half_tile, full_tile, carry):
    half = count // 2
    first_half = begin // half
    odd = jnp.where(first_half < 2 * chunk, first_half % 2, 0)
    carry = lax.fori_loop(0, odd, lambda _, c: half_tile(first_half // 2, c), carry)
    return lax.fori_loop((first_half + 1) // 2, chunk, full_tile, carry)


def attend_chunk(queries, keys, values_t, chunk, begin, start, bias, total, stat, blended):
    width, tokens = queries.shape
    head = width // H
    pair = 2 * head
    half = tokens // 2
    head_rows = [slice(h * head, (h + 1) * head) for h in range(H)]

    def scores(j, h, span):
        lanes = pl.ds((h // 2) * pair, pair)
        return dot_nn(keys[j, span, lanes], pad_head(queries[head_rows[h], :], h % 2))

    everything = slice(0, tokens)
    bias[...] = tile_bias(chunk * tokens, start, True, (tokens, tokens))
    parts = [scores(chunk, h, everything) for h in range(H)]
    uppers = [part[:half, :] + bias[:half, :] for part in parts]
    lowers = [part[half:, half:] + bias[half:, half:] for part in parts]
    tops, sums, weights = [], [], []
    for upper, lower in zip(uppers, lowers):
        top = jnp.max(upper, axis=0, keepdims=True)
        right = jnp.maximum(top[:, half:], jnp.max(lower, axis=0, keepdims=True))
        top = jnp.concatenate([top[:, :half], right], axis=1)
        upper = jnp.exp(upper - top)
        lower = jnp.exp(lower - right)
        added = jnp.sum(upper, axis=0, keepdims=True)
        right = added[:, half:] + jnp.sum(lower, axis=0, keepdims=True)
        tops.append(top)
        sums.append(jnp.concatenate([added[:, :half], right], axis=1))
        lower = lower.astype(BF)
        lower = jnp.concatenate([jnp.zeros_like(lower), lower], axis=1)
        weights.append(jnp.concatenate([upper.astype(BF), lower], axis=0))
    for rows, weight in zip(head_rows, weights):
        total[rows, :] = dot_nn(values_t[chunk, rows, :], weight)

    def step(j, span, size, carry):
        tops, sums = carry
        bias[:size, :] = tile_bias(j * tokens + span.start, start, False, (size, tokens))
        parts = [scores(j, h, span) + bias[:size, :] for h in range(H)]
        new_tops = [
            jnp.maximum(old, jnp.max(part, axis=0, keepdims=True))
            for old, part in zip(tops, parts)
        ]
        weights = [jnp.exp(part - top) for part, top in zip(parts, new_tops)]
        new_sums = [jnp.sum(weight, axis=0, keepdims=True) for weight in weights]
        terms = [
            dot_nn(values_t[j, rows, span], weight.astype(BF))
            for rows, weight in zip(head_rows, weights)
        ]
        fades = [jnp.exp(old - new) for old, new in zip(tops, new_tops)]
        for rows, term, fade in zip(head_rows, terms, fades):
            total[rows, :] = total[rows, :] * fade + term
        sums = [old * fade + new for old, fade, new in zip(sums, fades, new_sums)]
        return tuple(new_tops), tuple(sums)

    tops, sums = over_tiles(
        chunk, tokens, begin,
        lambda j, carry: step(j, slice(half, tokens), half, carry),
        lambda j, carry: step(j, everything, tokens, carry),
        (tuple(tops), tuple(sums)),
    )
    for h, rows in enumerate(head_rows):
        blended[rows, :] = (total[rows, :] / sums[h]).astype(BF)
        stat[h : h + 1, :] = tops[h] + jnp.log(sums[h])


def finish_layer(state, out_t, up_t, down_t, vec, post, stat, spread=False):
    width, tokens = state.shape
    hidden = up_t.shape[1]
    column = columns(vec, tokens, spread)
    middle = state + dot_nn(out_t[0], post[0:width, :]) + column(0, width)
    gain = column(4 * width, 5 * width)
    shift = column(5 * width, 6 * width)
    unit, inverse, normed = norm_forward(middle, gain, shift)
    post[width : 2 * width, :] = normed
    post[2 * width : 3 * width, :] = unit.astype(BF)
    stat[H : H + 1, :] = inverse
    z = dot_nn(up_t[0], normed) + column(6 * width, 6 * width + hidden)
    active, slope = gelu_and_slope(z)
    post[3 * width : 3 * width + hidden, :] = active.astype(BF)
    post[3 * width + hidden :, :] = slope.astype(BF)
    return (
        middle
        + dot_nn(down_t[0], post[3 * width : 3 * width + hidden, :])
        + column(width, 2 * width)
    )


def launch(
    name, body, place, grid, ins, outs, scratch=(), flops=0, aliases=(), near=(), free=(),
    on_split=True,
):
    scratch = dict(scratch)
    names = [*ins, *outs, *scratch]

    def kernel(here, loops, counts, lengths, *refs):
        me, split = here[0], here[1]
        row = split if on_split else row_of_slot(me, split, loops.shape[0])
        facts = types.SimpleNamespace(
            me=me, split=split, slot=here[2], two=loops[row] == 2, count=counts[row], counts=counts,
            all_lengths=lengths, lengths=[lengths[row, k] for k in range(lengths.shape[1])],
        )
        body(facts, types.SimpleNamespace(**dict(zip(names, refs))))

    space = lambda key: pltpu.VMEM if key in near else pltpu.HBM
    results = pl.pallas_call(
        kernel,
        grid_spec=pltpu.PrefetchScalarGridSpec(
            num_scalar_prefetch=len(place),
            grid=(grid,),
            in_specs=[spec for _, spec in ins.values()],
            out_specs=[spec for _, spec in outs.values()],
            scratch_shapes=list(scratch.values()),
        ),
        out_shape=[
            shape if key in free else space(key)(shape.shape, shape.dtype)
            for key, (shape, _) in outs.items()
        ],
        input_output_aliases={
            len(place) + list(ins).index(source): list(outs).index(target) for source, target in aliases
        },
        compiler_params=pltpu.CompilerParams(vmem_limit_bytes=VMEM_LIMIT),
        cost_estimate=pl.CostEstimate(flops=flops, bytes_accessed=1, transcendentals=0),
        name=name,
    )(
        *[pltpu.with_memory_space_constraint(array, pltpu.HBM) for array in place],
        *[
            array if key in free else pltpu.with_memory_space_constraint(array, space(key))
            for key, (array, _) in ins.items()
        ],
    )
    return dict(zip(outs, results))


def whole(array):
    return array, pl.BlockSpec(array.shape, lambda i, *_: (0,) * len(array.shape))


def of_layer(array, layer):
    return array, pl.BlockSpec((1,) + array.shape[1:], lambda i, *_: (layer, 0, 0))


def each(array):
    return array, pl.BlockSpec((1,) + array.shape[1:], lambda i, *_: (i, 0, 0))


def each_back(array):
    count = array.shape[0]
    return array, pl.BlockSpec(
        (1,) + array.shape[1:], lambda i, *_: (count - 1 - i, 0, 0)
    )


def shaped(dims, dtype):
    return jax.ShapeDtypeStruct(dims, dtype)


def segment_starts(place, first, count):
    position = lax.broadcasted_iota(jnp.int32, (1, count), 1) + first
    starts = jnp.zeros((1, count), jnp.int32)
    end = jnp.int32(0)
    begin = jnp.int32(0)
    for length in place.lengths:
        end = end + length
        starts = jnp.where(position >= end, end, starts)
        begin = jnp.where(first >= end, end, begin)
    return starts, begin


def gather_tokens(env, name, me):
    for hop in range(4):
        env.spread[me ^ hop] = getattr(env, f"{name}_{hop}")[...]


def deal_tokens(env, name, value, chunk, me):
    for hop in range(4):

        @pl.when(chunk == (me ^ hop))
        def _(hop=hop):
            getattr(env, f"{name}_{hop}")[...] = value


def token_ins(name, blocks):
    return {f"{name}_{hop}": whole(block) for hop, block in enumerate(blocks)}


def token_outs(name, tokens, width):
    return {f"{name}_{hop}": whole(shaped((tokens, width), BF)) for hop in range(4)}


def as_tokens(values):
    return values.astype(BF).T


def as_features(tokens):
    return tokens.T.astype(F32)


def forward_rows(layer, place, vec, weights, state=None, tokens=None, first_end=None):
    chunks = 4
    count = state.shape[2] if tokens is None else tokens[0].shape[0]
    qkv_t, out_t, up_t, down_t = weights
    width, hidden = out_t.shape[2], up_t.shape[1]
    post_rows = 3 * width + 2 * hidden

    def body(place, env):
        chunk = pl.program_id(0)
        me = place.me
        current = env.state.at[0] if state is not None else None
        if tokens is not None:

            @pl.when(chunk == 0)
            def _():
                gather_tokens(env, "tokens", me)

            added = as_features(env.spread[chunk])
            env.current[...] = added if state is None else added + env.state[0]
            current = env.current
        project_qkv(
            current[...], env.qkv_t, env.vec, env.pre.at[0], env.kv.at[0], env.stat_pre.at[0],
            (width // H) ** -0.5, spread=True,
        )
        env.keys[chunk] = env.kv[0, 0:width, :].T
        env.values_t[chunk] = env.kv[0, width : 2 * width, :]
        start, begin = segment_starts(place, chunk * count, count)
        attend_chunk(
            env.pre.at[0, width : 2 * width, :], env.keys, env.values_t, chunk, begin, start, env.bias, env.total, env.stat_post.at[0],
            env.post.at[0, 0:width, :],
        )
        result = finish_layer(
            current[...], env.out_t, env.up_t, env.down_t, env.vec, env.post.at[0],
            env.stat_post.at[0], spread=True,
        )
        if first_end is None:
            env.result[0] = result
        else:
            answer = jnp.where(place.two, result, env.first_end[0])
            deal_tokens(env, "answer", as_tokens(answer), chunk, me)

    ins = {"vec": of_layer(vec, layer)}
    for name, weight in zip(("qkv_t", "out_t", "up_t", "down_t"), weights):
        ins[name] = of_layer(weight, layer)
    scratch = {
        "keys": pltpu.VMEM((chunks, count, width), BF),
        "values_t": pltpu.VMEM((chunks, width, count), BF),
        "bias": pltpu.VMEM((count, count), F32),
        "total": pltpu.VMEM((width, count), F32),
    }
    if state is not None:
        ins["state"] = each(state)
    if tokens is not None:
        ins |= token_ins("tokens", tokens)
        scratch["spread"] = pltpu.VMEM((chunks, count, width), BF)
        scratch["current"] = pltpu.VMEM((width, count), F32)
    outs = {}
    if first_end is None:
        outs["result"] = each(shaped((chunks, width, count), F32))
    else:
        ins["first_end"] = each(first_end)
        outs |= token_outs("answer", count, width)
    outs["pre"] = each(shaped((chunks, 3 * width, count), BF))
    outs["kv"] = each(shaped((chunks, 2 * width, count), BF))
    outs["post"] = each(shaped((chunks, post_rows, count), BF))
    outs["stat_pre"] = each(shaped((chunks, 8, count), F32))
    outs["stat_post"] = each(shaped((chunks, 8, count), F32))
    flops = chunks * count * 6 * (4 * width * width + 2 * width * hidden)
    return launch(
        "forward_rows", body, place, chunks, ins, outs, scratch, flops,
        on_split=False,
        near=["state", "result", "vec", "qkv_t", "out_t", "up_t", "down_t"]
        + [f"tokens_{hop}" for hop in range(4) if state is None],
    )


def split_row(array):
    return array, pl.BlockSpec((1,) + array.shape[1:], lambda i, here, *_: (here[1], 0, 0))


def row_of_slot(slot, split, rows):
    return jnp.where(slot == split, rows - 1, slot)


def forward_split(
    place, vec, weights, last=None, following=None, state=None, prev=None, pre=None,
    block_input=None, embedding=None, first_end=None, only_parts=False,
):
    qkv_t, out_t, up_t, down_t = weights
    width, hidden = out_t.shape[2], up_t.shape[1]
    count = embedding.shape[1] if state is None else state.shape[1]

    def body(place, env):
        me = place.me
        if last is not None:
            for hop in range(4):
                arrived = getattr(env, f"kv_{hop}")
                env.keys[me ^ hop] = arrived[0:width, :].T
                env.values_t[me ^ hop] = arrived[width : 2 * width, :]
            start, begin = segment_starts(place, me * count, count)
            attend_chunk(
                env.pre_in.at[width : 2 * width, :], env.keys, env.values_t, me, begin, start,
                env.bias, env.total, env.stat_post, env.post.at[0:width, :],
            )
            current = finish_layer(
                env.state[...], env.out_t, env.up_t, env.down_t, env.vec, env.post, env.stat_post
            )
            if first_end is not None:
                answer = jnp.where(place.two, current, env.first_end[...])
                env.answer[...] = as_tokens(answer)
            else:
                env.result[...] = current
        if following is not None:
            if embedding is not None:
                added = as_features(env.embedding[0])
                if last is None:
                    current = as_features(env.block_input[0]) + added
                else:
                    current = env.result[...] + added
                env.begun[...] = current
            project_qkv(
                current, env.qkv_t, env.vec_next, env.pre, env.kv, env.stat_pre,
                (width // H) ** -0.5,
            )

    ins, outs, scratch = {}, {}, {}
    if last is not None:
        ins |= {f"kv_{hop}": whole(block) for hop, block in enumerate(prev)}
        ins |= {"state": whole(state), "pre_in": whole(pre)}
        ins["vec"] = of_layer(vec, last)
        for name, weight in zip(("out_t", "up_t", "down_t"), weights[1:]):
            ins[name] = of_layer(weight, last)
        if first_end is not None:
            ins["first_end"] = whole(first_end)
            outs["answer"] = whole(shaped((count, width), BF))
        else:
            outs["result"] = whole(shaped((width, count), F32))
        outs["post"] = whole(shaped((3 * width + 2 * hidden, count), BF))
        outs["stat_post"] = whole(shaped((8, count), F32))
        scratch = {
            "keys": pltpu.VMEM((4, count, width), BF),
            "values_t": pltpu.VMEM((4, width, count), BF),
            "bias": pltpu.VMEM((count, count), F32),
            "total": pltpu.VMEM((width, count), F32),
        }
    if following is not None:
        ins["vec_next"] = of_layer(vec, following)
        ins["qkv_t"] = of_layer(qkv_t, following)
        if embedding is not None:
            ins["embedding"] = split_row(embedding)
            outs["begun"] = whole(shaped((width, count), F32))
        if block_input is not None:
            ins["block_input"] = split_row(block_input)
        outs["pre"] = whole(shaped((3 * width, count), BF))
        outs["kv"] = whole(shaped((2 * width, count), BF))
        outs["stat_pre"] = whole(shaped((8, count), F32))
    flops = 0 if last is None else count * 6 * (4 * width * width + 2 * width * hidden)
    near = ["state", "result", "begun", "pre", "pre_in", "kv", "vec", "vec_next"]
    near += ["qkv_t", "out_t", "up_t", "down_t"] + [f"kv_{hop}" for hop in range(4)]
    if only_parts:
        return body, ins, outs, scratch, near
    return launch("forward_split", body, place, 1, ins, outs, scratch, flops, near=near)


def backward_ffn(grad, post, stat, wout, wup, wdown, vec, hidden_grad):
    width, tokens = grad.shape
    hidden = wup.shape[2]
    low_grad = grad.astype(BF)
    hidden_grad[...] = (
        dot_nn(wdown[0], low_grad) * post[3 * width + hidden :, :].astype(F32)
    ).astype(BF)
    normed_grad = dot_nn(wup[0], hidden_grad[...])
    unit = post[2 * width : 3 * width, :].astype(F32)
    gain = columns(vec, tokens)(4 * width, 5 * width)
    middle = grad + norm_backward(normed_grad, unit, stat[H : H + 1, :], gain)
    low_middle = middle.astype(BF)
    blend_grad = dot_nn(wout[0], low_middle).astype(BF)
    return low_grad, normed_grad, unit, middle, low_middle, blend_grad


def token_sum(rows):
    return dot_nt(jnp.ones((ONES_ROWS, rows.shape[1]), BF), rows.astype(BF))


def attend_backward(
    queries, blend_grad, blended, stat, keys, values, keys_t, chunk, begin, start,
    bias, query_grad, kv_grad,
):
    width, tokens = queries.shape
    head = width // H
    pair = 2 * head
    head_rows = [slice(h * head, (h + 1) * head) for h in range(H)]
    deltas = [
        jnp.sum(
            blend_grad[rows, :].astype(F32) * blended[rows, :].astype(F32), axis=0, keepdims=True
        )
        for rows in head_rows
    ]

    half = tokens // 2
    everything = slice(0, tokens)

    def products(j, span):
        parts, prob_grads = [], []
        for h, rows in enumerate(head_rows):
            lanes = pl.ds((h // 2) * pair, pair)
            parts.append(dot_nn(keys[j, span, lanes], pad_head(queries[rows, :], h % 2)))
            prob_grads.append(
                dot_nn(values[j, span, lanes], pad_head(blend_grad[rows, :], h % 2))
            )
        return parts, prob_grads

    def collect(j, span, probs, score_grads, first):
        for rows, prob, score_grad in zip(head_rows, probs, score_grads):
            value_rows = slice(width + rows.start, width + rows.stop)
            kv_grad[j, value_rows, span] += dot_nt(blend_grad[rows, :], prob)
            kv_grad[j, rows, span] += dot_nt(queries[rows, :], score_grad)
            term = dot_nn(keys_t(j, rows, span), score_grad)
            if first:
                query_grad[rows, :] = term
            else:
                query_grad[rows, :] += term

    def weigh(part, prob_grad, mask, logsum, delta):
        prob = jnp.exp(part + mask - logsum)
        return prob.astype(BF), (prob * (prob_grad - delta)).astype(BF)

    bias[...] = tile_bias(chunk * tokens, start, True, (tokens, tokens))
    probs, score_grads = [], []
    for h, (part, prob_grad) in enumerate(zip(*products(chunk, everything))):
        logsum, delta = stat[h : h + 1, :], deltas[h]
        upper = weigh(part[:half, :], prob_grad[:half, :], bias[:half, :], logsum, delta)
        lower = weigh(
            part[half:, half:], prob_grad[half:, half:], bias[half:, half:], logsum[:, half:],
            delta[:, half:],
        )
        for kept, above, below in zip((probs, score_grads), upper, lower):
            below = jnp.concatenate([jnp.zeros_like(below), below], axis=1)
            kept.append(jnp.concatenate([above, below], axis=0))
    collect(chunk, everything, probs, score_grads, True)

    def step(j, span, size, carry):
        bias[:size, :] = tile_bias(j * tokens + span.start, start, False, (size, tokens))
        pairs = [
            weigh(part, prob_grad, bias[:size, :], stat[h : h + 1, :], deltas[h])
            for h, (part, prob_grad) in enumerate(zip(*products(j, span)))
        ]
        collect(j, span, [p for p, _ in pairs], [d for _, d in pairs], False)
        return carry

    over_tiles(
        chunk, tokens, begin,
        lambda j, carry: step(j, slice(half, tokens), half, carry),
        lambda j, carry: step(j, everything, tokens, carry),
        0,
    )


def add_vec(sum_vec, width, low_grad, normed_grad, unit, low_middle, dz):
    sum_vec[:, 0:width] += token_sum(low_middle)
    sum_vec[:, width : 2 * width] += token_sum(low_grad)
    sum_vec[:, 4 * width : 5 * width] += token_sum(normed_grad * unit)
    sum_vec[:, 5 * width : 6 * width] += token_sum(normed_grad)
    sum_vec[:, 6 * width :] += token_sum(dz)


def finish_backward(middle, pre, stat, packed, wqkv, vec, sum_qkv, sum_vec):
    width, tokens = middle.shape
    sum_qkv[...] += dot_nt(pre[0:width, :], packed[...])
    normed_grad = dot_nn(wqkv[0], packed[...])
    unit = pre[2 * width : 3 * width, :].astype(F32)
    gain = columns(vec, tokens)(2 * width, 3 * width)
    sum_vec[:, 2 * width : 3 * width] += token_sum(normed_grad * unit)
    sum_vec[:, 3 * width : 4 * width] += token_sum(normed_grad)
    return middle + norm_backward(normed_grad, unit, stat[0:1, :], gain)


def pack_lanes(wire, blocks):
    at = 0
    for ref in blocks:
        rows = ref.shape[0]
        for first in range(0, ref.shape[1], 128):
            wire[at : at + rows, :] = ref[:, first : first + 128].astype(BF)
            at += rows


def put_pieces(keep, give, source, first, height, core):
    half = keep.shape[0]
    for ref, side in ((keep, core), (give, 1 - core)):
        for p in range(half):
            at = pl.multiple_of((side * half + p) * height, 16)
            ref[p, first : first + height, :] = source[pl.ds(at, height), :]


def count_digits(place, groups):
    tally = place.counts[0]
    for k in range(1, place.counts.shape[0]):
        tally = tally + place.counts[k]
    lane = lax.broadcasted_iota(jnp.int32, (16, 128), 1)
    row = lax.broadcasted_iota(jnp.int32, (16, 128), 0)
    digit = jnp.where(lane % 2 == 0, tally // 256, tally % 256)
    keep = (lane // 2 == place.slot) & (row == 0) & (place.me == 0)
    return jnp.where(keep, digit, 0).astype(F32).astype(BF)


def backward_rows(
    layer, place, saved, vec, weights, five, base=None, grad=None, tokens=None,
    keep=True, travel=False, part_done=None, ffn_only=False, half=0, digits=False,
    closing=None, others=None,
):
    chunks, _, count = saved["kv"].shape
    wqkv, wout, wup, wdown = weights
    width, hidden = wup.shape[1:]
    row_len = chunks * count
    first = base is None
    part = hidden // chunks
    vec_len = 6 * width + hidden
    with_ffn, with_attention = part_done is None, not ffn_only

    def body(place, env):
        order = pl.program_id(0)
        chunk = chunks - 1 - order
        me = place.me

        @pl.when(order == 0)
        def _():
            if tokens is not None:
                gather_tokens(env, "tokens", me)
            if with_ffn:
                env.sum_up[...] = jnp.zeros_like(env.sum_up)
                env.sum_down[...] = jnp.zeros_like(env.sum_down)
                env.sum_out[...] = dot_nt(env.blend_five[...], env.middle_five[...])
                env.sum_vec[...] = env.vec_five[...]
                if not first:
                    env.sum_vec[...] += env.base_vec[...]
            else:
                env.sum_vec[...] = env.vec_done[...]
            if with_attention:
                env.sum_qkv[...] = jnp.zeros_like(env.sum_qkv)
                env.kv_grad[...] = jnp.zeros_like(env.kv_grad)
                for j in range(chunks):
                    env.keys[j] = env.kv[j, 0:width, :].T
                    env.values[j] = env.kv[j, width : 2 * width, :].T

        def add_base(ref, old):
            rows = old.shape[0]
            ref[pl.ds(pl.multiple_of(order * rows, rows), rows), :] += old[...]

        if with_ffn:
            spread = pl.ds(pl.multiple_of(order * part, part), part)
            env.sum_down[spread, :] += dot_nt(env.active_five[...], env.low_five[...])
            env.sum_up[:, spread] += dot_nt(env.normed_five[...], env.hidden_five[...])
            if not first:
                env.sum_down[spread, :] += env.base_down[...]
                env.sum_up[:, spread] += env.base_up[...]
                add_base(env.sum_out, env.base_out)
            current = env.grad.at[0] if grad is not None else None
            if tokens is not None:
                top = as_features(env.spread[chunk]) * (place.count.astype(F32) * (1.0 / row_len))
                two = place.two
                env.current[...] = (
                    jnp.where(two, top, 0.0)
                    if grad is None
                    else jnp.where(two, env.grad[0], top)
                )
                current = env.current
            post = env.post.at[0]
            low_grad, normed_grad, unit, middle, low_middle, blend_grad = backward_ffn(
                current[...], post, env.stat_post.at[0], env.wout, env.wup, env.wdown, env.vec,
                env.hidden_grad,
            )
            env.sum_down[...] += dot_nt(post[3 * width : 3 * width + hidden, :], low_grad)
            env.sum_up[...] += dot_nt(post[width : 2 * width, :], env.hidden_grad[...])
            env.sum_out[...] += dot_nt(post[0:width, :], low_middle)
            add_vec(
                env.sum_vec, width, low_grad, normed_grad, unit, low_middle, env.hidden_grad[...]
            )
            blend_ref = env.blend_grad if with_attention else env.blend_out.at[0]
            blend_ref[...] = blend_grad
            if not first:

                @pl.when(order == chunks - 1)
                def _():
                    pack_lanes(env.wire, (env.sum_out, env.sum_up, env.sum_down))
                    height = env.wire.shape[0] // (2 * half)
                    put_pieces(env.keep, env.give, env.wire, 0, height, me % 2)
                    if digits:
                        blank = jnp.zeros((16, 128), BF)
                        for p in range(half):
                            env.keep[p, height:, :] = count_digits(place, half) if p == 0 else blank
                            env.give[p, height:, :] = blank

            if not with_attention:
                env.middle_out[0] = middle
                return
            blended = post.at[0:width, :]
        else:
            middle, blend_ref, blended = env.middle_in[0], env.blend_in.at[0], env.blended.at[0]
        if not first:
            add_base(env.sum_qkv, env.base_qkv)
        start, begin = segment_starts(place, chunk * count, count)
        attend_backward(
            env.pre.at[0, width : 2 * width, :], blend_ref, blended,
            env.stat_post.at[0], env.keys, env.values, lambda j, rows, span: env.kv[j, rows, span],
            chunk, begin, start, env.bias, env.query_grad, env.kv_grad,
        )
        env.packed[0:width, :] = (env.query_grad[...] * (width // H) ** -0.5).astype(BF)
        env.packed[width : 3 * width, :] = env.kv_grad[chunk].astype(BF)
        result = finish_backward(
            middle, env.pre.at[0], env.stat_pre.at[0], env.packed, env.wqkv, env.vec,
            env.sum_qkv, env.sum_vec,
        )
        if keep:
            env.result[0] = result
        if travel:
            deal_tokens(env, "travel", as_tokens(result), chunk, me)
        if closing is not None:

            @pl.when(order == chunks - 1)
            def _():
                ended = end_split_row(env, env.vec, env.sum_qkv, env.sum_vec)
                env.split_result[...] = ended.T
                write_last_payload(env, half, me % 2)

    ins = {"vec": of_layer(vec, layer), "stat_post": each_back(saved["stat_post"])}
    outs, scratch = {}, {}
    cut = lambda array, shape, at: (array, pl.BlockSpec(shape, lambda i, *_: at(i)))
    sums = {"sum_vec": (ONES_ROWS, vec_len)}
    if with_ffn:
        ins["post"] = each_back(saved["post"])
        for name, weight in zip(("wout", "wup", "wdown"), weights[1:]):
            ins[name] = of_layer(weight, layer)
        if grad is not None:
            ins["grad"] = each_back(grad)
        if tokens is not None:
            ins |= token_ins("tokens", tokens)
            scratch["spread"] = pltpu.VMEM((chunks, count, width), BF)
            scratch["current"] = pltpu.VMEM((width, count), F32)
        post_five = five["post"]
        ins["blend_five"] = cut(post_five, (width, count), lambda i: (0, 0))
        ins["normed_five"] = cut(post_five, (width, count), lambda i: (1, 0))
        ins["active_five"] = cut(post_five, (part, count), lambda i: (3 * width // part + i, 0))
        ins["hidden_five"] = cut(five["hidden"], (part, count), lambda i: (i, 0))
        for name in ("low", "middle", "vec"):
            ins[name + "_five"] = whole(five[name])
        sums |= {"sum_out": (width, width), "sum_up": (width, hidden), "sum_down": (hidden, width)}
        scratch["hidden_grad"] = pltpu.VMEM((hidden, count), BF)
        if not first:
            ins["base_out"] = cut(base["sum_out"], (width // chunks, width), lambda i: (i, 0))
            ins["base_up"] = cut(base["sum_up"], (width, part), lambda i: (0, i))
            ins["base_down"] = cut(base["sum_down"], (part, width), lambda i: (i, 0))
            ins["base_vec"] = whole(base["sum_vec"])
            wire_rows = (width * width + 2 * width * hidden) // 128
            scratch["wire"] = pltpu.VMEM((wire_rows, 128), BF)
            height = wire_rows // (2 * half) + (16 if digits else 0)
            outs["keep"] = whole(shaped((half, height, 128), BF))
            outs["give"] = whole(shaped((half, height, 128), BF))
        if not with_attention:
            outs["blend_out"] = each_back(shaped((chunks, width, count), BF))
            outs["middle_out"] = each_back(shaped((chunks, width, count), F32))
    else:
        ins["vec_done"] = whole(part_done["sum_vec"])
        ins["middle_in"] = each_back(part_done["middle_out"])
        ins["blend_in"] = each_back(part_done["blend_out"])
        ins["blended"] = (
            saved["post"],
            pl.BlockSpec((1, width, count), lambda i, *_: (chunks - 1 - i, 0, 0)),
        )
    if with_attention:
        ins["kv"] = whole(saved["kv"])
        ins["pre"] = each_back(saved["pre"])
        ins["stat_pre"] = each_back(saved["stat_pre"])
        ins["wqkv"] = of_layer(wqkv, layer)
        sums["sum_qkv"] = (width, 3 * width)
        if not first:
            ins["base_qkv"] = cut(base["sum_qkv"], (width // chunks, 3 * width), lambda i: (i, 0))
        if keep:
            outs["result"] = each_back(shaped((chunks, width, count), F32))
        if travel:
            outs |= token_outs("travel", count, width)
        scratch |= {
            "keys": pltpu.VMEM((chunks, count, width), BF),
            "values": pltpu.VMEM((chunks, count, width), BF),
            "bias": pltpu.VMEM((count, count), F32),
            "query_grad": pltpu.VMEM((width, count), F32),
            "kv_grad": pltpu.VMEM((chunks, 2 * width, count), F32),
            "blend_grad": pltpu.VMEM((width, count), BF),
            "packed": pltpu.VMEM((3 * width, count), BF),
        }
    if closing is not None:
        ins |= split_row_ins(closing)
        wire_rows = 3 * width * width // 128
        height = 2 * (wire_rows // (2 * half)) + 16
        ins["wire_other"] = whole(others["wire"])
        ins["vec_other"] = whole(others["vec"])
        outs["keep"] = whole(shaped((half, height, 128), BF))
        outs["give"] = whole(shaped((half, height, 128), BF))
        outs["split_result"] = whole(shaped((count, width), F32))
        scratch["wire"] = pltpu.VMEM((wire_rows, 128), BF)
        scratch["small"] = pltpu.VMEM((4 * half, 128), F32)
        scratch |= {name: pltpu.VMEM(dims, F32) for name, dims in sums.items()}
        sums = {}
    for name, dims in sums.items():
        if first or name in ("sum_qkv", "sum_vec"):
            outs[name] = whole(shaped(dims, F32))
        else:
            scratch[name] = pltpu.VMEM(dims, F32)
    flops = chunks * count * 12 * (4 * width * width + 2 * width * hidden)
    return launch(
        "backward_rows", body, place, chunks, ins, outs, scratch, flops, on_split=False,
        near=[
            "middle_in_split", "query_in", "own_in", "in_1", "in_2", "in_3",
            "grad", "result", "hidden_five", "low_five", "middle_five", "vec_five",
        ],
    )


def split_row_ins(ended):
    ins = {
        "middle_in_split": whole(ended["middle_out"]), "query_in": whole(ended["query_out"]),
        "own_in": whole(ended["own_out"]), "pre_last": whole(ended["pre"]),
        "stat_last": whole(ended["stat_pre"]),
    }
    return ins | {f"in_{hop}": whole(ended["arrived"][hop - 1]) for hop in range(1, 4)}


def end_split_row(env, vec, sum_qkv, sum_vec):
    width = env.query_in.shape[0]
    env.packed[0:width, :] = env.query_in[...]
    kv_total = env.own_in[...]
    for hop in range(1, 4):
        kv_total = kv_total + getattr(env, f"in_{hop}")[...].astype(F32)
    env.packed[width : 3 * width, :] = kv_total.astype(BF)
    return finish_backward(
        env.middle_in_split[...], env.pre_last, env.stat_last, env.packed, env.wqkv, vec,
        sum_qkv, sum_vec,
    )


def write_last_payload(env, half, core):
    pack_lanes(env.wire, (env.sum_qkv,))
    height = env.wire.shape[0] // (2 * half)
    put_pieces(env.keep, env.give, env.wire, 0, height, core)
    put_pieces(env.keep, env.give, env.wire_other, height, height, core)
    rows = env.sum_vec.shape[1] // 128
    env.small[...] = jnp.zeros_like(env.small)
    for at, ref in ((0, env.sum_vec), (rows, env.vec_other)):
        for k in range(rows):
            env.small[at + k : at + k + 1, :] = ref[0:1, 128 * k : 128 * k + 128]
    for p in range(half):
        left = env.small[2 * p : 2 * p + 2, :]
        right = env.small[2 * (p + half) : 2 * (p + half) + 2, :]
        for ref, first in ((env.keep, core == 0), (env.give, core == 1)):
            pair = jnp.where(first, left, right)
            blank = jnp.zeros((14, 128), F32)
            ref[p, 2 * height :, :] = jnp.concatenate([pair, blank]).astype(BF)


def backward_split(
    place, vec, weights, last=None, following=None, ended=None, sums=None, begun=None,
    cotangent=None, final=False, keep=False, row_len=None, only_parts=False,
):
    wqkv, wout, wup, wdown = weights
    width, hidden = wup.shape[1:]
    vec_len = 6 * width + hidden
    count = (ended or begun)["stat_pre"].shape[1]

    def body(place, env):
        me = place.me
        if last is not None:
            sum_qkv = env.total_qkv if final else env.sum_qkv
            sum_qkv[...] = env.old_qkv[...]
            env.sum_vec[...] = env.old_vec[...]
            current = end_split_row(env, env.vec_last, sum_qkv, env.sum_vec)
            if keep:
                env.result[...] = current.T
            if final:
                pack_lanes(env.wire, (sum_qkv,))
        if following is not None:
            if cotangent is not None:
                top = as_features(env.cotangent[0]) * (place.count.astype(F32) * (1.0 / row_len))
                two = place.two
                grad = jnp.where(two, top, 0.0) if last is None else jnp.where(two, current, top)
            else:
                grad = current
            env.kv_grad[...] = jnp.zeros_like(env.kv_grad)
            for hop in range(4):
                arrived = getattr(env, f"kv_{hop}")
                env.keys[me ^ hop] = arrived[0:width, :].T
                env.keys_t[me ^ hop] = arrived[0:width, :]
                env.values[me ^ hop] = arrived[width : 2 * width, :].T
            low_grad, normed_grad, unit, middle, low_middle, blend_grad = backward_ffn(
                grad, env.post, env.stat_post, env.wout, env.wup, env.wdown, env.vec, env.hidden
            )
            env.low[...] = low_grad
            env.middle[...] = low_middle
            env.middle_out[...] = middle
            env.vec_out[...] = jnp.zeros_like(env.vec_out)
            add_vec(
                env.vec_out, width, low_grad, normed_grad, unit, low_middle, env.hidden[...]
            )
            env.blend_grad[...] = blend_grad
            start, begin = segment_starts(place, me * count, count)
            attend_backward(
                env.pre.at[width : 2 * width, :], env.blend_grad, env.post.at[0:width, :],
                env.stat_post, env.keys, env.values, lambda j, rows, span: env.keys_t[j, rows, span],
                me, begin, start, env.bias, env.query_grad, env.kv_grad,
            )
            env.query_out[...] = (env.query_grad[...] * (width // H) ** -0.5).astype(BF)
            env.own_out[...] = env.kv_grad[me]
            for hop in range(1, 4):
                getattr(env, f"away_{hop}")[...] = env.kv_grad[me ^ hop].astype(BF)

    ins, outs, scratch = {}, {}, {}
    if last is not None:
        ins |= split_row_ins(ended)
        ins["vec_last"] = of_layer(vec, last)
        ins["wqkv"] = of_layer(wqkv, last)
        ins["old_qkv"] = whole(sums["sum_qkv"])
        ins["old_vec"] = whole(sums["sum_vec"])
        if keep:
            outs["result"] = whole(shaped((count, width), F32))
        if final:
            outs["wire"] = whole(shaped((3 * width * width // 128, 128), BF))
        if final:
            scratch["total_qkv"] = pltpu.VMEM((width, 3 * width), F32)
        else:
            outs["sum_qkv"] = whole(shaped((width, 3 * width), F32))
        outs["sum_vec"] = whole(shaped((ONES_ROWS, vec_len), F32))
        scratch["packed"] = pltpu.VMEM((3 * width, count), BF)
    if following is not None:
        for name in ("pre", "post", "stat_post"):
            ins[name] = whole(begun[name])
        for hop in range(4):
            ins[f"kv_{hop}"] = whole(begun["kv"][hop])
        ins["vec"] = of_layer(vec, following)
        for name, weight in zip(("wout", "wup", "wdown"), weights[1:]):
            ins[name] = of_layer(weight, following)
        if cotangent is not None:
            ins["cotangent"] = split_row(cotangent)
        outs["middle_out"] = whole(shaped((width, count), F32))
        outs["query_out"] = whole(shaped((width, count), BF))
        outs["own_out"] = whole(shaped((2 * width, count), F32))
        for hop in range(1, 4):
            outs[f"away_{hop}"] = whole(shaped((2 * width, count), BF))
        outs["low"] = whole(shaped((width, count), BF))
        outs["hidden"] = whole(shaped((hidden, count), BF))
        outs["middle"] = whole(shaped((width, count), BF))
        outs["vec_out"] = whole(shaped((ONES_ROWS, vec_len), F32))
        scratch |= {
            "keys": pltpu.VMEM((4, count, width), BF),
            "values": pltpu.VMEM((4, count, width), BF),
            "keys_t": pltpu.VMEM((4, width, count), BF),
            "bias": pltpu.VMEM((count, count), F32),
            "query_grad": pltpu.VMEM((width, count), F32),
            "kv_grad": pltpu.VMEM((4, 2 * width, count), F32),
            "blend_grad": pltpu.VMEM((width, count), BF),
        }
    flops = count * 12 * (4 * width * width + 2 * width * hidden)
    near = [
        "middle_in_split", "query_in", "own_in", "in_1", "in_2", "in_3", "middle_out",
        "query_out", "own_out", "away_1", "away_2", "away_3", "low", "hidden", "middle", "vec_out",
    ]
    if only_parts:
        return body, ins, outs, scratch, near
    return launch("backward_split", body, place, 1, ins, outs, scratch, flops, near=near)


def turn_split(
    place, vec, forward_weights, backward_weights, layer, state, blocks, pre, stat_pre, first_end,
    cotangent, row_len,
):
    forward, ins, outs, scratch, near = forward_split(
        place, vec, forward_weights, last=layer, state=state, prev=blocks, pre=pre,
        first_end=first_end, only_parts=True,
    )
    begun = {"pre": pre, "kv": blocks, "stat_pre": stat_pre, "post": pre, "stat_post": stat_pre}
    backward, more_ins, more_outs, more_scratch, more_near = backward_split(
        place, vec, backward_weights, following=layer, begun=begun, cotangent=cotangent,
        row_len=row_len, only_parts=True,
    )
    shared = ("pre", "post", "stat_post", "vec", *(f"kv_{hop}" for hop in range(4)))
    more_ins = {key: value for key, value in more_ins.items() if key not in shared}

    def body(place, env):
        forward(place, env)
        env.pre = env.pre_in
        backward(place, env)

    return launch(
        "turn_split", body, place, 1, ins | more_ins, outs | more_outs, scratch | more_scratch,
        near=near + more_near,
    )


def cut_tokens(place, *pairs):
    arrays = [array for pair in pairs for array in pair]
    rows, count, width = arrays[0].shape

    def body(place, env):
        me = place.me
        best, longest = jnp.int32(0), jnp.int32(0)
        for row in range(rows):
            most = place.all_lengths[row, 0]
            for k in range(1, place.all_lengths.shape[1]):
                most = jnp.maximum(most, place.all_lengths[row, k])
            longest = jnp.where(most > best, row, longest)
            best = jnp.maximum(most, best)
        env.here[0] = me
        env.here[1] = longest
        env.here[2] = place.slot
        for hop in range(4):
            row = row_of_slot(me ^ hop, longest, rows)
            at = 0
            for index, pair in enumerate(pairs):
                value = getattr(env, f"in_{at}")[row].astype(F32)
                for extra in range(1, len(pair)):
                    value = value + getattr(env, f"in_{at + extra}")[row].astype(F32)
                at += len(pair)
                getattr(env, f"out{index}_{hop}")[...] = value.astype(BF)

    ins = {f"in_{k}": whole(array) for k, array in enumerate(arrays)}
    outs = {}
    for index in range(len(pairs)):
        outs |= token_outs(f"out{index}", count, width)
    outs["here"] = (shaped((3,), jnp.int32), pl.BlockSpec(memory_space=pltpu.SMEM))
    results = launch("cut_tokens", body, place, 1, ins, outs, free=("here",))
    blocks = [[results[f"out{index}_{hop}"] for hop in range(4)] for index in range(len(pairs))]
    return results["here"], blocks


def prepare(place, weights, vectors):
    out_bias, down_bias, norm_gain, norm_shift, up_bias = vectors
    layers, width = out_bias.shape
    hidden = up_bias.shape[1]
    rows = (6 * width + hidden) // 128
    rows += -rows % 8

    def body(place, env):
        layer = pl.program_id(0)
        for k in range(4):
            getattr(env, f"turned_{k}")[0] = getattr(env, f"weight_{k}")[0].T
        env.vec[...] = jnp.zeros_like(env.vec)
        pick = lambda ref: ref[pl.ds(layer, 1), :]
        parts = [pick(env.out_bias), pick(env.down_bias)]
        for k in range(2):
            parts += [env.norm_gain[0, k : k + 1, :], env.norm_shift[0, k : k + 1, :]]
        at = 0
        for part in parts + [pick(env.up_bias)]:
            for lanes in range(0, part.shape[1], 128):
                env.vec[0, at : at + 1, :] = part[:, lanes : lanes + 128]
                at += 1

    ins = {f"weight_{k}": each(weight) for k, weight in enumerate(weights)}
    ins |= {"out_bias": whole(out_bias), "down_bias": whole(down_bias), "up_bias": whole(up_bias)}
    ins |= {"norm_gain": each(norm_gain), "norm_shift": each(norm_shift)}
    outs = {
        f"turned_{k}": each(shaped((layers, weight.shape[2], weight.shape[1]), BF))
        for k, weight in enumerate(weights)
    }
    outs["vec"] = each(shaped((layers, rows, 128), F32))
    results = launch("prepare", body, place, layers, ins, outs, near=list(outs))
    return tuple(results[f"turned_{k}"] for k in range(4)), results["vec"]


def piece_reader(payloads, me):
    mine, other = payloads
    half = mine.shape[0]

    def piece(p, first, rows):
        left, right = (ref[p % half, first : first + rows, :] for ref in (mine, other))
        return jnp.where(me % 2 == p // half, left, right).astype(F32)

    return piece


def spread_pieces(piece, pieces, first, rows_each, targets, factor):
    edges, at = [], 0
    for ref in targets:
        for lanes in range(0, ref.shape[2], 128):
            edges.append((at, at + ref.shape[1], ref, lanes))
            at += ref.shape[1]
    for p in range(pieces):
        values = piece(p, first, rows_each) * factor
        begin = p * rows_each
        for low, high, ref, lanes in edges:
            left, right = max(low, begin), min(high, begin + rows_each)
            if left < right:
                ref[0, left - low : right - low, lanes : lanes + 128] = values[
                    left - begin : right - begin, :
                ]


def finish_tokens(
    place, payload, answer, answer_split, first, first_split, second, second_split,
    hidden, groups, row_len,
):
    count, width = first_split.shape
    rows = 5
    pieces = 2 * payload[0].shape[0]
    ffn_rows = (width * width + 2 * width * hidden) // 128 // pieces

    def body(place, env):
        step = pl.program_id(0)
        me = place.me
        piece = piece_reader((env.mine, env.other), me)
        lane = lax.broadcasted_iota(jnp.int32, (1, 128), 1)
        total = jnp.zeros((1, 1), F32)
        for extra in range(-(-2 * groups // 128)):
            row = piece(extra, ffn_rows, 16)[0:1, :]
            worth = jnp.where(lane % 2 == 0, 256.0, 1.0)
            row = jnp.where(lane + extra * 128 < 2 * groups, row * worth, 0.0)
            total = total + jnp.sum(row, axis=1, keepdims=True)
        factor = row_len / total
        token_factor = factor * float(rows * groups)

        @pl.when(step == 0)
        def _():
            env.scale[...] = jnp.broadcast_to(factor, env.scale.shape)
            spread_pieces(piece, pieces, 0, ffn_rows, (env.out, env.up, env.down), factor)

        for hop in range(4):

            @pl.when(step == row_of_slot(me ^ hop, place.split, rows))
            def _(hop=hop):
                env.block_output[0] = getattr(env, f"answer_{hop}")[...]
                one = getattr(env, f"first_{hop}")[...].astype(F32)
                two = getattr(env, f"second_{hop}")[...].astype(F32)
                env.input_grad[0] = one * token_factor
                env.embed_grad[0] = (one + two) * token_factor

        @pl.when(step == place.split)
        def _():
            env.block_output[0] = env.answer_split[...]
            one = env.first_split[...]
            env.input_grad[0] = one * token_factor
            env.embed_grad[0] = (one + env.second_split[...]) * token_factor

    ins = {"mine": whole(payload[0]), "other": whole(payload[1])}
    ins |= token_ins("answer", answer) | token_ins("first", first) | token_ins("second", second)
    ins["answer_split"] = whole(answer_split)
    ins["first_split"] = whole(first_split)
    ins["second_split"] = whole(second_split)
    later = lambda *dims: (
        shaped(dims, F32), pl.BlockSpec((1,) + dims[1:], lambda i, *_: (LAYERS - 1, 0, 0))
    )
    outs = {
        "block_output": each(shaped((rows, count, width), BF)),
        "input_grad": each(shaped((rows, count, width), F32)),
        "embed_grad": each(shaped((rows, count, width), F32)),
        "out": later(LAYERS, width, width),
        "up": later(LAYERS, width, hidden),
        "down": later(LAYERS, hidden, width),
        "scale": whole(shaped((8, 128), F32)),
    }
    return launch(
        "finish_tokens", body, place, rows, ins, outs, free=("mine", "other")
    )


def finish_weights(place, payload, done, width, hidden):
    pieces = 2 * payload[0].shape[0]
    ffn_rows = (width * width + 2 * width * hidden) // 128 // pieces
    qkv_rows = 3 * width * width // 128 // pieces
    small_at = ffn_rows + LAYERS * qkv_rows
    vec_len = 6 * width + hidden

    def body(place, env):
        step = pl.program_id(0)
        piece = piece_reader((env.mine, env.other), place.me)
        factor = env.scale[0:1, 0:1]

        @pl.when(step == 0)
        def _():
            spread_pieces(piece, pieces, 0, ffn_rows, (env.out, env.up, env.down), factor)
            for here in range(LAYERS):
                for ref, slot, at, size in (
                    (env.out_b, None, 0, width),
                    (env.down_b, None, width, width),
                    (env.gain, 0, 2 * width, width),
                    (env.shift, 0, 3 * width, width),
                    (env.gain, 1, 4 * width, width),
                    (env.shift, 1, 5 * width, width),
                    (env.up_b, None, 6 * width, hidden),
                ):
                    for lanes in range(0, size, 128):
                        index = (here * vec_len + at + lanes) // 128
                        row = piece(index // 2, small_at, 16)[index % 2 : index % 2 + 1, :]
                        row = row * factor
                        if slot is None:
                            ref[here : here + 1, lanes : lanes + 128] = row
                        else:
                            ref[here, slot : slot + 1, lanes : lanes + 128] = row

        for here in range(LAYERS):

            @pl.when(step == here)
            def _(here=here):
                spread_pieces(
                    piece, pieces, ffn_rows + here * qkv_rows, qkv_rows, (env.qkv,), factor
                )

    ins = {"mine": whole(payload[0]), "other": whole(payload[1]), "scale": whole(done["scale"])}
    names = ("out", "up", "down")
    for name in names:
        ins[name + "_done"] = (done[name], pl.BlockSpec(memory_space=pl.ANY))
    start = lambda array: (
        array, pl.BlockSpec((1,) + array.shape[1:], lambda i, *_: (0, 0, 0))
    )
    outs = {name: start(shaped(done[name].shape, F32)) for name in names}
    outs["qkv"] = each(shaped((LAYERS, width, 3 * width), F32))
    outs["out_b"] = whole(shaped((LAYERS, width), F32))
    outs["up_b"] = whole(shaped((LAYERS, hidden), F32))
    outs["down_b"] = whole(shaped((LAYERS, width), F32))
    outs["gain"] = whole(shaped((LAYERS, 2, width), F32))
    outs["shift"] = whole(shaped((LAYERS, 2, width), F32))
    return launch(
        "finish_weights", body, place, LAYERS, ins, outs,
        aliases=[(name + "_done", name) for name in names],
        free=("mine", "other"),
    )


SEQ = ("y", "core")
CHIPS = ("dp", "y")


def swap(values, hop):
    return lax.ppermute(values, SEQ, [(i, i ^ hop) for i in range(lax.axis_size(SEQ))])


def swap_blocks(blocks):
    return [blocks[0]] + [swap(block, hop) for hop, block in enumerate(blocks[1:], 1)]


def sum_cores(keep, got):
    return (keep.astype(F32) + got.astype(F32)).astype(BF)


def sum_chips(part):
    part = lax.all_to_all(part, CHIPS, 0, 0, tiled=True)
    return jnp.sum(part.astype(F32), axis=0).astype(BF)


def share_chips(part):
    copies = jnp.broadcast_to(part[None], (lax.axis_size(CHIPS),) + part.shape)
    return lax.all_to_all(copies, CHIPS, 0, 0, tiled=True)


def fast_device(
    block_input, embedding, cotangent, qkv_weight, out_weight, out_bias, up_weight, up_bias,
    down_weight, down_bias, norm_gain, norm_shift, seg_lengths, loop_counts, token_counts,
):
    row_count, tokens, width = block_input.shape
    chunks = lax.axis_size(SEQ)
    groups = lax.axis_size("dp")
    devices = groups * chunks
    row_len = tokens * chunks
    me = lax.axis_index(SEQ)
    hidden = up_weight.shape[2]
    tie = lax.optimization_barrier
    half = devices // 2
    steps = LAYERS * 2

    here = jnp.stack([me, jnp.zeros_like(me), lax.axis_index("dp")]).astype(jnp.int32)
    here, (sent, sent_embed, sent_top) = cut_tokens(
        (here, loop_counts, token_counts, seg_lengths), (block_input, embedding), (embedding,),
        (cotangent,),
    )
    moved = swap_blocks(sent)
    here, sent = tie((here, sent))
    place = (here, loop_counts, token_counts, seg_lengths)
    backward_weights = (qkv_weight, out_weight, up_weight, down_weight)
    vectors = (out_bias, down_bias, norm_gain, norm_shift, up_bias)
    forward_weights, vec = prepare(place, backward_weights, vectors)

    moved_embed, moved_top = ([blocks[0]] + [None] * 3 for blocks in (sent_embed, sent_top))
    waiting = [(sent_embed, moved_embed, hop) for hop in range(1, 4)]
    waiting += [(sent_top, moved_top, hop) for hop in range(1, 4)]
    saved, saved_split = [], []
    begun = forward_split(
        place, vec, forward_weights, following=0, block_input=block_input,
        embedding=embedding,
    )
    state_split = begun["begun"]
    state = None
    first_end = first_end_split = None
    for step in range(steps):
        layer = step % LAYERS
        pre, kv, stat_pre = begun["pre"], begun["kv"], begun["stat_pre"]
        arrived = [swap(kv, hop) for hop in range(1, 4)]
        source = {}
        if step == 0:
            moved, kv = tie((moved, kv))
            source["tokens"] = moved
        elif step == LAYERS:
            state, moved_embed, kv = tie((state, moved_embed, kv))
            source["state"], source["tokens"] = state, moved_embed
        else:
            state, kv = tie((state, kv))
            source["state"] = state
        riders = waiting[2 * step : 2 * step + 2]
        blocks_out, kv = tie(([blocks[hop] for blocks, _, hop in riders], kv))
        riding = [swap(block, hop) for block, (_, _, hop) in zip(blocks_out, riders)]
        if step == steps - 1:
            source["first_end"] = first_end
        kept = forward_rows(layer, place, vec, forward_weights, **source)
        saved.append(kept)
        if step == steps - 1:
            answer = [kept[f"answer_{hop}"] for hop in range(4)]
            answer, arrived = tie((answer, arrived))
        else:
            state, arrived = tie((kept["result"], arrived))
        arrived, riding = tie((arrived, riding))
        for block, (_, target, hop) in zip(riding, riders):
            target[hop] = block
        boundary = step == LAYERS - 1
        if boundary:
            first_end = state
        extra = {}
        if step < steps - 1:
            extra["following"] = (layer + 1) % LAYERS
            if boundary:
                extra["embedding"] = embedding
        blocks = (kv, *arrived)
        if step == steps - 1:
            begun = turned = turn_split(
                place, vec, forward_weights, backward_weights, layer, state_split, blocks, pre,
                stat_pre, first_end_split, cotangent, row_len,
            )
        else:
            begun = forward_split(
                place, vec, forward_weights, last=layer, state=state_split,
                prev=blocks, pre=pre, **extra,
            )
        saved_split.append(
            {
                "pre": pre, "kv": blocks, "stat_pre": stat_pre,
                "post": begun["post"], "stat_post": begun["stat_post"],
            }
        )
        if step == steps - 1:
            answer_split = begun["answer"]
        else:
            state_split = begun["result"]
        if boundary:
            first_end_split = state_split
            state_split = begun["begun"]

    sums = [None] * LAYERS
    early = None
    grad = None
    ended = None
    for step in reversed(range(steps)):
        layer = step % LAYERS
        between = step == LAYERS - 1
        option = {}
        if between:
            option = {"cotangent": cotangent, "row_len": row_len}
        if ended is not None:
            last = (step + 1) % LAYERS
            option |= {
                "last": last, "ended": ended, "sums": sums[last], "keep": between,
                "final": step == 0,
            }
        begun = turned
        if step < steps - 1:
            begun = backward_split(
                place, vec, backward_weights, following=layer, begun=saved_split[step], **option
            )
        if ended is not None:
            if step == 0:
                others = {"wire": begun["wire"], "vec": begun["sum_vec"]}
            else:
                sums[last] |= {"sum_qkv": begun["sum_qkv"], "sum_vec": begun["sum_vec"]}
            if between:
                second_split = begun["result"]
        arrived = [swap(begun[f"away_{hop}"], hop) for hop in range(1, 4)]
        five = {
            "post": saved_split[step]["post"], "hidden": begun["hidden"], "low": begun["low"],
            "middle": begun["middle"], "vec": begun["vec_out"],
        }
        source = {}
        if step == steps - 1:
            moved_answer = [answer[0]] + [None] * 3
            waiting = [(answer, moved_answer, hop) for hop in range(1, 4)]
            source["tokens"] = moved_top
        elif between:
            moved_second = [second[0]] + [None] * 3
            waiting += [(second, moved_second, hop) for hop in range(1, 4)]
            source["tokens"] = moved_top
        riders, waiting = waiting[:2], waiting[2:]
        riding = [swap(blocks[hop], hop) for blocks, _, hop in riders]
        if grad is not None:
            source["grad"] = grad
        if step < LAYERS:
            source |= {"half": half, "digits": step == 1}
        source |= {"base": sums[layer], "keep": step > 0, "travel": step in (0, LAYERS)}
        fixed = (layer, place, saved[step], vec, backward_weights, five)
        if step == 0:
            early = sum_cores(*early)
            grad, early = tie((grad, early))
            source["grad"] = grad
            half_way = backward_rows(*fixed, ffn_only=True, **source)
            early = sum_chips(early)
            half_way, early, arrived = tie((half_way, early, arrived))
            early = share_chips(early)
            late_ffn = sum_cores(half_way["keep"], swap(half_way["give"], 1))
            half_way, late_ffn = tie((half_way, late_ffn))
            closing = {name: begun[name] for name in ("middle_out", "query_out", "own_out")}
            closing |= {"arrived": arrived, "pre": saved_split[step]["pre"]}
            closing["stat_pre"] = saved_split[step]["stat_pre"]
            kept = backward_rows(
                *fixed, part_done=half_way, closing=closing, others=others, **source
            )
            kept["keep"], early = tie((kept["keep"], early))
            for block, (_, target, hop) in zip(riding, riders):
                target[hop] = block
            first = [kept[f"travel_{hop}"] for hop in range(4)]
            break
        kept = backward_rows(*fixed, **source)
        grad, arrived = tie((kept["result"], arrived))
        if step == LAYERS:
            second = [kept[f"travel_{hop}"] for hop in range(4)]
        if between:
            arrived, riding, kept["give"] = tie((arrived, riding, kept["give"]))
            early = (kept["keep"], swap(kept["give"], 1))
        else:
            arrived, riding = tie((arrived, riding))
        for block, (_, target, hop) in zip(riding, riders):
            target[hop] = block
        if sums[layer] is None:
            names = ("sum_qkv", "sum_out", "sum_up", "sum_down", "sum_vec")
            sums[layer] = {name: kept[name] for name in names}
        else:
            sums[layer] = {name: kept[name] for name in ("sum_qkv", "sum_vec")}
        ended = {name: begun[name] for name in ("middle_out", "query_out", "own_out")}
        ended |= {"arrived": arrived, "pre": saved_split[step]["pre"]}
        ended["stat_pre"] = saved_split[step]["stat_pre"]
    moved_first = swap_blocks(first)
    first_split = kept["split_result"]

    part = jnp.concatenate(
        [
            late_ffn,
            sum_cores(kept["keep"], swap(kept["give"], 1)),
        ],
        axis=1,
    )
    early_other = swap(early, 1)
    part, moved_first, early, early_other = tie(
        (sum_chips(part), moved_first, early, early_other)
    )
    late = share_chips(part)
    done = finish_tokens(
        place, (early, early_other), moved_answer, answer_split, moved_first, first_split,
        moved_second, second_split, hidden, groups, float(row_len),
    )
    late, done = tie((late, done))
    more = finish_weights(place, (late, swap(late, 1)), done, width, hidden)
    return (
        done["block_output"],
        done["input_grad"],
        done["embed_grad"],
        more["qkv"],
        more["out"],
        more["out_b"],
        more["up"],
        more["up_b"],
        more["down"],
        more["down_b"],
        more["gain"],
        more["shift"],
    )


def solution(mesh):
    if mesh.shape["seq"] == 4:
        fine = Mesh(mesh.devices.reshape(-1, 2, 2), ("dp", "y", "core"))
        return jax.shard_map(
            fast_device,
            mesh=fine,
            in_specs=(
                P("dp", SEQ, None),
                P("dp", SEQ, None),
                P("dp", SEQ, None),
                P(),
                P(),
                P(),
                P(),
                P(),
                P(),
                P(),
                P(),
                P(),
                P("dp", None),
                P("dp"),
                P("dp"),
            ),
            out_specs=(
                P("dp", SEQ, None),
                P("dp", SEQ, None),
                P("dp", SEQ, None),
                P(),
                P(),
                P(),
                P(),
                P(),
                P(),
                P(),
                P(),
                P(),
            ),
            check_vma=False,
        )
    return jax.shard_map(
        on_device,
        mesh=mesh,
        in_specs=(
            P("dp", "seq", None),
            P("dp", "seq", None),
            P("dp", "seq", None),
            P(),
            P(),
            P(),
            P(),
            P(),
            P(),
            P(),
            P(),
            P(),
            P("dp", None),
            P("dp"),
            P("dp"),
        ),
        out_specs=(
            P("dp", "seq", None),
            P("dp", "seq", None),
            P("dp", "seq", None),
            P(),
            P(),
            P(),
            P(),
            P(),
            P(),
            P(),
            P(),
            P(),
        ),
        check_vma=False,
    )
```

```python
import types

import jax
import jax.numpy as jnp
from jax import lax
from jax.experimental import pallas as pl
from jax.experimental.pallas import tpu as pltpu
from jax.sharding import Mesh, PartitionSpec as P

H = 4
LAYERS = 2


NORM_EPS = 1e-05
MASKED = -1e30


def layer_norm(values, gain, shift):
    center = values - jnp.mean(values, axis=-1, keepdims=True)
    spread = jnp.mean(center * center, axis=-1, keepdims=True)
    return center * lax.rsqrt(spread + NORM_EPS) * gain + shift


def gelu_exact(values):
    return jax.nn.gelu(values, approximate=False)


def matmul(left_side, right_side):
    return jnp.dot(left_side, right_side, preferred_element_type=jnp.float32)


def left_dot(left_side, right_side):
    return lax.dot_general(
        left_side, right_side, (((0,), (0,)), ((), ())), preferred_element_type=jnp.float32
    )


def right_dot(left_side, right_side):
    return lax.dot_general(
        left_side, right_side, (((1,), (1,)), ((), ())), preferred_element_type=jnp.float32
    )


def split_heads(packed, head_count):
    return packed.reshape(packed.shape[0], head_count, packed.shape[1] // head_count)


def attend_forward(queries, key_vals, allowed, head_count, score_scale):
    model_width = queries.shape[1]
    key_rows = split_heads(key_vals[:, :model_width], head_count)
    value_rows = split_heads(key_vals[:, model_width:], head_count)
    scores = (
        jnp.einsum(
            "qhd,khd->hqk",
            split_heads(queries, head_count),
            key_rows,
            preferred_element_type=jnp.float32,
        )
        * score_scale
    )
    scores = jnp.where(allowed[None], scores, MASKED)
    row_max = jnp.max(scores, axis=-1, keepdims=True)
    shifted_exp = jnp.exp(scores - row_max)
    row_total = jnp.sum(shifted_exp, axis=-1, keepdims=True)
    attn_probs = (shifted_exp / row_total).astype(jnp.bfloat16)
    blended = jnp.einsum("hqk,khd->qhd", attn_probs, value_rows, preferred_element_type=jnp.float32)
    return (blended.reshape(queries.shape[0], model_width), (row_max + jnp.log(row_total))[..., 0])


def attention_core(
    query_part, key_part, value_part, grad_part, allowed_part, logsum_part, head_count, score_scale
):
    scores = (
        jnp.einsum(
            "qhd,khd->hqk",
            split_heads(query_part, head_count),
            split_heads(key_part, head_count),
            preferred_element_type=jnp.float32,
        )
        * score_scale
    )
    scores = jnp.where(allowed_part[None], scores, MASKED)
    attn_probs = jnp.exp(scores - logsum_part[..., None])
    grad_probs = jnp.einsum(
        "qhd,khd->hqk",
        split_heads(grad_part, head_count),
        split_heads(value_part, head_count),
        preferred_element_type=jnp.float32,
    )
    return (attn_probs, grad_probs)


def query_grads(grad_scores, key_part, head_count, score_scale):
    result = (
        jnp.einsum(
            "hqk,khd->qhd",
            grad_scores,
            split_heads(key_part, head_count),
            preferred_element_type=jnp.float32,
        )
        * score_scale
    )
    return result.reshape(result.shape[0], -1)


def keyval_grads(grad_scores, attn_probs, query_part, grad_part, head_count, score_scale):
    grad_keys = (
        jnp.einsum(
            "hqk,qhd->khd",
            grad_scores,
            split_heads(query_part, head_count),
            preferred_element_type=jnp.float32,
        )
        * score_scale
    )
    grad_values = jnp.einsum(
        "hqk,qhd->khd",
        attn_probs.astype(jnp.bfloat16),
        split_heads(grad_part, head_count),
        preferred_element_type=jnp.float32,
    )
    return jnp.concatenate(
        [grad_keys.reshape(grad_keys.shape[0], -1), grad_values.reshape(grad_values.shape[0], -1)],
        axis=-1,
    )


def on_device(
    block_input,
    embedding,
    cotangent,
    qkv_weight,
    out_weight,
    out_bias,
    up_weight,
    up_bias,
    down_weight,
    down_bias,
    norm_gain,
    norm_shift,
    seg_lengths,
    loop_counts,
    token_counts,
):
    row_count, block_len, model_width = block_input.shape
    head_count = H
    score_scale = (model_width // head_count) ** (-0.5)
    row_len = block_len * lax.axis_size("seq")
    flat_rows = row_count * block_len
    offset = lax.axis_index("seq") * block_len
    key_pos = jnp.arange(row_len, dtype=jnp.int32)
    own_pos = offset + jnp.arange(block_len, dtype=jnp.int32)
    seg_ends = jnp.cumsum(seg_lengths, axis=-1)
    seg_all = jnp.sum((seg_ends[:, None, :] <= key_pos[None, :, None]).astype(jnp.int32), axis=-1)
    seg_own = lax.dynamic_slice_in_dim(seg_all, offset, block_len, 1)
    allowed = (seg_own[:, :, None] == seg_all[:, None, :]) & (
        key_pos[None, None, :] <= own_pos[None, :, None]
    )
    current = block_input.astype(jnp.float32)
    inject = embedding.astype(jnp.float32)
    stored = []
    finals = []
    for repeat in range(2):
        current = current + inject
        for layer_index in range(LAYERS):
            forward_normed = layer_norm(
                current, norm_gain[layer_index, 0], norm_shift[layer_index, 0]
            ).astype(jnp.bfloat16)
            forward_packed = matmul(
                forward_normed.reshape(flat_rows, model_width), qkv_weight[layer_index]
            ).astype(jnp.bfloat16)
            forward_packed = forward_packed.reshape(row_count, block_len, 3 * model_width)
            forward_key_vals = lax.all_gather(
                forward_packed[:, :, model_width:], "seq", axis=1, tiled=True
            )

            def forward_row(inputs):
                return attend_forward(inputs[0], inputs[1], inputs[2], head_count, score_scale)

            forward_blended, forward_logsum = lax.map(
                forward_row, (forward_packed[:, :, :model_width], forward_key_vals, allowed)
            )
            forward_blended = forward_blended.astype(jnp.bfloat16)
            branch_out = matmul(
                forward_blended.reshape(flat_rows, model_width), out_weight[layer_index]
            ).reshape(row_count, block_len, model_width)
            forward_middle = current + branch_out + out_bias[layer_index]
            forward_normed_two = layer_norm(
                forward_middle, norm_gain[layer_index, 1], norm_shift[layer_index, 1]
            ).astype(jnp.bfloat16)
            forward_up_proj = (
                matmul(forward_normed_two.reshape(flat_rows, model_width), up_weight[layer_index])
                + up_bias[layer_index]
            )
            forward_active = gelu_exact(forward_up_proj).astype(jnp.bfloat16)
            result = (
                forward_middle
                + matmul(forward_active, down_weight[layer_index]).reshape(
                    row_count, block_len, model_width
                )
                + down_bias[layer_index]
            )
            current, stored_layer = (
                result,
                (
                    current,
                    forward_normed,
                    forward_packed,
                    forward_key_vals,
                    forward_logsum,
                    forward_blended,
                    forward_middle,
                    forward_normed_two,
                    forward_up_proj,
                    forward_active,
                ),
            )
            stored.append(stored_layer)
        finals.append(current)
    two_loops = (loop_counts == 2)[:, None, None]
    block_output = jnp.where(two_loops, finals[1], finals[0]).astype(jnp.bfloat16)
    row_weight = token_counts.astype(jnp.float32) / row_len
    grad_top = cotangent.astype(jnp.float32) * row_weight[:, None, None]
    grad_state = jnp.where(two_loops, grad_top, 0.0)
    layer_sums = [None] * LAYERS
    second_pass = grad_state
    for repeat in (1, 0):
        for layer_index in reversed(range(LAYERS)):
            backward_stored_layer = stored[repeat * LAYERS + layer_index]
            (
                backward_current,
                normed,
                packed,
                key_vals,
                logsum,
                blended,
                middle,
                normed_two,
                up_proj,
                active,
            ) = backward_stored_layer
            grad_flat = grad_state.reshape(flat_rows, model_width)
            grad_low = grad_flat.astype(jnp.bfloat16)
            grad_down = left_dot(active, grad_low)
            grad_down_bias = jnp.sum(grad_flat, axis=0)
            grad_active = right_dot(grad_low, down_weight[layer_index])
            grad_up_proj = jax.vjp(gelu_exact, up_proj)[1](grad_active)[0].astype(jnp.bfloat16)
            grad_up_bias = jnp.sum(grad_up_proj.astype(jnp.float32), axis=0)
            grad_up = left_dot(normed_two.reshape(flat_rows, model_width), grad_up_proj)
            grad_normed_two = right_dot(grad_up_proj, up_weight[layer_index]).reshape(
                row_count, block_len, model_width
            )
            pull_two = jax.vjp(
                layer_norm, middle, norm_gain[layer_index, 1], norm_shift[layer_index, 1]
            )[1]
            grad_middle, gain_two, shift_two = pull_two(grad_normed_two)
            grad_middle = grad_middle + grad_state
            middle_flat = grad_middle.reshape(flat_rows, model_width)
            middle_low = middle_flat.astype(jnp.bfloat16)
            grad_out = left_dot(blended.reshape(flat_rows, model_width), middle_low)
            grad_out_bias = jnp.sum(middle_flat, axis=0)
            grad_blend = (
                right_dot(middle_low, out_weight[layer_index])
                .astype(jnp.bfloat16)
                .reshape(row_count, block_len, model_width)
            )
            queries = packed[:, :, :model_width]

            def full_row(inputs):
                query_part, keyval_part, grad_part, allowed_part, logsum_part = inputs
                attn_probs, grad_probs = attention_core(
                    query_part,
                    keyval_part[:, :model_width],
                    keyval_part[:, model_width:],
                    grad_part,
                    allowed_part,
                    logsum_part,
                    head_count,
                    score_scale,
                )
                row_delta = jnp.sum(attn_probs * grad_probs, axis=-1, keepdims=True)
                grad_scores = (attn_probs * (grad_probs - row_delta)).astype(jnp.bfloat16)
                return (
                    query_grads(grad_scores, keyval_part[:, :model_width], head_count, score_scale),
                    keyval_grads(
                        grad_scores, attn_probs, query_part, grad_part, head_count, score_scale
                    ),
                )

            grad_query, partial_kv = lax.map(
                full_row, (queries, key_vals, grad_blend, allowed, logsum)
            )
            grad_keyval = lax.psum_scatter(
                partial_kv.astype(jnp.bfloat16), "seq", scatter_dimension=1, tiled=True
            )
            grad_packed = jnp.concatenate(
                [grad_query.astype(jnp.bfloat16), grad_keyval], axis=-1
            ).reshape(flat_rows, 3 * model_width)
            grad_qkv = left_dot(normed.reshape(flat_rows, model_width), grad_packed)
            grad_normed = right_dot(grad_packed, qkv_weight[layer_index]).reshape(
                row_count, block_len, model_width
            )
            pull_one = jax.vjp(
                layer_norm, backward_current, norm_gain[layer_index, 0], norm_shift[layer_index, 0]
            )[1]
            grad_current, gain_one, shift_one = pull_one(grad_normed)
            grad_current = grad_current + grad_middle
            grad_state = grad_current
            grad_set = (
                grad_qkv,
                grad_out,
                grad_out_bias,
                grad_up,
                grad_up_bias,
                grad_down,
                grad_down_bias,
                jnp.stack([gain_one, gain_two]),
                jnp.stack([shift_one, shift_two]),
            )
            if repeat == 1:
                layer_sums[layer_index] = grad_set
            else:
                layer_sums[layer_index] = jax.tree.map(jnp.add, layer_sums[layer_index], grad_set)
        if repeat == 1:
            second_pass = grad_state
            grad_state = jnp.where(two_loops, grad_state, grad_top)
    grad_embed = grad_state + second_pass
    stacked = jax.tree.map(lambda *members: jnp.stack(members), *layer_sums)
    (
        sum_qkv,
        sum_out,
        sum_out_bias,
        sum_up,
        sum_up_bias,
        sum_down,
        sum_down_bias,
        sum_gain,
        sum_shift,
    ) = stacked
    total = lax.psum(jnp.sum(token_counts), "dp").astype(jnp.float32)
    summed = lax.psum(
        (
            sum_qkv,
            sum_out,
            sum_out_bias,
            sum_up,
            sum_up_bias,
            sum_down,
            sum_down_bias,
            sum_gain,
            sum_shift,
        ),
        ("dp", "seq"),
    )
    input_scale = row_count * lax.axis_size("dp") * row_len / total
    weight_scale = row_len / total
    return (
        block_output,
        grad_state * input_scale,
        grad_embed * input_scale,
        summed[0] * weight_scale,
        summed[1] * weight_scale,
        summed[2] * weight_scale,
        summed[3] * weight_scale,
        summed[4] * weight_scale,
        summed[5] * weight_scale,
        summed[6] * weight_scale,
        summed[7] * weight_scale,
        summed[8] * weight_scale,
    )


BF = jnp.bfloat16
F32 = jnp.float32
ERF_TERMS = (7.97869712e-01, 3.63922863e-02, -8.78266373e-05, -3.66934271e-05, 1.42500458e-06)
DENSITY_RATE = -0.7213475204444817
DENSITY_BASE = -1.3257480647361593
VMEM_LIMIT = 24 * 1024 * 1024
ONES_ROWS = 16


def dot_nn(left_side, right_side):
    return jnp.dot(left_side, right_side, preferred_element_type=F32)


def dot_nt(left_side, right_side):
    return lax.dot_general(
        left_side, right_side, (((1,), (1,)), ((), ())), preferred_element_type=F32
    )


def gelu_and_slope(z):
    square = z * z
    series = ERF_TERMS[-1] * square + ERF_TERMS[-2]
    for term in ERF_TERMS[-3::-1]:
        series = series * square + term
    cdf = 0.5 + 0.5 * jnp.tanh(z * series)
    density = jnp.exp2(square * DENSITY_RATE + DENSITY_BASE)
    return z * cdf, cdf + z * density


def norm_forward(values, gain, shift):
    center = values - jnp.mean(values, axis=0, keepdims=True)
    spread = jnp.mean(center * center, axis=0, keepdims=True)
    inverse = lax.rsqrt(spread + NORM_EPS)
    unit = center * inverse
    return unit, inverse, (unit * gain + shift).astype(BF)


def norm_backward(grad, unit, inverse, gain):
    scaled = grad * gain
    first = jnp.mean(scaled, axis=0, keepdims=True)
    second = jnp.mean(scaled * unit, axis=0, keepdims=True)
    return inverse * (scaled - first - unit * second)


def columns(vec, tokens, spread=False):
    turned = vec[0].T

    def column(first, last):
        parts = [turned[:, k : k + 1] for k in range(first // 128, last // 128)]
        if spread:
            parts = [jnp.broadcast_to(part, (128, 128)) for part in parts]
            parts = [jnp.concatenate([part] * (tokens // 128), axis=1) for part in parts]
        return jnp.concatenate(parts, axis=0)

    return column


def project_qkv(state, qkv_t, vec, pre, kv, stat, scale, spread=False):
    width = state.shape[0]
    column = columns(vec, state.shape[1], spread)
    gain = column(2 * width, 3 * width)
    shift = column(3 * width, 4 * width)
    unit, inverse, normed = norm_forward(state, gain, shift)
    pre[0:width, :] = normed
    pre[2 * width : 3 * width, :] = unit.astype(BF)
    pre[width : 2 * width, :] = (dot_nn(qkv_t[0, 0:width, :], normed) * scale).astype(BF)
    kv[0:width, :] = dot_nn(qkv_t[0, width : 2 * width, :], normed).astype(BF)
    kv[width : 2 * width, :] = dot_nn(qkv_t[0, 2 * width : 3 * width, :], normed).astype(BF)
    stat[0:1, :] = inverse


def pad_head(block, odd):
    blank = jnp.zeros_like(block)
    return jnp.concatenate([blank, block] if odd else [block, blank], axis=0)


def tile_bias(first_key, start, causal, shape):
    key_at = lax.broadcasted_iota(jnp.int32, shape, 0)
    keep = key_at + first_key >= start
    if causal:
        keep = keep & (key_at <= lax.broadcasted_iota(jnp.int32, shape, 1))
    return jnp.where(keep, 0.0, MASKED)


def over_tiles(chunk, count, begin, half_tile, full_tile, carry, full_pair=None):
    half = count // 2
    first_half = begin // half
    odd = jnp.where(first_half < 2 * chunk, first_half % 2, 0)
    carry = lax.fori_loop(0, odd, lambda _, c: half_tile(first_half // 2, c), carry)
    first = (first_half + 1) // 2
    if full_pair is not None:
        pairs = jnp.maximum(chunk - first, 0) // 2
        carry = lax.fori_loop(0, pairs, lambda k, c: full_pair(first + 2 * k, c), carry)
        first = first + 2 * pairs
    return lax.fori_loop(first, chunk, full_tile, carry)


def attend_chunk(
    queries, keys, values_t, chunk, begin, start, bias, total, stat, blended, paired=False
):
    width, tokens = queries.shape
    head = width // H
    pair = 2 * head
    half = tokens // 2
    head_rows = [slice(h * head, (h + 1) * head) for h in range(H)]

    def scores(j, h, span):
        lanes = pl.ds((h // 2) * pair, pair)
        return dot_nn(keys[j, span, lanes], pad_head(queries[head_rows[h], :], h % 2))

    everything = slice(0, tokens)
    bias[:tokens, :] = tile_bias(chunk * tokens, start, True, (tokens, tokens))
    parts = [scores(chunk, h, everything) for h in range(H)]
    uppers = [part[:half, :] + bias[:half, :] for part in parts]
    lowers = [part[half:, half:] + bias[half:tokens, half:] for part in parts]
    tops, sums, weights = [], [], []
    for upper, lower in zip(uppers, lowers):
        top = jnp.max(upper, axis=0, keepdims=True)
        right = jnp.maximum(top[:, half:], jnp.max(lower, axis=0, keepdims=True))
        top = jnp.concatenate([top[:, :half], right], axis=1)
        upper = jnp.exp(upper - top)
        lower = jnp.exp(lower - right)
        added = jnp.sum(upper, axis=0, keepdims=True)
        right = added[:, half:] + jnp.sum(lower, axis=0, keepdims=True)
        tops.append(top)
        sums.append(jnp.concatenate([added[:, :half], right], axis=1))
        lower = lower.astype(BF)
        lower = jnp.concatenate([jnp.zeros_like(lower), lower], axis=1)
        weights.append(jnp.concatenate([upper.astype(BF), lower], axis=0))
    for rows, weight in zip(head_rows, weights):
        total[rows, :] = dot_nn(values_t[chunk, rows, :], weight)

    def step(tiles, span, size, carry):
        tops, sums = carry
        each_part, spans = [], []
        for at, j in enumerate(tiles):
            mask = slice(at * tokens, at * tokens + size)
            bias[mask, :] = tile_bias(j * tokens + span.start, start, False, (size, tokens))
            each_part.append([scores(j, h, span) + bias[mask, :] for h in range(H)])
        new_tops = list(tops)
        for parts in each_part:
            new_tops = [
                jnp.maximum(old, jnp.max(part, axis=0, keepdims=True))
                for old, part in zip(new_tops, parts)
            ]
        fades = [jnp.exp(old - new) for old, new in zip(tops, new_tops)]
        sums = [old * fade for old, fade in zip(sums, fades)]
        each_weight = [
            [jnp.exp(part - top) for part, top in zip(parts, new_tops)] for parts in each_part
        ]
        terms = [0.0] * H
        for j, weights in zip(tiles, each_weight):
            sums = [
                old + jnp.sum(weight, axis=0, keepdims=True)
                for old, weight in zip(sums, weights)
            ]
            terms = [
                old + dot_nn(values_t[j, rows, span], weight.astype(BF))
                for old, rows, weight in zip(terms, head_rows, weights)
            ]
        for rows, term, fade in zip(head_rows, terms, fades):
            total[rows, :] = total[rows, :] * fade + term
        return tuple(new_tops), tuple(sums)

    tops, sums = over_tiles(
        chunk, tokens, begin,
        lambda j, carry: step([j], slice(half, tokens), half, carry),
        lambda j, carry: step([j], everything, tokens, carry),
        (tuple(tops), tuple(sums)),
        (lambda j, carry: step([j, j + 1], everything, tokens, carry)) if paired else None,
    )
    for h, rows in enumerate(head_rows):
        blended[rows, :] = (total[rows, :] / sums[h]).astype(BF)
        stat[h : h + 1, :] = tops[h] + jnp.log(sums[h])


def finish_layer(state, out_t, up_t, down_t, vec, post, stat, spread=False):
    width, tokens = state.shape
    hidden = up_t.shape[1]
    column = columns(vec, tokens, spread)
    middle = state + dot_nn(out_t[0], post[0:width, :]) + column(0, width)
    gain = column(4 * width, 5 * width)
    shift = column(5 * width, 6 * width)
    unit, inverse, normed = norm_forward(middle, gain, shift)
    post[width : 2 * width, :] = normed
    post[2 * width : 3 * width, :] = unit.astype(BF)
    stat[H : H + 1, :] = inverse
    z = dot_nn(up_t[0], normed) + column(6 * width, 6 * width + hidden)
    active, slope = gelu_and_slope(z)
    post[3 * width : 3 * width + hidden, :] = active.astype(BF)
    post[3 * width + hidden :, :] = slope.astype(BF)
    return (
        middle
        + dot_nn(down_t[0], post[3 * width : 3 * width + hidden, :])
        + column(width, 2 * width)
    )


def launch(
    name, body, place, grid, ins, outs, scratch=(), flops=0, aliases=(), near=(), free=(),
    on_split=True,
):
    scratch = dict(scratch)
    names = [*ins, *outs, *scratch]

    def kernel(here, loops, counts, lengths, *refs):
        me, split = here[0], here[1]
        row = split if on_split else row_of_slot(me, split, loops.shape[0])
        facts = types.SimpleNamespace(
            me=me, split=split, slot=here[2], two=loops[row] == 2, count=counts[row], counts=counts,
            all_lengths=lengths, lengths=[lengths[row, k] for k in range(lengths.shape[1])],
        )
        body(facts, types.SimpleNamespace(**dict(zip(names, refs))))

    space = lambda key: pltpu.VMEM if key in near else pltpu.HBM
    results = pl.pallas_call(
        kernel,
        grid_spec=pltpu.PrefetchScalarGridSpec(
            num_scalar_prefetch=len(place),
            grid=(grid,),
            in_specs=[spec for _, spec in ins.values()],
            out_specs=[spec for _, spec in outs.values()],
            scratch_shapes=list(scratch.values()),
        ),
        out_shape=[
            shape if key in free else space(key)(shape.shape, shape.dtype)
            for key, (shape, _) in outs.items()
        ],
        input_output_aliases={
            len(place) + list(ins).index(source): list(outs).index(target) for source, target in aliases
        },
        compiler_params=pltpu.CompilerParams(vmem_limit_bytes=VMEM_LIMIT),
        cost_estimate=pl.CostEstimate(flops=flops, bytes_accessed=1, transcendentals=0),
        name=name,
    )(
        *[pltpu.with_memory_space_constraint(array, pltpu.HBM) for array in place],
        *[
            array if key in free else pltpu.with_memory_space_constraint(array, space(key))
            for key, (array, _) in ins.items()
        ],
    )
    return dict(zip(outs, results))


def whole(array):
    return array, pl.BlockSpec(array.shape, lambda i, *_: (0,) * len(array.shape))


def of_layer(array, layer):
    return array, pl.BlockSpec((1,) + array.shape[1:], lambda i, *_: (layer, 0, 0))


def each(array):
    return array, pl.BlockSpec((1,) + array.shape[1:], lambda i, *_: (i, 0, 0))


def each_back(array):
    count = array.shape[0]
    return array, pl.BlockSpec(
        (1,) + array.shape[1:], lambda i, *_: (count - 1 - i, 0, 0)
    )


def shaped(dims, dtype):
    return jax.ShapeDtypeStruct(dims, dtype)


def segment_starts(place, first, count):
    position = lax.broadcasted_iota(jnp.int32, (1, count), 1) + first
    starts = jnp.zeros((1, count), jnp.int32)
    end = jnp.int32(0)
    begin = jnp.int32(0)
    for length in place.lengths:
        end = end + length
        starts = jnp.where(position >= end, end, starts)
        begin = jnp.where(first >= end, end, begin)
    return starts, begin


def gather_tokens(env, name, me):
    for hop in range(4):
        env.spread[me ^ hop] = getattr(env, f"{name}_{hop}")[...]


def deal_tokens(env, name, value, chunk, me):
    for hop in range(4):

        @pl.when(chunk == (me ^ hop))
        def _(hop=hop):
            getattr(env, f"{name}_{hop}")[...] = value


def token_ins(name, blocks):
    return {f"{name}_{hop}": whole(block) for hop, block in enumerate(blocks)}


def token_outs(name, tokens, width):
    return {f"{name}_{hop}": whole(shaped((tokens, width), BF)) for hop in range(4)}


def as_tokens(values):
    return values.astype(BF).T


def as_features(tokens):
    return tokens.T.astype(F32)


def forward_rows(layer, place, vec, weights, state=None, tokens=None, first_end=None):
    chunks = 4
    count = state.shape[2] if tokens is None else tokens[0].shape[0]
    qkv_t, out_t, up_t, down_t = weights
    width, hidden = out_t.shape[2], up_t.shape[1]
    post_rows = 3 * width + 2 * hidden

    def body(place, env):
        chunk = pl.program_id(0)
        me = place.me
        current = env.state.at[0] if state is not None else None
        if tokens is not None:

            @pl.when(chunk == 0)
            def _():
                gather_tokens(env, "tokens", me)

            added = as_features(env.spread[chunk])
            env.current[...] = added if state is None else added + env.state[0]
            current = env.current
        project_qkv(
            current[...], env.qkv_t, env.vec, env.pre.at[0], env.kv.at[0], env.stat_pre.at[0],
            (width // H) ** -0.5, spread=True,
        )
        env.keys[chunk] = env.kv[0, 0:width, :].T
        env.values_t[chunk] = env.kv[0, width : 2 * width, :]
        start, begin = segment_starts(place, chunk * count, count)
        attend_chunk(
            env.pre.at[0, width : 2 * width, :], env.keys, env.values_t, chunk, begin, start, env.bias, env.total, env.stat_post.at[0],
            env.post.at[0, 0:width, :],
        )
        result = finish_layer(
            current[...], env.out_t, env.up_t, env.down_t, env.vec, env.post.at[0],
            env.stat_post.at[0], spread=True,
        )
        if first_end is None:
            env.result[0] = result
        else:
            answer = jnp.where(place.two, result, env.first_end[0])
            deal_tokens(env, "answer", as_tokens(answer), chunk, me)

    ins = {"vec": of_layer(vec, layer)}
    for name, weight in zip(("qkv_t", "out_t", "up_t", "down_t"), weights):
        ins[name] = of_layer(weight, layer)
    scratch = {
        "keys": pltpu.VMEM((chunks, count, width), BF),
        "values_t": pltpu.VMEM((chunks, width, count), BF),
        "bias": pltpu.VMEM((count, count), F32),
        "total": pltpu.VMEM((width, count), F32),
    }
    if state is not None:
        ins["state"] = each(state)
    if tokens is not None:
        ins |= token_ins("tokens", tokens)
        scratch["spread"] = pltpu.VMEM((chunks, count, width), BF)
        scratch["current"] = pltpu.VMEM((width, count), F32)
    outs = {}
    if first_end is None:
        outs["result"] = each(shaped((chunks, width, count), F32))
    else:
        ins["first_end"] = each(first_end)
        outs |= token_outs("answer", count, width)
    outs["pre"] = each(shaped((chunks, 3 * width, count), BF))
    outs["kv"] = each(shaped((chunks, 2 * width, count), BF))
    outs["post"] = each(shaped((chunks, post_rows, count), BF))
    outs["stat_pre"] = each(shaped((chunks, 8, count), F32))
    outs["stat_post"] = each(shaped((chunks, 8, count), F32))
    flops = chunks * count * 6 * (4 * width * width + 2 * width * hidden)
    return launch(
        "forward_rows", body, place, chunks, ins, outs, scratch, flops,
        on_split=False,
        near=["state", "result", "vec", "qkv_t", "out_t", "up_t", "down_t"]
        + [f"tokens_{hop}" for hop in range(4) if state is None],
    )


def split_row(array):
    return array, pl.BlockSpec((1,) + array.shape[1:], lambda i, here, *_: (here[1], 0, 0))


def row_of_slot(slot, split, rows):
    return jnp.where(slot == split, rows - 1, slot)


def forward_split(
    place, vec, weights, last=None, following=None, state=None, prev=None, pre=None,
    block_input=None, embedding=None, first_end=None, only_parts=False,
):
    qkv_t, out_t, up_t, down_t = weights
    width, hidden = out_t.shape[2], up_t.shape[1]
    count = embedding.shape[1] if state is None else state.shape[1]

    def body(place, env):
        me = place.me
        if last is not None:
            for hop in range(4):
                arrived = getattr(env, f"kv_{hop}")
                env.keys[me ^ hop] = arrived[0:width, :].T
                env.values_t[me ^ hop] = arrived[width : 2 * width, :]
            start, begin = segment_starts(place, me * count, count)
            attend_chunk(
                env.pre_in.at[width : 2 * width, :], env.keys, env.values_t, me, begin, start,
                env.bias, env.total, env.stat_post, env.post.at[0:width, :], paired=True,
            )
            current = finish_layer(
                env.state[...], env.out_t, env.up_t, env.down_t, env.vec, env.post, env.stat_post
            )
            if first_end is not None:
                answer = jnp.where(place.two, current, env.first_end[...])
                env.answer[...] = as_tokens(answer)
            else:
                env.result[...] = current
        if following is not None:
            if embedding is not None:
                added = as_features(env.embedding[0])
                if last is None:
                    current = as_features(env.block_input[0]) + added
                else:
                    current = env.result[...] + added
                env.begun[...] = current
            project_qkv(
                current, env.qkv_t, env.vec_next, env.pre, env.kv, env.stat_pre,
                (width // H) ** -0.5,
            )

    ins, outs, scratch = {}, {}, {}
    if last is not None:
        ins |= {f"kv_{hop}": whole(block) for hop, block in enumerate(prev)}
        ins |= {"state": whole(state), "pre_in": whole(pre)}
        ins["vec"] = of_layer(vec, last)
        for name, weight in zip(("out_t", "up_t", "down_t"), weights[1:]):
            ins[name] = of_layer(weight, last)
        if first_end is not None:
            ins["first_end"] = whole(first_end)
            outs["answer"] = whole(shaped((count, width), BF))
        else:
            outs["result"] = whole(shaped((width, count), F32))
        outs["post"] = whole(shaped((3 * width + 2 * hidden, count), BF))
        outs["stat_post"] = whole(shaped((8, count), F32))
        scratch = {
            "keys": pltpu.VMEM((4, count, width), BF),
            "values_t": pltpu.VMEM((4, width, count), BF),
            "bias": pltpu.VMEM((2 * count, count), F32),
            "total": pltpu.VMEM((width, count), F32),
        }
    if following is not None:
        ins["vec_next"] = of_layer(vec, following)
        ins["qkv_t"] = of_layer(qkv_t, following)
        if embedding is not None:
            ins["embedding"] = split_row(embedding)
            outs["begun"] = whole(shaped((width, count), F32))
        if block_input is not None:
            ins["block_input"] = split_row(block_input)
        outs["pre"] = whole(shaped((3 * width, count), BF))
        outs["kv"] = whole(shaped((2 * width, count), BF))
        outs["stat_pre"] = whole(shaped((8, count), F32))
    flops = 0 if last is None else count * 6 * (4 * width * width + 2 * width * hidden)
    near = ["state", "result", "begun", "pre", "pre_in", "kv", "vec", "vec_next"]
    near += ["qkv_t", "out_t", "up_t", "down_t"] + [f"kv_{hop}" for hop in range(4)]
    if only_parts:
        return body, ins, outs, scratch, near
    return launch("forward_split", body, place, 1, ins, outs, scratch, flops, near=near)


def backward_ffn(grad, post, stat, wout, wup, wdown, vec, hidden_grad):
    width, tokens = grad.shape
    hidden = wup.shape[2]
    low_grad = grad.astype(BF)
    hidden_grad[...] = (
        dot_nn(wdown[0], low_grad) * post[3 * width + hidden :, :].astype(F32)
    ).astype(BF)
    normed_grad = dot_nn(wup[0], hidden_grad[...])
    unit = post[2 * width : 3 * width, :].astype(F32)
    gain = columns(vec, tokens)(4 * width, 5 * width)
    middle = grad + norm_backward(normed_grad, unit, stat[H : H + 1, :], gain)
    low_middle = middle.astype(BF)
    blend_grad = dot_nn(wout[0], low_middle).astype(BF)
    return low_grad, normed_grad, unit, middle, low_middle, blend_grad


def token_sum(rows):
    return dot_nt(jnp.ones((ONES_ROWS, rows.shape[1]), BF), rows.astype(BF))


def attend_backward(
    queries, blend_grad, blended, stat, keys, values, keys_t, chunk, begin, start,
    bias, query_grad, kv_grad, paired=False,
):
    width, tokens = queries.shape
    head = width // H
    pair = 2 * head
    head_rows = [slice(h * head, (h + 1) * head) for h in range(H)]
    deltas = [
        jnp.sum(
            blend_grad[rows, :].astype(F32) * blended[rows, :].astype(F32), axis=0, keepdims=True
        )
        for rows in head_rows
    ]

    half = tokens // 2
    everything = slice(0, tokens)

    def products(j, span):
        parts, prob_grads = [], []
        for h, rows in enumerate(head_rows):
            lanes = pl.ds((h // 2) * pair, pair)
            parts.append(dot_nn(keys[j, span, lanes], pad_head(queries[rows, :], h % 2)))
            prob_grads.append(
                dot_nn(values[j, span, lanes], pad_head(blend_grad[rows, :], h % 2))
            )
        return parts, prob_grads

    def collect(j, span, probs, score_grads, first):
        for rows, prob, score_grad in zip(head_rows, probs, score_grads):
            value_rows = slice(width + rows.start, width + rows.stop)
            kv_grad[j, value_rows, span] += dot_nt(blend_grad[rows, :], prob)
            kv_grad[j, rows, span] += dot_nt(queries[rows, :], score_grad)
            term = dot_nn(keys_t(j, rows, span), score_grad)
            if first:
                query_grad[rows, :] = term
            else:
                query_grad[rows, :] += term

    def weigh(part, prob_grad, mask, logsum, delta):
        prob = jnp.exp(part + mask - logsum)
        return prob.astype(BF), (prob * (prob_grad - delta)).astype(BF)

    bias[:tokens, :] = tile_bias(chunk * tokens, start, True, (tokens, tokens))
    probs, score_grads = [], []
    for h, (part, prob_grad) in enumerate(zip(*products(chunk, everything))):
        logsum, delta = stat[h : h + 1, :], deltas[h]
        upper = weigh(part[:half, :], prob_grad[:half, :], bias[:half, :], logsum, delta)
        lower = weigh(
            part[half:, half:], prob_grad[half:, half:], bias[half:tokens, half:], logsum[:, half:],
            delta[:, half:],
        )
        for kept, above, below in zip((probs, score_grads), upper, lower):
            below = jnp.concatenate([jnp.zeros_like(below), below], axis=1)
            kept.append(jnp.concatenate([above, below], axis=0))
    collect(chunk, everything, probs, score_grads, True)

    def step(tiles, span, size, carry):
        made = []
        for at, j in enumerate(tiles):
            mask = slice(at * tokens, at * tokens + size)
            bias[mask, :] = tile_bias(j * tokens + span.start, start, False, (size, tokens))
            made.append((mask, *products(j, span)))
        weighed = [
            [
                weigh(part, prob_grad, bias[mask, :], stat[h : h + 1, :], deltas[h])
                for h, (part, prob_grad) in enumerate(zip(parts, prob_grads))
            ]
            for mask, parts, prob_grads in made
        ]
        for j, pairs in zip(tiles, weighed):
            collect(j, span, [p for p, _ in pairs], [d for _, d in pairs], False)
        return carry

    over_tiles(
        chunk, tokens, begin,
        lambda j, carry: step([j], slice(half, tokens), half, carry),
        lambda j, carry: step([j], everything, tokens, carry),
        0,
        (lambda j, carry: step([j, j + 1], everything, tokens, carry)) if paired else None,
    )


def add_vec(sum_vec, width, low_grad, normed_grad, unit, low_middle, dz):
    sum_vec[:, 0:width] += token_sum(low_middle)
    sum_vec[:, width : 2 * width] += token_sum(low_grad)
    sum_vec[:, 4 * width : 5 * width] += token_sum(normed_grad * unit)
    sum_vec[:, 5 * width : 6 * width] += token_sum(normed_grad)
    sum_vec[:, 6 * width :] += token_sum(dz)


def finish_backward(middle, pre, stat, packed, wqkv, vec, sum_qkv, sum_vec):
    width, tokens = middle.shape
    sum_qkv[...] += dot_nt(pre[0:width, :], packed[...])
    normed_grad = dot_nn(wqkv[0], packed[...])
    unit = pre[2 * width : 3 * width, :].astype(F32)
    gain = columns(vec, tokens)(2 * width, 3 * width)
    sum_vec[:, 2 * width : 3 * width] += token_sum(normed_grad * unit)
    sum_vec[:, 3 * width : 4 * width] += token_sum(normed_grad)
    return middle + norm_backward(normed_grad, unit, stat[0:1, :], gain)


def pack_lanes(wire, blocks):
    at = 0
    for ref in blocks:
        rows = ref.shape[0]
        for first in range(0, ref.shape[1], 128):
            wire[at : at + rows, :] = ref[:, first : first + 128].astype(BF)
            at += rows


def put_pieces(keep, give, source, first, height, core):
    half = keep.shape[0]
    for ref, side in ((keep, core), (give, 1 - core)):
        for p in range(half):
            at = pl.multiple_of((side * half + p) * height, 16)
            ref[p, first : first + height, :] = source[pl.ds(at, height), :]


def count_digits(place, groups):
    tally = place.counts[0]
    for k in range(1, place.counts.shape[0]):
        tally = tally + place.counts[k]
    lane = lax.broadcasted_iota(jnp.int32, (16, 128), 1)
    row = lax.broadcasted_iota(jnp.int32, (16, 128), 0)
    digit = jnp.where(lane % 2 == 0, tally // 256, tally % 256)
    keep = (lane // 2 == place.slot) & (row == 0) & (place.me == 0)
    return jnp.where(keep, digit, 0).astype(F32).astype(BF)


def backward_rows(
    layer, place, saved, vec, weights, five, base=None, grad=None, tokens=None,
    keep=True, travel=False, part_done=None, ffn_only=False, half=0, digits=False,
    closing=None, others=None,
):
    chunks, _, count = saved["kv"].shape
    wqkv, wout, wup, wdown = weights
    width, hidden = wup.shape[1:]
    row_len = chunks * count
    first = base is None
    part = hidden // chunks
    vec_len = 6 * width + hidden
    with_ffn, with_attention = part_done is None, not ffn_only

    def body(place, env):
        order = pl.program_id(0)
        chunk = chunks - 1 - order
        me = place.me

        @pl.when(order == 0)
        def _():
            if tokens is not None:
                gather_tokens(env, "tokens", me)
            if with_ffn:
                env.sum_up[...] = jnp.zeros_like(env.sum_up)
                env.sum_down[...] = jnp.zeros_like(env.sum_down)
                env.sum_out[...] = dot_nt(env.blend_five[...], env.middle_five[...])
                env.sum_vec[...] = env.vec_five[...]
                if not first:
                    env.sum_vec[...] += env.base_vec[...]
            else:
                env.sum_vec[...] = env.vec_done[...]
            if with_attention:
                env.sum_qkv[...] = jnp.zeros_like(env.sum_qkv)
                env.kv_grad[...] = jnp.zeros_like(env.kv_grad)
                for j in range(chunks):
                    env.keys[j] = env.kv[j, 0:width, :].T
                    env.values[j] = env.kv[j, width : 2 * width, :].T

        def add_base(ref, old):
            rows = old.shape[0]
            ref[pl.ds(pl.multiple_of(order * rows, rows), rows), :] += old[...]

        if with_ffn:
            spread = pl.ds(pl.multiple_of(order * part, part), part)
            env.sum_down[spread, :] += dot_nt(env.active_five[...], env.low_five[...])
            env.sum_up[:, spread] += dot_nt(env.normed_five[...], env.hidden_five[...])
            if not first:
                env.sum_down[spread, :] += env.base_down[...]
                env.sum_up[:, spread] += env.base_up[...]
                add_base(env.sum_out, env.base_out)
            current = env.grad.at[0] if grad is not None else None
            if tokens is not None:
                top = as_features(env.spread[chunk]) * (place.count.astype(F32) * (1.0 / row_len))
                two = place.two
                env.current[...] = (
                    jnp.where(two, top, 0.0)
                    if grad is None
                    else jnp.where(two, env.grad[0], top)
                )
                current = env.current
            post = env.post.at[0]
            low_grad, normed_grad, unit, middle, low_middle, blend_grad = backward_ffn(
                current[...], post, env.stat_post.at[0], env.wout, env.wup, env.wdown, env.vec,
                env.hidden_grad,
            )
            env.sum_down[...] += dot_nt(post[3 * width : 3 * width + hidden, :], low_grad)
            env.sum_up[...] += dot_nt(post[width : 2 * width, :], env.hidden_grad[...])
            env.sum_out[...] += dot_nt(post[0:width, :], low_middle)
            add_vec(
                env.sum_vec, width, low_grad, normed_grad, unit, low_middle, env.hidden_grad[...]
            )
            blend_ref = env.blend_grad if with_attention else env.blend_out.at[0]
            blend_ref[...] = blend_grad
            if not first:

                @pl.when(order == chunks - 1)
                def _():
                    pack_lanes(env.wire, (env.sum_out, env.sum_up, env.sum_down))
                    height = env.wire.shape[0] // (2 * half)
                    put_pieces(env.keep, env.give, env.wire, 0, height, me % 2)
                    if digits:
                        blank = jnp.zeros((16, 128), BF)
                        for p in range(half):
                            env.keep[p, height:, :] = count_digits(place, half) if p == 0 else blank
                            env.give[p, height:, :] = blank

            if not with_attention:
                env.middle_out[0] = middle
                return
            blended = post.at[0:width, :]
        else:
            middle, blend_ref, blended = env.middle_in[0], env.blend_in.at[0], env.blended.at[0]
        if not first:
            add_base(env.sum_qkv, env.base_qkv)
        start, begin = segment_starts(place, chunk * count, count)
        attend_backward(
            env.pre.at[0, width : 2 * width, :], blend_ref, blended,
            env.stat_post.at[0], env.keys, env.values, lambda j, rows, span: env.kv[j, rows, span],
            chunk, begin, start, env.bias, env.query_grad, env.kv_grad,
        )
        env.packed[0:width, :] = (env.query_grad[...] * (width // H) ** -0.5).astype(BF)
        env.packed[width : 3 * width, :] = env.kv_grad[chunk].astype(BF)
        result = finish_backward(
            middle, env.pre.at[0], env.stat_pre.at[0], env.packed, env.wqkv, env.vec,
            env.sum_qkv, env.sum_vec,
        )
        if keep:
            env.result[0] = result
        if travel:
            deal_tokens(env, "travel", as_tokens(result), chunk, me)
        if closing is not None:

            @pl.when(order == chunks - 1)
            def _():
                ended = end_split_row(env, env.vec, env.sum_qkv, env.sum_vec)
                env.split_result[...] = ended.T
                write_last_payload(env, half, me % 2)

    ins = {"vec": of_layer(vec, layer), "stat_post": each_back(saved["stat_post"])}
    outs, scratch = {}, {}
    cut = lambda array, shape, at: (array, pl.BlockSpec(shape, lambda i, *_: at(i)))
    sums = {"sum_vec": (ONES_ROWS, vec_len)}
    if with_ffn:
        ins["post"] = each_back(saved["post"])
        for name, weight in zip(("wout", "wup", "wdown"), weights[1:]):
            ins[name] = of_layer(weight, layer)
        if grad is not None:
            ins["grad"] = each_back(grad)
        if tokens is not None:
            ins |= token_ins("tokens", tokens)
            scratch["spread"] = pltpu.VMEM((chunks, count, width), BF)
            scratch["current"] = pltpu.VMEM((width, count), F32)
        post_five = five["post"]
        ins["blend_five"] = cut(post_five, (width, count), lambda i: (0, 0))
        ins["normed_five"] = cut(post_five, (width, count), lambda i: (1, 0))
        ins["active_five"] = cut(post_five, (part, count), lambda i: (3 * width // part + i, 0))
        ins["hidden_five"] = cut(five["hidden"], (part, count), lambda i: (i, 0))
        for name in ("low", "middle", "vec"):
            ins[name + "_five"] = whole(five[name])
        sums |= {"sum_out": (width, width), "sum_up": (width, hidden), "sum_down": (hidden, width)}
        scratch["hidden_grad"] = pltpu.VMEM((hidden, count), BF)
        if not first:
            ins["base_out"] = cut(base["sum_out"], (width // chunks, width), lambda i: (i, 0))
            ins["base_up"] = cut(base["sum_up"], (width, part), lambda i: (0, i))
            ins["base_down"] = cut(base["sum_down"], (part, width), lambda i: (i, 0))
            ins["base_vec"] = whole(base["sum_vec"])
            wire_rows = (width * width + 2 * width * hidden) // 128
            scratch["wire"] = pltpu.VMEM((wire_rows, 128), BF)
            height = wire_rows // (2 * half) + (16 if digits else 0)
            outs["keep"] = whole(shaped((half, height, 128), BF))
            outs["give"] = whole(shaped((half, height, 128), BF))
        if not with_attention:
            outs["blend_out"] = each_back(shaped((chunks, width, count), BF))
            outs["middle_out"] = each_back(shaped((chunks, width, count), F32))
    else:
        ins["vec_done"] = whole(part_done["sum_vec"])
        ins["middle_in"] = each_back(part_done["middle_out"])
        ins["blend_in"] = each_back(part_done["blend_out"])
        ins["blended"] = (
            saved["post"],
            pl.BlockSpec((1, width, count), lambda i, *_: (chunks - 1 - i, 0, 0)),
        )
    if with_attention:
        ins["kv"] = whole(saved["kv"])
        ins["pre"] = each_back(saved["pre"])
        ins["stat_pre"] = each_back(saved["stat_pre"])
        ins["wqkv"] = of_layer(wqkv, layer)
        sums["sum_qkv"] = (width, 3 * width)
        if not first:
            ins["base_qkv"] = cut(base["sum_qkv"], (width // chunks, 3 * width), lambda i: (i, 0))
        if keep:
            outs["result"] = each_back(shaped((chunks, width, count), F32))
        if travel:
            outs |= token_outs("travel", count, width)
        scratch |= {
            "keys": pltpu.VMEM((chunks, count, width), BF),
            "values": pltpu.VMEM((chunks, count, width), BF),
            "bias": pltpu.VMEM((count, count), F32),
            "query_grad": pltpu.VMEM((width, count), F32),
            "kv_grad": pltpu.VMEM((chunks, 2 * width, count), F32),
            "blend_grad": pltpu.VMEM((width, count), BF),
            "packed": pltpu.VMEM((3 * width, count), BF),
        }
    if closing is not None:
        ins |= split_row_ins(closing)
        wire_rows = 3 * width * width // 128
        height = 2 * (wire_rows // (2 * half)) + 16
        ins["wire_other"] = whole(others["wire"])
        ins["vec_other"] = whole(others["vec"])
        outs["keep"] = whole(shaped((half, height, 128), BF))
        outs["give"] = whole(shaped((half, height, 128), BF))
        outs["split_result"] = whole(shaped((count, width), F32))
        scratch["wire"] = pltpu.VMEM((wire_rows, 128), BF)
        scratch["small"] = pltpu.VMEM((4 * half, 128), F32)
        scratch |= {name: pltpu.VMEM(dims, F32) for name, dims in sums.items()}
        sums = {}
    for name, dims in sums.items():
        if first or name in ("sum_qkv", "sum_vec"):
            outs[name] = whole(shaped(dims, F32))
        else:
            scratch[name] = pltpu.VMEM(dims, F32)
    flops = chunks * count * 12 * (4 * width * width + 2 * width * hidden)
    return launch(
        "backward_rows", body, place, chunks, ins, outs, scratch, flops, on_split=False,
        near=[
            "middle_in_split", "query_in", "own_in", "in_1", "in_2", "in_3",
            "hidden_five", "low_five", "middle_five", "vec_five",
        ],
    )


def split_row_ins(ended):
    ins = {
        "middle_in_split": whole(ended["middle_out"]), "query_in": whole(ended["query_out"]),
        "own_in": whole(ended["own_out"]), "pre_last": whole(ended["pre"]),
        "stat_last": whole(ended["stat_pre"]),
    }
    return ins | {f"in_{hop}": whole(ended["arrived"][hop - 1]) for hop in range(1, 4)}


def end_split_row(env, vec, sum_qkv, sum_vec):
    width = env.query_in.shape[0]
    env.packed[0:width, :] = env.query_in[...]
    kv_total = env.own_in[...]
    for hop in range(1, 4):
        kv_total = kv_total + getattr(env, f"in_{hop}")[...].astype(F32)
    env.packed[width : 3 * width, :] = kv_total.astype(BF)
    return finish_backward(
        env.middle_in_split[...], env.pre_last, env.stat_last, env.packed, env.wqkv, vec,
        sum_qkv, sum_vec,
    )


def write_last_payload(env, half, core):
    pack_lanes(env.wire, (env.sum_qkv,))
    height = env.wire.shape[0] // (2 * half)
    put_pieces(env.keep, env.give, env.wire, 0, height, core)
    put_pieces(env.keep, env.give, env.wire_other, height, height, core)
    rows = env.sum_vec.shape[1] // 128
    env.small[...] = jnp.zeros_like(env.small)
    for at, ref in ((0, env.sum_vec), (rows, env.vec_other)):
        for k in range(rows):
            env.small[at + k : at + k + 1, :] = ref[0:1, 128 * k : 128 * k + 128]
    for p in range(half):
        left = env.small[2 * p : 2 * p + 2, :]
        right = env.small[2 * (p + half) : 2 * (p + half) + 2, :]
        for ref, first in ((env.keep, core == 0), (env.give, core == 1)):
            pair = jnp.where(first, left, right)
            blank = jnp.zeros((14, 128), F32)
            ref[p, 2 * height :, :] = jnp.concatenate([pair, blank]).astype(BF)


def backward_split(
    place, vec, weights, last=None, following=None, ended=None, sums=None, begun=None,
    cotangent=None, final=False, keep=False, row_len=None, only_parts=False,
):
    wqkv, wout, wup, wdown = weights
    width, hidden = wup.shape[1:]
    vec_len = 6 * width + hidden
    count = (ended or begun)["stat_pre"].shape[1]

    def body(place, env):
        me = place.me
        if last is not None:
            sum_qkv = env.total_qkv if final else env.sum_qkv
            sum_qkv[...] = env.old_qkv[...]
            env.sum_vec[...] = env.old_vec[...]
            current = end_split_row(env, env.vec_last, sum_qkv, env.sum_vec)
            if keep:
                env.result[...] = current.T
            if final:
                pack_lanes(env.wire, (sum_qkv,))
        if following is not None:
            if cotangent is not None:
                top = as_features(env.cotangent[0]) * (place.count.astype(F32) * (1.0 / row_len))
                two = place.two
                grad = jnp.where(two, top, 0.0) if last is None else jnp.where(two, current, top)
            else:
                grad = current
            env.kv_grad[...] = jnp.zeros_like(env.kv_grad)
            for hop in range(4):
                arrived = getattr(env, f"kv_{hop}")
                env.keys[me ^ hop] = arrived[0:width, :].T
                env.keys_t[me ^ hop] = arrived[0:width, :]
                env.values[me ^ hop] = arrived[width : 2 * width, :].T
            low_grad, normed_grad, unit, middle, low_middle, blend_grad = backward_ffn(
                grad, env.post, env.stat_post, env.wout, env.wup, env.wdown, env.vec, env.hidden
            )
            env.low[...] = low_grad
            env.middle[...] = low_middle
            env.middle_out[...] = middle
            env.vec_out[...] = jnp.zeros_like(env.vec_out)
            add_vec(
                env.vec_out, width, low_grad, normed_grad, unit, low_middle, env.hidden[...]
            )
            env.blend_grad[...] = blend_grad
            start, begin = segment_starts(place, me * count, count)
            attend_backward(
                env.pre.at[width : 2 * width, :], env.blend_grad, env.post.at[0:width, :],
                env.stat_post, env.keys, env.values, lambda j, rows, span: env.keys_t[j, rows, span],
                me, begin, start, env.bias, env.query_grad, env.kv_grad, paired=True,
            )
            env.query_out[...] = (env.query_grad[...] * (width // H) ** -0.5).astype(BF)
            env.own_out[...] = env.kv_grad[me]
            for hop in range(1, 4):
                getattr(env, f"away_{hop}")[...] = env.kv_grad[me ^ hop].astype(BF)

    ins, outs, scratch = {}, {}, {}
    if last is not None:
        ins |= split_row_ins(ended)
        ins["vec_last"] = of_layer(vec, last)
        ins["wqkv"] = of_layer(wqkv, last)
        ins["old_qkv"] = whole(sums["sum_qkv"])
        ins["old_vec"] = whole(sums["sum_vec"])
        if keep:
            outs["result"] = whole(shaped((count, width), F32))
        if final:
            outs["wire"] = whole(shaped((3 * width * width // 128, 128), BF))
        if final:
            scratch["total_qkv"] = pltpu.VMEM((width, 3 * width), F32)
        else:
            outs["sum_qkv"] = whole(shaped((width, 3 * width), F32))
        outs["sum_vec"] = whole(shaped((ONES_ROWS, vec_len), F32))
        scratch["packed"] = pltpu.VMEM((3 * width, count), BF)
    if following is not None:
        for name in ("pre", "post", "stat_post"):
            ins[name] = whole(begun[name])
        for hop in range(4):
            ins[f"kv_{hop}"] = whole(begun["kv"][hop])
        ins["vec"] = of_layer(vec, following)
        for name, weight in zip(("wout", "wup", "wdown"), weights[1:]):
            ins[name] = of_layer(weight, following)
        if cotangent is not None:
            ins["cotangent"] = split_row(cotangent)
        outs["middle_out"] = whole(shaped((width, count), F32))
        outs["query_out"] = whole(shaped((width, count), BF))
        outs["own_out"] = whole(shaped((2 * width, count), F32))
        for hop in range(1, 4):
            outs[f"away_{hop}"] = whole(shaped((2 * width, count), BF))
        outs["low"] = whole(shaped((width, count), BF))
        outs["hidden"] = whole(shaped((hidden, count), BF))
        outs["middle"] = whole(shaped((width, count), BF))
        outs["vec_out"] = whole(shaped((ONES_ROWS, vec_len), F32))
        scratch |= {
            "keys": pltpu.VMEM((4, count, width), BF),
            "values": pltpu.VMEM((4, count, width), BF),
            "keys_t": pltpu.VMEM((4, width, count), BF),
            "bias": pltpu.VMEM((2 * count, count), F32),
            "query_grad": pltpu.VMEM((width, count), F32),
            "kv_grad": pltpu.VMEM((4, 2 * width, count), F32),
            "blend_grad": pltpu.VMEM((width, count), BF),
        }
    flops = count * 12 * (4 * width * width + 2 * width * hidden)
    near = [
        "middle_in_split", "query_in", "own_in", "in_1", "in_2", "in_3", "middle_out",
        "query_out", "own_out", "away_1", "away_2", "away_3", "low", "hidden", "middle", "vec_out",
    ]
    if only_parts:
        return body, ins, outs, scratch, near
    return launch("backward_split", body, place, 1, ins, outs, scratch, flops, near=near)


def turn_split(
    place, vec, forward_weights, backward_weights, layer, state, blocks, pre, stat_pre, first_end,
    cotangent, row_len,
):
    forward, ins, outs, scratch, near = forward_split(
        place, vec, forward_weights, last=layer, state=state, prev=blocks, pre=pre,
        first_end=first_end, only_parts=True,
    )
    begun = {"pre": pre, "kv": blocks, "stat_pre": stat_pre, "post": pre, "stat_post": stat_pre}
    backward, more_ins, more_outs, more_scratch, more_near = backward_split(
        place, vec, backward_weights, following=layer, begun=begun, cotangent=cotangent,
        row_len=row_len, only_parts=True,
    )
    shared = ("pre", "post", "stat_post", "vec", *(f"kv_{hop}" for hop in range(4)))
    more_ins = {key: value for key, value in more_ins.items() if key not in shared}

    def body(place, env):
        forward(place, env)
        env.pre = env.pre_in
        backward(place, env)

    return launch(
        "turn_split", body, place, 1, ins | more_ins, outs | more_outs, scratch | more_scratch,
        near=near + more_near,
    )


def cut_tokens(place, *pairs):
    arrays = [array for pair in pairs for array in pair]
    rows, count, width = arrays[0].shape

    def body(place, env):
        me = place.me
        best, longest = jnp.int32(0), jnp.int32(0)
        for row in range(rows):
            most = place.all_lengths[row, 0]
            for k in range(1, place.all_lengths.shape[1]):
                most = jnp.maximum(most, place.all_lengths[row, k])
            longest = jnp.where(most > best, row, longest)
            best = jnp.maximum(most, best)
        env.here[0] = me
        env.here[1] = longest
        env.here[2] = place.slot
        for hop in range(4):
            row = row_of_slot(me ^ hop, longest, rows)
            at = 0
            for index, pair in enumerate(pairs):
                value = getattr(env, f"in_{at}")[row].astype(F32)
                for extra in range(1, len(pair)):
                    value = value + getattr(env, f"in_{at + extra}")[row].astype(F32)
                at += len(pair)
                getattr(env, f"out{index}_{hop}")[...] = value.astype(BF)

    ins = {f"in_{k}": whole(array) for k, array in enumerate(arrays)}
    outs = {}
    for index in range(len(pairs)):
        outs |= token_outs(f"out{index}", count, width)
    outs["here"] = (shaped((3,), jnp.int32), pl.BlockSpec(memory_space=pltpu.SMEM))
    results = launch("cut_tokens", body, place, 1, ins, outs, free=("here",))
    blocks = [[results[f"out{index}_{hop}"] for hop in range(4)] for index in range(len(pairs))]
    return results["here"], blocks


def prepare(place, weights, vectors):
    out_bias, down_bias, norm_gain, norm_shift, up_bias = vectors
    layers, width = out_bias.shape
    hidden = up_bias.shape[1]
    rows = (6 * width + hidden) // 128
    rows += -rows % 8

    def body(place, env):
        layer = pl.program_id(0)
        for k in range(4):
            getattr(env, f"turned_{k}")[0] = getattr(env, f"weight_{k}")[0].T
        env.vec[...] = jnp.zeros_like(env.vec)
        pick = lambda ref: ref[pl.ds(layer, 1), :]
        parts = [pick(env.out_bias), pick(env.down_bias)]
        for k in range(2):
            parts += [env.norm_gain[0, k : k + 1, :], env.norm_shift[0, k : k + 1, :]]
        at = 0
        for part in parts + [pick(env.up_bias)]:
            for lanes in range(0, part.shape[1], 128):
                env.vec[0, at : at + 1, :] = part[:, lanes : lanes + 128]
                at += 1

    ins = {f"weight_{k}": each(weight) for k, weight in enumerate(weights)}
    ins |= {"out_bias": whole(out_bias), "down_bias": whole(down_bias), "up_bias": whole(up_bias)}
    ins |= {"norm_gain": each(norm_gain), "norm_shift": each(norm_shift)}
    outs = {
        f"turned_{k}": each(shaped((layers, weight.shape[2], weight.shape[1]), BF))
        for k, weight in enumerate(weights)
    }
    outs["vec"] = each(shaped((layers, rows, 128), F32))
    results = launch("prepare", body, place, layers, ins, outs, near=list(outs))
    return tuple(results[f"turned_{k}"] for k in range(4)), results["vec"]


def piece_reader(payloads, me):
    mine, other = payloads
    half = mine.shape[0]

    def piece(p, first, rows):
        left, right = (ref[p % half, first : first + rows, :] for ref in (mine, other))
        return jnp.where(me % 2 == p // half, left, right).astype(F32)

    return piece


def spread_pieces(piece, pieces, first, rows_each, targets, factor):
    edges, at = [], 0
    for ref in targets:
        for lanes in range(0, ref.shape[2], 128):
            edges.append((at, at + ref.shape[1], ref, lanes))
            at += ref.shape[1]
    for p in range(pieces):
        values = piece(p, first, rows_each) * factor
        begin = p * rows_each
        for low, high, ref, lanes in edges:
            left, right = max(low, begin), min(high, begin + rows_each)
            if left < right:
                ref[0, left - low : right - low, lanes : lanes + 128] = values[
                    left - begin : right - begin, :
                ]


def finish_tokens(
    place, payload, answer, answer_split, first, first_split, second, second_split,
    hidden, groups, row_len,
):
    count, width = first_split.shape
    rows = 5
    pieces = 2 * payload[0].shape[0]
    ffn_rows = (width * width + 2 * width * hidden) // 128 // pieces

    def body(place, env):
        step = pl.program_id(0)
        me = place.me
        piece = piece_reader((env.mine, env.other), me)
        lane = lax.broadcasted_iota(jnp.int32, (1, 128), 1)
        total = jnp.zeros((1, 1), F32)
        for extra in range(-(-2 * groups // 128)):
            row = piece(extra, ffn_rows, 16)[0:1, :]
            worth = jnp.where(lane % 2 == 0, 256.0, 1.0)
            row = jnp.where(lane + extra * 128 < 2 * groups, row * worth, 0.0)
            total = total + jnp.sum(row, axis=1, keepdims=True)
        factor = row_len / total
        token_factor = factor * float(rows * groups)

        @pl.when(step == 0)
        def _():
            env.scale[...] = jnp.broadcast_to(factor, env.scale.shape)
            spread_pieces(piece, pieces, 0, ffn_rows, (env.out, env.up, env.down), factor)

        for hop in range(4):

            @pl.when(step == row_of_slot(me ^ hop, place.split, rows))
            def _(hop=hop):
                env.block_output[0] = getattr(env, f"answer_{hop}")[...]
                one = getattr(env, f"first_{hop}")[...].astype(F32)
                two = getattr(env, f"second_{hop}")[...].astype(F32)
                env.input_grad[0] = one * token_factor
                env.embed_grad[0] = (one + two) * token_factor

        @pl.when(step == place.split)
        def _():
            env.block_output[0] = env.answer_split[...]
            one = env.first_split[...]
            env.input_grad[0] = one * token_factor
            env.embed_grad[0] = (one + env.second_split[...]) * token_factor

    ins = {"mine": whole(payload[0]), "other": whole(payload[1])}
    ins |= token_ins("answer", answer) | token_ins("first", first) | token_ins("second", second)
    ins["answer_split"] = whole(answer_split)
    ins["first_split"] = whole(first_split)
    ins["second_split"] = whole(second_split)
    later = lambda *dims: (
        shaped(dims, F32), pl.BlockSpec((1,) + dims[1:], lambda i, *_: (LAYERS - 1, 0, 0))
    )
    outs = {
        "block_output": each(shaped((rows, count, width), BF)),
        "input_grad": each(shaped((rows, count, width), F32)),
        "embed_grad": each(shaped((rows, count, width), F32)),
        "out": later(LAYERS, width, width),
        "up": later(LAYERS, width, hidden),
        "down": later(LAYERS, hidden, width),
        "scale": whole(shaped((8, 128), F32)),
    }
    return launch(
        "finish_tokens", body, place, rows, ins, outs, free=("mine", "other")
    )


def finish_weights(place, payload, done, width, hidden):
    pieces = 2 * payload[0].shape[0]
    ffn_rows = (width * width + 2 * width * hidden) // 128 // pieces
    qkv_rows = 3 * width * width // 128 // pieces
    small_at = ffn_rows + LAYERS * qkv_rows
    vec_len = 6 * width + hidden

    def body(place, env):
        step = pl.program_id(0)
        piece = piece_reader((env.mine, env.other), place.me)
        factor = env.scale[0:1, 0:1]

        @pl.when(step == 0)
        def _():
            spread_pieces(piece, pieces, 0, ffn_rows, (env.out, env.up, env.down), factor)
            for here in range(LAYERS):
                for ref, slot, at, size in (
                    (env.out_b, None, 0, width),
                    (env.down_b, None, width, width),
                    (env.gain, 0, 2 * width, width),
                    (env.shift, 0, 3 * width, width),
                    (env.gain, 1, 4 * width, width),
                    (env.shift, 1, 5 * width, width),
                    (env.up_b, None, 6 * width, hidden),
                ):
                    for lanes in range(0, size, 128):
                        index = (here * vec_len + at + lanes) // 128
                        row = piece(index // 2, small_at, 16)[index % 2 : index % 2 + 1, :]
                        row = row * factor
                        if slot is None:
                            ref[here : here + 1, lanes : lanes + 128] = row
                        else:
                            ref[here, slot : slot + 1, lanes : lanes + 128] = row

        for here in range(LAYERS):

            @pl.when(step == here)
            def _(here=here):
                spread_pieces(
                    piece, pieces, ffn_rows + here * qkv_rows, qkv_rows, (env.qkv,), factor
                )

    ins = {"mine": whole(payload[0]), "other": whole(payload[1]), "scale": whole(done["scale"])}
    names = ("out", "up", "down")
    for name in names:
        ins[name + "_done"] = (done[name], pl.BlockSpec(memory_space=pl.ANY))
    start = lambda array: (
        array, pl.BlockSpec((1,) + array.shape[1:], lambda i, *_: (0, 0, 0))
    )
    outs = {name: start(shaped(done[name].shape, F32)) for name in names}
    outs["qkv"] = each(shaped((LAYERS, width, 3 * width), F32))
    outs["out_b"] = whole(shaped((LAYERS, width), F32))
    outs["up_b"] = whole(shaped((LAYERS, hidden), F32))
    outs["down_b"] = whole(shaped((LAYERS, width), F32))
    outs["gain"] = whole(shaped((LAYERS, 2, width), F32))
    outs["shift"] = whole(shaped((LAYERS, 2, width), F32))
    return launch(
        "finish_weights", body, place, LAYERS, ins, outs,
        aliases=[(name + "_done", name) for name in names],
        free=("mine", "other"),
    )


SEQ = ("y", "core")
CHIPS = ("dp", "y")


def swap(values, hop):
    return lax.ppermute(values, SEQ, [(i, i ^ hop) for i in range(lax.axis_size(SEQ))])


def swap_blocks(blocks):
    return [blocks[0]] + [swap(block, hop) for hop, block in enumerate(blocks[1:], 1)]


def sum_cores(keep, got):
    return (keep.astype(F32) + got.astype(F32)).astype(BF)


def sum_chips(part):
    part = lax.all_to_all(part, CHIPS, 0, 0, tiled=True)
    return jnp.sum(part.astype(F32), axis=0).astype(BF)


def share_chips(part):
    copies = jnp.broadcast_to(part[None], (lax.axis_size(CHIPS),) + part.shape)
    return lax.all_to_all(copies, CHIPS, 0, 0, tiled=True)


def fast_device(
    block_input, embedding, cotangent, qkv_weight, out_weight, out_bias, up_weight, up_bias,
    down_weight, down_bias, norm_gain, norm_shift, seg_lengths, loop_counts, token_counts,
):
    row_count, tokens, width = block_input.shape
    chunks = lax.axis_size(SEQ)
    groups = lax.axis_size("dp")
    devices = groups * chunks
    row_len = tokens * chunks
    me = lax.axis_index(SEQ)
    hidden = up_weight.shape[2]
    tie = lax.optimization_barrier
    half = devices // 2
    steps = LAYERS * 2

    here = jnp.stack([me, jnp.zeros_like(me), lax.axis_index("dp")]).astype(jnp.int32)
    here, (sent, sent_embed, sent_top) = cut_tokens(
        (here, loop_counts, token_counts, seg_lengths), (block_input, embedding), (embedding,),
        (cotangent,),
    )
    moved = swap_blocks(sent)
    here, sent = tie((here, sent))
    place = (here, loop_counts, token_counts, seg_lengths)
    backward_weights = (qkv_weight, out_weight, up_weight, down_weight)
    vectors = (out_bias, down_bias, norm_gain, norm_shift, up_bias)
    forward_weights, vec = prepare(place, backward_weights, vectors)

    moved_embed, moved_top = ([blocks[0]] + [None] * 3 for blocks in (sent_embed, sent_top))
    waiting = [(sent_embed, moved_embed, hop) for hop in range(1, 4)]
    waiting += [(sent_top, moved_top, hop) for hop in range(1, 4)]
    saved, saved_split = [], []
    begun = forward_split(
        place, vec, forward_weights, following=0, block_input=block_input,
        embedding=embedding,
    )
    state_split = begun["begun"]
    state = None
    first_end = first_end_split = None
    for step in range(steps):
        layer = step % LAYERS
        pre, kv, stat_pre = begun["pre"], begun["kv"], begun["stat_pre"]
        arrived = [swap(kv, hop) for hop in range(1, 4)]
        source = {}
        if step == 0:
            moved, kv = tie((moved, kv))
            source["tokens"] = moved
        elif step == LAYERS:
            state, moved_embed, kv = tie((state, moved_embed, kv))
            source["state"], source["tokens"] = state, moved_embed
        else:
            state, kv = tie((state, kv))
            source["state"] = state
        riders = waiting[2 * step : 2 * step + 2]
        blocks_out, kv = tie(([blocks[hop] for blocks, _, hop in riders], kv))
        riding = [swap(block, hop) for block, (_, _, hop) in zip(blocks_out, riders)]
        if step == steps - 1:
            source["first_end"] = first_end
        kept = forward_rows(layer, place, vec, forward_weights, **source)
        saved.append(kept)
        if step == steps - 1:
            answer = [kept[f"answer_{hop}"] for hop in range(4)]
            answer, arrived = tie((answer, arrived))
        else:
            state, arrived = tie((kept["result"], arrived))
        arrived, riding = tie((arrived, riding))
        for block, (_, target, hop) in zip(riding, riders):
            target[hop] = block
        boundary = step == LAYERS - 1
        if boundary:
            first_end = state
        extra = {}
        if step < steps - 1:
            extra["following"] = (layer + 1) % LAYERS
            if boundary:
                extra["embedding"] = embedding
        blocks = (kv, *arrived)
        if step == steps - 1:
            begun = turned = turn_split(
                place, vec, forward_weights, backward_weights, layer, state_split, blocks, pre,
                stat_pre, first_end_split, cotangent, row_len,
            )
        else:
            begun = forward_split(
                place, vec, forward_weights, last=layer, state=state_split,
                prev=blocks, pre=pre, **extra,
            )
        saved_split.append(
            {
                "pre": pre, "kv": blocks, "stat_pre": stat_pre,
                "post": begun["post"], "stat_post": begun["stat_post"],
            }
        )
        if step == steps - 1:
            answer_split = begun["answer"]
        else:
            state_split = begun["result"]
        if boundary:
            first_end_split = state_split
            state_split = begun["begun"]

    sums = [None] * LAYERS
    early = None
    grad = None
    ended = None
    for step in reversed(range(steps)):
        layer = step % LAYERS
        between = step == LAYERS - 1
        option = {}
        if between:
            option = {"cotangent": cotangent, "row_len": row_len}
        if ended is not None:
            last = (step + 1) % LAYERS
            option |= {
                "last": last, "ended": ended, "sums": sums[last], "keep": between,
                "final": step == 0,
            }
        begun = turned
        if step < steps - 1:
            begun = backward_split(
                place, vec, backward_weights, following=layer, begun=saved_split[step], **option
            )
        if ended is not None:
            if step == 0:
                others = {"wire": begun["wire"], "vec": begun["sum_vec"]}
            else:
                sums[last] |= {"sum_qkv": begun["sum_qkv"], "sum_vec": begun["sum_vec"]}
            if between:
                second_split = begun["result"]
        arrived = [swap(begun[f"away_{hop}"], hop) for hop in range(1, 4)]
        five = {
            "post": saved_split[step]["post"], "hidden": begun["hidden"], "low": begun["low"],
            "middle": begun["middle"], "vec": begun["vec_out"],
        }
        source = {}
        if step == steps - 1:
            moved_answer = [answer[0]] + [None] * 3
            waiting = [(answer, moved_answer, hop) for hop in range(1, 4)]
            source["tokens"] = moved_top
        elif between:
            moved_second = [second[0]] + [None] * 3
            waiting += [(second, moved_second, hop) for hop in range(1, 4)]
            source["tokens"] = moved_top
        riders, waiting = waiting[:2], waiting[2:]
        riding = [swap(blocks[hop], hop) for blocks, _, hop in riders]
        if grad is not None:
            source["grad"] = grad
        if step < LAYERS:
            source |= {"half": half, "digits": step == 1}
        source |= {"base": sums[layer], "keep": step > 0, "travel": step in (0, LAYERS)}
        fixed = (layer, place, saved[step], vec, backward_weights, five)
        if step == 0:
            early = sum_cores(*early)
            grad, early = tie((grad, early))
            source["grad"] = grad
            half_way = backward_rows(*fixed, ffn_only=True, **source)
            early = sum_chips(early)
            half_way, early, arrived = tie((half_way, early, arrived))
            early = share_chips(early)
            late_ffn = sum_cores(half_way["keep"], swap(half_way["give"], 1))
            half_way, late_ffn = tie((half_way, late_ffn))
            closing = {name: begun[name] for name in ("middle_out", "query_out", "own_out")}
            closing |= {"arrived": arrived, "pre": saved_split[step]["pre"]}
            closing["stat_pre"] = saved_split[step]["stat_pre"]
            kept = backward_rows(
                *fixed, part_done=half_way, closing=closing, others=others, **source
            )
            kept["keep"], early = tie((kept["keep"], early))
            for block, (_, target, hop) in zip(riding, riders):
                target[hop] = block
            first = [kept[f"travel_{hop}"] for hop in range(4)]
            break
        kept = backward_rows(*fixed, **source)
        grad, arrived = tie((kept["result"], arrived))
        if step == LAYERS:
            second = [kept[f"travel_{hop}"] for hop in range(4)]
        if between:
            arrived, riding, kept["give"] = tie((arrived, riding, kept["give"]))
            early = (kept["keep"], swap(kept["give"], 1))
        else:
            arrived, riding = tie((arrived, riding))
        for block, (_, target, hop) in zip(riding, riders):
            target[hop] = block
        if sums[layer] is None:
            names = ("sum_qkv", "sum_out", "sum_up", "sum_down", "sum_vec")
            sums[layer] = {name: kept[name] for name in names}
        else:
            sums[layer] = {name: kept[name] for name in ("sum_qkv", "sum_vec")}
        ended = {name: begun[name] for name in ("middle_out", "query_out", "own_out")}
        ended |= {"arrived": arrived, "pre": saved_split[step]["pre"]}
        ended["stat_pre"] = saved_split[step]["stat_pre"]
    moved_first = swap_blocks(first)
    first_split = kept["split_result"]

    part = jnp.concatenate(
        [
            late_ffn,
            sum_cores(kept["keep"], swap(kept["give"], 1)),
        ],
        axis=1,
    )
    early_other = swap(early, 1)
    part, moved_first, early, early_other = tie(
        (sum_chips(part), moved_first, early, early_other)
    )
    late = share_chips(part)
    done = finish_tokens(
        place, (early, early_other), moved_answer, answer_split, moved_first, first_split,
        moved_second, second_split, hidden, groups, float(row_len),
    )
    late, done = tie((late, done))
    more = finish_weights(place, (late, swap(late, 1)), done, width, hidden)
    return (
        done["block_output"],
        done["input_grad"],
        done["embed_grad"],
        more["qkv"],
        more["out"],
        more["out_b"],
        more["up"],
        more["up_b"],
        more["down"],
        more["down_b"],
        more["gain"],
        more["shift"],
    )


def solution(mesh):
    if mesh.shape["seq"] == 4:
        fine = Mesh(mesh.devices.reshape(-1, 2, 2), ("dp", "y", "core"))
        return jax.shard_map(
            fast_device,
            mesh=fine,
            in_specs=(
                P("dp", SEQ, None),
                P("dp", SEQ, None),
                P("dp", SEQ, None),
                P(),
                P(),
                P(),
                P(),
                P(),
                P(),
                P(),
                P(),
                P(),
                P("dp", None),
                P("dp"),
                P("dp"),
            ),
            out_specs=(
                P("dp", SEQ, None),
                P("dp", SEQ, None),
                P("dp", SEQ, None),
                P(),
                P(),
                P(),
                P(),
                P(),
                P(),
                P(),
                P(),
                P(),
            ),
            check_vma=False,
        )
    return jax.shard_map(
        on_device,
        mesh=mesh,
        in_specs=(
            P("dp", "seq", None),
            P("dp", "seq", None),
            P("dp", "seq", None),
            P(),
            P(),
            P(),
            P(),
            P(),
            P(),
            P(),
            P(),
            P(),
            P("dp", None),
            P("dp"),
            P("dp"),
        ),
        out_specs=(
            P("dp", "seq", None),
            P("dp", "seq", None),
            P("dp", "seq", None),
            P(),
            P(),
            P(),
            P(),
            P(),
            P(),
            P(),
            P(),
            P(),
        ),
        check_vma=False,
    )
```

```python
import types

import jax
import jax.numpy as jnp
from jax import lax
from jax.experimental import pallas as pl
from jax.experimental.pallas import tpu as pltpu
from jax.sharding import Mesh, PartitionSpec as P

H = 4
LAYERS = 2


NORM_EPS = 1e-05
MASKED = -1e30


def layer_norm(values, gain, shift):
    center = values - jnp.mean(values, axis=-1, keepdims=True)
    spread = jnp.mean(center * center, axis=-1, keepdims=True)
    return center * lax.rsqrt(spread + NORM_EPS) * gain + shift


def gelu_exact(values):
    return jax.nn.gelu(values, approximate=False)


def matmul(left_side, right_side):
    return jnp.dot(left_side, right_side, preferred_element_type=jnp.float32)


def left_dot(left_side, right_side):
    return lax.dot_general(
        left_side, right_side, (((0,), (0,)), ((), ())), preferred_element_type=jnp.float32
    )


def right_dot(left_side, right_side):
    return lax.dot_general(
        left_side, right_side, (((1,), (1,)), ((), ())), preferred_element_type=jnp.float32
    )


def split_heads(packed, head_count):
    return packed.reshape(packed.shape[0], head_count, packed.shape[1] // head_count)


def attend_forward(queries, key_vals, allowed, head_count, score_scale):
    model_width = queries.shape[1]
    key_rows = split_heads(key_vals[:, :model_width], head_count)
    value_rows = split_heads(key_vals[:, model_width:], head_count)
    scores = (
        jnp.einsum(
            "qhd,khd->hqk",
            split_heads(queries, head_count),
            key_rows,
            preferred_element_type=jnp.float32,
        )
        * score_scale
    )
    scores = jnp.where(allowed[None], scores, MASKED)
    row_max = jnp.max(scores, axis=-1, keepdims=True)
    shifted_exp = jnp.exp(scores - row_max)
    row_total = jnp.sum(shifted_exp, axis=-1, keepdims=True)
    attn_probs = (shifted_exp / row_total).astype(jnp.bfloat16)
    blended = jnp.einsum("hqk,khd->qhd", attn_probs, value_rows, preferred_element_type=jnp.float32)
    return (blended.reshape(queries.shape[0], model_width), (row_max + jnp.log(row_total))[..., 0])


def attention_core(
    query_part, key_part, value_part, grad_part, allowed_part, logsum_part, head_count, score_scale
):
    scores = (
        jnp.einsum(
            "qhd,khd->hqk",
            split_heads(query_part, head_count),
            split_heads(key_part, head_count),
            preferred_element_type=jnp.float32,
        )
        * score_scale
    )
    scores = jnp.where(allowed_part[None], scores, MASKED)
    attn_probs = jnp.exp(scores - logsum_part[..., None])
    grad_probs = jnp.einsum(
        "qhd,khd->hqk",
        split_heads(grad_part, head_count),
        split_heads(value_part, head_count),
        preferred_element_type=jnp.float32,
    )
    return (attn_probs, grad_probs)


def query_grads(grad_scores, key_part, head_count, score_scale):
    result = (
        jnp.einsum(
            "hqk,khd->qhd",
            grad_scores,
            split_heads(key_part, head_count),
            preferred_element_type=jnp.float32,
        )
        * score_scale
    )
    return result.reshape(result.shape[0], -1)


def keyval_grads(grad_scores, attn_probs, query_part, grad_part, head_count, score_scale):
    grad_keys = (
        jnp.einsum(
            "hqk,qhd->khd",
            grad_scores,
            split_heads(query_part, head_count),
            preferred_element_type=jnp.float32,
        )
        * score_scale
    )
    grad_values = jnp.einsum(
        "hqk,qhd->khd",
        attn_probs.astype(jnp.bfloat16),
        split_heads(grad_part, head_count),
        preferred_element_type=jnp.float32,
    )
    return jnp.concatenate(
        [grad_keys.reshape(grad_keys.shape[0], -1), grad_values.reshape(grad_values.shape[0], -1)],
        axis=-1,
    )


def on_device(
    block_input,
    embedding,
    cotangent,
    qkv_weight,
    out_weight,
    out_bias,
    up_weight,
    up_bias,
    down_weight,
    down_bias,
    norm_gain,
    norm_shift,
    seg_lengths,
    loop_counts,
    token_counts,
):
    row_count, block_len, model_width = block_input.shape
    head_count = H
    score_scale = (model_width // head_count) ** (-0.5)
    row_len = block_len * lax.axis_size("seq")
    flat_rows = row_count * block_len
    offset = lax.axis_index("seq") * block_len
    key_pos = jnp.arange(row_len, dtype=jnp.int32)
    own_pos = offset + jnp.arange(block_len, dtype=jnp.int32)
    seg_ends = jnp.cumsum(seg_lengths, axis=-1)
    seg_all = jnp.sum((seg_ends[:, None, :] <= key_pos[None, :, None]).astype(jnp.int32), axis=-1)
    seg_own = lax.dynamic_slice_in_dim(seg_all, offset, block_len, 1)
    allowed = (seg_own[:, :, None] == seg_all[:, None, :]) & (
        key_pos[None, None, :] <= own_pos[None, :, None]
    )
    current = block_input.astype(jnp.float32)
    inject = embedding.astype(jnp.float32)
    stored = []
    finals = []
    for repeat in range(2):
        current = current + inject
        for layer_index in range(LAYERS):
            forward_normed = layer_norm(
                current, norm_gain[layer_index, 0], norm_shift[layer_index, 0]
            ).astype(jnp.bfloat16)
            forward_packed = matmul(
                forward_normed.reshape(flat_rows, model_width), qkv_weight[layer_index]
            ).astype(jnp.bfloat16)
            forward_packed = forward_packed.reshape(row_count, block_len, 3 * model_width)
            forward_key_vals = lax.all_gather(
                forward_packed[:, :, model_width:], "seq", axis=1, tiled=True
            )

            def forward_row(inputs):
                return attend_forward(inputs[0], inputs[1], inputs[2], head_count, score_scale)

            forward_blended, forward_logsum = lax.map(
                forward_row, (forward_packed[:, :, :model_width], forward_key_vals, allowed)
            )
            forward_blended = forward_blended.astype(jnp.bfloat16)
            branch_out = matmul(
                forward_blended.reshape(flat_rows, model_width), out_weight[layer_index]
            ).reshape(row_count, block_len, model_width)
            forward_middle = current + branch_out + out_bias[layer_index]
            forward_normed_two = layer_norm(
                forward_middle, norm_gain[layer_index, 1], norm_shift[layer_index, 1]
            ).astype(jnp.bfloat16)
            forward_up_proj = (
                matmul(forward_normed_two.reshape(flat_rows, model_width), up_weight[layer_index])
                + up_bias[layer_index]
            )
            forward_active = gelu_exact(forward_up_proj).astype(jnp.bfloat16)
            result = (
                forward_middle
                + matmul(forward_active, down_weight[layer_index]).reshape(
                    row_count, block_len, model_width
                )
                + down_bias[layer_index]
            )
            current, stored_layer = (
                result,
                (
                    current,
                    forward_normed,
                    forward_packed,
                    forward_key_vals,
                    forward_logsum,
                    forward_blended,
                    forward_middle,
                    forward_normed_two,
                    forward_up_proj,
                    forward_active,
                ),
            )
            stored.append(stored_layer)
        finals.append(current)
    two_loops = (loop_counts == 2)[:, None, None]
    block_output = jnp.where(two_loops, finals[1], finals[0]).astype(jnp.bfloat16)
    row_weight = token_counts.astype(jnp.float32) / row_len
    grad_top = cotangent.astype(jnp.float32) * row_weight[:, None, None]
    grad_state = jnp.where(two_loops, grad_top, 0.0)
    layer_sums = [None] * LAYERS
    second_pass = grad_state
    for repeat in (1, 0):
        for layer_index in reversed(range(LAYERS)):
            backward_stored_layer = stored[repeat * LAYERS + layer_index]
            (
                backward_current,
                normed,
                packed,
                key_vals,
                logsum,
                blended,
                middle,
                normed_two,
                up_proj,
                active,
            ) = backward_stored_layer
            grad_flat = grad_state.reshape(flat_rows, model_width)
            grad_low = grad_flat.astype(jnp.bfloat16)
            grad_down = left_dot(active, grad_low)
            grad_down_bias = jnp.sum(grad_flat, axis=0)
            grad_active = right_dot(grad_low, down_weight[layer_index])
            grad_up_proj = jax.vjp(gelu_exact, up_proj)[1](grad_active)[0].astype(jnp.bfloat16)
            grad_up_bias = jnp.sum(grad_up_proj.astype(jnp.float32), axis=0)
            grad_up = left_dot(normed_two.reshape(flat_rows, model_width), grad_up_proj)
            grad_normed_two = right_dot(grad_up_proj, up_weight[layer_index]).reshape(
                row_count, block_len, model_width
            )
            pull_two = jax.vjp(
                layer_norm, middle, norm_gain[layer_index, 1], norm_shift[layer_index, 1]
            )[1]
            grad_middle, gain_two, shift_two = pull_two(grad_normed_two)
            grad_middle = grad_middle + grad_state
            middle_flat = grad_middle.reshape(flat_rows, model_width)
            middle_low = middle_flat.astype(jnp.bfloat16)
            grad_out = left_dot(blended.reshape(flat_rows, model_width), middle_low)
            grad_out_bias = jnp.sum(middle_flat, axis=0)
            grad_blend = (
                right_dot(middle_low, out_weight[layer_index])
                .astype(jnp.bfloat16)
                .reshape(row_count, block_len, model_width)
            )
            queries = packed[:, :, :model_width]

            def full_row(inputs):
                query_part, keyval_part, grad_part, allowed_part, logsum_part = inputs
                attn_probs, grad_probs = attention_core(
                    query_part,
                    keyval_part[:, :model_width],
                    keyval_part[:, model_width:],
                    grad_part,
                    allowed_part,
                    logsum_part,
                    head_count,
                    score_scale,
                )
                row_delta = jnp.sum(attn_probs * grad_probs, axis=-1, keepdims=True)
                grad_scores = (attn_probs * (grad_probs - row_delta)).astype(jnp.bfloat16)
                return (
                    query_grads(grad_scores, keyval_part[:, :model_width], head_count, score_scale),
                    keyval_grads(
                        grad_scores, attn_probs, query_part, grad_part, head_count, score_scale
                    ),
                )

            grad_query, partial_kv = lax.map(
                full_row, (queries, key_vals, grad_blend, allowed, logsum)
            )
            grad_keyval = lax.psum_scatter(
                partial_kv.astype(jnp.bfloat16), "seq", scatter_dimension=1, tiled=True
            )
            grad_packed = jnp.concatenate(
                [grad_query.astype(jnp.bfloat16), grad_keyval], axis=-1
            ).reshape(flat_rows, 3 * model_width)
            grad_qkv = left_dot(normed.reshape(flat_rows, model_width), grad_packed)
            grad_normed = right_dot(grad_packed, qkv_weight[layer_index]).reshape(
                row_count, block_len, model_width
            )
            pull_one = jax.vjp(
                layer_norm, backward_current, norm_gain[layer_index, 0], norm_shift[layer_index, 0]
            )[1]
            grad_current, gain_one, shift_one = pull_one(grad_normed)
            grad_current = grad_current + grad_middle
            grad_state = grad_current
            grad_set = (
                grad_qkv,
                grad_out,
                grad_out_bias,
                grad_up,
                grad_up_bias,
                grad_down,
                grad_down_bias,
                jnp.stack([gain_one, gain_two]),
                jnp.stack([shift_one, shift_two]),
            )
            if repeat == 1:
                layer_sums[layer_index] = grad_set
            else:
                layer_sums[layer_index] = jax.tree.map(jnp.add, layer_sums[layer_index], grad_set)
        if repeat == 1:
            second_pass = grad_state
            grad_state = jnp.where(two_loops, grad_state, grad_top)
    grad_embed = grad_state + second_pass
    stacked = jax.tree.map(lambda *members: jnp.stack(members), *layer_sums)
    (
        sum_qkv,
        sum_out,
        sum_out_bias,
        sum_up,
        sum_up_bias,
        sum_down,
        sum_down_bias,
        sum_gain,
        sum_shift,
    ) = stacked
    total = lax.psum(jnp.sum(token_counts), "dp").astype(jnp.float32)
    summed = lax.psum(
        (
            sum_qkv,
            sum_out,
            sum_out_bias,
            sum_up,
            sum_up_bias,
            sum_down,
            sum_down_bias,
            sum_gain,
            sum_shift,
        ),
        ("dp", "seq"),
    )
    input_scale = row_count * lax.axis_size("dp") * row_len / total
    weight_scale = row_len / total
    return (
        block_output,
        grad_state * input_scale,
        grad_embed * input_scale,
        summed[0] * weight_scale,
        summed[1] * weight_scale,
        summed[2] * weight_scale,
        summed[3] * weight_scale,
        summed[4] * weight_scale,
        summed[5] * weight_scale,
        summed[6] * weight_scale,
        summed[7] * weight_scale,
        summed[8] * weight_scale,
    )


BF = jnp.bfloat16
F32 = jnp.float32
ERF_TERMS = (7.97869712e-01, 3.63922863e-02, -8.78266373e-05, -3.66934271e-05, 1.42500458e-06)
DENSITY_RATE = -0.7213475204444817
DENSITY_BASE = -1.3257480647361593
VMEM_LIMIT = 24 * 1024 * 1024
ONES_ROWS = 16


def dot_nn(left_side, right_side):
    return jnp.dot(left_side, right_side, preferred_element_type=F32)


def dot_nt(left_side, right_side):
    return lax.dot_general(
        left_side, right_side, (((1,), (1,)), ((), ())), preferred_element_type=F32
    )


def gelu_and_slope(z):
    square = z * z
    series = ERF_TERMS[-1] * square + ERF_TERMS[-2]
    for term in ERF_TERMS[-3::-1]:
        series = series * square + term
    cdf = 0.5 + 0.5 * jnp.tanh(z * series)
    density = jnp.exp2(square * DENSITY_RATE + DENSITY_BASE)
    return z * cdf, cdf + z * density


def norm_forward(values, gain, shift):
    center = values - jnp.mean(values, axis=0, keepdims=True)
    spread = jnp.mean(center * center, axis=0, keepdims=True)
    inverse = lax.rsqrt(spread + NORM_EPS)
    unit = center * inverse
    return unit, inverse, (unit * gain + shift).astype(BF)


def norm_backward(grad, unit, inverse, gain):
    scaled = grad * gain
    first = jnp.mean(scaled, axis=0, keepdims=True)
    second = jnp.mean(scaled * unit, axis=0, keepdims=True)
    return inverse * (scaled - first - unit * second)


def columns(vec, tokens, spread=False):
    turned = vec[0].T

    def column(first, last):
        parts = [turned[:, k : k + 1] for k in range(first // 128, last // 128)]
        if spread:
            parts = [jnp.broadcast_to(part, (128, 128)) for part in parts]
            parts = [jnp.concatenate([part] * (tokens // 128), axis=1) for part in parts]
        return jnp.concatenate(parts, axis=0)

    return column


def project_qkv(state, qkv_t, vec, pre, kv, stat, scale, spread=False):
    width = state.shape[0]
    column = columns(vec, state.shape[1], spread)
    gain = column(2 * width, 3 * width)
    shift = column(3 * width, 4 * width)
    unit, inverse, normed = norm_forward(state, gain, shift)
    pre[0:width, :] = normed
    pre[2 * width : 3 * width, :] = unit.astype(BF)
    pre[width : 2 * width, :] = (dot_nn(qkv_t[0, 0:width, :], normed) * scale).astype(BF)
    kv[0:width, :] = dot_nn(qkv_t[0, width : 2 * width, :], normed).astype(BF)
    kv[width : 2 * width, :] = dot_nn(qkv_t[0, 2 * width : 3 * width, :], normed).astype(BF)
    stat[0:1, :] = inverse


def pad_head(block, odd):
    blank = jnp.zeros_like(block)
    return jnp.concatenate([blank, block] if odd else [block, blank], axis=0)


def tile_bias(first_key, start, causal, shape):
    key_at = lax.broadcasted_iota(jnp.int32, shape, 0)
    keep = key_at + first_key >= start
    if causal:
        keep = keep & (key_at <= lax.broadcasted_iota(jnp.int32, shape, 1))
    return jnp.where(keep, 0.0, MASKED)


def over_tiles(chunk, count, begin, half_tile, full_tile, carry, full_pair=None):
    half = count // 2
    first_half = begin // half
    odd = jnp.where(first_half < 2 * chunk, first_half % 2, 0)
    carry = lax.fori_loop(0, odd, lambda _, c: half_tile(first_half // 2, c), carry)
    first = (first_half + 1) // 2
    if full_pair is not None:
        pairs = jnp.maximum(chunk - first, 0) // 2
        carry = lax.fori_loop(0, pairs, lambda k, c: full_pair(first + 2 * k, c), carry)
        first = first + 2 * pairs
    return lax.fori_loop(first, chunk, full_tile, carry)


def attend_chunk(
    queries, keys, values_t, chunk, begin, start, bias, total, stat, blended, paired=False
):
    width, tokens = queries.shape
    head = width // H
    pair = 2 * head
    half = tokens // 2
    head_rows = [slice(h * head, (h + 1) * head) for h in range(H)]

    def scores(j, h, span):
        lanes = pl.ds((h // 2) * pair, pair)
        return dot_nn(keys[j, span, lanes], pad_head(queries[head_rows[h], :], h % 2))

    everything = slice(0, tokens)
    bias[:tokens, :] = tile_bias(chunk * tokens, start, True, (tokens, tokens))
    parts = [scores(chunk, h, everything) for h in range(H)]
    uppers = [part[:half, :] + bias[:half, :] for part in parts]
    lowers = [part[half:, half:] + bias[half:tokens, half:] for part in parts]
    tops, sums, weights = [], [], []
    for upper, lower in zip(uppers, lowers):
        top = jnp.max(upper, axis=0, keepdims=True)
        right = jnp.maximum(top[:, half:], jnp.max(lower, axis=0, keepdims=True))
        top = jnp.concatenate([top[:, :half], right], axis=1)
        upper = jnp.exp(upper - top)
        lower = jnp.exp(lower - right)
        added = jnp.sum(upper, axis=0, keepdims=True)
        right = added[:, half:] + jnp.sum(lower, axis=0, keepdims=True)
        tops.append(top)
        sums.append(jnp.concatenate([added[:, :half], right], axis=1))
        lower = lower.astype(BF)
        lower = jnp.concatenate([jnp.zeros_like(lower), lower], axis=1)
        weights.append(jnp.concatenate([upper.astype(BF), lower], axis=0))
    for rows, weight in zip(head_rows, weights):
        total[rows, :] = dot_nn(values_t[chunk, rows, :], weight)

    def step(tiles, span, size, carry):
        tops, sums = carry
        each_part, spans = [], []
        for at, j in enumerate(tiles):
            mask = slice(at * tokens, at * tokens + size)
            bias[mask, :] = tile_bias(j * tokens + span.start, start, False, (size, tokens))
            each_part.append([scores(j, h, span) + bias[mask, :] for h in range(H)])
        new_tops = list(tops)
        for parts in each_part:
            new_tops = [
                jnp.maximum(old, jnp.max(part, axis=0, keepdims=True))
                for old, part in zip(new_tops, parts)
            ]
        fades = [jnp.exp(old - new) for old, new in zip(tops, new_tops)]
        sums = [old * fade for old, fade in zip(sums, fades)]
        each_weight = [
            [jnp.exp(part - top) for part, top in zip(parts, new_tops)] for parts in each_part
        ]
        terms = [0.0] * H
        for j, weights in zip(tiles, each_weight):
            sums = [
                old + jnp.sum(weight, axis=0, keepdims=True)
                for old, weight in zip(sums, weights)
            ]
            terms = [
                old + dot_nn(values_t[j, rows, span], weight.astype(BF))
                for old, rows, weight in zip(terms, head_rows, weights)
            ]
        for rows, term, fade in zip(head_rows, terms, fades):
            total[rows, :] = total[rows, :] * fade + term
        return tuple(new_tops), tuple(sums)

    tops, sums = over_tiles(
        chunk, tokens, begin,
        lambda j, carry: step([j], slice(half, tokens), half, carry),
        lambda j, carry: step([j], everything, tokens, carry),
        (tuple(tops), tuple(sums)),
        (lambda j, carry: step([j, j + 1], everything, tokens, carry)) if paired else None,
    )
    for h, rows in enumerate(head_rows):
        blended[rows, :] = (total[rows, :] / sums[h]).astype(BF)
        stat[h : h + 1, :] = tops[h] + jnp.log(sums[h])


def finish_layer(state, out_t, up_t, down_t, vec, post, stat, spread=False):
    width, tokens = state.shape
    hidden = up_t.shape[1]
    column = columns(vec, tokens, spread)
    middle = state + dot_nn(out_t[0], post[0:width, :]) + column(0, width)
    gain = column(4 * width, 5 * width)
    shift = column(5 * width, 6 * width)
    unit, inverse, normed = norm_forward(middle, gain, shift)
    post[width : 2 * width, :] = normed
    post[2 * width : 3 * width, :] = unit.astype(BF)
    stat[H : H + 1, :] = inverse
    z = dot_nn(up_t[0], normed) + column(6 * width, 6 * width + hidden)
    active, slope = gelu_and_slope(z)
    post[3 * width : 3 * width + hidden, :] = active.astype(BF)
    post[3 * width + hidden :, :] = slope.astype(BF)
    return (
        middle
        + dot_nn(down_t[0], post[3 * width : 3 * width + hidden, :])
        + column(width, 2 * width)
    )


def launch(
    name, body, place, grid, ins, outs, scratch=(), flops=0, aliases=(), near=(), free=(),
    on_split=True,
):
    scratch = dict(scratch)
    names = [*ins, *outs, *scratch]

    def kernel(here, loops, counts, lengths, *refs):
        me, split = here[0], here[1]
        row = split if on_split else row_of_slot(me, split, loops.shape[0])
        facts = types.SimpleNamespace(
            me=me, split=split, slot=here[2], two=loops[row] == 2, count=counts[row], counts=counts,
            all_lengths=lengths, lengths=[lengths[row, k] for k in range(lengths.shape[1])],
        )
        body(facts, types.SimpleNamespace(**dict(zip(names, refs))))

    space = lambda key: pltpu.VMEM if key in near else pltpu.HBM
    results = pl.pallas_call(
        kernel,
        grid_spec=pltpu.PrefetchScalarGridSpec(
            num_scalar_prefetch=len(place),
            grid=(grid,),
            in_specs=[spec for _, spec in ins.values()],
            out_specs=[spec for _, spec in outs.values()],
            scratch_shapes=list(scratch.values()),
        ),
        out_shape=[
            shape if key in free else space(key)(shape.shape, shape.dtype)
            for key, (shape, _) in outs.items()
        ],
        input_output_aliases={
            len(place) + list(ins).index(source): list(outs).index(target) for source, target in aliases
        },
        compiler_params=pltpu.CompilerParams(vmem_limit_bytes=VMEM_LIMIT),
        cost_estimate=pl.CostEstimate(flops=flops, bytes_accessed=1, transcendentals=0),
        name=name,
    )(
        *[pltpu.with_memory_space_constraint(array, pltpu.HBM) for array in place],
        *[
            array if key in free else pltpu.with_memory_space_constraint(array, space(key))
            for key, (array, _) in ins.items()
        ],
    )
    return dict(zip(outs, results))


def whole(array):
    return array, pl.BlockSpec(array.shape, lambda i, *_: (0,) * len(array.shape))


def of_layer(array, layer):
    return array, pl.BlockSpec((1,) + array.shape[1:], lambda i, *_: (layer, 0, 0))


def each(array):
    return array, pl.BlockSpec((1,) + array.shape[1:], lambda i, *_: (i, 0, 0))


def each_back(array):
    count = array.shape[0]
    return array, pl.BlockSpec(
        (1,) + array.shape[1:], lambda i, *_: (count - 1 - i, 0, 0)
    )


def shaped(dims, dtype):
    return jax.ShapeDtypeStruct(dims, dtype)


def segment_starts(place, first, count):
    position = lax.broadcasted_iota(jnp.int32, (1, count), 1) + first
    starts = jnp.zeros((1, count), jnp.int32)
    end = jnp.int32(0)
    begin = jnp.int32(0)
    for length in place.lengths:
        end = end + length
        starts = jnp.where(position >= end, end, starts)
        begin = jnp.where(first >= end, end, begin)
    return starts, begin


def gather_tokens(env, name, me):
    for hop in range(4):
        env.spread[me ^ hop] = getattr(env, f"{name}_{hop}")[...]


def deal_tokens(env, name, value, chunk, me):
    for hop in range(4):

        @pl.when(chunk == (me ^ hop))
        def _(hop=hop):
            getattr(env, f"{name}_{hop}")[...] = value


def token_ins(name, blocks):
    return {f"{name}_{hop}": whole(block) for hop, block in enumerate(blocks)}


def token_outs(name, tokens, width):
    return {f"{name}_{hop}": whole(shaped((tokens, width), BF)) for hop in range(4)}


def as_tokens(values):
    return values.astype(BF).T


def as_features(tokens):
    return tokens.T.astype(F32)


def forward_rows(layer, place, vec, weights, state=None, tokens=None, first_end=None):
    chunks = 4
    count = state.shape[2] if tokens is None else tokens[0].shape[0]
    qkv_t, out_t, up_t, down_t = weights
    width, hidden = out_t.shape[2], up_t.shape[1]
    post_rows = 3 * width + 2 * hidden

    def body(place, env):
        chunk = pl.program_id(0)
        me = place.me
        current = env.state.at[0] if state is not None else None
        if tokens is not None:

            @pl.when(chunk == 0)
            def _():
                gather_tokens(env, "tokens", me)

            added = as_features(env.spread[chunk])
            env.current[...] = added if state is None else added + env.state[0]
            current = env.current
        project_qkv(
            current[...], env.qkv_t, env.vec, env.pre.at[0], env.kv.at[0], env.stat_pre.at[0],
            (width // H) ** -0.5, spread=True,
        )
        env.keys[chunk] = env.kv[0, 0:width, :].T
        env.values_t[chunk] = env.kv[0, width : 2 * width, :]
        start, begin = segment_starts(place, chunk * count, count)
        attend_chunk(
            env.pre.at[0, width : 2 * width, :], env.keys, env.values_t, chunk, begin, start, env.bias, env.total, env.stat_post.at[0],
            env.post.at[0, 0:width, :],
        )
        result = finish_layer(
            current[...], env.out_t, env.up_t, env.down_t, env.vec, env.post.at[0],
            env.stat_post.at[0], spread=True,
        )
        if first_end is None:
            env.result[0] = result
        else:
            answer = jnp.where(place.two, result, env.first_end[0])
            deal_tokens(env, "answer", as_tokens(answer), chunk, me)

    ins = {"vec": of_layer(vec, layer)}
    for name, weight in zip(("qkv_t", "out_t", "up_t", "down_t"), weights):
        ins[name] = of_layer(weight, layer)
    scratch = {
        "keys": pltpu.VMEM((chunks, count, width), BF),
        "values_t": pltpu.VMEM((chunks, width, count), BF),
        "bias": pltpu.VMEM((count, count), F32),
        "total": pltpu.VMEM((width, count), F32),
    }
    if state is not None:
        ins["state"] = each(state)
    if tokens is not None:
        ins |= token_ins("tokens", tokens)
        scratch["spread"] = pltpu.VMEM((chunks, count, width), BF)
        scratch["current"] = pltpu.VMEM((width, count), F32)
    outs = {}
    if first_end is None:
        outs["result"] = each(shaped((chunks, width, count), F32))
    else:
        ins["first_end"] = each(first_end)
        outs |= token_outs("answer", count, width)
    outs["pre"] = each(shaped((chunks, 3 * width, count), BF))
    outs["kv"] = each(shaped((chunks, 2 * width, count), BF))
    outs["post"] = each(shaped((chunks, post_rows, count), BF))
    outs["stat_pre"] = each(shaped((chunks, 8, count), F32))
    outs["stat_post"] = each(shaped((chunks, 8, count), F32))
    flops = chunks * count * 6 * (4 * width * width + 2 * width * hidden)
    return launch(
        "forward_rows", body, place, chunks, ins, outs, scratch, flops,
        on_split=False,
        near=["state", "result", "vec", "qkv_t", "out_t", "up_t", "down_t"]
        + [f"tokens_{hop}" for hop in range(4) if state is None],
    )


def split_row(array):
    return array, pl.BlockSpec((1,) + array.shape[1:], lambda i, here, *_: (here[1], 0, 0))


def row_of_slot(slot, split, rows):
    return jnp.where(slot == split, rows - 1, slot)


def forward_split(
    place, vec, weights, last=None, following=None, state=None, prev=None, pre=None,
    block_input=None, embedding=None, first_end=None, only_parts=False,
):
    qkv_t, out_t, up_t, down_t = weights
    width, hidden = out_t.shape[2], up_t.shape[1]
    count = embedding.shape[1] if state is None else state.shape[1]

    def body(place, env):
        me = place.me
        if last is not None:
            for hop in range(4):
                arrived = getattr(env, f"kv_{hop}")
                env.keys[me ^ hop] = arrived[0:width, :].T
                env.values_t[me ^ hop] = arrived[width : 2 * width, :]
            start, begin = segment_starts(place, me * count, count)
            attend_chunk(
                env.pre_in.at[width : 2 * width, :], env.keys, env.values_t, me, begin, start,
                env.bias, env.total, env.stat_post, env.post.at[0:width, :], paired=True,
            )
            current = finish_layer(
                env.state[...], env.out_t, env.up_t, env.down_t, env.vec, env.post, env.stat_post
            )
            if first_end is not None:
                answer = jnp.where(place.two, current, env.first_end[...])
                env.answer[...] = as_tokens(answer)
            else:
                env.result[...] = current
        if following is not None:
            if embedding is not None:
                added = as_features(env.embedding[0])
                if last is None:
                    current = as_features(env.block_input[0]) + added
                else:
                    current = env.result[...] + added
                env.begun[...] = current
            project_qkv(
                current, env.qkv_t, env.vec_next, env.pre, env.kv, env.stat_pre,
                (width // H) ** -0.5,
            )

    ins, outs, scratch = {}, {}, {}
    if last is not None:
        ins |= {f"kv_{hop}": whole(block) for hop, block in enumerate(prev)}
        ins |= {"state": whole(state), "pre_in": whole(pre)}
        ins["vec"] = of_layer(vec, last)
        for name, weight in zip(("out_t", "up_t", "down_t"), weights[1:]):
            ins[name] = of_layer(weight, last)
        if first_end is not None:
            ins["first_end"] = whole(first_end)
            outs["answer"] = whole(shaped((count, width), BF))
        else:
            outs["result"] = whole(shaped((width, count), F32))
        outs["post"] = whole(shaped((3 * width + 2 * hidden, count), BF))
        outs["stat_post"] = whole(shaped((8, count), F32))
        scratch = {
            "keys": pltpu.VMEM((4, count, width), BF),
            "values_t": pltpu.VMEM((4, width, count), BF),
            "bias": pltpu.VMEM((2 * count, count), F32),
            "total": pltpu.VMEM((width, count), F32),
        }
    if following is not None:
        ins["vec_next"] = of_layer(vec, following)
        ins["qkv_t"] = of_layer(qkv_t, following)
        if embedding is not None:
            ins["embedding"] = split_row(embedding)
            outs["begun"] = whole(shaped((width, count), F32))
        if block_input is not None:
            ins["block_input"] = split_row(block_input)
        outs["pre"] = whole(shaped((3 * width, count), BF))
        outs["kv"] = whole(shaped((2 * width, count), BF))
        outs["stat_pre"] = whole(shaped((8, count), F32))
    flops = 0 if last is None else count * 6 * (4 * width * width + 2 * width * hidden)
    near = ["state", "result", "begun", "pre", "pre_in", "kv", "vec", "vec_next"]
    near += ["qkv_t", "out_t", "up_t", "down_t"] + [f"kv_{hop}" for hop in range(4)]
    if only_parts:
        return body, ins, outs, scratch, near
    return launch("forward_split", body, place, 1, ins, outs, scratch, flops, near=near)


def backward_ffn(grad, unit, slope, stat, wout, wup, wdown, vec, hidden_grad):
    width, tokens = grad.shape
    low_grad = grad.astype(BF)
    hidden_grad[...] = (
        dot_nn(wdown[0], low_grad)
        * jnp.concatenate([ref[...] for ref in slope], axis=0).astype(F32)
    ).astype(BF)
    normed_grad = dot_nn(wup[0], hidden_grad[...])
    unit = unit[...].astype(F32)
    gain = columns(vec, tokens)(4 * width, 5 * width)
    middle = grad + norm_backward(normed_grad, unit, stat[H : H + 1, :], gain)
    low_middle = middle.astype(BF)
    blend_grad = dot_nn(wout[0], low_middle).astype(BF)
    return low_grad, normed_grad, unit, middle, low_middle, blend_grad


def token_sum(rows):
    return dot_nt(jnp.ones((ONES_ROWS, rows.shape[1]), BF), rows.astype(BF))


def attend_backward(
    queries, blend_grad, blended, stat, keys, values, keys_t, chunk, begin, start,
    bias, query_grad, kv_grad, paired=False,
):
    width, tokens = queries.shape
    head = width // H
    pair = 2 * head
    head_rows = [slice(h * head, (h + 1) * head) for h in range(H)]
    deltas = [
        jnp.sum(
            blend_grad[rows, :].astype(F32) * blended[rows, :].astype(F32), axis=0, keepdims=True
        )
        for rows in head_rows
    ]

    half = tokens // 2
    everything = slice(0, tokens)

    def products(j, span):
        parts, prob_grads = [], []
        for h, rows in enumerate(head_rows):
            lanes = pl.ds((h // 2) * pair, pair)
            parts.append(dot_nn(keys[j, span, lanes], pad_head(queries[rows, :], h % 2)))
            prob_grads.append(
                dot_nn(values[j, span, lanes], pad_head(blend_grad[rows, :], h % 2))
            )
        return parts, prob_grads

    def collect(j, span, probs, score_grads, first):
        for rows, prob, score_grad in zip(head_rows, probs, score_grads):
            value_rows = slice(width + rows.start, width + rows.stop)
            kv_grad[j, value_rows, span] += dot_nt(blend_grad[rows, :], prob)
            kv_grad[j, rows, span] += dot_nt(queries[rows, :], score_grad)
            term = dot_nn(keys_t(j, rows, span), score_grad)
            if first:
                query_grad[rows, :] = term
            else:
                query_grad[rows, :] += term

    def weigh(part, prob_grad, mask, logsum, delta):
        prob = jnp.exp(part + mask - logsum)
        return prob.astype(BF), (prob * (prob_grad - delta)).astype(BF)

    bias[:tokens, :] = tile_bias(chunk * tokens, start, True, (tokens, tokens))
    probs, score_grads = [], []
    for h, (part, prob_grad) in enumerate(zip(*products(chunk, everything))):
        logsum, delta = stat[h : h + 1, :], deltas[h]
        upper = weigh(part[:half, :], prob_grad[:half, :], bias[:half, :], logsum, delta)
        lower = weigh(
            part[half:, half:], prob_grad[half:, half:], bias[half:tokens, half:], logsum[:, half:],
            delta[:, half:],
        )
        for kept, above, below in zip((probs, score_grads), upper, lower):
            below = jnp.concatenate([jnp.zeros_like(below), below], axis=1)
            kept.append(jnp.concatenate([above, below], axis=0))
    collect(chunk, everything, probs, score_grads, True)

    def step(tiles, span, size, carry):
        made = []
        for at, j in enumerate(tiles):
            mask = slice(at * tokens, at * tokens + size)
            bias[mask, :] = tile_bias(j * tokens + span.start, start, False, (size, tokens))
            made.append((mask, *products(j, span)))
        weighed = [
            [
                weigh(part, prob_grad, bias[mask, :], stat[h : h + 1, :], deltas[h])
                for h, (part, prob_grad) in enumerate(zip(parts, prob_grads))
            ]
            for mask, parts, prob_grads in made
        ]
        for j, pairs in zip(tiles, weighed):
            collect(j, span, [p for p, _ in pairs], [d for _, d in pairs], False)
        return carry

    over_tiles(
        chunk, tokens, begin,
        lambda j, carry: step([j], slice(half, tokens), half, carry),
        lambda j, carry: step([j], everything, tokens, carry),
        0,
        (lambda j, carry: step([j, j + 1], everything, tokens, carry)) if paired else None,
    )


def add_vec(sum_vec, width, low_grad, normed_grad, unit, low_middle, dz):
    sum_vec[:, 0:width] += token_sum(low_middle)
    sum_vec[:, width : 2 * width] += token_sum(low_grad)
    sum_vec[:, 4 * width : 5 * width] += token_sum(normed_grad * unit)
    sum_vec[:, 5 * width : 6 * width] += token_sum(normed_grad)
    sum_vec[:, 6 * width :] += token_sum(dz)


def finish_backward(middle, pre, stat, packed, wqkv, vec, sum_qkv, sum_vec):
    width, tokens = middle.shape
    sum_qkv[...] += dot_nt(pre[0:width, :], packed[...])
    normed_grad = dot_nn(wqkv[0], packed[...])
    unit = pre[2 * width : 3 * width, :].astype(F32)
    gain = columns(vec, tokens)(2 * width, 3 * width)
    sum_vec[:, 2 * width : 3 * width] += token_sum(normed_grad * unit)
    sum_vec[:, 3 * width : 4 * width] += token_sum(normed_grad)
    return middle + norm_backward(normed_grad, unit, stat[0:1, :], gain)


def pack_lanes(wire, blocks):
    at = 0
    for ref in blocks:
        rows = ref.shape[0]
        for first in range(0, ref.shape[1], 128):
            wire[at : at + rows, :] = ref[:, first : first + 128].astype(BF)
            at += rows


def put_pieces(keep, give, source, first, height, core):
    half = keep.shape[0]
    for ref, side in ((keep, core), (give, 1 - core)):
        for p in range(half):
            at = pl.multiple_of((side * half + p) * height, 16)
            ref[p, first : first + height, :] = source[pl.ds(at, height), :]


def count_digits(place, groups):
    tally = place.counts[0]
    for k in range(1, place.counts.shape[0]):
        tally = tally + place.counts[k]
    lane = lax.broadcasted_iota(jnp.int32, (16, 128), 1)
    row = lax.broadcasted_iota(jnp.int32, (16, 128), 0)
    digit = jnp.where(lane % 2 == 0, tally // 256, tally % 256)
    keep = (lane // 2 == place.slot) & (row == 0) & (place.me == 0)
    return jnp.where(keep, digit, 0).astype(F32).astype(BF)


def backward_rows(
    layer, place, saved, vec, weights, five, base=None, grad=None, tokens=None,
    keep=True, travel=False, part_done=None, ffn_only=False, half=0, digits=False,
    closing=None, others=None,
):
    chunks, _, count = saved["kv"].shape
    wqkv, wout, wup, wdown = weights
    width, hidden = wup.shape[1:]
    row_len = chunks * count
    first = base is None
    part = hidden // chunks
    vec_len = 6 * width + hidden
    with_ffn, with_attention = part_done is None, not ffn_only

    def body(place, env):
        order = pl.program_id(0)
        chunk = chunks - 1 - order
        me = place.me

        @pl.when(order == 0)
        def _():
            if tokens is not None:
                gather_tokens(env, "tokens", me)
            if with_ffn:
                env.sum_up[...] = jnp.zeros_like(env.sum_up)
                env.sum_down[...] = jnp.zeros_like(env.sum_down)
                env.sum_out[...] = dot_nt(env.blend_five[...], env.middle_five[...])
                env.sum_vec[...] = env.vec_five[...]
                if not first:
                    env.sum_vec[...] += env.base_vec[...]
            else:
                env.sum_vec[...] = env.vec_done[...]
            if with_attention:
                env.sum_qkv[...] = jnp.zeros_like(env.sum_qkv)
                env.kv_grad[...] = jnp.zeros_like(env.kv_grad)
                for j in range(chunks):
                    env.keys[j] = env.kv[j, 0:width, :].T
                    env.values[j] = env.kv[j, width : 2 * width, :].T

        def add_base(ref, old):
            rows = old.shape[0]
            ref[pl.ds(pl.multiple_of(order * rows, rows), rows), :] += old[...].astype(F32)

        if with_ffn:
            spread = pl.ds(pl.multiple_of(order * part, part), part)
            env.sum_down[spread, :] += dot_nt(env.active_five[...], env.low_five[...])
            env.sum_up[:, spread] += dot_nt(env.normed_five[...], env.hidden_five[...])
            if not first:
                env.sum_down[spread, :] += env.base_down[...].astype(F32)
                env.sum_up[:, spread] += env.base_up[...].astype(F32)
                add_base(env.sum_out, env.base_out)
            current = env.grad.at[0] if grad is not None else None
            if tokens is not None:
                top = as_features(env.spread[chunk]) * (place.count.astype(F32) * (1.0 / row_len))
                two = place.two
                env.current[...] = (
                    jnp.where(two, top, 0.0)
                    if grad is None
                    else jnp.where(two, env.grad[0], top)
                )
                current = env.current
            post = env.post.at[0]
            low_grad, normed_grad, unit, middle, low_middle, blend_grad = backward_ffn(
                current[...], post.at[2 * width : 3 * width, :],
                [post.at[3 * width + hidden : 3 * width + 2 * hidden, :]], env.stat_post.at[0], env.wout, env.wup, env.wdown, env.vec,
                env.hidden_grad,
            )
            env.sum_down[...] += dot_nt(post[3 * width : 3 * width + hidden, :], low_grad)
            env.sum_up[...] += dot_nt(post[width : 2 * width, :], env.hidden_grad[...])
            env.sum_out[...] += dot_nt(post[0:width, :], low_middle)
            add_vec(
                env.sum_vec, width, low_grad, normed_grad, unit, low_middle, env.hidden_grad[...]
            )
            blend_ref = env.blend_grad if with_attention else env.blend_out.at[0]
            blend_ref[...] = blend_grad
            if first:

                @pl.when(order == chunks - 1)
                def _():
                    for name in ("sum_out", "sum_up", "sum_down"):
                        getattr(env, name + "_low")[...] = getattr(env, name)[...].astype(BF)

            if not first:

                @pl.when(order == chunks - 1)
                def _():
                    pack_lanes(env.wire, (env.sum_out, env.sum_up, env.sum_down))
                    height = env.wire.shape[0] // (2 * half)
                    put_pieces(env.keep, env.give, env.wire, 0, height, me % 2)
                    if digits:
                        blank = jnp.zeros((16, 128), BF)
                        for p in range(half):
                            env.keep[p, height:, :] = count_digits(place, half) if p == 0 else blank
                            env.give[p, height:, :] = blank

            if not with_attention:
                env.middle_out[0] = middle
                return
            blended = post.at[0:width, :]
        else:
            middle, blend_ref, blended = env.middle_in[0], env.blend_in.at[0], env.blended.at[0]
        if not first:
            add_base(env.sum_qkv, env.base_qkv)
        start, begin = segment_starts(place, chunk * count, count)
        attend_backward(
            env.pre.at[0, width : 2 * width, :], blend_ref, blended,
            env.stat_post.at[0], env.keys, env.values, lambda j, rows, span: env.kv[j, rows, span],
            chunk, begin, start, env.bias, env.query_grad, env.kv_grad,
        )
        env.packed[0:width, :] = (env.query_grad[...] * (width // H) ** -0.5).astype(BF)
        env.packed[width : 3 * width, :] = env.kv_grad[chunk].astype(BF)
        result = finish_backward(
            middle, env.pre.at[0], env.stat_pre.at[0], env.packed, env.wqkv, env.vec,
            env.sum_qkv, env.sum_vec,
        )
        if keep:
            env.result[0] = result
        if travel:
            deal_tokens(env, "travel", as_tokens(result), chunk, me)
        if closing is not None:

            @pl.when(order == chunks - 1)
            def _():
                ended = end_split_row(env, env.vec, env.sum_qkv, env.sum_vec)
                env.split_result[...] = ended.T
                write_last_payload(env, half, me % 2)

    ins = {"vec": of_layer(vec, layer), "stat_post": each_back(saved["stat_post"])}
    outs, scratch = {}, {}
    cut = lambda array, shape, at: (array, pl.BlockSpec(shape, lambda i, *_: at(i)))
    sums = {"sum_vec": (ONES_ROWS, vec_len)}
    if with_ffn:
        ins["post"] = each_back(saved["post"])
        for name, weight in zip(("wout", "wup", "wdown"), weights[1:]):
            ins[name] = of_layer(weight, layer)
        if grad is not None:
            ins["grad"] = each_back(grad)
        if tokens is not None:
            ins |= token_ins("tokens", tokens)
            scratch["spread"] = pltpu.VMEM((chunks, count, width), BF)
            scratch["current"] = pltpu.VMEM((width, count), F32)
        post_five = five["post"]
        ins["blend_five"] = cut(post_five, (width, count), lambda i: (0, 0))
        ins["normed_five"] = cut(post_five, (width, count), lambda i: (1, 0))
        ins["active_five"] = cut(post_five, (part, count), lambda i: (3 * width // part + i, 0))
        ins["hidden_five"] = cut(five["hidden"], (part, count), lambda i: (i, 0))
        for name in ("low", "middle", "vec"):
            ins[name + "_five"] = whole(five[name])
        sums |= {"sum_out": (width, width), "sum_up": (width, hidden), "sum_down": (hidden, width)}
        scratch["hidden_grad"] = pltpu.VMEM((hidden, count), BF)
        if not first:
            ins["base_out"] = cut(base["sum_out_low"], (width // chunks, width), lambda i: (i, 0))
            ins["base_up"] = cut(base["sum_up_low"], (width, part), lambda i: (0, i))
            ins["base_down"] = cut(base["sum_down_low"], (part, width), lambda i: (i, 0))
            ins["base_vec"] = whole(base["sum_vec"])
            wire_rows = (width * width + 2 * width * hidden) // 128
            scratch["wire"] = pltpu.VMEM((wire_rows, 128), BF)
            height = wire_rows // (2 * half) + (16 if digits else 0)
            outs["keep"] = whole(shaped((half, height, 128), BF))
            outs["give"] = whole(shaped((half, height, 128), BF))
        if not with_attention:
            outs["blend_out"] = each_back(shaped((chunks, width, count), BF))
            outs["middle_out"] = each_back(shaped((chunks, width, count), F32))
    else:
        ins["vec_done"] = whole(part_done["sum_vec"])
        ins["middle_in"] = each_back(part_done["middle_out"])
        ins["blend_in"] = each_back(part_done["blend_out"])
        ins["blended"] = (
            saved["post"],
            pl.BlockSpec((1, width, count), lambda i, *_: (chunks - 1 - i, 0, 0)),
        )
    if with_attention:
        ins["kv"] = whole(saved["kv"])
        ins["pre"] = each_back(saved["pre"])
        ins["stat_pre"] = each_back(saved["stat_pre"])
        ins["wqkv"] = of_layer(wqkv, layer)
        sums["sum_qkv"] = (width, 3 * width)
        if not first:
            ins["base_qkv"] = cut(base["sum_qkv"], (width // chunks, 3 * width), lambda i: (i, 0))
        if keep:
            outs["result"] = each_back(shaped((chunks, width, count), F32))
        if travel:
            outs |= token_outs("travel", count, width)
        scratch |= {
            "keys": pltpu.VMEM((chunks, count, width), BF),
            "values": pltpu.VMEM((chunks, count, width), BF),
            "bias": pltpu.VMEM((count, count), F32),
            "query_grad": pltpu.VMEM((width, count), F32),
            "kv_grad": pltpu.VMEM((chunks, 2 * width, count), F32),
            "blend_grad": pltpu.VMEM((width, count), BF),
            "packed": pltpu.VMEM((3 * width, count), BF),
        }
    if closing is not None:
        ins |= split_row_ins(closing)
        wire_rows = 3 * width * width // 128
        height = 2 * (wire_rows // (2 * half)) + 16
        ins["wire_other"] = whole(others["wire"])
        ins["vec_other"] = whole(others["vec"])
        outs["keep"] = whole(shaped((half, height, 128), BF))
        outs["give"] = whole(shaped((half, height, 128), BF))
        outs["split_result"] = whole(shaped((count, width), F32))
        scratch["wire"] = pltpu.VMEM((wire_rows, 128), BF)
        scratch["small"] = pltpu.VMEM((4 * half, 128), F32)
        scratch |= {name: pltpu.VMEM(dims, F32) for name, dims in sums.items()}
        sums = {}
    for name, dims in sums.items():
        if name in ("sum_qkv", "sum_vec"):
            outs[name] = whole(shaped(dims, F32))
        else:
            scratch[name] = pltpu.VMEM(dims, F32)
            if first:
                outs[name + "_low"] = whole(shaped(dims, BF))
    flops = chunks * count * 12 * (4 * width * width + 2 * width * hidden)
    return launch(
        "backward_rows", body, place, chunks, ins, outs, scratch, flops, on_split=False,
        near=[
            "middle_in_split", "query_in", "own_in", "in_1", "in_2", "in_3",
            "hidden_five", "low_five", "middle_five", "vec_five",
        ],
    )


def split_row_ins(ended):
    ins = {
        "middle_in_split": whole(ended["middle_out"]), "query_in": whole(ended["query_out"]),
        "own_in": whole(ended["own_out"]), "pre_last": whole(ended["pre"]),
        "stat_last": whole(ended["stat_pre"]),
    }
    return ins | {f"in_{hop}": whole(ended["arrived"][hop - 1]) for hop in range(1, 4)}


def end_split_row(env, vec, sum_qkv, sum_vec):
    width = env.query_in.shape[0]
    env.packed[0:width, :] = env.query_in[...]
    kv_total = env.own_in[...]
    for hop in range(1, 4):
        kv_total = kv_total + getattr(env, f"in_{hop}")[...].astype(F32)
    env.packed[width : 3 * width, :] = kv_total.astype(BF)
    return finish_backward(
        env.middle_in_split[...], env.pre_last, env.stat_last, env.packed, env.wqkv, vec,
        sum_qkv, sum_vec,
    )


def write_last_payload(env, half, core):
    pack_lanes(env.wire, (env.sum_qkv,))
    height = env.wire.shape[0] // (2 * half)
    put_pieces(env.keep, env.give, env.wire, 0, height, core)
    put_pieces(env.keep, env.give, env.wire_other, height, height, core)
    rows = env.sum_vec.shape[1] // 128
    env.small[...] = jnp.zeros_like(env.small)
    for at, ref in ((0, env.sum_vec), (rows, env.vec_other)):
        for k in range(rows):
            env.small[at + k : at + k + 1, :] = ref[0:1, 128 * k : 128 * k + 128]
    for p in range(half):
        left = env.small[2 * p : 2 * p + 2, :]
        right = env.small[2 * (p + half) : 2 * (p + half) + 2, :]
        for ref, first in ((env.keep, core == 0), (env.give, core == 1)):
            pair = jnp.where(first, left, right)
            blank = jnp.zeros((14, 128), F32)
            ref[p, 2 * height :, :] = jnp.concatenate([pair, blank]).astype(BF)


def backward_split(
    place, vec, weights, last=None, following=None, ended=None, sums=None, begun=None,
    cotangent=None, final=False, keep=False, row_len=None, only_parts=False,
):
    wqkv, wout, wup, wdown = weights
    width, hidden = wup.shape[1:]
    vec_len = 6 * width + hidden
    count = (ended or begun)["stat_pre"].shape[1]

    def body(place, env):
        me = place.me
        if last is not None:
            sum_qkv = env.total_qkv if final else env.sum_qkv
            sum_qkv[...] = env.old_qkv[...]
            env.sum_vec[...] = env.old_vec[...]
            current = end_split_row(env, env.vec_last, sum_qkv, env.sum_vec)
            if keep:
                env.result[...] = current.T
            if final:
                pack_lanes(env.wire, (sum_qkv,))
        if following is not None:
            if cotangent is not None:
                top = as_features(env.cotangent[0]) * (place.count.astype(F32) * (1.0 / row_len))
                two = place.two
                grad = jnp.where(two, top, 0.0) if last is None else jnp.where(two, current, top)
            else:
                grad = current
            env.kv_grad[...] = jnp.zeros_like(env.kv_grad)
            for hop in range(4):
                arrived = getattr(env, f"kv_{hop}")
                env.keys[me ^ hop] = arrived[0:width, :].T
                env.keys_t[me ^ hop] = arrived[0:width, :]
                env.values[me ^ hop] = arrived[width : 2 * width, :].T
            if hasattr(env, "post"):
                queries = env.pre.at[width : 2 * width, :]
                blended, unit_rows = env.post.at[0:width, :], env.post.at[2 * width : 3 * width, :]
                slope = [env.post.at[3 * width + hidden : 3 * width + 2 * hidden, :]]
            else:
                queries, blended, unit_rows = env.queries, env.blended, env.unit
                slope = [getattr(env, f"slope_{k}") for k in range(hidden // width)]
            low_grad, normed_grad, unit, middle, low_middle, blend_grad = backward_ffn(
                grad, unit_rows, slope, env.stat_post, env.wout, env.wup, env.wdown, env.vec, env.hidden
            )
            env.low[...] = low_grad
            env.middle[...] = low_middle
            env.middle_out[...] = middle
            env.vec_out[...] = jnp.zeros_like(env.vec_out)
            add_vec(
                env.vec_out, width, low_grad, normed_grad, unit, low_middle, env.hidden[...]
            )
            env.blend_grad[...] = blend_grad
            start, begin = segment_starts(place, me * count, count)
            attend_backward(
                queries, env.blend_grad, blended,
                env.stat_post, env.keys, env.values, lambda j, rows, span: env.keys_t[j, rows, span],
                me, begin, start, env.bias, env.query_grad, env.kv_grad, paired=True,
            )
            env.query_out[...] = (env.query_grad[...] * (width // H) ** -0.5).astype(BF)
            env.own_out[...] = env.kv_grad[me]
            for hop in range(1, 4):
                getattr(env, f"away_{hop}")[...] = env.kv_grad[me ^ hop].astype(BF)

    ins, outs, scratch = {}, {}, {}
    if last is not None:
        ins |= split_row_ins(ended)
        ins["vec_last"] = of_layer(vec, last)
        ins["wqkv"] = of_layer(wqkv, last)
        ins["old_qkv"] = whole(sums["sum_qkv"])
        ins["old_vec"] = whole(sums["sum_vec"])
        if keep:
            outs["result"] = whole(shaped((count, width), F32))
        if final:
            outs["wire"] = whole(shaped((3 * width * width // 128, 128), BF))
        if final:
            scratch["total_qkv"] = pltpu.VMEM((width, 3 * width), F32)
        else:
            outs["sum_qkv"] = whole(shaped((width, 3 * width), F32))
        outs["sum_vec"] = whole(shaped((ONES_ROWS, vec_len), F32))
        scratch["packed"] = pltpu.VMEM((3 * width, count), BF)
    if following is not None:
        rows_at = lambda array, k: (array, pl.BlockSpec((width, count), lambda i, *_: (k, 0)))
        ins["queries"] = rows_at(begun["pre"], 1)
        ins["blended"] = rows_at(begun["post"], 0)
        ins["unit"] = rows_at(begun["post"], 2)
        for k in range(hidden // width):
            ins[f"slope_{k}"] = rows_at(begun["post"], 3 + hidden // width + k)
        ins["stat_post"] = whole(begun["stat_post"])
        for hop in range(4):
            ins[f"kv_{hop}"] = whole(begun["kv"][hop])
        ins["vec"] = of_layer(vec, following)
        for name, weight in zip(("wout", "wup", "wdown"), weights[1:]):
            ins[name] = of_layer(weight, following)
        if cotangent is not None:
            ins["cotangent"] = split_row(cotangent)
        outs["middle_out"] = whole(shaped((width, count), F32))
        outs["query_out"] = whole(shaped((width, count), BF))
        outs["own_out"] = whole(shaped((2 * width, count), F32))
        for hop in range(1, 4):
            outs[f"away_{hop}"] = whole(shaped((2 * width, count), BF))
        outs["low"] = whole(shaped((width, count), BF))
        outs["hidden"] = whole(shaped((hidden, count), BF))
        outs["middle"] = whole(shaped((width, count), BF))
        outs["vec_out"] = whole(shaped((ONES_ROWS, vec_len), F32))
        scratch |= {
            "keys": pltpu.VMEM((4, count, width), BF),
            "values": pltpu.VMEM((4, count, width), BF),
            "keys_t": pltpu.VMEM((4, width, count), BF),
            "bias": pltpu.VMEM((2 * count, count), F32),
            "query_grad": pltpu.VMEM((width, count), F32),
            "kv_grad": pltpu.VMEM((4, 2 * width, count), F32),
            "blend_grad": pltpu.VMEM((width, count), BF),
        }
    flops = count * 12 * (4 * width * width + 2 * width * hidden)
    near = [
        "middle_in_split", "query_in", "own_in", "in_1", "in_2", "in_3", "middle_out",
        "query_out", "own_out", "away_1", "away_2", "away_3", "low", "hidden", "middle", "vec_out",
    ]
    if only_parts:
        return body, ins, outs, scratch, near
    return launch("backward_split", body, place, 1, ins, outs, scratch, flops, near=near)


def turn_split(
    place, vec, forward_weights, backward_weights, layer, state, blocks, pre, stat_pre, first_end,
    cotangent, row_len,
):
    forward, ins, outs, scratch, near = forward_split(
        place, vec, forward_weights, last=layer, state=state, prev=blocks, pre=pre,
        first_end=first_end, only_parts=True,
    )
    begun = {"pre": pre, "kv": blocks, "stat_pre": stat_pre, "post": pre, "stat_post": stat_pre}
    backward, more_ins, more_outs, more_scratch, more_near = backward_split(
        place, vec, backward_weights, following=layer, begun=begun, cotangent=cotangent,
        row_len=row_len, only_parts=True,
    )
    shared = ["queries", "blended", "unit", "stat_post", "vec"]
    shared += [key for key in more_ins if key.startswith(("kv_", "slope_"))]
    more_ins = {key: value for key, value in more_ins.items() if key not in shared}

    def body(place, env):
        forward(place, env)
        env.pre = env.pre_in
        backward(place, env)

    return launch(
        "turn_split", body, place, 1, ins | more_ins, outs | more_outs, scratch | more_scratch,
        near=near + more_near,
    )


def cut_tokens(place, *pairs):
    arrays = [array for pair in pairs for array in pair]
    rows, count, width = arrays[0].shape

    def body(place, env):
        me = place.me
        best, longest = jnp.int32(0), jnp.int32(0)
        for row in range(rows):
            most = place.all_lengths[row, 0]
            for k in range(1, place.all_lengths.shape[1]):
                most = jnp.maximum(most, place.all_lengths[row, k])
            longest = jnp.where(most > best, row, longest)
            best = jnp.maximum(most, best)
        env.here[0] = me
        env.here[1] = longest
        env.here[2] = place.slot
        for hop in range(4):
            row = row_of_slot(me ^ hop, longest, rows)
            at = 0
            for index, pair in enumerate(pairs):
                value = getattr(env, f"in_{at}")[row].astype(F32)
                for extra in range(1, len(pair)):
                    value = value + getattr(env, f"in_{at + extra}")[row].astype(F32)
                at += len(pair)
                getattr(env, f"out{index}_{hop}")[...] = value.astype(BF)

    ins = {f"in_{k}": whole(array) for k, array in enumerate(arrays)}
    outs = {}
    for index in range(len(pairs)):
        outs |= token_outs(f"out{index}", count, width)
    outs["here"] = (shaped((3,), jnp.int32), pl.BlockSpec(memory_space=pltpu.SMEM))
    results = launch("cut_tokens", body, place, 1, ins, outs, free=("here",))
    blocks = [[results[f"out{index}_{hop}"] for hop in range(4)] for index in range(len(pairs))]
    return results["here"], blocks


def prepare(place, weights, vectors):
    out_bias, down_bias, norm_gain, norm_shift, up_bias = vectors
    layers, width = out_bias.shape
    hidden = up_bias.shape[1]
    rows = (6 * width + hidden) // 128
    rows += -rows % 8

    def body(place, env):
        layer = pl.program_id(0)
        for k in range(4):
            getattr(env, f"turned_{k}")[0] = getattr(env, f"weight_{k}")[0].T
        env.vec[...] = jnp.zeros_like(env.vec)
        pick = lambda ref: ref[pl.ds(layer, 1), :]
        parts = [pick(env.out_bias), pick(env.down_bias)]
        for k in range(2):
            parts += [env.norm_gain[0, k : k + 1, :], env.norm_shift[0, k : k + 1, :]]
        at = 0
        for part in parts + [pick(env.up_bias)]:
            for lanes in range(0, part.shape[1], 128):
                env.vec[0, at : at + 1, :] = part[:, lanes : lanes + 128]
                at += 1

    ins = {f"weight_{k}": each(weight) for k, weight in enumerate(weights)}
    ins |= {"out_bias": whole(out_bias), "down_bias": whole(down_bias), "up_bias": whole(up_bias)}
    ins |= {"norm_gain": each(norm_gain), "norm_shift": each(norm_shift)}
    outs = {
        f"turned_{k}": each(shaped((layers, weight.shape[2], weight.shape[1]), BF))
        for k, weight in enumerate(weights)
    }
    outs["vec"] = each(shaped((layers, rows, 128), F32))
    results = launch("prepare", body, place, layers, ins, outs, near=list(outs))
    return tuple(results[f"turned_{k}"] for k in range(4)), results["vec"]


def piece_reader(payloads, me):
    mine, other = payloads
    half = mine.shape[0]

    def piece(p, first, rows):
        left, right = (ref[p % half, first : first + rows, :] for ref in (mine, other))
        return jnp.where(me % 2 == p // half, left, right).astype(F32)

    return piece


def spread_pieces(piece, pieces, first, rows_each, targets, factor):
    edges, at = [], 0
    for ref in targets:
        for lanes in range(0, ref.shape[2], 128):
            edges.append((at, at + ref.shape[1], ref, lanes))
            at += ref.shape[1]
    for p in range(pieces):
        values = piece(p, first, rows_each) * factor
        begin = p * rows_each
        for low, high, ref, lanes in edges:
            left, right = max(low, begin), min(high, begin + rows_each)
            if left < right:
                ref[0, left - low : right - low, lanes : lanes + 128] = values[
                    left - begin : right - begin, :
                ]


def finish_tokens(
    place, payload, answer, answer_split, first, first_split, second, second_split,
    hidden, groups, row_len,
):
    count, width = first_split.shape
    rows = 5
    pieces = 2 * payload[0].shape[0]
    ffn_rows = (width * width + 2 * width * hidden) // 128 // pieces

    def body(place, env):
        step = pl.program_id(0)
        me = place.me
        piece = piece_reader((env.mine, env.other), me)
        lane = lax.broadcasted_iota(jnp.int32, (1, 128), 1)
        total = jnp.zeros((1, 1), F32)
        for extra in range(-(-2 * groups // 128)):
            row = piece(extra, ffn_rows, 16)[0:1, :]
            worth = jnp.where(lane % 2 == 0, 256.0, 1.0)
            row = jnp.where(lane + extra * 128 < 2 * groups, row * worth, 0.0)
            total = total + jnp.sum(row, axis=1, keepdims=True)
        factor = row_len / total
        token_factor = factor * float(rows * groups)

        @pl.when(step == 0)
        def _():
            env.scale[...] = jnp.broadcast_to(factor, env.scale.shape)
            spread_pieces(piece, pieces, 0, ffn_rows, (env.out, env.up, env.down), factor)

        for hop in range(4):

            @pl.when(step == row_of_slot(me ^ hop, place.split, rows))
            def _(hop=hop):
                env.block_output[0] = getattr(env, f"answer_{hop}")[...]
                one = getattr(env, f"first_{hop}")[...].astype(F32)
                two = getattr(env, f"second_{hop}")[...].astype(F32)
                env.input_grad[0] = one * token_factor
                env.embed_grad[0] = (one + two) * token_factor

        @pl.when(step == place.split)
        def _():
            env.block_output[0] = env.answer_split[...]
            one = env.first_split[...]
            env.input_grad[0] = one * token_factor
            env.embed_grad[0] = (one + env.second_split[...]) * token_factor

    ins = {"mine": whole(payload[0]), "other": whole(payload[1])}
    ins |= token_ins("answer", answer) | token_ins("first", first) | token_ins("second", second)
    ins["answer_split"] = whole(answer_split)
    ins["first_split"] = whole(first_split)
    ins["second_split"] = whole(second_split)
    later = lambda *dims: (
        shaped(dims, F32), pl.BlockSpec((1,) + dims[1:], lambda i, *_: (LAYERS - 1, 0, 0))
    )
    outs = {
        "block_output": each(shaped((rows, count, width), BF)),
        "input_grad": each(shaped((rows, count, width), F32)),
        "embed_grad": each(shaped((rows, count, width), F32)),
        "out": later(LAYERS, width, width),
        "up": later(LAYERS, width, hidden),
        "down": later(LAYERS, hidden, width),
        "scale": whole(shaped((8, 128), F32)),
    }
    return launch(
        "finish_tokens", body, place, rows, ins, outs, free=("mine", "other")
    )


def finish_weights(place, payload, done, width, hidden):
    pieces = 2 * payload[0].shape[0]
    ffn_rows = (width * width + 2 * width * hidden) // 128 // pieces
    qkv_rows = 3 * width * width // 128 // pieces
    small_at = ffn_rows + LAYERS * qkv_rows
    vec_len = 6 * width + hidden

    def body(place, env):
        step = pl.program_id(0)
        piece = piece_reader((env.mine, env.other), place.me)
        factor = env.scale[0:1, 0:1]

        @pl.when(step == 0)
        def _():
            spread_pieces(piece, pieces, 0, ffn_rows, (env.out, env.up, env.down), factor)
            for here in range(LAYERS):
                for ref, slot, at, size in (
                    (env.out_b, None, 0, width),
                    (env.down_b, None, width, width),
                    (env.gain, 0, 2 * width, width),
                    (env.shift, 0, 3 * width, width),
                    (env.gain, 1, 4 * width, width),
                    (env.shift, 1, 5 * width, width),
                    (env.up_b, None, 6 * width, hidden),
                ):
                    for lanes in range(0, size, 128):
                        index = (here * vec_len + at + lanes) // 128
                        row = piece(index // 2, small_at, 16)[index % 2 : index % 2 + 1, :]
                        row = row * factor
                        if slot is None:
                            ref[here : here + 1, lanes : lanes + 128] = row
                        else:
                            ref[here, slot : slot + 1, lanes : lanes + 128] = row

        for here in range(LAYERS):

            @pl.when(step == here)
            def _(here=here):
                spread_pieces(
                    piece, pieces, ffn_rows + here * qkv_rows, qkv_rows, (env.qkv,), factor
                )

    ins = {"mine": whole(payload[0]), "other": whole(payload[1]), "scale": whole(done["scale"])}
    names = ("out", "up", "down")
    for name in names:
        ins[name + "_done"] = (done[name], pl.BlockSpec(memory_space=pl.ANY))
    start = lambda array: (
        array, pl.BlockSpec((1,) + array.shape[1:], lambda i, *_: (0, 0, 0))
    )
    outs = {name: start(shaped(done[name].shape, F32)) for name in names}
    outs["qkv"] = each(shaped((LAYERS, width, 3 * width), F32))
    outs["out_b"] = whole(shaped((LAYERS, width), F32))
    outs["up_b"] = whole(shaped((LAYERS, hidden), F32))
    outs["down_b"] = whole(shaped((LAYERS, width), F32))
    outs["gain"] = whole(shaped((LAYERS, 2, width), F32))
    outs["shift"] = whole(shaped((LAYERS, 2, width), F32))
    return launch(
        "finish_weights", body, place, LAYERS, ins, outs,
        aliases=[(name + "_done", name) for name in names],
        free=("mine", "other"),
    )


SEQ = ("y", "core")
CHIPS = ("dp", "y")


def swap(values, hop):
    return lax.ppermute(values, SEQ, [(i, i ^ hop) for i in range(lax.axis_size(SEQ))])


def swap_blocks(blocks):
    return [blocks[0]] + [swap(block, hop) for hop, block in enumerate(blocks[1:], 1)]


def sum_cores(keep, got):
    return (keep.astype(F32) + got.astype(F32)).astype(BF)


def sum_chips(part):
    part = lax.all_to_all(part, CHIPS, 0, 0, tiled=True)
    return jnp.sum(part.astype(F32), axis=0).astype(BF)


def share_chips(part):
    copies = jnp.broadcast_to(part[None], (lax.axis_size(CHIPS),) + part.shape)
    return lax.all_to_all(copies, CHIPS, 0, 0, tiled=True)


def fast_device(
    block_input, embedding, cotangent, qkv_weight, out_weight, out_bias, up_weight, up_bias,
    down_weight, down_bias, norm_gain, norm_shift, seg_lengths, loop_counts, token_counts,
):
    row_count, tokens, width = block_input.shape
    chunks = lax.axis_size(SEQ)
    groups = lax.axis_size("dp")
    devices = groups * chunks
    row_len = tokens * chunks
    me = lax.axis_index(SEQ)
    hidden = up_weight.shape[2]
    tie = lax.optimization_barrier
    half = devices // 2
    steps = LAYERS * 2

    here = jnp.stack([me, jnp.zeros_like(me), lax.axis_index("dp")]).astype(jnp.int32)
    here, (sent, sent_embed, sent_top) = cut_tokens(
        (here, loop_counts, token_counts, seg_lengths), (block_input, embedding), (embedding,),
        (cotangent,),
    )
    moved = swap_blocks(sent)
    here, sent = tie((here, sent))
    place = (here, loop_counts, token_counts, seg_lengths)
    backward_weights = (qkv_weight, out_weight, up_weight, down_weight)
    vectors = (out_bias, down_bias, norm_gain, norm_shift, up_bias)
    forward_weights, vec = prepare(place, backward_weights, vectors)

    moved_embed, moved_top = ([blocks[0]] + [None] * 3 for blocks in (sent_embed, sent_top))
    waiting = [(sent_embed, moved_embed, hop) for hop in range(1, 4)]
    waiting += [(sent_top, moved_top, hop) for hop in range(1, 4)]
    saved, saved_split = [], []
    begun = forward_split(
        place, vec, forward_weights, following=0, block_input=block_input,
        embedding=embedding,
    )
    state_split = begun["begun"]
    state = None
    first_end = first_end_split = None
    for step in range(steps):
        layer = step % LAYERS
        pre, kv, stat_pre = begun["pre"], begun["kv"], begun["stat_pre"]
        arrived = [swap(kv, hop) for hop in range(1, 4)]
        source = {}
        if step == 0:
            moved, kv = tie((moved, kv))
            source["tokens"] = moved
        elif step == LAYERS:
            state, moved_embed, kv = tie((state, moved_embed, kv))
            source["state"], source["tokens"] = state, moved_embed
        else:
            state, kv = tie((state, kv))
            source["state"] = state
        riders = waiting[2 * step : 2 * step + 2]
        blocks_out, kv = tie(([blocks[hop] for blocks, _, hop in riders], kv))
        riding = [swap(block, hop) for block, (_, _, hop) in zip(blocks_out, riders)]
        if step == steps - 1:
            source["first_end"] = first_end
        kept = forward_rows(layer, place, vec, forward_weights, **source)
        saved.append(kept)
        if step == steps - 1:
            answer = [kept[f"answer_{hop}"] for hop in range(4)]
            answer, arrived = tie((answer, arrived))
        else:
            state, arrived = tie((kept["result"], arrived))
        arrived, riding = tie((arrived, riding))
        for block, (_, target, hop) in zip(riding, riders):
            target[hop] = block
        boundary = step == LAYERS - 1
        if boundary:
            first_end = state
        extra = {}
        if step < steps - 1:
            extra["following"] = (layer + 1) % LAYERS
            if boundary:
                extra["embedding"] = embedding
        blocks = (kv, *arrived)
        if step == steps - 1:
            begun = turned = turn_split(
                place, vec, forward_weights, backward_weights, layer, state_split, blocks, pre,
                stat_pre, first_end_split, cotangent, row_len,
            )
        else:
            begun = forward_split(
                place, vec, forward_weights, last=layer, state=state_split,
                prev=blocks, pre=pre, **extra,
            )
        saved_split.append(
            {
                "pre": pre, "kv": blocks, "stat_pre": stat_pre,
                "post": begun["post"], "stat_post": begun["stat_post"],
            }
        )
        if step == steps - 1:
            answer_split = begun["answer"]
        else:
            state_split = begun["result"]
        if boundary:
            first_end_split = state_split
            state_split = begun["begun"]

    sums = [None] * LAYERS
    early = None
    grad = None
    ended = None
    for step in reversed(range(steps)):
        layer = step % LAYERS
        between = step == LAYERS - 1
        option = {}
        if between:
            option = {"cotangent": cotangent, "row_len": row_len}
        if ended is not None:
            last = (step + 1) % LAYERS
            option |= {
                "last": last, "ended": ended, "sums": sums[last], "keep": between,
                "final": step == 0,
            }
        begun = turned
        if step < steps - 1:
            begun = backward_split(
                place, vec, backward_weights, following=layer, begun=saved_split[step], **option
            )
        if ended is not None:
            if step == 0:
                others = {"wire": begun["wire"], "vec": begun["sum_vec"]}
            else:
                sums[last] |= {"sum_qkv": begun["sum_qkv"], "sum_vec": begun["sum_vec"]}
            if between:
                second_split = begun["result"]
        arrived = [swap(begun[f"away_{hop}"], hop) for hop in range(1, 4)]
        five = {
            "post": saved_split[step]["post"], "hidden": begun["hidden"], "low": begun["low"],
            "middle": begun["middle"], "vec": begun["vec_out"],
        }
        source = {}
        if step == steps - 1:
            moved_answer = [answer[0]] + [None] * 3
            waiting = [(answer, moved_answer, hop) for hop in range(1, 4)]
            source["tokens"] = moved_top
        elif between:
            moved_second = [second[0]] + [None] * 3
            waiting += [(second, moved_second, hop) for hop in range(1, 4)]
            source["tokens"] = moved_top
        riders, waiting = waiting[:2], waiting[2:]
        riding = [swap(blocks[hop], hop) for blocks, _, hop in riders]
        if grad is not None:
            source["grad"] = grad
        if step < LAYERS:
            source |= {"half": half, "digits": step == 1}
        source |= {"base": sums[layer], "keep": step > 0, "travel": step in (0, LAYERS)}
        fixed = (layer, place, saved[step], vec, backward_weights, five)
        if step == 0:
            early = sum_cores(*early)
            grad, early = tie((grad, early))
            source["grad"] = grad
            half_way = backward_rows(*fixed, ffn_only=True, **source)
            early = sum_chips(early)
            half_way, early, arrived = tie((half_way, early, arrived))
            early = share_chips(early)
            late_ffn = sum_cores(half_way["keep"], swap(half_way["give"], 1))
            half_way, late_ffn = tie((half_way, late_ffn))
            closing = {name: begun[name] for name in ("middle_out", "query_out", "own_out")}
            closing |= {"arrived": arrived, "pre": saved_split[step]["pre"]}
            closing["stat_pre"] = saved_split[step]["stat_pre"]
            kept = backward_rows(
                *fixed, part_done=half_way, closing=closing, others=others, **source
            )
            kept["keep"], early = tie((kept["keep"], early))
            for block, (_, target, hop) in zip(riding, riders):
                target[hop] = block
            first = [kept[f"travel_{hop}"] for hop in range(4)]
            break
        kept = backward_rows(*fixed, **source)
        grad, arrived = tie((kept["result"], arrived))
        if step == LAYERS:
            second = [kept[f"travel_{hop}"] for hop in range(4)]
        if between:
            arrived, riding, kept["give"] = tie((arrived, riding, kept["give"]))
            early = (kept["keep"], swap(kept["give"], 1))
        else:
            arrived, riding = tie((arrived, riding))
        for block, (_, target, hop) in zip(riding, riders):
            target[hop] = block
        if sums[layer] is None:
            names = ("sum_qkv", "sum_out_low", "sum_up_low", "sum_down_low", "sum_vec")
            sums[layer] = {name: kept[name] for name in names}
        else:
            sums[layer] = {name: kept[name] for name in ("sum_qkv", "sum_vec")}
        ended = {name: begun[name] for name in ("middle_out", "query_out", "own_out")}
        ended |= {"arrived": arrived, "pre": saved_split[step]["pre"]}
        ended["stat_pre"] = saved_split[step]["stat_pre"]
    moved_first = swap_blocks(first)
    first_split = kept["split_result"]

    part = jnp.concatenate(
        [
            late_ffn,
            sum_cores(kept["keep"], swap(kept["give"], 1)),
        ],
        axis=1,
    )
    early_other = swap(early, 1)
    part, moved_first, early, early_other = tie(
        (sum_chips(part), moved_first, early, early_other)
    )
    late = share_chips(part)
    done = finish_tokens(
        place, (early, early_other), moved_answer, answer_split, moved_first, first_split,
        moved_second, second_split, hidden, groups, float(row_len),
    )
    late, done = tie((late, done))
    more = finish_weights(place, (late, swap(late, 1)), done, width, hidden)
    return (
        done["block_output"],
        done["input_grad"],
        done["embed_grad"],
        more["qkv"],
        more["out"],
        more["out_b"],
        more["up"],
        more["up_b"],
        more["down"],
        more["down_b"],
        more["gain"],
        more["shift"],
    )


def solution(mesh):
    if mesh.shape["seq"] == 4:
        fine = Mesh(mesh.devices.reshape(-1, 2, 2), ("dp", "y", "core"))
        return jax.shard_map(
            fast_device,
            mesh=fine,
            in_specs=(
                P("dp", SEQ, None),
                P("dp", SEQ, None),
                P("dp", SEQ, None),
                P(),
                P(),
                P(),
                P(),
                P(),
                P(),
                P(),
                P(),
                P(),
                P("dp", None),
                P("dp"),
                P("dp"),
            ),
            out_specs=(
                P("dp", SEQ, None),
                P("dp", SEQ, None),
                P("dp", SEQ, None),
                P(),
                P(),
                P(),
                P(),
                P(),
                P(),
                P(),
                P(),
                P(),
            ),
            check_vma=False,
        )
    return jax.shard_map(
        on_device,
        mesh=mesh,
        in_specs=(
            P("dp", "seq", None),
            P("dp", "seq", None),
            P("dp", "seq", None),
            P(),
            P(),
            P(),
            P(),
            P(),
            P(),
            P(),
            P(),
            P(),
            P("dp", None),
            P("dp"),
            P("dp"),
        ),
        out_specs=(
            P("dp", "seq", None),
            P("dp", "seq", None),
            P("dp", "seq", None),
            P(),
            P(),
            P(),
            P(),
            P(),
            P(),
            P(),
            P(),
            P(),
        ),
        check_vma=False,
    )
```

```python
import types

import jax
import jax.numpy as jnp
from jax import lax
from jax.experimental import pallas as pl
from jax.experimental.pallas import tpu as pltpu
from jax.sharding import Mesh, PartitionSpec as P

H = 4
LAYERS = 2


NORM_EPS = 1e-05
MASKED = -1e30


def layer_norm(values, gain, shift):
    center = values - jnp.mean(values, axis=-1, keepdims=True)
    spread = jnp.mean(center * center, axis=-1, keepdims=True)
    return center * lax.rsqrt(spread + NORM_EPS) * gain + shift


def gelu_exact(values):
    return jax.nn.gelu(values, approximate=False)


def matmul(left_side, right_side):
    return jnp.dot(left_side, right_side, preferred_element_type=jnp.float32)


def left_dot(left_side, right_side):
    return lax.dot_general(
        left_side, right_side, (((0,), (0,)), ((), ())), preferred_element_type=jnp.float32
    )


def right_dot(left_side, right_side):
    return lax.dot_general(
        left_side, right_side, (((1,), (1,)), ((), ())), preferred_element_type=jnp.float32
    )


def split_heads(packed, head_count):
    return packed.reshape(packed.shape[0], head_count, packed.shape[1] // head_count)


def attend_forward(queries, key_vals, allowed, head_count, score_scale):
    model_width = queries.shape[1]
    key_rows = split_heads(key_vals[:, :model_width], head_count)
    value_rows = split_heads(key_vals[:, model_width:], head_count)
    scores = (
        jnp.einsum(
            "qhd,khd->hqk",
            split_heads(queries, head_count),
            key_rows,
            preferred_element_type=jnp.float32,
        )
        * score_scale
    )
    scores = jnp.where(allowed[None], scores, MASKED)
    row_max = jnp.max(scores, axis=-1, keepdims=True)
    shifted_exp = jnp.exp(scores - row_max)
    row_total = jnp.sum(shifted_exp, axis=-1, keepdims=True)
    attn_probs = (shifted_exp / row_total).astype(jnp.bfloat16)
    blended = jnp.einsum("hqk,khd->qhd", attn_probs, value_rows, preferred_element_type=jnp.float32)
    return (blended.reshape(queries.shape[0], model_width), (row_max + jnp.log(row_total))[..., 0])


def attention_core(
    query_part, key_part, value_part, grad_part, allowed_part, logsum_part, head_count, score_scale
):
    scores = (
        jnp.einsum(
            "qhd,khd->hqk",
            split_heads(query_part, head_count),
            split_heads(key_part, head_count),
            preferred_element_type=jnp.float32,
        )
        * score_scale
    )
    scores = jnp.where(allowed_part[None], scores, MASKED)
    attn_probs = jnp.exp(scores - logsum_part[..., None])
    grad_probs = jnp.einsum(
        "qhd,khd->hqk",
        split_heads(grad_part, head_count),
        split_heads(value_part, head_count),
        preferred_element_type=jnp.float32,
    )
    return (attn_probs, grad_probs)


def query_grads(grad_scores, key_part, head_count, score_scale):
    result = (
        jnp.einsum(
            "hqk,khd->qhd",
            grad_scores,
            split_heads(key_part, head_count),
            preferred_element_type=jnp.float32,
        )
        * score_scale
    )
    return result.reshape(result.shape[0], -1)


def keyval_grads(grad_scores, attn_probs, query_part, grad_part, head_count, score_scale):
    grad_keys = (
        jnp.einsum(
            "hqk,qhd->khd",
            grad_scores,
            split_heads(query_part, head_count),
            preferred_element_type=jnp.float32,
        )
        * score_scale
    )
    grad_values = jnp.einsum(
        "hqk,qhd->khd",
        attn_probs.astype(jnp.bfloat16),
        split_heads(grad_part, head_count),
        preferred_element_type=jnp.float32,
    )
    return jnp.concatenate(
        [grad_keys.reshape(grad_keys.shape[0], -1), grad_values.reshape(grad_values.shape[0], -1)],
        axis=-1,
    )


def on_device(
    block_input,
    embedding,
    cotangent,
    qkv_weight,
    out_weight,
    out_bias,
    up_weight,
    up_bias,
    down_weight,
    down_bias,
    norm_gain,
    norm_shift,
    seg_lengths,
    loop_counts,
    token_counts,
):
    row_count, block_len, model_width = block_input.shape
    head_count = H
    score_scale = (model_width // head_count) ** (-0.5)
    row_len = block_len * lax.axis_size("seq")
    flat_rows = row_count * block_len
    offset = lax.axis_index("seq") * block_len
    key_pos = jnp.arange(row_len, dtype=jnp.int32)
    own_pos = offset + jnp.arange(block_len, dtype=jnp.int32)
    seg_ends = jnp.cumsum(seg_lengths, axis=-1)
    seg_all = jnp.sum((seg_ends[:, None, :] <= key_pos[None, :, None]).astype(jnp.int32), axis=-1)
    seg_own = lax.dynamic_slice_in_dim(seg_all, offset, block_len, 1)
    allowed = (seg_own[:, :, None] == seg_all[:, None, :]) & (
        key_pos[None, None, :] <= own_pos[None, :, None]
    )
    current = block_input.astype(jnp.float32)
    inject = embedding.astype(jnp.float32)
    stored = []
    finals = []
    for repeat in range(2):
        current = current + inject
        for layer_index in range(LAYERS):
            forward_normed = layer_norm(
                current, norm_gain[layer_index, 0], norm_shift[layer_index, 0]
            ).astype(jnp.bfloat16)
            forward_packed = matmul(
                forward_normed.reshape(flat_rows, model_width), qkv_weight[layer_index]
            ).astype(jnp.bfloat16)
            forward_packed = forward_packed.reshape(row_count, block_len, 3 * model_width)
            forward_key_vals = lax.all_gather(
                forward_packed[:, :, model_width:], "seq", axis=1, tiled=True
            )

            def forward_row(inputs):
                return attend_forward(inputs[0], inputs[1], inputs[2], head_count, score_scale)

            forward_blended, forward_logsum = lax.map(
                forward_row, (forward_packed[:, :, :model_width], forward_key_vals, allowed)
            )
            forward_blended = forward_blended.astype(jnp.bfloat16)
            branch_out = matmul(
                forward_blended.reshape(flat_rows, model_width), out_weight[layer_index]
            ).reshape(row_count, block_len, model_width)
            forward_middle = current + branch_out + out_bias[layer_index]
            forward_normed_two = layer_norm(
                forward_middle, norm_gain[layer_index, 1], norm_shift[layer_index, 1]
            ).astype(jnp.bfloat16)
            forward_up_proj = (
                matmul(forward_normed_two.reshape(flat_rows, model_width), up_weight[layer_index])
                + up_bias[layer_index]
            )
            forward_active = gelu_exact(forward_up_proj).astype(jnp.bfloat16)
            result = (
                forward_middle
                + matmul(forward_active, down_weight[layer_index]).reshape(
                    row_count, block_len, model_width
                )
                + down_bias[layer_index]
            )
            current, stored_layer = (
                result,
                (
                    current,
                    forward_normed,
                    forward_packed,
                    forward_key_vals,
                    forward_logsum,
                    forward_blended,
                    forward_middle,
                    forward_normed_two,
                    forward_up_proj,
                    forward_active,
                ),
            )
            stored.append(stored_layer)
        finals.append(current)
    two_loops = (loop_counts == 2)[:, None, None]
    block_output = jnp.where(two_loops, finals[1], finals[0]).astype(jnp.bfloat16)
    row_weight = token_counts.astype(jnp.float32) / row_len
    grad_top = cotangent.astype(jnp.float32) * row_weight[:, None, None]
    grad_state = jnp.where(two_loops, grad_top, 0.0)
    layer_sums = [None] * LAYERS
    second_pass = grad_state
    for repeat in (1, 0):
        for layer_index in reversed(range(LAYERS)):
            backward_stored_layer = stored[repeat * LAYERS + layer_index]
            (
                backward_current,
                normed,
                packed,
                key_vals,
                logsum,
                blended,
                middle,
                normed_two,
                up_proj,
                active,
            ) = backward_stored_layer
            grad_flat = grad_state.reshape(flat_rows, model_width)
            grad_low = grad_flat.astype(jnp.bfloat16)
            grad_down = left_dot(active, grad_low)
            grad_down_bias = jnp.sum(grad_flat, axis=0)
            grad_active = right_dot(grad_low, down_weight[layer_index])
            grad_up_proj = jax.vjp(gelu_exact, up_proj)[1](grad_active)[0].astype(jnp.bfloat16)
            grad_up_bias = jnp.sum(grad_up_proj.astype(jnp.float32), axis=0)
            grad_up = left_dot(normed_two.reshape(flat_rows, model_width), grad_up_proj)
            grad_normed_two = right_dot(grad_up_proj, up_weight[layer_index]).reshape(
                row_count, block_len, model_width
            )
            pull_two = jax.vjp(
                layer_norm, middle, norm_gain[layer_index, 1], norm_shift[layer_index, 1]
            )[1]
            grad_middle, gain_two, shift_two = pull_two(grad_normed_two)
            grad_middle = grad_middle + grad_state
            middle_flat = grad_middle.reshape(flat_rows, model_width)
            middle_low = middle_flat.astype(jnp.bfloat16)
            grad_out = left_dot(blended.reshape(flat_rows, model_width), middle_low)
            grad_out_bias = jnp.sum(middle_flat, axis=0)
            grad_blend = (
                right_dot(middle_low, out_weight[layer_index])
                .astype(jnp.bfloat16)
                .reshape(row_count, block_len, model_width)
            )
            queries = packed[:, :, :model_width]

            def full_row(inputs):
                query_part, keyval_part, grad_part, allowed_part, logsum_part = inputs
                attn_probs, grad_probs = attention_core(
                    query_part,
                    keyval_part[:, :model_width],
                    keyval_part[:, model_width:],
                    grad_part,
                    allowed_part,
                    logsum_part,
                    head_count,
                    score_scale,
                )
                row_delta = jnp.sum(attn_probs * grad_probs, axis=-1, keepdims=True)
                grad_scores = (attn_probs * (grad_probs - row_delta)).astype(jnp.bfloat16)
                return (
                    query_grads(grad_scores, keyval_part[:, :model_width], head_count, score_scale),
                    keyval_grads(
                        grad_scores, attn_probs, query_part, grad_part, head_count, score_scale
                    ),
                )

            grad_query, partial_kv = lax.map(
                full_row, (queries, key_vals, grad_blend, allowed, logsum)
            )
            grad_keyval = lax.psum_scatter(
                partial_kv.astype(jnp.bfloat16), "seq", scatter_dimension=1, tiled=True
            )
            grad_packed = jnp.concatenate(
                [grad_query.astype(jnp.bfloat16), grad_keyval], axis=-1
            ).reshape(flat_rows, 3 * model_width)
            grad_qkv = left_dot(normed.reshape(flat_rows, model_width), grad_packed)
            grad_normed = right_dot(grad_packed, qkv_weight[layer_index]).reshape(
                row_count, block_len, model_width
            )
            pull_one = jax.vjp(
                layer_norm, backward_current, norm_gain[layer_index, 0], norm_shift[layer_index, 0]
            )[1]
            grad_current, gain_one, shift_one = pull_one(grad_normed)
            grad_current = grad_current + grad_middle
            grad_state = grad_current
            grad_set = (
                grad_qkv,
                grad_out,
                grad_out_bias,
                grad_up,
                grad_up_bias,
                grad_down,
                grad_down_bias,
                jnp.stack([gain_one, gain_two]),
                jnp.stack([shift_one, shift_two]),
            )
            if repeat == 1:
                layer_sums[layer_index] = grad_set
            else:
                layer_sums[layer_index] = jax.tree.map(jnp.add, layer_sums[layer_index], grad_set)
        if repeat == 1:
            second_pass = grad_state
            grad_state = jnp.where(two_loops, grad_state, grad_top)
    grad_embed = grad_state + second_pass
    stacked = jax.tree.map(lambda *members: jnp.stack(members), *layer_sums)
    (
        sum_qkv,
        sum_out,
        sum_out_bias,
        sum_up,
        sum_up_bias,
        sum_down,
        sum_down_bias,
        sum_gain,
        sum_shift,
    ) = stacked
    total = lax.psum(jnp.sum(token_counts), "dp").astype(jnp.float32)
    summed = lax.psum(
        (
            sum_qkv,
            sum_out,
            sum_out_bias,
            sum_up,
            sum_up_bias,
            sum_down,
            sum_down_bias,
            sum_gain,
            sum_shift,
        ),
        ("dp", "seq"),
    )
    input_scale = row_count * lax.axis_size("dp") * row_len / total
    weight_scale = row_len / total
    return (
        block_output,
        grad_state * input_scale,
        grad_embed * input_scale,
        summed[0] * weight_scale,
        summed[1] * weight_scale,
        summed[2] * weight_scale,
        summed[3] * weight_scale,
        summed[4] * weight_scale,
        summed[5] * weight_scale,
        summed[6] * weight_scale,
        summed[7] * weight_scale,
        summed[8] * weight_scale,
    )


BF = jnp.bfloat16
F32 = jnp.float32
ERF_TERMS = (7.97869712e-01, 3.63922863e-02, -8.78266373e-05, -3.66934271e-05, 1.42500458e-06)
DENSITY_RATE = -0.7213475204444817
DENSITY_BASE = -1.3257480647361593
VMEM_LIMIT = 24 * 1024 * 1024
ONES_ROWS = 16


def dot_nn(left_side, right_side):
    return jnp.dot(left_side, right_side, preferred_element_type=F32)


def dot_nt(left_side, right_side):
    return lax.dot_general(
        left_side, right_side, (((1,), (1,)), ((), ())), preferred_element_type=F32
    )


def gelu_and_slope(z):
    square = z * z
    series = ERF_TERMS[-1] * square + ERF_TERMS[-2]
    for term in ERF_TERMS[-3::-1]:
        series = series * square + term
    cdf = 0.5 + 0.5 * jnp.tanh(z * series)
    density = jnp.exp2(square * DENSITY_RATE + DENSITY_BASE)
    return z * cdf, cdf + z * density


def norm_forward(values, gain, shift):
    center = values - jnp.mean(values, axis=0, keepdims=True)
    spread = jnp.mean(center * center, axis=0, keepdims=True)
    inverse = lax.rsqrt(spread + NORM_EPS)
    unit = center * inverse
    return unit, inverse, (unit * gain + shift).astype(BF)


def norm_backward(grad, unit, inverse, gain):
    scaled = grad * gain
    first = jnp.mean(scaled, axis=0, keepdims=True)
    second = jnp.mean(scaled * unit, axis=0, keepdims=True)
    return inverse * (scaled - first - unit * second)


def columns(vec, tokens, spread=False):
    turned = vec[0].T

    def column(first, last):
        parts = [turned[:, k : k + 1] for k in range(first // 128, last // 128)]
        if spread:
            parts = [jnp.broadcast_to(part, (128, 128)) for part in parts]
            parts = [jnp.concatenate([part] * (tokens // 128), axis=1) for part in parts]
        return jnp.concatenate(parts, axis=0)

    return column


def project_qkv(state, qkv_t, vec, pre, kv, stat, scale, spread=False):
    width = state.shape[0]
    column = columns(vec, state.shape[1], spread)
    gain = column(2 * width, 3 * width)
    shift = column(3 * width, 4 * width)
    unit, inverse, normed = norm_forward(state, gain, shift)
    pre[0:width, :] = normed
    pre[2 * width : 3 * width, :] = unit.astype(BF)
    pre[width : 2 * width, :] = (dot_nn(qkv_t[0, 0:width, :], normed) * scale).astype(BF)
    kv[0:width, :] = dot_nn(qkv_t[0, width : 2 * width, :], normed).astype(BF)
    kv[width : 2 * width, :] = dot_nn(qkv_t[0, 2 * width : 3 * width, :], normed).astype(BF)
    stat[0:1, :] = inverse


def pad_head(block, odd):
    blank = jnp.zeros_like(block)
    return jnp.concatenate([blank, block] if odd else [block, blank], axis=0)


def tile_bias(first_key, start, causal, shape):
    key_at = lax.broadcasted_iota(jnp.int32, shape, 0)
    keep = key_at + first_key >= start
    if causal:
        keep = keep & (key_at <= lax.broadcasted_iota(jnp.int32, shape, 1))
    return jnp.where(keep, 0.0, MASKED)


def over_tiles(chunk, count, begin, half_tile, full_tile, carry, full_pair=None):
    half = count // 2
    first_half = begin // half
    odd = jnp.where(first_half < 2 * chunk, first_half % 2, 0)
    carry = lax.fori_loop(0, odd, lambda _, c: half_tile(first_half // 2, c), carry)
    first = (first_half + 1) // 2
    if full_pair is not None:
        pairs = jnp.maximum(chunk - first, 0) // 2
        carry = lax.fori_loop(0, pairs, lambda k, c: full_pair(first + 2 * k, c), carry)
        first = first + 2 * pairs
    return lax.fori_loop(first, chunk, full_tile, carry)


def attend_chunk(
    queries, keys, values_t, chunk, begin, start, bias, total, stat, blended, paired=False
):
    width, tokens = queries.shape
    head = width // H
    pair = 2 * head
    half = tokens // 2
    head_rows = [slice(h * head, (h + 1) * head) for h in range(H)]

    def scores(j, h, span):
        lanes = pl.ds((h // 2) * pair, pair)
        return dot_nn(keys[j, span, lanes], pad_head(queries[head_rows[h], :], h % 2))

    everything = slice(0, tokens)
    bias[:tokens, :] = tile_bias(chunk * tokens, start, True, (tokens, tokens))
    parts = [scores(chunk, h, everything) for h in range(H)]
    uppers = [part[:half, :] + bias[:half, :] for part in parts]
    lowers = [part[half:, half:] + bias[half:tokens, half:] for part in parts]
    tops, sums, weights = [], [], []
    for upper, lower in zip(uppers, lowers):
        top = jnp.max(upper, axis=0, keepdims=True)
        right = jnp.maximum(top[:, half:], jnp.max(lower, axis=0, keepdims=True))
        top = jnp.concatenate([top[:, :half], right], axis=1)
        upper = jnp.exp(upper - top)
        lower = jnp.exp(lower - right)
        added = jnp.sum(upper, axis=0, keepdims=True)
        right = added[:, half:] + jnp.sum(lower, axis=0, keepdims=True)
        tops.append(top)
        sums.append(jnp.concatenate([added[:, :half], right], axis=1))
        lower = lower.astype(BF)
        lower = jnp.concatenate([jnp.zeros_like(lower), lower], axis=1)
        weights.append(jnp.concatenate([upper.astype(BF), lower], axis=0))
    for rows, weight in zip(head_rows, weights):
        total[rows, :] = dot_nn(values_t[chunk, rows, :], weight)

    def step(tiles, span, size, carry):
        tops, sums = carry
        each_part, spans = [], []
        for at, j in enumerate(tiles):
            mask = slice(at * tokens, at * tokens + size)
            bias[mask, :] = tile_bias(j * tokens + span.start, start, False, (size, tokens))
            each_part.append([scores(j, h, span) + bias[mask, :] for h in range(H)])
        new_tops = list(tops)
        for parts in each_part:
            new_tops = [
                jnp.maximum(old, jnp.max(part, axis=0, keepdims=True))
                for old, part in zip(new_tops, parts)
            ]
        fades = [jnp.exp(old - new) for old, new in zip(tops, new_tops)]
        sums = [old * fade for old, fade in zip(sums, fades)]
        each_weight = [
            [jnp.exp(part - top) for part, top in zip(parts, new_tops)] for parts in each_part
        ]
        terms = [0.0] * H
        for j, weights in zip(tiles, each_weight):
            sums = [
                old + jnp.sum(weight, axis=0, keepdims=True)
                for old, weight in zip(sums, weights)
            ]
            terms = [
                old + dot_nn(values_t[j, rows, span], weight.astype(BF))
                for old, rows, weight in zip(terms, head_rows, weights)
            ]
        for rows, term, fade in zip(head_rows, terms, fades):
            total[rows, :] = total[rows, :] * fade + term
        return tuple(new_tops), tuple(sums)

    tops, sums = over_tiles(
        chunk, tokens, begin,
        lambda j, carry: step([j], slice(half, tokens), half, carry),
        lambda j, carry: step([j], everything, tokens, carry),
        (tuple(tops), tuple(sums)),
        (lambda j, carry: step([j, j + 1], everything, tokens, carry)) if paired else None,
    )
    for h, rows in enumerate(head_rows):
        blended[rows, :] = (total[rows, :] / sums[h]).astype(BF)
        stat[h : h + 1, :] = tops[h] + jnp.log(sums[h])


def finish_layer(state, out_t, up_t, down_t, vec, post, stat, spread=False):
    width, tokens = state.shape
    hidden = up_t.shape[1]
    column = columns(vec, tokens, spread)
    middle = state + dot_nn(out_t[0], post[0:width, :]) + column(0, width)
    gain = column(4 * width, 5 * width)
    shift = column(5 * width, 6 * width)
    unit, inverse, normed = norm_forward(middle, gain, shift)
    post[width : 2 * width, :] = normed
    post[2 * width : 3 * width, :] = unit.astype(BF)
    stat[H : H + 1, :] = inverse
    z = dot_nn(up_t[0], normed) + column(6 * width, 6 * width + hidden)
    active, slope = gelu_and_slope(z)
    post[3 * width : 3 * width + hidden, :] = active.astype(BF)
    post[3 * width + hidden :, :] = slope.astype(BF)
    return (
        middle
        + dot_nn(down_t[0], post[3 * width : 3 * width + hidden, :])
        + column(width, 2 * width)
    )


def launch(
    name, body, place, grid, ins, outs, scratch=(), flops=0, aliases=(), near=(), free=(),
    on_split=True,
):
    scratch = dict(scratch)
    names = [*ins, *outs, *scratch]

    def kernel(here, loops, counts, lengths, *refs):
        me, split = here[0], here[1]
        row = split if on_split else row_of_slot(me, split, loops.shape[0])
        facts = types.SimpleNamespace(
            me=me, split=split, slot=here[2], two=loops[row] == 2, count=counts[row], counts=counts,
            all_lengths=lengths, lengths=[lengths[row, k] for k in range(lengths.shape[1])],
        )
        body(facts, types.SimpleNamespace(**dict(zip(names, refs))))

    space = lambda key: pltpu.VMEM if key in near else pltpu.HBM
    results = pl.pallas_call(
        kernel,
        grid_spec=pltpu.PrefetchScalarGridSpec(
            num_scalar_prefetch=len(place),
            grid=(grid,),
            in_specs=[spec for _, spec in ins.values()],
            out_specs=[spec for _, spec in outs.values()],
            scratch_shapes=list(scratch.values()),
        ),
        out_shape=[
            shape if key in free else space(key)(shape.shape, shape.dtype)
            for key, (shape, _) in outs.items()
        ],
        input_output_aliases={
            len(place) + list(ins).index(source): list(outs).index(target) for source, target in aliases
        },
        compiler_params=pltpu.CompilerParams(vmem_limit_bytes=VMEM_LIMIT),
        cost_estimate=pl.CostEstimate(flops=flops, bytes_accessed=1, transcendentals=0),
        name=name,
    )(
        *[pltpu.with_memory_space_constraint(array, pltpu.HBM) for array in place],
        *[
            array if key in free else pltpu.with_memory_space_constraint(array, space(key))
            for key, (array, _) in ins.items()
        ],
    )
    return dict(zip(outs, results))


def whole(array):
    return array, pl.BlockSpec(array.shape, lambda i, *_: (0,) * len(array.shape))


def of_layer(array, layer):
    return array, pl.BlockSpec((1,) + array.shape[1:], lambda i, *_: (layer, 0, 0))


def each(array):
    return array, pl.BlockSpec((1,) + array.shape[1:], lambda i, *_: (i, 0, 0))


def each_back(array):
    count = array.shape[0]
    return array, pl.BlockSpec(
        (1,) + array.shape[1:], lambda i, *_: (count - 1 - i, 0, 0)
    )


def shaped(dims, dtype):
    return jax.ShapeDtypeStruct(dims, dtype)


def segment_starts(place, first, count):
    position = lax.broadcasted_iota(jnp.int32, (1, count), 1) + first
    starts = jnp.zeros((1, count), jnp.int32)
    end = jnp.int32(0)
    begin = jnp.int32(0)
    for length in place.lengths:
        end = end + length
        starts = jnp.where(position >= end, end, starts)
        begin = jnp.where(first >= end, end, begin)
    return starts, begin


def gather_tokens(env, name, me):
    for hop in range(4):
        env.spread[me ^ hop] = getattr(env, f"{name}_{hop}")[...]


def deal_tokens(env, name, value, chunk, me):
    for hop in range(4):

        @pl.when(chunk == (me ^ hop))
        def _(hop=hop):
            getattr(env, f"{name}_{hop}")[...] = value


def token_ins(name, blocks):
    return {f"{name}_{hop}": whole(block) for hop, block in enumerate(blocks)}


def token_outs(name, tokens, width):
    return {f"{name}_{hop}": whole(shaped((tokens, width), BF)) for hop in range(4)}


def as_tokens(values):
    return values.astype(BF).T


def as_features(tokens):
    return tokens.T.astype(F32)


def forward_rows(layer, place, vec, weights, state=None, tokens=None, first_end=None):
    chunks = 4
    count = state.shape[2] if tokens is None else tokens[0].shape[0]
    qkv_t, out_t, up_t, down_t = weights
    width, hidden = out_t.shape[2], up_t.shape[1]
    post_rows = 3 * width + 2 * hidden

    def body(place, env):
        chunk = pl.program_id(0)
        me = place.me
        current = env.state.at[0] if state is not None else None
        if tokens is not None:

            @pl.when(chunk == 0)
            def _():
                gather_tokens(env, "tokens", me)

            added = as_features(env.spread[chunk])
            env.current[...] = added if state is None else added + env.state[0]
            current = env.current
        project_qkv(
            current[...], env.qkv_t, env.vec, env.pre.at[0], env.kv.at[0], env.stat_pre.at[0],
            (width // H) ** -0.5, spread=True,
        )
        env.keys[chunk] = env.kv[0, 0:width, :].T
        env.values_t[chunk] = env.kv[0, width : 2 * width, :]
        start, begin = segment_starts(place, chunk * count, count)
        attend_chunk(
            env.pre.at[0, width : 2 * width, :], env.keys, env.values_t, chunk, begin, start, env.bias, env.total, env.stat_post.at[0],
            env.post.at[0, 0:width, :],
        )
        result = finish_layer(
            current[...], env.out_t, env.up_t, env.down_t, env.vec, env.post.at[0],
            env.stat_post.at[0], spread=True,
        )
        if first_end is None:
            env.result[0] = result
        else:
            answer = jnp.where(place.two, result, env.first_end[0])
            deal_tokens(env, "answer", as_tokens(answer), chunk, me)

    ins = {"vec": of_layer(vec, layer)}
    for name, weight in zip(("qkv_t", "out_t", "up_t", "down_t"), weights):
        ins[name] = of_layer(weight, layer)
    scratch = {
        "keys": pltpu.VMEM((chunks, count, width), BF),
        "values_t": pltpu.VMEM((chunks, width, count), BF),
        "bias": pltpu.VMEM((count, count), F32),
        "total": pltpu.VMEM((width, count), F32),
    }
    if state is not None:
        ins["state"] = each(state)
    if tokens is not None:
        ins |= token_ins("tokens", tokens)
        scratch["spread"] = pltpu.VMEM((chunks, count, width), BF)
        scratch["current"] = pltpu.VMEM((width, count), F32)
    outs = {}
    if first_end is None:
        outs["result"] = each(shaped((chunks, width, count), F32))
    else:
        ins["first_end"] = each(first_end)
        outs |= token_outs("answer", count, width)
    outs["pre"] = each(shaped((chunks, 3 * width, count), BF))
    outs["kv"] = each(shaped((chunks, 2 * width, count), BF))
    outs["post"] = each(shaped((chunks, post_rows, count), BF))
    outs["stat_pre"] = each(shaped((chunks, 8, count), F32))
    outs["stat_post"] = each(shaped((chunks, 8, count), F32))
    flops = chunks * count * 6 * (4 * width * width + 2 * width * hidden)
    return launch(
        "forward_rows", body, place, chunks, ins, outs, scratch, flops,
        on_split=False,
        near=["state", "result", "vec", "qkv_t", "out_t", "up_t", "down_t"]
        + [f"tokens_{hop}" for hop in range(4) if state is None],
    )


def split_row(array):
    return array, pl.BlockSpec((1,) + array.shape[1:], lambda i, here, *_: (here[1], 0, 0))


def row_of_slot(slot, split, rows):
    return jnp.where(slot == split, rows - 1, slot)


def forward_split(
    place, vec, weights, last=None, following=None, state=None, prev=None, pre=None,
    block_input=None, embedding=None, first_end=None, only_parts=False,
):
    qkv_t, out_t, up_t, down_t = weights
    width, hidden = out_t.shape[2], up_t.shape[1]
    count = embedding.shape[1] if state is None else state.shape[1]

    def body(place, env):
        me = place.me
        if last is not None:
            for hop in range(4):
                arrived = getattr(env, f"kv_{hop}")
                env.keys[me ^ hop] = arrived[0:width, :].T
                env.values_t[me ^ hop] = arrived[width : 2 * width, :]
            start, begin = segment_starts(place, me * count, count)
            attend_chunk(
                env.pre_in.at[width : 2 * width, :], env.keys, env.values_t, me, begin, start,
                env.bias, env.total, env.stat_post, env.post.at[0:width, :], paired=True,
            )
            current = finish_layer(
                env.state[...], env.out_t, env.up_t, env.down_t, env.vec, env.post, env.stat_post
            )
            if first_end is not None:
                answer = jnp.where(place.two, current, env.first_end[...])
                env.answer[...] = as_tokens(answer)
            else:
                env.result[...] = current
        if following is not None:
            if embedding is not None:
                added = as_features(env.embedding[0])
                if last is None:
                    current = as_features(env.block_input[0]) + added
                else:
                    current = env.result[...] + added
                env.begun[...] = current
            project_qkv(
                current, env.qkv_t, env.vec_next, env.pre, env.kv, env.stat_pre,
                (width // H) ** -0.5,
            )

    ins, outs, scratch = {}, {}, {}
    if last is not None:
        ins |= {f"kv_{hop}": whole(block) for hop, block in enumerate(prev)}
        ins |= {"state": whole(state), "pre_in": whole(pre)}
        ins["vec"] = of_layer(vec, last)
        for name, weight in zip(("out_t", "up_t", "down_t"), weights[1:]):
            ins[name] = of_layer(weight, last)
        if first_end is not None:
            ins["first_end"] = whole(first_end)
            outs["answer"] = whole(shaped((count, width), BF))
        else:
            outs["result"] = whole(shaped((width, count), F32))
        outs["post"] = whole(shaped((3 * width + 2 * hidden, count), BF))
        outs["stat_post"] = whole(shaped((8, count), F32))
        scratch = {
            "keys": pltpu.VMEM((4, count, width), BF),
            "values_t": pltpu.VMEM((4, width, count), BF),
            "bias": pltpu.VMEM((2 * count, count), F32),
            "total": pltpu.VMEM((width, count), F32),
        }
    if following is not None:
        ins["vec_next"] = of_layer(vec, following)
        ins["qkv_t"] = of_layer(qkv_t, following)
        if embedding is not None:
            ins["embedding"] = split_row(embedding)
            outs["begun"] = whole(shaped((width, count), F32))
        if block_input is not None:
            ins["block_input"] = split_row(block_input)
        outs["pre"] = whole(shaped((3 * width, count), BF))
        outs["kv"] = whole(shaped((2 * width, count), BF))
        outs["stat_pre"] = whole(shaped((8, count), F32))
    flops = 0 if last is None else count * 6 * (4 * width * width + 2 * width * hidden)
    near = ["state", "result", "begun", "pre", "pre_in", "kv", "vec", "vec_next"]
    near += ["qkv_t", "out_t", "up_t", "down_t"] + [f"kv_{hop}" for hop in range(4)]
    if only_parts:
        return body, ins, outs, scratch, near
    return launch("forward_split", body, place, 1, ins, outs, scratch, flops, near=near)


def backward_ffn(grad, unit, slope, stat, wout, wup, wdown, vec, hidden_grad):
    width, tokens = grad.shape
    low_grad = grad.astype(BF)
    hidden_grad[...] = (
        dot_nn(wdown[0], low_grad)
        * jnp.concatenate([ref[...] for ref in slope], axis=0).astype(F32)
    ).astype(BF)
    normed_grad = dot_nn(wup[0], hidden_grad[...])
    unit = unit[...].astype(F32)
    gain = columns(vec, tokens)(4 * width, 5 * width)
    middle = grad + norm_backward(normed_grad, unit, stat[H : H + 1, :], gain)
    low_middle = middle.astype(BF)
    blend_grad = dot_nn(wout[0], low_middle).astype(BF)
    return low_grad, normed_grad, unit, middle, low_middle, blend_grad


def token_sum(rows):
    return dot_nt(jnp.ones((ONES_ROWS, rows.shape[1]), BF), rows.astype(BF))


def attend_backward(
    queries, blend_grad, blended, stat, keys, values, keys_t, chunk, begin, start,
    bias, query_grad, kv_grad, paired=False,
):
    width, tokens = queries.shape
    head = width // H
    pair = 2 * head
    head_rows = [slice(h * head, (h + 1) * head) for h in range(H)]
    deltas = [
        jnp.sum(
            blend_grad[rows, :].astype(F32) * blended[rows, :].astype(F32), axis=0, keepdims=True
        )
        for rows in head_rows
    ]

    half = tokens // 2
    everything = slice(0, tokens)

    def products(j, span):
        parts, prob_grads = [], []
        for h, rows in enumerate(head_rows):
            lanes = pl.ds((h // 2) * pair, pair)
            parts.append(dot_nn(keys[j, span, lanes], pad_head(queries[rows, :], h % 2)))
            prob_grads.append(
                dot_nn(values[j, span, lanes], pad_head(blend_grad[rows, :], h % 2))
            )
        return parts, prob_grads

    def collect(j, span, probs, score_grads, first):
        for rows, prob, score_grad in zip(head_rows, probs, score_grads):
            value_rows = slice(width + rows.start, width + rows.stop)
            kv_grad[j, value_rows, span] += dot_nt(blend_grad[rows, :], prob)
            kv_grad[j, rows, span] += dot_nt(queries[rows, :], score_grad)
            term = dot_nn(keys_t(j, rows, span), score_grad)
            if first:
                query_grad[rows, :] = term
            else:
                query_grad[rows, :] += term

    def weigh(part, prob_grad, mask, logsum, delta):
        prob = jnp.exp(part + mask - logsum)
        return prob.astype(BF), (prob * (prob_grad - delta)).astype(BF)

    bias[:tokens, :] = tile_bias(chunk * tokens, start, True, (tokens, tokens))
    probs, score_grads = [], []
    for h, (part, prob_grad) in enumerate(zip(*products(chunk, everything))):
        logsum, delta = stat[h : h + 1, :], deltas[h]
        upper = weigh(part[:half, :], prob_grad[:half, :], bias[:half, :], logsum, delta)
        lower = weigh(
            part[half:, half:], prob_grad[half:, half:], bias[half:tokens, half:], logsum[:, half:],
            delta[:, half:],
        )
        for kept, above, below in zip((probs, score_grads), upper, lower):
            below = jnp.concatenate([jnp.zeros_like(below), below], axis=1)
            kept.append(jnp.concatenate([above, below], axis=0))
    collect(chunk, everything, probs, score_grads, True)

    def step(tiles, span, size, carry):
        made = []
        for at, j in enumerate(tiles):
            mask = slice(at * tokens, at * tokens + size)
            bias[mask, :] = tile_bias(j * tokens + span.start, start, False, (size, tokens))
            made.append((mask, *products(j, span)))
        weighed = [
            [
                weigh(part, prob_grad, bias[mask, :], stat[h : h + 1, :], deltas[h])
                for h, (part, prob_grad) in enumerate(zip(parts, prob_grads))
            ]
            for mask, parts, prob_grads in made
        ]
        for j, pairs in zip(tiles, weighed):
            collect(j, span, [p for p, _ in pairs], [d for _, d in pairs], False)
        return carry

    over_tiles(
        chunk, tokens, begin,
        lambda j, carry: step([j], slice(half, tokens), half, carry),
        lambda j, carry: step([j], everything, tokens, carry),
        0,
        (lambda j, carry: step([j, j + 1], everything, tokens, carry)) if paired else None,
    )


def add_vec(sum_vec, width, low_grad, normed_grad, unit, low_middle, dz):
    sum_vec[:, 0:width] += token_sum(low_middle)
    sum_vec[:, width : 2 * width] += token_sum(low_grad)
    sum_vec[:, 4 * width : 5 * width] += token_sum(normed_grad * unit)
    sum_vec[:, 5 * width : 6 * width] += token_sum(normed_grad)
    sum_vec[:, 6 * width :] += token_sum(dz)


def finish_backward(middle, pre, stat, packed, wqkv, vec, sum_qkv, sum_vec):
    width, tokens = middle.shape
    sum_qkv[...] += dot_nt(pre[0:width, :], packed[...])
    normed_grad = dot_nn(wqkv[0], packed[...])
    unit = pre[2 * width : 3 * width, :].astype(F32)
    gain = columns(vec, tokens)(2 * width, 3 * width)
    sum_vec[:, 2 * width : 3 * width] += token_sum(normed_grad * unit)
    sum_vec[:, 3 * width : 4 * width] += token_sum(normed_grad)
    return middle + norm_backward(normed_grad, unit, stat[0:1, :], gain)


def pack_lanes(wire, blocks):
    at = 0
    for ref in blocks:
        rows = ref.shape[0]
        for first in range(0, ref.shape[1], 128):
            wire[at : at + rows, :] = ref[:, first : first + 128].astype(BF)
            at += rows


def put_pieces(keep, give, source, first, height, core):
    half = keep.shape[0]
    for ref, side in ((keep, core), (give, 1 - core)):
        for p in range(half):
            at = pl.multiple_of((side * half + p) * height, 16)
            ref[p, first : first + height, :] = source[pl.ds(at, height), :]


def count_digits(place, groups):
    tally = place.counts[0]
    for k in range(1, place.counts.shape[0]):
        tally = tally + place.counts[k]
    lane = lax.broadcasted_iota(jnp.int32, (16, 128), 1)
    row = lax.broadcasted_iota(jnp.int32, (16, 128), 0)
    digit = jnp.where(lane % 2 == 0, tally // 256, tally % 256)
    keep = (lane // 2 == place.slot) & (row == 0) & (place.me == 0)
    return jnp.where(keep, digit, 0).astype(F32).astype(BF)


def backward_rows(
    layer, place, saved, vec, weights, five, base=None, grad=None, tokens=None,
    keep=True, travel=False, part_done=None, ffn_only=False, half=0, digits=False,
    closing=None, others=None,
):
    chunks, _, count = saved["kv"].shape
    wqkv, wout, wup, wdown = weights
    width, hidden = wup.shape[1:]
    row_len = chunks * count
    first = base is None
    part = hidden // chunks
    vec_len = 6 * width + hidden
    with_ffn, with_attention = part_done is None, not ffn_only

    def body(place, env):
        order = pl.program_id(0)
        chunk = chunks - 1 - order
        me = place.me

        @pl.when(order == 0)
        def _():
            if tokens is not None:
                gather_tokens(env, "tokens", me)
            if with_ffn:
                env.sum_out[...] = dot_nt(env.blend_five[...], env.middle_five[...])
                env.sum_vec[...] = env.vec_five[...]
                if not first:
                    env.sum_vec[...] += env.base_vec[...]
            else:
                env.sum_vec[...] = env.vec_done[...]
            if with_attention:
                env.sum_qkv[...] = jnp.zeros_like(env.sum_qkv)
                env.kv_grad[...] = jnp.zeros_like(env.kv_grad)
                for j in range(chunks):
                    env.keys[j] = env.kv[j, 0:width, :].T
                    env.values[j] = env.kv[j, width : 2 * width, :].T

        def add_base(ref, old):
            rows = old.shape[0]
            ref[pl.ds(pl.multiple_of(order * rows, rows), rows), :] += old[...].astype(F32)

        if with_ffn:
            current = env.grad.at[0] if grad is not None else None
            if tokens is not None:
                top = as_features(env.spread[chunk]) * (place.count.astype(F32) * (1.0 / row_len))
                two = place.two
                env.current[...] = (
                    jnp.where(two, top, 0.0)
                    if grad is None
                    else jnp.where(two, env.grad[0], top)
                )
                current = env.current
            post = env.post.at[0]
            low_grad, normed_grad, unit, middle, low_middle, blend_grad = backward_ffn(
                current[...], post.at[2 * width : 3 * width, :],
                [post.at[3 * width + hidden : 3 * width + 2 * hidden, :]], env.stat_post.at[0], env.wout, env.wup, env.wdown, env.vec,
                env.hidden_grad,
            )
            down = dot_nt(post[3 * width : 3 * width + hidden, :], low_grad)
            env.sum_down[...] = jnp.where(order == 0, 0.0, env.sum_down[...]) + down
            up = dot_nt(post[width : 2 * width, :], env.hidden_grad[...])
            env.sum_up[...] = jnp.where(order == 0, 0.0, env.sum_up[...]) + up
            spread = pl.ds(pl.multiple_of(order * part, part), part)
            env.sum_down[spread, :] += dot_nt(env.active_five[...], env.low_five[...])
            env.sum_up[:, spread] += dot_nt(env.normed_five[...], env.hidden_five[...])
            if not first:
                env.sum_down[spread, :] += env.base_down[...].astype(F32)
                env.sum_up[:, spread] += env.base_up[...].astype(F32)
                add_base(env.sum_out, env.base_out)
            env.sum_out[...] += dot_nt(post[0:width, :], low_middle)
            add_vec(
                env.sum_vec, width, low_grad, normed_grad, unit, low_middle, env.hidden_grad[...]
            )
            blend_ref = env.blend_grad if with_attention else env.blend_out.at[0]
            blend_ref[...] = blend_grad
            if first:

                @pl.when(order == chunks - 1)
                def _():
                    for name in ("sum_out", "sum_up", "sum_down"):
                        getattr(env, name + "_low")[...] = getattr(env, name)[...].astype(BF)

            if not first:

                @pl.when(order == chunks - 1)
                def _():
                    pack_lanes(env.wire, (env.sum_out, env.sum_up, env.sum_down))
                    height = env.wire.shape[0] // (2 * half)
                    put_pieces(env.keep, env.give, env.wire, 0, height, me % 2)
                    if digits:
                        blank = jnp.zeros((16, 128), BF)
                        for p in range(half):
                            env.keep[p, height:, :] = count_digits(place, half) if p == 0 else blank
                            env.give[p, height:, :] = blank

            if not with_attention:
                env.middle_out[0] = middle
                return
            blended = post.at[0:width, :]
        else:
            middle, blend_ref, blended = env.middle_in[0], env.blend_in.at[0], env.blended.at[0]
        if not first:
            add_base(env.sum_qkv, env.base_qkv)
        start, begin = segment_starts(place, chunk * count, count)
        attend_backward(
            env.pre.at[0, width : 2 * width, :], blend_ref, blended,
            env.stat_post.at[0], env.keys, env.values, lambda j, rows, span: env.kv[j, rows, span],
            chunk, begin, start, env.bias, env.query_grad, env.kv_grad,
        )
        env.packed[0:width, :] = (env.query_grad[...] * (width // H) ** -0.5).astype(BF)
        env.packed[width : 3 * width, :] = env.kv_grad[chunk].astype(BF)
        result = finish_backward(
            middle, env.pre.at[0], env.stat_pre.at[0], env.packed, env.wqkv, env.vec,
            env.sum_qkv, env.sum_vec,
        )
        if keep:
            env.result[0] = result
        if travel:
            deal_tokens(env, "travel", as_tokens(result), chunk, me)
        if closing is not None:

            @pl.when(order == chunks - 1)
            def _():
                ended = end_split_row(env, env.vec, env.sum_qkv, env.sum_vec)
                env.split_result[...] = ended.T
                write_last_payload(env, half, me % 2)

    ins = {"vec": of_layer(vec, layer), "stat_post": each_back(saved["stat_post"])}
    outs, scratch = {}, {}
    cut = lambda array, shape, at: (array, pl.BlockSpec(shape, lambda i, *_: at(i)))
    sums = {"sum_vec": (ONES_ROWS, vec_len)}
    if with_ffn:
        ins["post"] = each_back(saved["post"])
        for name, weight in zip(("wout", "wup", "wdown"), weights[1:]):
            ins[name] = of_layer(weight, layer)
        if grad is not None:
            ins["grad"] = each_back(grad)
        if tokens is not None:
            ins |= token_ins("tokens", tokens)
            scratch["spread"] = pltpu.VMEM((chunks, count, width), BF)
            scratch["current"] = pltpu.VMEM((width, count), F32)
        post_five = five["post"]
        ins["blend_five"] = cut(post_five, (width, count), lambda i: (0, 0))
        ins["normed_five"] = cut(post_five, (width, count), lambda i: (1, 0))
        ins["active_five"] = cut(post_five, (part, count), lambda i: (3 * width // part + i, 0))
        ins["hidden_five"] = cut(five["hidden"], (part, count), lambda i: (i, 0))
        for name in ("low", "middle", "vec"):
            ins[name + "_five"] = whole(five[name])
        sums |= {"sum_out": (width, width), "sum_up": (width, hidden), "sum_down": (hidden, width)}
        scratch["hidden_grad"] = pltpu.VMEM((hidden, count), BF)
        if not first:
            ins["base_out"] = cut(base["sum_out_low"], (width // chunks, width), lambda i: (i, 0))
            ins["base_up"] = cut(base["sum_up_low"], (width, part), lambda i: (0, i))
            ins["base_down"] = cut(base["sum_down_low"], (part, width), lambda i: (i, 0))
            ins["base_vec"] = whole(base["sum_vec"])
            wire_rows = (width * width + 2 * width * hidden) // 128
            scratch["wire"] = pltpu.VMEM((wire_rows, 128), BF)
            height = wire_rows // (2 * half) + (16 if digits else 0)
            outs["keep"] = whole(shaped((half, height, 128), BF))
            outs["give"] = whole(shaped((half, height, 128), BF))
        if not with_attention:
            outs["blend_out"] = each_back(shaped((chunks, width, count), BF))
            outs["middle_out"] = each_back(shaped((chunks, width, count), F32))
    else:
        ins["vec_done"] = whole(part_done["sum_vec"])
        ins["middle_in"] = each_back(part_done["middle_out"])
        ins["blend_in"] = each_back(part_done["blend_out"])
        ins["blended"] = (
            saved["post"],
            pl.BlockSpec((1, width, count), lambda i, *_: (chunks - 1 - i, 0, 0)),
        )
    if with_attention:
        ins["kv"] = whole(saved["kv"])
        ins["pre"] = each_back(saved["pre"])
        ins["stat_pre"] = each_back(saved["stat_pre"])
        ins["wqkv"] = of_layer(wqkv, layer)
        sums["sum_qkv"] = (width, 3 * width)
        if not first:
            ins["base_qkv"] = cut(base["sum_qkv"], (width // chunks, 3 * width), lambda i: (i, 0))
        if keep:
            outs["result"] = each_back(shaped((chunks, width, count), F32))
        if travel:
            outs |= token_outs("travel", count, width)
        scratch |= {
            "keys": pltpu.VMEM((chunks, count, width), BF),
            "values": pltpu.VMEM((chunks, count, width), BF),
            "bias": pltpu.VMEM((count, count), F32),
            "query_grad": pltpu.VMEM((width, count), F32),
            "kv_grad": pltpu.VMEM((chunks, 2 * width, count), F32),
            "blend_grad": pltpu.VMEM((width, count), BF),
            "packed": pltpu.VMEM((3 * width, count), BF),
        }
    if closing is not None:
        ins |= split_row_ins(closing)
        wire_rows = 3 * width * width // 128
        height = 2 * (wire_rows // (2 * half)) + 16
        ins["wire_other"] = whole(others["wire"])
        ins["vec_other"] = whole(others["vec"])
        outs["keep"] = whole(shaped((half, height, 128), BF))
        outs["give"] = whole(shaped((half, height, 128), BF))
        outs["split_result"] = whole(shaped((count, width), F32))
        scratch["wire"] = pltpu.VMEM((wire_rows, 128), BF)
        scratch["small"] = pltpu.VMEM((4 * half, 128), F32)
        scratch |= {name: pltpu.VMEM(dims, F32) for name, dims in sums.items()}
        sums = {}
    for name, dims in sums.items():
        if name in ("sum_qkv", "sum_vec"):
            outs[name] = whole(shaped(dims, F32))
        else:
            scratch[name] = pltpu.VMEM(dims, F32)
            if first:
                outs[name + "_low"] = whole(shaped(dims, BF))
    flops = chunks * count * 12 * (4 * width * width + 2 * width * hidden)
    return launch(
        "backward_rows", body, place, chunks, ins, outs, scratch, flops, on_split=False,
        near=[
            "middle_in_split", "query_in", "own_in", "in_1", "in_2", "in_3",
            "hidden_five", "low_five", "middle_five", "vec_five",
        ],
    )


def split_row_ins(ended):
    ins = {
        "middle_in_split": whole(ended["middle_out"]), "query_in": whole(ended["query_out"]),
        "own_in": whole(ended["own_out"]), "pre_last": whole(ended["pre"]),
        "stat_last": whole(ended["stat_pre"]),
    }
    return ins | {f"in_{hop}": whole(ended["arrived"][hop - 1]) for hop in range(1, 4)}


def end_split_row(env, vec, sum_qkv, sum_vec):
    width = env.query_in.shape[0]
    env.packed[0:width, :] = env.query_in[...]
    kv_total = env.own_in[...]
    for hop in range(1, 4):
        kv_total = kv_total + getattr(env, f"in_{hop}")[...].astype(F32)
    env.packed[width : 3 * width, :] = kv_total.astype(BF)
    return finish_backward(
        env.middle_in_split[...], env.pre_last, env.stat_last, env.packed, env.wqkv, vec,
        sum_qkv, sum_vec,
    )


def write_last_payload(env, half, core):
    pack_lanes(env.wire, (env.sum_qkv,))
    height = env.wire.shape[0] // (2 * half)
    put_pieces(env.keep, env.give, env.wire, 0, height, core)
    put_pieces(env.keep, env.give, env.wire_other, height, height, core)
    rows = env.sum_vec.shape[1] // 128
    env.small[...] = jnp.zeros_like(env.small)
    for at, ref in ((0, env.sum_vec), (rows, env.vec_other)):
        for k in range(rows):
            env.small[at + k : at + k + 1, :] = ref[0:1, 128 * k : 128 * k + 128]
    for p in range(half):
        left = env.small[2 * p : 2 * p + 2, :]
        right = env.small[2 * (p + half) : 2 * (p + half) + 2, :]
        for ref, first in ((env.keep, core == 0), (env.give, core == 1)):
            pair = jnp.where(first, left, right)
            blank = jnp.zeros((14, 128), F32)
            ref[p, 2 * height :, :] = jnp.concatenate([pair, blank]).astype(BF)


def backward_split(
    place, vec, weights, last=None, following=None, ended=None, sums=None, begun=None,
    cotangent=None, final=False, keep=False, row_len=None, only_parts=False,
):
    wqkv, wout, wup, wdown = weights
    width, hidden = wup.shape[1:]
    vec_len = 6 * width + hidden
    count = (ended or begun)["stat_pre"].shape[1]

    def body(place, env):
        me = place.me
        if last is not None:
            sum_qkv = env.total_qkv if final else env.sum_qkv
            sum_qkv[...] = env.old_qkv[...]
            env.sum_vec[...] = env.old_vec[...]
            current = end_split_row(env, env.vec_last, sum_qkv, env.sum_vec)
            if keep:
                env.result[...] = current.T
            if final:
                pack_lanes(env.wire, (sum_qkv,))
        if following is not None:
            if cotangent is not None:
                top = as_features(env.cotangent[0]) * (place.count.astype(F32) * (1.0 / row_len))
                two = place.two
                grad = jnp.where(two, top, 0.0) if last is None else jnp.where(two, current, top)
            else:
                grad = current
            env.kv_grad[...] = jnp.zeros_like(env.kv_grad)
            for hop in range(4):
                arrived = getattr(env, f"kv_{hop}")
                env.keys[me ^ hop] = arrived[0:width, :].T
                env.keys_t[me ^ hop] = arrived[0:width, :]
                env.values[me ^ hop] = arrived[width : 2 * width, :].T
            if hasattr(env, "post"):
                queries = env.pre.at[width : 2 * width, :]
                blended, unit_rows = env.post.at[0:width, :], env.post.at[2 * width : 3 * width, :]
                slope = [env.post.at[3 * width + hidden : 3 * width + 2 * hidden, :]]
            else:
                queries, blended, unit_rows = env.queries, env.blended, env.unit
                slope = [getattr(env, f"slope_{k}") for k in range(hidden // width)]
            low_grad, normed_grad, unit, middle, low_middle, blend_grad = backward_ffn(
                grad, unit_rows, slope, env.stat_post, env.wout, env.wup, env.wdown, env.vec, env.hidden
            )
            env.low[...] = low_grad
            env.middle[...] = low_middle
            env.middle_out[...] = middle
            env.vec_out[...] = jnp.zeros_like(env.vec_out)
            add_vec(
                env.vec_out, width, low_grad, normed_grad, unit, low_middle, env.hidden[...]
            )
            env.blend_grad[...] = blend_grad
            start, begin = segment_starts(place, me * count, count)
            attend_backward(
                queries, env.blend_grad, blended,
                env.stat_post, env.keys, env.values, lambda j, rows, span: env.keys_t[j, rows, span],
                me, begin, start, env.bias, env.query_grad, env.kv_grad, paired=True,
            )
            env.query_out[...] = (env.query_grad[...] * (width // H) ** -0.5).astype(BF)
            env.own_out[...] = env.kv_grad[me]
            for hop in range(1, 4):
                getattr(env, f"away_{hop}")[...] = env.kv_grad[me ^ hop].astype(BF)

    ins, outs, scratch = {}, {}, {}
    if last is not None:
        ins |= split_row_ins(ended)
        ins["vec_last"] = of_layer(vec, last)
        ins["wqkv"] = of_layer(wqkv, last)
        ins["old_qkv"] = whole(sums["sum_qkv"])
        ins["old_vec"] = whole(sums["sum_vec"])
        if keep:
            outs["result"] = whole(shaped((count, width), F32))
        if final:
            outs["wire"] = whole(shaped((3 * width * width // 128, 128), BF))
        if final:
            scratch["total_qkv"] = pltpu.VMEM((width, 3 * width), F32)
        else:
            outs["sum_qkv"] = whole(shaped((width, 3 * width), F32))
        outs["sum_vec"] = whole(shaped((ONES_ROWS, vec_len), F32))
        scratch["packed"] = pltpu.VMEM((3 * width, count), BF)
    if following is not None:
        rows_at = lambda array, k: (array, pl.BlockSpec((width, count), lambda i, *_: (k, 0)))
        ins["queries"] = rows_at(begun["pre"], 1)
        ins["blended"] = rows_at(begun["post"], 0)
        ins["unit"] = rows_at(begun["post"], 2)
        for k in range(hidden // width):
            ins[f"slope_{k}"] = rows_at(begun["post"], 3 + hidden // width + k)
        ins["stat_post"] = whole(begun["stat_post"])
        for hop in range(4):
            ins[f"kv_{hop}"] = whole(begun["kv"][hop])
        ins["vec"] = of_layer(vec, following)
        for name, weight in zip(("wout", "wup", "wdown"), weights[1:]):
            ins[name] = of_layer(weight, following)
        if cotangent is not None:
            ins["cotangent"] = split_row(cotangent)
        outs["middle_out"] = whole(shaped((width, count), F32))
        outs["query_out"] = whole(shaped((width, count), BF))
        outs["own_out"] = whole(shaped((2 * width, count), F32))
        for hop in range(1, 4):
            outs[f"away_{hop}"] = whole(shaped((2 * width, count), BF))
        outs["low"] = whole(shaped((width, count), BF))
        outs["hidden"] = whole(shaped((hidden, count), BF))
        outs["middle"] = whole(shaped((width, count), BF))
        outs["vec_out"] = whole(shaped((ONES_ROWS, vec_len), F32))
        scratch |= {
            "keys": pltpu.VMEM((4, count, width), BF),
            "values": pltpu.VMEM((4, count, width), BF),
            "keys_t": pltpu.VMEM((4, width, count), BF),
            "bias": pltpu.VMEM((2 * count, count), F32),
            "query_grad": pltpu.VMEM((width, count), F32),
            "kv_grad": pltpu.VMEM((4, 2 * width, count), F32),
            "blend_grad": pltpu.VMEM((width, count), BF),
        }
    flops = count * 12 * (4 * width * width + 2 * width * hidden)
    near = [
        "middle_in_split", "query_in", "own_in", "in_1", "in_2", "in_3", "middle_out",
        "query_out", "own_out", "away_1", "away_2", "away_3", "low", "hidden", "middle", "vec_out",
    ]
    if only_parts:
        return body, ins, outs, scratch, near
    return launch("backward_split", body, place, 1, ins, outs, scratch, flops, near=near)


def turn_split(
    place, vec, forward_weights, backward_weights, layer, state, blocks, pre, stat_pre, first_end,
    cotangent, row_len,
):
    forward, ins, outs, scratch, near = forward_split(
        place, vec, forward_weights, last=layer, state=state, prev=blocks, pre=pre,
        first_end=first_end, only_parts=True,
    )
    begun = {"pre": pre, "kv": blocks, "stat_pre": stat_pre, "post": pre, "stat_post": stat_pre}
    backward, more_ins, more_outs, more_scratch, more_near = backward_split(
        place, vec, backward_weights, following=layer, begun=begun, cotangent=cotangent,
        row_len=row_len, only_parts=True,
    )
    shared = ["queries", "blended", "unit", "stat_post", "vec"]
    shared += [key for key in more_ins if key.startswith(("kv_", "slope_"))]
    more_ins = {key: value for key, value in more_ins.items() if key not in shared}

    def body(place, env):
        forward(place, env)
        env.pre = env.pre_in
        backward(place, env)

    return launch(
        "turn_split", body, place, 1, ins | more_ins, outs | more_outs, scratch | more_scratch,
        near=near + more_near,
    )


def cut_tokens(place, *pairs):
    arrays = [array for pair in pairs for array in pair]
    rows, count, width = arrays[0].shape

    def body(place, env):
        me = place.me
        best, longest = jnp.int32(0), jnp.int32(0)
        for row in range(rows):
            most = place.all_lengths[row, 0]
            for k in range(1, place.all_lengths.shape[1]):
                most = jnp.maximum(most, place.all_lengths[row, k])
            longest = jnp.where(most > best, row, longest)
            best = jnp.maximum(most, best)
        env.here[0] = me
        env.here[1] = longest
        env.here[2] = place.slot
        for hop in range(4):
            row = row_of_slot(me ^ hop, longest, rows)
            at = 0
            for index, pair in enumerate(pairs):
                value = getattr(env, f"in_{at}")[row].astype(F32)
                for extra in range(1, len(pair)):
                    value = value + getattr(env, f"in_{at + extra}")[row].astype(F32)
                at += len(pair)
                getattr(env, f"out{index}_{hop}")[...] = value.astype(BF)

    ins = {f"in_{k}": whole(array) for k, array in enumerate(arrays)}
    outs = {}
    for index in range(len(pairs)):
        outs |= token_outs(f"out{index}", count, width)
    outs["here"] = (shaped((3,), jnp.int32), pl.BlockSpec(memory_space=pltpu.SMEM))
    results = launch("cut_tokens", body, place, 1, ins, outs, free=("here",))
    blocks = [[results[f"out{index}_{hop}"] for hop in range(4)] for index in range(len(pairs))]
    return results["here"], blocks


def prepare(place, weights, vectors):
    out_bias, down_bias, norm_gain, norm_shift, up_bias = vectors
    layers, width = out_bias.shape
    hidden = up_bias.shape[1]
    rows = (6 * width + hidden) // 128
    rows += -rows % 8

    def body(place, env):
        layer = pl.program_id(0)
        for k in range(4):
            getattr(env, f"turned_{k}")[0] = getattr(env, f"weight_{k}")[0].T
        env.vec[...] = jnp.zeros_like(env.vec)
        pick = lambda ref: ref[pl.ds(layer, 1), :]
        parts = [pick(env.out_bias), pick(env.down_bias)]
        for k in range(2):
            parts += [env.norm_gain[0, k : k + 1, :], env.norm_shift[0, k : k + 1, :]]
        at = 0
        for part in parts + [pick(env.up_bias)]:
            for lanes in range(0, part.shape[1], 128):
                env.vec[0, at : at + 1, :] = part[:, lanes : lanes + 128]
                at += 1

    ins = {f"weight_{k}": each(weight) for k, weight in enumerate(weights)}
    ins |= {"out_bias": whole(out_bias), "down_bias": whole(down_bias), "up_bias": whole(up_bias)}
    ins |= {"norm_gain": each(norm_gain), "norm_shift": each(norm_shift)}
    outs = {
        f"turned_{k}": each(shaped((layers, weight.shape[2], weight.shape[1]), BF))
        for k, weight in enumerate(weights)
    }
    outs["vec"] = each(shaped((layers, rows, 128), F32))
    results = launch("prepare", body, place, layers, ins, outs, near=list(outs))
    return tuple(results[f"turned_{k}"] for k in range(4)), results["vec"]


def piece_reader(payloads, me):
    mine, other = payloads
    half = mine.shape[0]

    def piece(p, first, rows):
        left, right = (ref[p % half, first : first + rows, :] for ref in (mine, other))
        return jnp.where(me % 2 == p // half, left, right).astype(F32)

    return piece


def spread_pieces(piece, pieces, first, rows_each, targets, factor):
    edges, at = [], 0
    for ref in targets:
        for lanes in range(0, ref.shape[2], 128):
            edges.append((at, at + ref.shape[1], ref, lanes))
            at += ref.shape[1]
    for p in range(pieces):
        values = piece(p, first, rows_each) * factor
        begin = p * rows_each
        for low, high, ref, lanes in edges:
            left, right = max(low, begin), min(high, begin + rows_each)
            if left < right:
                ref[0, left - low : right - low, lanes : lanes + 128] = values[
                    left - begin : right - begin, :
                ]


def finish_tokens(
    place, payload, answer, answer_split, first, first_split, second, second_split,
    hidden, groups, row_len,
):
    count, width = first_split.shape
    rows = 5
    pieces = 2 * payload[0].shape[0]
    ffn_rows = (width * width + 2 * width * hidden) // 128 // pieces

    def body(place, env):
        step = pl.program_id(0)
        me = place.me
        piece = piece_reader((env.mine, env.other), me)
        lane = lax.broadcasted_iota(jnp.int32, (1, 128), 1)
        total = jnp.zeros((1, 1), F32)
        for extra in range(-(-2 * groups // 128)):
            row = piece(extra, ffn_rows, 16)[0:1, :]
            worth = jnp.where(lane % 2 == 0, 256.0, 1.0)
            row = jnp.where(lane + extra * 128 < 2 * groups, row * worth, 0.0)
            total = total + jnp.sum(row, axis=1, keepdims=True)
        factor = row_len / total
        token_factor = factor * float(rows * groups)

        @pl.when(step == 0)
        def _():
            env.scale[...] = jnp.broadcast_to(factor, env.scale.shape)
            spread_pieces(piece, pieces, 0, ffn_rows, (env.out, env.up, env.down), factor)

        for hop in range(4):

            @pl.when(step == row_of_slot(me ^ hop, place.split, rows))
            def _(hop=hop):
                env.block_output[0] = getattr(env, f"answer_{hop}")[...]
                one = getattr(env, f"first_{hop}")[...].astype(F32)
                two = getattr(env, f"second_{hop}")[...].astype(F32)
                env.input_grad[0] = one * token_factor
                env.embed_grad[0] = (one + two) * token_factor

        @pl.when(step == place.split)
        def _():
            env.block_output[0] = env.answer_split[...]
            one = env.first_split[...]
            env.input_grad[0] = one * token_factor
            env.embed_grad[0] = (one + env.second_split[...]) * token_factor

    ins = {"mine": whole(payload[0]), "other": whole(payload[1])}
    ins |= token_ins("answer", answer) | token_ins("first", first) | token_ins("second", second)
    ins["answer_split"] = whole(answer_split)
    ins["first_split"] = whole(first_split)
    ins["second_split"] = whole(second_split)
    later = lambda *dims: (
        shaped(dims, F32), pl.BlockSpec((1,) + dims[1:], lambda i, *_: (LAYERS - 1, 0, 0))
    )
    outs = {
        "block_output": each(shaped((rows, count, width), BF)),
        "input_grad": each(shaped((rows, count, width), F32)),
        "embed_grad": each(shaped((rows, count, width), F32)),
        "out": later(LAYERS, width, width),
        "up": later(LAYERS, width, hidden),
        "down": later(LAYERS, hidden, width),
        "scale": whole(shaped((8, 128), F32)),
    }
    return launch(
        "finish_tokens", body, place, rows, ins, outs, free=("mine", "other")
    )


def finish_weights(place, payload, done, width, hidden):
    pieces = 2 * payload[0].shape[0]
    ffn_rows = (width * width + 2 * width * hidden) // 128 // pieces
    qkv_rows = 3 * width * width // 128 // pieces
    small_at = ffn_rows + LAYERS * qkv_rows
    vec_len = 6 * width + hidden

    def body(place, env):
        step = pl.program_id(0)
        piece = piece_reader((env.mine, env.other), place.me)
        factor = env.scale[0:1, 0:1]

        @pl.when(step == 0)
        def _():
            spread_pieces(piece, pieces, 0, ffn_rows, (env.out, env.up, env.down), factor)
            for here in range(LAYERS):
                for ref, slot, at, size in (
                    (env.out_b, None, 0, width),
                    (env.down_b, None, width, width),
                    (env.gain, 0, 2 * width, width),
                    (env.shift, 0, 3 * width, width),
                    (env.gain, 1, 4 * width, width),
                    (env.shift, 1, 5 * width, width),
                    (env.up_b, None, 6 * width, hidden),
                ):
                    for lanes in range(0, size, 128):
                        index = (here * vec_len + at + lanes) // 128
                        row = piece(index // 2, small_at, 16)[index % 2 : index % 2 + 1, :]
                        row = row * factor
                        if slot is None:
                            ref[here : here + 1, lanes : lanes + 128] = row
                        else:
                            ref[here, slot : slot + 1, lanes : lanes + 128] = row

        for here in range(LAYERS):

            @pl.when(step == here)
            def _(here=here):
                spread_pieces(
                    piece, pieces, ffn_rows + here * qkv_rows, qkv_rows, (env.qkv,), factor
                )

    ins = {"mine": whole(payload[0]), "other": whole(payload[1]), "scale": whole(done["scale"])}
    names = ("out", "up", "down")
    for name in names:
        ins[name + "_done"] = (done[name], pl.BlockSpec(memory_space=pl.ANY))
    start = lambda array: (
        array, pl.BlockSpec((1,) + array.shape[1:], lambda i, *_: (0, 0, 0))
    )
    outs = {name: start(shaped(done[name].shape, F32)) for name in names}
    outs["qkv"] = each(shaped((LAYERS, width, 3 * width), F32))
    outs["out_b"] = whole(shaped((LAYERS, width), F32))
    outs["up_b"] = whole(shaped((LAYERS, hidden), F32))
    outs["down_b"] = whole(shaped((LAYERS, width), F32))
    outs["gain"] = whole(shaped((LAYERS, 2, width), F32))
    outs["shift"] = whole(shaped((LAYERS, 2, width), F32))
    return launch(
        "finish_weights", body, place, LAYERS, ins, outs,
        aliases=[(name + "_done", name) for name in names],
        free=("mine", "other"),
    )


SEQ = ("y", "core")
CHIPS = ("dp", "y")


def swap(values, hop):
    return lax.ppermute(values, SEQ, [(i, i ^ hop) for i in range(lax.axis_size(SEQ))])


def swap_blocks(blocks):
    return [blocks[0]] + [swap(block, hop) for hop, block in enumerate(blocks[1:], 1)]


def sum_cores(keep, got):
    return (keep.astype(F32) + got.astype(F32)).astype(BF)


def sum_chips(part):
    part = lax.all_to_all(part, CHIPS, 0, 0, tiled=True)
    return jnp.sum(part.astype(F32), axis=0).astype(BF)


def share_chips(part):
    copies = jnp.broadcast_to(part[None], (lax.axis_size(CHIPS),) + part.shape)
    return lax.all_to_all(copies, CHIPS, 0, 0, tiled=True)


def fast_device(
    block_input, embedding, cotangent, qkv_weight, out_weight, out_bias, up_weight, up_bias,
    down_weight, down_bias, norm_gain, norm_shift, seg_lengths, loop_counts, token_counts,
):
    row_count, tokens, width = block_input.shape
    chunks = lax.axis_size(SEQ)
    groups = lax.axis_size("dp")
    devices = groups * chunks
    row_len = tokens * chunks
    me = lax.axis_index(SEQ)
    hidden = up_weight.shape[2]
    tie = lax.optimization_barrier
    half = devices // 2
    steps = LAYERS * 2

    here = jnp.stack([me, jnp.zeros_like(me), lax.axis_index("dp")]).astype(jnp.int32)
    here, (sent, sent_embed, sent_top) = cut_tokens(
        (here, loop_counts, token_counts, seg_lengths), (block_input, embedding), (embedding,),
        (cotangent,),
    )
    moved = swap_blocks(sent)
    here, sent = tie((here, sent))
    place = (here, loop_counts, token_counts, seg_lengths)
    backward_weights = (qkv_weight, out_weight, up_weight, down_weight)
    vectors = (out_bias, down_bias, norm_gain, norm_shift, up_bias)
    forward_weights, vec = prepare(place, backward_weights, vectors)

    moved_embed, moved_top = ([blocks[0]] + [None] * 3 for blocks in (sent_embed, sent_top))
    waiting = [(sent_embed, moved_embed, hop) for hop in range(1, 4)]
    waiting += [(sent_top, moved_top, hop) for hop in range(1, 4)]
    saved, saved_split = [], []
    begun = forward_split(
        place, vec, forward_weights, following=0, block_input=block_input,
        embedding=embedding,
    )
    state_split = begun["begun"]
    state = None
    first_end = first_end_split = None
    for step in range(steps):
        layer = step % LAYERS
        pre, kv, stat_pre = begun["pre"], begun["kv"], begun["stat_pre"]
        arrived = [swap(kv, hop) for hop in range(1, 4)]
        source = {}
        if step == 0:
            moved, kv = tie((moved, kv))
            source["tokens"] = moved
        elif step == LAYERS:
            state, moved_embed, kv = tie((state, moved_embed, kv))
            source["state"], source["tokens"] = state, moved_embed
        else:
            state, kv = tie((state, kv))
            source["state"] = state
        riders = waiting[2 * step : 2 * step + 2]
        blocks_out, kv = tie(([blocks[hop] for blocks, _, hop in riders], kv))
        riding = [swap(block, hop) for block, (_, _, hop) in zip(blocks_out, riders)]
        if step == steps - 1:
            source["first_end"] = first_end
        kept = forward_rows(layer, place, vec, forward_weights, **source)
        saved.append(kept)
        if step == steps - 1:
            answer = [kept[f"answer_{hop}"] for hop in range(4)]
            answer, arrived = tie((answer, arrived))
        else:
            state, arrived = tie((kept["result"], arrived))
        arrived, riding = tie((arrived, riding))
        for block, (_, target, hop) in zip(riding, riders):
            target[hop] = block
        boundary = step == LAYERS - 1
        if boundary:
            first_end = state
        extra = {}
        if step < steps - 1:
            extra["following"] = (layer + 1) % LAYERS
            if boundary:
                extra["embedding"] = embedding
        blocks = (kv, *arrived)
        if step == steps - 1:
            begun = turned = turn_split(
                place, vec, forward_weights, backward_weights, layer, state_split, blocks, pre,
                stat_pre, first_end_split, cotangent, row_len,
            )
        else:
            begun = forward_split(
                place, vec, forward_weights, last=layer, state=state_split,
                prev=blocks, pre=pre, **extra,
            )
        saved_split.append(
            {
                "pre": pre, "kv": blocks, "stat_pre": stat_pre,
                "post": begun["post"], "stat_post": begun["stat_post"],
            }
        )
        if step == steps - 1:
            answer_split = begun["answer"]
        else:
            state_split = begun["result"]
        if boundary:
            first_end_split = state_split
            state_split = begun["begun"]

    sums = [None] * LAYERS
    early = None
    grad = None
    ended = None
    for step in reversed(range(steps)):
        layer = step % LAYERS
        between = step == LAYERS - 1
        option = {}
        if between:
            option = {"cotangent": cotangent, "row_len": row_len}
        if ended is not None:
            last = (step + 1) % LAYERS
            option |= {
                "last": last, "ended": ended, "sums": sums[last], "keep": between,
                "final": step == 0,
            }
        begun = turned
        if step < steps - 1:
            begun = backward_split(
                place, vec, backward_weights, following=layer, begun=saved_split[step], **option
            )
        if ended is not None:
            if step == 0:
                others = {"wire": begun["wire"], "vec": begun["sum_vec"]}
            else:
                sums[last] |= {"sum_qkv": begun["sum_qkv"], "sum_vec": begun["sum_vec"]}
            if between:
                second_split = begun["result"]
        arrived = [swap(begun[f"away_{hop}"], hop) for hop in range(1, 4)]
        five = {
            "post": saved_split[step]["post"], "hidden": begun["hidden"], "low": begun["low"],
            "middle": begun["middle"], "vec": begun["vec_out"],
        }
        source = {}
        if step == steps - 1:
            moved_answer = [answer[0]] + [None] * 3
            waiting = [(answer, moved_answer, hop) for hop in range(1, 4)]
            source["tokens"] = moved_top
        elif between:
            moved_second = [second[0]] + [None] * 3
            waiting += [(second, moved_second, hop) for hop in range(1, 4)]
            source["tokens"] = moved_top
        riders, waiting = waiting[:2], waiting[2:]
        riding = [swap(blocks[hop], hop) for blocks, _, hop in riders]
        if grad is not None:
            source["grad"] = grad
        if step < LAYERS:
            source |= {"half": half, "digits": step == 1}
        source |= {"base": sums[layer], "keep": step > 0, "travel": step in (0, LAYERS)}
        fixed = (layer, place, saved[step], vec, backward_weights, five)
        if step == 0:
            early = sum_cores(*early)
            grad, early = tie((grad, early))
            source["grad"] = grad
            half_way = backward_rows(*fixed, ffn_only=True, **source)
            early = sum_chips(early)
            half_way, early, arrived = tie((half_way, early, arrived))
            early = share_chips(early)
            late_ffn = sum_cores(half_way["keep"], swap(half_way["give"], 1))
            half_way, late_ffn = tie((half_way, late_ffn))
            closing = {name: begun[name] for name in ("middle_out", "query_out", "own_out")}
            closing |= {"arrived": arrived, "pre": saved_split[step]["pre"]}
            closing["stat_pre"] = saved_split[step]["stat_pre"]
            kept = backward_rows(
                *fixed, part_done=half_way, closing=closing, others=others, **source
            )
            kept["keep"], early = tie((kept["keep"], early))
            for block, (_, target, hop) in zip(riding, riders):
                target[hop] = block
            first = [kept[f"travel_{hop}"] for hop in range(4)]
            break
        kept = backward_rows(*fixed, **source)
        grad, arrived = tie((kept["result"], arrived))
        if step == LAYERS:
            second = [kept[f"travel_{hop}"] for hop in range(4)]
        if between:
            arrived, riding, kept["give"] = tie((arrived, riding, kept["give"]))
            early = (kept["keep"], swap(kept["give"], 1))
        else:
            arrived, riding = tie((arrived, riding))
        for block, (_, target, hop) in zip(riding, riders):
            target[hop] = block
        if sums[layer] is None:
            names = ("sum_qkv", "sum_out_low", "sum_up_low", "sum_down_low", "sum_vec")
            sums[layer] = {name: kept[name] for name in names}
        else:
            sums[layer] = {name: kept[name] for name in ("sum_qkv", "sum_vec")}
        ended = {name: begun[name] for name in ("middle_out", "query_out", "own_out")}
        ended |= {"arrived": arrived, "pre": saved_split[step]["pre"]}
        ended["stat_pre"] = saved_split[step]["stat_pre"]
    moved_first = swap_blocks(first)
    first_split = kept["split_result"]

    part = jnp.concatenate(
        [
            late_ffn,
            sum_cores(kept["keep"], swap(kept["give"], 1)),
        ],
        axis=1,
    )
    early_other = swap(early, 1)
    part, moved_first, early, early_other = tie(
        (sum_chips(part), moved_first, early, early_other)
    )
    late = share_chips(part)
    done = finish_tokens(
        place, (early, early_other), moved_answer, answer_split, moved_first, first_split,
        moved_second, second_split, hidden, groups, float(row_len),
    )
    late, done = tie((late, done))
    more = finish_weights(place, (late, swap(late, 1)), done, width, hidden)
    return (
        done["block_output"],
        done["input_grad"],
        done["embed_grad"],
        more["qkv"],
        more["out"],
        more["out_b"],
        more["up"],
        more["up_b"],
        more["down"],
        more["down_b"],
        more["gain"],
        more["shift"],
    )


def solution(mesh):
    if mesh.shape["seq"] == 4:
        fine = Mesh(mesh.devices.reshape(-1, 2, 2), ("dp", "y", "core"))
        return jax.shard_map(
            fast_device,
            mesh=fine,
            in_specs=(
                P("dp", SEQ, None),
                P("dp", SEQ, None),
                P("dp", SEQ, None),
                P(),
                P(),
                P(),
                P(),
                P(),
                P(),
                P(),
                P(),
                P(),
                P("dp", None),
                P("dp"),
                P("dp"),
            ),
            out_specs=(
                P("dp", SEQ, None),
                P("dp", SEQ, None),
                P("dp", SEQ, None),
                P(),
                P(),
                P(),
                P(),
                P(),
                P(),
                P(),
                P(),
                P(),
            ),
            check_vma=False,
        )
    return jax.shard_map(
        on_device,
        mesh=mesh,
        in_specs=(
            P("dp", "seq", None),
            P("dp", "seq", None),
            P("dp", "seq", None),
            P(),
            P(),
            P(),
            P(),
            P(),
            P(),
            P(),
            P(),
            P(),
            P("dp", None),
            P("dp"),
            P("dp"),
        ),
        out_specs=(
            P("dp", "seq", None),
            P("dp", "seq", None),
            P("dp", "seq", None),
            P(),
            P(),
            P(),
            P(),
            P(),
            P(),
            P(),
            P(),
            P(),
        ),
        check_vma=False,
    )
```
